128 devices in a mesh: dp: 32 (over z, y, core), mp: 4 (over x).
Axes of the slice: x: 4, y: 4, z: 4, core: 2. Of those that a mesh axis runs over, the one named last changes fastest.
Arguments:
- tokens: bfloat16 [16384, 2048], P(('dp', 'mp')), may hold values from -6 to 6
- cotangent: bfloat16 [16384, 2048], P(('dp', 'mp')), may hold values from -6 to 6
- token_grouped_position: int32 [16384], replicated, may hold values from 0 to 16383, as said below
- sequence_lengths: int32 [32, 3], P('dp'), may hold values from 1 to 384, 512 in all within a row
- adapter_index_per_seq: int32 [32, 3], P('dp'), may hold values from 0 to 7
- mixer_norm_gain: float32 [2048], replicated, may hold values from 0.25 to 1.75
- query_key_matrix: bfloat16 [2, 2048, 2048], P(None, None, 'mp'), may hold values from -0.125 to 0.125
- value_gate_matrix: bfloat16 [2, 2048, 4096], P(None, None, 'mp'), may hold values from -0.125 to 0.125
- decay_step_matrix: bfloat16 [2, 2048, 16], P(None, None, 'mp'), may hold values from -0.125 to 0.125
- query_key_filters: float32 [2, 4, 2048], P(None, None, 'mp'), may hold values from -0.6 to 1
- value_filters: float32 [4, 4096], P(None, 'mp'), may hold values from -0.6 to 1
- decay_scale_logarithm: float32 [16], P('mp'), may hold values from -1 to 1.5
- decay_step_bias: float32 [16], P('mp'), may hold values from -6 to -2.5
- head_output_norm_gain: float32 [256], replicated, may hold values from 0.25 to 1.75
- output_matrix: bfloat16 [4096, 2048], P('mp'), may hold values from -0.1875 to 0.1875
- feedfwd_norm_gain: float32 [2048], replicated, may hold values from 0.25 to 1.75
- gate_up_matrix: bfloat16 [2, 2048, 5632], P(None, None, 'mp'), may hold values from -0.125 to 0.125
- down_matrix: bfloat16 [5632, 2048], P('mp'), may hold values from -0.109375 to 0.109375
- adapter_mixer_first: bfloat16 [2048, 768], replicated, may hold values from -0.125 to 0.125
- adapter_query_key_second: bfloat16 [2, 128, 2048], P(None, None, 'mp'), may hold values from -0.75 to 0.75
- adapter_value_gate_second: bfloat16 [2, 128, 4096], P(None, None, 'mp'), may hold values from -0.75 to 0.75
- adapter_decay_step_second: bfloat16 [2, 128, 16], P(None, None, 'mp'), may hold values from -1.5 to 1.5
- adapter_output_first: bfloat16 [4096, 128], P('mp'), may hold values from -0.1875 to 0.1875
- adapter_output_second: bfloat16 [128, 2048], replicated, may hold values from -0.75 to 0.75
- adapter_feedfwd_first: bfloat16 [2048, 256], replicated, may hold values from -0.125 to 0.125
- adapter_gate_up_second: bfloat16 [2, 128, 5632], P(None, None, 'mp'), may hold values from -0.75 to 0.75
- adapter_down_first: bfloat16 [5632, 128], P('mp'), may hold values from -0.109375 to 0.109375
- adapter_down_second: bfloat16 [128, 2048], replicated, may hold values from -0.75 to 0.75
Outputs:
- block_out: bfloat16 [16384, 2048], P(('dp', 'mp'))
- grad_tokens: bfloat16 [16384, 2048], P(('dp', 'mp'))
- grad_lora_in: float32 [2048, 768], P(None, ('dp', 'mp'))
- grad_lora_qk: float32 [2, 128, 2048], P(None, 'dp', 'mp')
- grad_lora_vg: float32 [2, 128, 4096], P(None, 'dp', 'mp')
- grad_lora_ab: float32 [2, 128, 16], P(None, 'dp', 'mp')
- grad_lora_out_in: float32 [4096, 128], P('mp', 'dp')
- grad_lora_out: float32 [128, 2048], P(None, ('dp', 'mp'))
- grad_lora_ffn_in: float32 [2048, 256], P(None, ('dp', 'mp'))
- grad_lora_gu: float32 [2, 128, 5632], P(None, 'dp', 'mp')
- grad_lora_down_in: float32 [5632, 128], P('mp', 'dp')
- grad_lora_down: float32 [128, 2048], P(None, ('dp', 'mp'))
The draws below stay inside these ranges and needn't reach their ends.
Inputs may be any that keep to these rules, and one draw needn't show every extreme that they name: `token_grouped_position`: a permutation of the grouped positions; each device's 128 tokens go exactly 4 to each group, all to the device of that group with the same mp index. `sequence_lengths`: each group's lengths sum to 512; its longest is 384.
All inputs are finite; a program needn't handle non-finite values.
Results may differ from the reference program's by a relative error of at most 0.028.
Values may be sent and summed in bfloat16 or wider, within the bound.
A program may use at most 256 MiB of HBM per device.

```python
import math
import jax
import jax.numpy as jnp
import numpy as np
from jax import lax

MODEL_WIDTH = 2048
HEAD_COUNT = 16
DV = 256
FEEDFWD_UNITS = 5632
CONV = 4
ADAPTER_RANK = 16
NADAPT = 8
SPAN = 64
SEQ_GROUP = 3
TOK_DEV = 128
GROUP_TOK = 512
LONGEST = 384
TOKENS = 16384
ADAPTER_COLUMNS = 128
KEY_WIDTH = 2048
VALUE_WIDTH = 4096
N_DP = 32
N_MP = 4


def draw_token_grouped_position(key, part):
    share = TOK_DEV // N_DP
    first_keys = jax.random.split(jax.random.fold_in(key, 11), N_DP * N_MP)
    second_keys = jax.random.split(jax.random.fold_in(key, 23), N_DP * N_MP)
    picked = jax.vmap(lambda one: jax.random.permutation(one, TOK_DEV))(first_keys).reshape(N_DP, N_MP, TOK_DEV).astype(jnp.int32)
    slot_order = jax.vmap(lambda one: jax.random.permutation(one, TOK_DEV))(second_keys).reshape(N_DP, N_MP, TOK_DEV).astype(jnp.int32)
    counter = jnp.arange(TOK_DEV, dtype=jnp.int32)
    source = jnp.arange(N_DP, dtype=jnp.int32)
    model_place = jnp.arange(N_MP, dtype=jnp.int32)
    dest_group = counter // share
    incoming = source[:, None] * share + counter[None, :] % share
    slot = slot_order[dest_group[None, None, :], model_place[None, :, None], incoming[:, None, :]]
    target = (dest_group[None, None, :] * N_MP + model_place[None, :, None]) * TOK_DEV + slot
    route = jnp.zeros((N_DP, N_MP, TOK_DEV), jnp.int32)
    route = route.at[source[:, None, None], model_place[None, :, None], picked].set(target)
    return route.reshape(-1)


def plant(values, rng, low, largest):
    shape = values.shape
    spot = [jax.random.randint(jax.random.fold_in(rng, axis), (), 0, shape[axis]) for axis in range(len(shape))]
    values = values.at[tuple(spot)].set(low)
    longest = shape.index(max(shape))
    spot[longest] = (spot[longest] + 1) % shape[longest]
    return values.at[tuple(spot)].set(largest)


def steps_of(stream_key, dims, pieces, smallest, top_value):
    factor_of = 1.0
    for dim, parts in pieces:
        steps = jax.random.uniform(jax.random.fold_in(jax.random.fold_in(stream_key, 6), dim), (parts,), jnp.float32, smallest / len(pieces), top_value / len(pieces))
        factor_of = factor_of * jnp.repeat(jnp.exp(steps), dims[dim] // parts).reshape((-1,) + (1,) * (len(dims) - 1 - dim))
    return factor_of


def profile(amount, total, bound, skew):
    portions = [(1 << 20) // math.isqrt(standing ** skew) + 1 for standing in range(2, amount + 1)]
    rest, given = total - bound - (amount - 1), [1] * (amount - 1)
    while rest > 0:
        movable = [i for i in range(amount - 1) if given[i] < bound]
        whole, left = sum([portions[i] for i in movable]), rest
        for i in movable:
            extra = min(bound - given[i], max(1, left * portions[i] // whole), rest)
            given[i] = given[i] + extra
            rest = rest - extra
    return np.array([bound] + given)


def uneven(own_key, amount, total, limit, slope):
    if amount == 2:
        one = jax.random.randint(own_key, (), max(1, total - limit), min(limit, total - 1) + 1)
        return jnp.stack([one, total - one])
    tallies = jnp.asarray(profile(amount, total, limit, slope), jnp.int32)
    pairs = (amount - 1) // 2
    donor, sink = tallies[1:1 + 2 * pairs:2], tallies[2:2 + 2 * pairs:2]
    slack = jnp.minimum(donor - 1, limit - sink)
    moved = jax.random.randint(jax.random.fold_in(own_key, 1), (pairs,), 0, 1 << 20) % (slack + 1)
    tallies = tallies.at[1:1 + 2 * pairs:2].set(donor - moved).at[2:2 + 2 * pairs:2].set(sink + moved)
    return tallies[jax.random.permutation(jax.random.fold_in(own_key, 2), amount)]


def normal_values(key, shape, width, bound, pieces=(), kind=jnp.bfloat16):
    level = steps_of(key, shape, pieces, -0.22, 0.18) if pieces else 1.0
    entries = jax.random.normal(key, shape, jnp.float32) * width * level
    return jnp.minimum(jnp.maximum(entries, -bound), bound).astype(kind)


def setup_inputs(seed: int = 0) -> dict:
    seeds = jax.random.split(jax.random.key(seed), 29)
    return {
        "tokens": normal_values(seeds[0], (TOKENS, MODEL_WIDTH), 1.0, 6.0, ((0, 128),)),
        "cotangent": normal_values(seeds[1], (TOKENS, MODEL_WIDTH), 1.0, 6.0, ((0, 128),)),
        "token_grouped_position": draw_token_grouped_position(jax.random.fold_in(seeds[28], 71), 0),
        "sequence_lengths": jax.vmap(lambda own: uneven(own, SEQ_GROUP, GROUP_TOK, LONGEST, 1))(jax.random.split(seeds[3], N_DP)).reshape((N_DP, SEQ_GROUP)).astype(jnp.int32),
        "adapter_index_per_seq": plant(jax.random.randint(seeds[4], (N_DP, SEQ_GROUP), 0, NADAPT), jax.random.fold_in(seeds[4], 1), 0, NADAPT - 1).astype(jnp.int32),
        "mixer_norm_gain": jnp.clip(1.0 + 0.15 * jax.random.normal(seeds[5], (MODEL_WIDTH,), jnp.float32), 0.25, 1.75),
        "query_key_matrix": normal_values(seeds[6], (2, MODEL_WIDTH, KEY_WIDTH), MODEL_WIDTH ** -0.5, 0.125, ((2, 4),)),
        "value_gate_matrix": normal_values(seeds[7], (2, MODEL_WIDTH, VALUE_WIDTH), MODEL_WIDTH ** -0.5, 0.125, ((2, 4),)),
        "decay_step_matrix": normal_values(seeds[8], (2, MODEL_WIDTH, HEAD_COUNT), MODEL_WIDTH ** -0.5, 0.125, ((2, 4),)),
        "query_key_filters": jnp.clip(-0.6 + 1.6 * jax.random.uniform(seeds[9], (2, CONV, KEY_WIDTH), jnp.float32) ** steps_of(seeds[9], (2, CONV, KEY_WIDTH), ((2, 4),), -0.2, 0.2), -0.6, 1.0),
        "value_filters": jnp.clip(-0.6 + 1.6 * jax.random.uniform(seeds[10], (CONV, VALUE_WIDTH), jnp.float32) ** steps_of(seeds[10], (CONV, VALUE_WIDTH), ((1, 4),), -0.2, 0.2), -0.6, 1.0),
        "decay_scale_logarithm": jnp.clip(-1.0 + 2.5 * jax.random.uniform(seeds[11], (HEAD_COUNT,), jnp.float32) ** steps_of(seeds[11], (HEAD_COUNT,), ((0, 4),), -0.2, 0.2), -1.0, 1.5),
        "decay_step_bias": jnp.clip(-6.0 + 3.5 * jax.random.uniform(seeds[12], (HEAD_COUNT,), jnp.float32) ** steps_of(seeds[12], (HEAD_COUNT,), ((0, 4),), -0.2, 0.2), -6.0, -2.5),
        "head_output_norm_gain": jnp.clip(1.0 + 0.15 * jax.random.normal(seeds[13], (DV,), jnp.float32), 0.25, 1.75),
        "output_matrix": normal_values(seeds[14], (VALUE_WIDTH, MODEL_WIDTH), (VALUE_WIDTH // 4) ** -0.5, 0.1875, ((0, 4),)),
        "feedfwd_norm_gain": jnp.clip(1.0 + 0.15 * jax.random.normal(seeds[15], (MODEL_WIDTH,), jnp.float32), 0.25, 1.75),
        "gate_up_matrix": normal_values(seeds[16], (2, MODEL_WIDTH, FEEDFWD_UNITS), MODEL_WIDTH ** -0.5, 0.125, ((2, 4),)),
        "down_matrix": normal_values(seeds[17], (FEEDFWD_UNITS, MODEL_WIDTH), (FEEDFWD_UNITS // 2) ** -0.5, 0.109375, ((0, 4),)),
        "adapter_mixer_first": normal_values(seeds[18], (MODEL_WIDTH, 6 * ADAPTER_COLUMNS), MODEL_WIDTH ** -0.5, 0.125),
        "adapter_query_key_second": normal_values(seeds[19], (2, ADAPTER_COLUMNS, KEY_WIDTH), (4 * ADAPTER_RANK) ** -0.5, 0.75, ((2, 4),)),
        "adapter_value_gate_second": normal_values(seeds[20], (2, ADAPTER_COLUMNS, VALUE_WIDTH), (4 * ADAPTER_RANK) ** -0.5, 0.75, ((2, 4),)),
        "adapter_decay_step_second": normal_values(seeds[21], (2, ADAPTER_COLUMNS, HEAD_COUNT), ADAPTER_RANK ** -0.5, 1.5, ((2, 4),)),
        "adapter_output_first": normal_values(seeds[22], (VALUE_WIDTH, ADAPTER_COLUMNS), (VALUE_WIDTH // 4) ** -0.5, 0.1875, ((0, 4),)),
        "adapter_output_second": normal_values(seeds[23], (ADAPTER_COLUMNS, MODEL_WIDTH), (4 * ADAPTER_RANK) ** -0.5, 0.75),
        "adapter_feedfwd_first": normal_values(seeds[24], (MODEL_WIDTH, 2 * ADAPTER_COLUMNS), MODEL_WIDTH ** -0.5, 0.125),
        "adapter_gate_up_second": normal_values(seeds[25], (2, ADAPTER_COLUMNS, FEEDFWD_UNITS), (4 * ADAPTER_RANK) ** -0.5, 0.75, ((2, 4),)),
        "adapter_down_first": normal_values(seeds[26], (FEEDFWD_UNITS, ADAPTER_COLUMNS), (FEEDFWD_UNITS // 2) ** -0.5, 0.109375, ((0, 4),)),
        "adapter_down_second": normal_values(seeds[27], (ADAPTER_COLUMNS, MODEL_WIDTH), (4 * ADAPTER_RANK) ** -0.5, 0.75),
    }


HIGH_PRECISION = lax.Precision.HIGHEST
EPSILON = 1e-06

@jax.custom_vjp
def low(v):
    return lax.optimization_barrier(v.astype(jnp.bfloat16)).astype(jnp.float32)

@jax.custom_vjp
def low_back(v):
    return v

def low_keep(v):
    return (low(v), None)

def low_pass(kept, grad):
    return (grad,)

def back_keep(v):
    return (v, None)

def back_low(kept, grad):
    return (low(grad),)
low.defvjp(low_keep, low_pass)
low_back.defvjp(back_keep, back_low)

def matmul(left, right):
    return jnp.matmul(left, right, precision=HIGH_PRECISION)

def rms_norm(values, gain_vec):
    return values * lax.rsqrt(lax.optimization_barrier(jnp.mean(values * values, axis=-1, keepdims=True)) + EPSILON) * gain_vec

def unit_norm(values):
    return values * lax.rsqrt(lax.optimization_barrier(jnp.sum(values * values, axis=-1, keepdims=True)) + EPSILON)

def short_conv(series, kernel, segment):
    total = series * kernel[0]
    for shift in range(1, kernel.shape[0]):
        moved = jnp.pad(series, ((shift, 0), (0, 0)))[:-shift]
        earlier = jnp.pad(segment, (shift, 0), constant_values=-1)[:-shift]
        total = total + moved * (earlier == segment)[:, None].astype(series.dtype) * kernel[shift]
    return total

def recurrence(queries, key_rows, value_rows, log_decay, beta_gate, segment):
    length, heads, key_size = queries.shape
    fresh = jnp.concatenate([jnp.ones((1,), bool), segment[1:] != segment[:-1]])
    factor = jnp.exp(log_decay) * jnp.where(fresh, 0.0, 1.0)[:, None].astype(queries.dtype)

    def per_token(carried_state, inputs_tuple):
        query_now, key_current, value_now, factor_now, beta_now = inputs_tuple
        carried_state = carried_state * factor_now[:, None, None]
        guess = jnp.einsum('hvk,hk->hv', carried_state, key_current, precision=HIGH_PRECISION)
        carried_state = carried_state + jnp.einsum('hv,hk->hvk', beta_now[:, None] * (value_now - guess), key_current, precision=HIGH_PRECISION)
        return (carried_state, jnp.einsum('hvk,hk->hv', carried_state, query_now, precision=HIGH_PRECISION))

    def per_block(carried_state, inputs_tuple):
        return lax.scan(per_token, carried_state, inputs_tuple)
    count = length // SPAN
    blocks = tuple((array.reshape((count, SPAN) + array.shape[1:]) for array in (queries, key_rows, value_rows, factor, beta_gate)))
    start = jnp.zeros((heads, value_rows.shape[-1], key_size), queries.dtype)
    _, outputs = lax.scan(jax.checkpoint(per_block), start, blocks)
    return outputs.reshape(length, heads, -1)

def mixer(pre_q, pre_k, pre_v, pre_g, pre_a, pre_b, query_key_filters, value_filters, decay_scale_logarithm, decay_step_bias, head_output_norm_gain, segment):
    length = pre_q.shape[0]
    heads = decay_scale_logarithm.shape[0]
    queries = jax.nn.silu(short_conv(pre_q, query_key_filters[0], segment)).reshape(length, heads, -1)
    key_rows = jax.nn.silu(short_conv(pre_k, query_key_filters[1], segment)).reshape(length, heads, -1)
    value_rows = jax.nn.silu(short_conv(pre_v, value_filters, segment)).reshape(length, heads, -1)
    queries = unit_norm(queries) * queries.shape[-1] ** (-0.5)
    key_rows = unit_norm(key_rows)
    log_decay = -jnp.exp(decay_scale_logarithm) * jax.nn.softplus(pre_a + decay_step_bias)
    beta_gate = jax.nn.sigmoid(pre_b)
    output = recurrence(queries, key_rows, value_rows, log_decay, beta_gate, segment)
    gated = rms_norm(output, head_output_norm_gain) * jax.nn.silu(pre_g.reshape(length, heads, -1))
    return gated.reshape(length, -1)

def reference(tokens, cotangent, token_grouped_position, sequence_lengths, adapter_index_per_seq, mixer_norm_gain, query_key_matrix, value_gate_matrix, decay_step_matrix, query_key_filters, value_filters, decay_scale_logarithm, decay_step_bias, head_output_norm_gain, output_matrix, feedfwd_norm_gain, gate_up_matrix, down_matrix, adapter_mixer_first, adapter_query_key_second, adapter_value_gate_second, adapter_decay_step_second, adapter_output_first, adapter_output_second, adapter_feedfwd_first, adapter_gate_up_second, adapter_down_first, adapter_down_second):

    def widen_adapters(array):
        return array.astype(jnp.float32)
    gain_one, gain_two, gain_out = (widen_adapters(mixer_norm_gain), widen_adapters(feedfwd_norm_gain), widen_adapters(head_output_norm_gain))
    weight_qk, weight_vg, weight_ab = (widen_adapters(query_key_matrix), widen_adapters(value_gate_matrix), widen_adapters(decay_step_matrix))
    kernel_qk, kernel_vals = (widen_adapters(query_key_filters), widen_adapters(value_filters))
    scale_log, scale_bias = (widen_adapters(decay_scale_logarithm), widen_adapters(decay_step_bias))
    weight_out, weight_gu, weight_down = (widen_adapters(output_matrix), widen_adapters(gate_up_matrix), widen_adapters(down_matrix))
    position = jnp.arange(GROUP_TOK, dtype=jnp.int32)
    ends = jnp.cumsum(sequence_lengths, axis=1)
    segment = lax.optimization_barrier(jnp.sum((position[None, :, None] >= ends[:, None, :]).astype(jnp.int32), axis=2)).astype(jnp.int32)
    which = jnp.take_along_axis(adapter_index_per_seq, segment, axis=1)
    adapter_selection = (jnp.arange(ADAPTER_COLUMNS, dtype=jnp.int32)[None, None, :] // ADAPTER_RANK == which[..., None]).astype(jnp.float32)
    inverse = jnp.argsort(token_grouped_position).astype(jnp.int32)

    def block(resid, seg_rows, select_rows, adapters):
        a_in, b_qk, b_vg, b_ab, a_out, b_out, a_ffn, b_gu, a_down, b_down = adapters
        normed = low(rms_norm(resid, gain_one))
        adapter_activations = low(low_back(matmul(normed, a_in) * jnp.tile(select_rows, (1, 6))))

        def project(weight, place, second):
            return low_back(matmul(normed, weight) + matmul(adapter_activations[:, place * ADAPTER_COLUMNS:(place + 1) * ADAPTER_COLUMNS], second))
        pre_q = project(weight_qk[0], 0, b_qk[0])
        pre_k = project(weight_qk[1], 1, b_qk[1])
        pre_v = project(weight_vg[0], 2, b_vg[0])
        pre_g = project(weight_vg[1], 3, b_vg[1])
        pre_a = project(weight_ab[0], 4, b_ab[0])
        pre_b = project(weight_ab[1], 5, b_ab[1])
        mixer_output = low(mixer(pre_q, pre_k, pre_v, pre_g, pre_a, pre_b, kernel_qk, kernel_vals, scale_log, scale_bias, gain_out, seg_rows))
        output_adapter_activations = low(low_back(matmul(mixer_output, a_out) * select_rows))
        middle_rows = resid + low_back(matmul(mixer_output, weight_out) + matmul(output_adapter_activations, b_out))
        normed_two = low(rms_norm(middle_rows, gain_two))
        feedfwd_adapter_activations = low(low_back(matmul(normed_two, a_ffn) * jnp.tile(select_rows, (1, 2))))
        gate_activation = low_back(matmul(normed_two, weight_gu[0]) + matmul(feedfwd_adapter_activations[:, :ADAPTER_COLUMNS], b_gu[0]))
        up_activation = low_back(matmul(normed_two, weight_gu[1]) + matmul(feedfwd_adapter_activations[:, ADAPTER_COLUMNS:], b_gu[1]))
        hidden_units = low(jax.nn.silu(gate_activation) * up_activation)
        down_adapter_activations = low(low_back(matmul(hidden_units, a_down) * select_rows))
        return middle_rows + low_back(matmul(hidden_units, weight_down) + matmul(down_adapter_activations, b_down))

    def forward(inputs, *adapters):
        grouped = inputs[inverse].reshape(N_DP, GROUP_TOK, MODEL_WIDTH)

        def one_group(group_items):
            return block(group_items[0], group_items[1], group_items[2], adapters)
        done = lax.map(one_group, (grouped, segment, adapter_selection))
        return done.reshape(TOKENS, MODEL_WIDTH)[token_grouped_position]
    primal_inputs = (widen_adapters(tokens), widen_adapters(adapter_mixer_first), widen_adapters(adapter_query_key_second), widen_adapters(adapter_value_gate_second), widen_adapters(adapter_decay_step_second), widen_adapters(adapter_output_first), widen_adapters(adapter_output_second), widen_adapters(adapter_feedfwd_first), widen_adapters(adapter_gate_up_second), widen_adapters(adapter_down_first), widen_adapters(adapter_down_second))
    result, pullback = jax.vjp(forward, *primal_inputs)
    grads = pullback(widen_adapters(cotangent))
    return (result.astype(jnp.bfloat16), grads[0].astype(jnp.bfloat16), grads[1], grads[2], grads[3], grads[4], grads[5], grads[6], grads[7], grads[8], grads[9], grads[10])
```

```python
import functools
import jax
import jax.numpy as jnp
from jax import lax
from jax.experimental import pallas as pl
from jax.experimental.pallas import tpu as pltpu
from jax.sharding import PartitionSpec as P

EPSILON = 1e-06
F32 = jnp.float32
BF16 = jnp.bfloat16
CH = 128
BASE = 16
DK = 128
DVAL = 256
INV_ROOT = DK ** -0.5


def mm(a, b):
    return jnp.dot(a.astype(BF16), b.astype(BF16), preferred_element_type=F32)


def mm_nt(a, b):
    return lax.dot_general(a.astype(BF16), b.astype(BF16), (((1,), (1,)), ((), ())), preferred_element_type=F32)


def mm_tn(a, b):
    return lax.dot_general(a.astype(BF16), b.astype(BF16), (((0,), (0,)), ((), ())), preferred_element_type=F32)


def exact_tn(a, b):
    b1 = b.astype(BF16)
    r1 = b - b1.astype(F32)
    b2 = r1.astype(BF16)
    b3 = (r1 - b2.astype(F32)).astype(BF16)
    return mm_tn(a, b1) + mm_tn(a, b2) + mm_tn(a, b3)


def iota2(shape, dim):
    return lax.broadcasted_iota(jnp.int32, shape, dim)


def sigmoid(x):
    return 1.0 / (1.0 + jnp.exp(-x))


def conv_rows(x, taps, masks_ref, length):
    total = x * taps[0:1]
    for shift in range(1, 4):
        total = total + pltpu.roll(x, shift, 0) * masks_ref[shift - 1] * taps[shift : shift + 1]
    return total


def conv_rows_back(d, taps, masks_ref, length):
    total = d * taps[0:1]
    for shift in range(1, 4):
        total = total + pltpu.roll(d * masks_ref[shift - 1], length - shift, 0) * taps[shift : shift + 1]
    return total


def gate_columns(ab, dsl, bias):
    z = ab + bias
    soft = jnp.maximum(z, 0.0) + jnp.log1p(jnp.exp(-jnp.abs(z)))
    return -jnp.exp(dsl) * soft, z


def base_inverse(mats):
    nb = CH // BASE
    lane = iota2((1, CH), 1)
    lane_masks = [(lane // BASE == b).astype(F32) for b in range(nb)]
    packed = []
    for a in mats:
        d = a[0:BASE] * lane_masks[0]
        for b in range(1, nb):
            d = d + a[b * BASE : (b + 1) * BASE] * lane_masks[b]
        packed.append(d)
    d = jnp.concatenate(packed, axis=0)
    hi = d.astype(BF16)
    lo = (d - hi.astype(F32)).astype(BF16)
    row = iota2((CH, CH), 0)
    col = iota2((CH, CH), 1)
    same = row // BASE == col // BASE
    spread = jnp.concatenate(
        [(same & (row % BASE == j)).astype(BF16) for j in range(BASE - 1)], axis=1
    )
    wide = mm(hi, spread) + mm(lo, spread)
    sub = iota2((BASE, CH), 0)
    eye = (sub == iota2((BASE, CH), 1) % BASE).astype(F32)
    out = []
    for n in range(len(mats)):
        t = eye
        for j in range(BASE - 1):
            t = t - wide[n * BASE : (n + 1) * BASE, j * CH : (j + 1) * CH] * t[j : j + 1]
        out.append(jnp.concatenate([t * lane_masks[b] for b in range(nb)], axis=0))
    return out


def full_inverse(mats):
    ts = base_inverse(mats)
    row = iota2((CH, CH), 0)
    col = iota2((CH, CH), 1)
    size = BASE
    while size < CH:
        pick = ((row // size) % 2 == 1) & (col // size == row // size - 1)
        steps = [mm(jnp.where(pick, a, 0.0), t) for a, t in zip(mats, ts)]
        ts = [t - mm(t, s) for t, s in zip(ts, steps)]
        size *= 2
    return ts


def mixer_fwd_kernel(
    heads, preq, prek, prev, preg, ab_ref, masks, segc, segr, taps_q, taps_k, taps_v, gate_par, gain,
    mixed, cq, ck, cv, t_out, s_out, u_out, o_out,
    qn, kn, vn, cum_s, state,
):
    length = preq.shape[0]
    count = length // CH

    def key_tile(h, carry):
        cols = pl.ds(pl.multiple_of(h * DK, DK), DK)
        for src, taps, save, dst, scale in ((preq, taps_q, cq, qn, INV_ROOT), (prek, taps_k, ck, kn, 1.0)):
            c = conv_rows(src[:, cols], taps[:, cols], masks, length)
            save[:, cols] = c.astype(BF16)
            u = c * sigmoid(c)
            n = lax.rsqrt(jnp.sum(u * u, axis=-1, keepdims=True) + EPSILON) * scale
            dst[:, cols] = (u * n).astype(BF16)
        for half in range(2):
            vcols = pl.ds(pl.multiple_of(h * DVAL + half * DK, DK), DK)
            c = conv_rows(prev[:, vcols], taps_v[:, vcols], masks, length)
            cv[:, vcols] = c.astype(BF16)
            vn[:, vcols] = c * sigmoid(c)
        return carry

    lax.fori_loop(0, heads, key_tile, 0)
    row = iota2((CH, CH), 0)
    col = iota2((CH, CH), 1)
    upper = (row <= col).astype(BF16)
    log_decay, _ = gate_columns(ab_ref[...], gate_par[0:1], gate_par[1:2])
    beta_all = sigmoid(ab_ref[...])
    for n in range(count):
        cum_s[n * CH : (n + 1) * CH] = exact_tn(upper, log_decay[n * CH : (n + 1) * CH])
    cum_s[length : length + CH] = jnp.zeros((CH, DK), F32)
    for h in range(heads):
        state[h] = jnp.zeros((DK, DVAL), F32)

    for n in range(count):
        r = pl.ds(n * CH, CH)
        seg_col = segc[r]
        seg_row = segr[0:1, n * CH : (n + 1) * CH]
        keep = (seg_col == seg_row) & (row >= col)
        keepf = keep.astype(F32)
        strict = (row > col).astype(F32)
        cum = cum_s[r]
        cum_t = cum.T
        beta_c = beta_all[n * CH : (n + 1) * CH]
        prev_last = segc[n * CH - 1 : n * CH] if n else jnp.full((1, CH), -1.0, F32)
        start = jnp.exp(cum) * (seg_col == prev_last).astype(F32)
        last_seg = segc[(n + 1) * CH - 1 : (n + 1) * CH]
        tail = jnp.exp(cum[CH - 1 : CH] - cum) * (seg_col == last_seg).astype(F32)
        mats, scores = [], []
        for h in range(heads):
            q = qn[r, h * DK : (h + 1) * DK]
            k = kn[r, h * DK : (h + 1) * DK]
            ratio = jnp.exp(jnp.minimum(cum[:, h : h + 1] - cum_t[h : h + 1], 0.0)) * keepf
            beta = beta_c[:, heads + h : heads + h + 1]
            both = mm_nt(jnp.concatenate([q, k], axis=0), k)
            scores.append((ratio * both[:CH]).astype(BF16))
            mats.append(beta * ratio * strict * both[CH:])
        ts = full_inverse(mats)
        for h in range(heads):
            q = qn[r, h * DK : (h + 1) * DK]
            k = kn[r, h * DK : (h + 1) * DK]
            vcols = slice(h * DVAL, (h + 1) * DVAL)
            beta = beta_c[:, heads + h : heads + h + 1]
            st = start[:, h : h + 1]
            tb = ts[h].astype(BF16)
            s0 = state[h]
            s0b = s0.astype(BF16)
            t_out[n, h] = tb
            s_out[n, h] = s0b
            both = mm(jnp.concatenate([q, k], axis=0), s0b)
            res = beta * (vn[r, vcols] - st * both[CH:])
            un = mm(tb, res).astype(BF16)
            u_out[r, vcols] = un
            o = st * both[:CH] + mm(scores[h], un)
            state[h] = start[CH - 1 : CH, h : h + 1] * s0 + mm_tn(k.astype(F32) * tail[:, h : h + 1], un)
            o_out[r, vcols] = o.astype(BF16)
            g = preg[r, vcols]
            rn = lax.rsqrt(jnp.mean(o * o, axis=-1, keepdims=True) + EPSILON)
            mixed[r, vcols] = (o * rn * gain[...] * (g * sigmoid(g))).astype(BF16)


def mixer_fwd(preq, prek, prev, preg, ab, masks, segc, segr, taps_q, taps_k, taps_v, gate_par, gain):
    length = preq.shape[0]
    heads = preq.shape[1] // DK
    count = length // CH
    vm = pl.BlockSpec(memory_space=pltpu.VMEM)
    out_shape = (
        jax.ShapeDtypeStruct((length, heads * DVAL), BF16),
        jax.ShapeDtypeStruct((length, heads * DK), BF16),
        jax.ShapeDtypeStruct((length, heads * DK), BF16),
        jax.ShapeDtypeStruct((length, heads * DVAL), BF16),
        jax.ShapeDtypeStruct((count, heads, CH, CH), BF16),
        jax.ShapeDtypeStruct((count, heads, DK, DVAL), BF16),
        jax.ShapeDtypeStruct((length, heads * DVAL), BF16),
        jax.ShapeDtypeStruct((length, heads * DVAL), BF16),
    )
    return pl.pallas_call(
        functools.partial(mixer_fwd_kernel, heads),
        out_shape=out_shape,
        in_specs=[vm] * 13,
        out_specs=[vm] * len(out_shape),
        scratch_shapes=[
            pltpu.VMEM((length, heads * DK), BF16),
            pltpu.VMEM((length, heads * DK), BF16),
            pltpu.VMEM((length, heads * DVAL), F32),
            pltpu.VMEM((length + CH, CH), F32),
            pltpu.VMEM((heads, DK, DVAL), F32),
        ],
        compiler_params=pltpu.CompilerParams(vmem_limit_bytes=60 * 2**20),
        name="mixer_forward",
    )(preq, prek, prev, preg, ab, masks, segc, segr, taps_q, taps_k, taps_v, gate_par, gain)


def mixer_bwd_kernel(
    heads, dmix, preg, ab_ref, masks, segc, segr, taps_q, taps_k, taps_v, gate_par, gain,
    cq, ck, cv, t_in, s_in, u_in, o_in,
    dpq, dpk, dpv, dpg, dab,
    qn, kn, vn, cum_s, dstate, dqs, dks, dvs, gcol,
):
    length = dmix.shape[0]
    count = length // CH

    def key_tile(h, carry):
        cols = pl.ds(pl.multiple_of(h * DK, DK), DK)
        for save, dst, scale in ((cq, qn, INV_ROOT), (ck, kn, 1.0)):
            c = save[:, cols].astype(F32)
            u = c * sigmoid(c)
            n = lax.rsqrt(jnp.sum(u * u, axis=-1, keepdims=True) + EPSILON) * scale
            dst[:, cols] = (u * n).astype(BF16)
        for half in range(2):
            vcols = pl.ds(pl.multiple_of(h * DVAL + half * DK, DK), DK)
            c = cv[:, vcols].astype(F32)
            vn[:, vcols] = c * sigmoid(c)
        return carry

    lax.fori_loop(0, heads, key_tile, 0)
    row = iota2((CH, CH), 0)
    col = iota2((CH, CH), 1)
    upper = (row <= col).astype(BF16)
    lower = (row >= col).astype(BF16)
    log_decay, z_all = gate_columns(ab_ref[...], gate_par[0:1], gate_par[1:2])
    beta_all = sigmoid(ab_ref[...])
    for n in range(count):
        cum_s[n * CH : (n + 1) * CH] = exact_tn(upper, log_decay[n * CH : (n + 1) * CH])
    for h in range(heads):
        dstate[h] = jnp.zeros((DK, DVAL), F32)
    lane = iota2((1, CH), 1)
    strict = (row > col).astype(F32)
    ones = jnp.ones((CH, CH), BF16)

    for n in range(count - 1, -1, -1):
        r = pl.ds(n * CH, CH)
        seg_col = segc[r]
        seg_row = segr[0:1, n * CH : (n + 1) * CH]
        keepf = ((seg_col == seg_row) & (row >= col)).astype(F32)
        cum = cum_s[r]
        cum_t = cum.T
        beta_c = beta_all[n * CH : (n + 1) * CH]
        prev_last = segc[n * CH - 1 : n * CH] if n else jnp.full((1, CH), -1.0, F32)
        start = jnp.exp(cum) * (seg_col == prev_last).astype(F32)
        last_seg = segc[(n + 1) * CH - 1 : (n + 1) * CH]
        tail = jnp.exp(cum[CH - 1 : CH] - cum) * (seg_col == last_seg).astype(F32)
        dcum_all = jnp.zeros((CH, CH), F32)
        dbeta_all = jnp.zeros((CH, CH), F32)
        dlast_all = jnp.zeros((1, CH), F32)
        for h in range(heads):
            qc = slice(h * DK, (h + 1) * DK)
            vcols = slice(h * DVAL, (h + 1) * DVAL)
            here = (lane == h).astype(F32)
            o = o_in[r, vcols].astype(F32)
            g = preg[r, vcols]
            dm = dmix[r, vcols]
            sg = sigmoid(g)
            rn = lax.rsqrt(jnp.mean(o * o, axis=-1, keepdims=True) + EPSILON)
            on = o * rn
            y = on * gain[...]
            dpg[r, vcols] = (dm * y * (sg * (1.0 + g * (1.0 - sg)))).astype(BF16)
            dy = dm * (g * sg) * gain[...]
            do = rn * (dy - on * jnp.mean(dy * on, axis=-1, keepdims=True))
            dob = do.astype(BF16)
            q = qn[r, qc]
            k = kn[r, qc]
            kf = k.astype(F32)
            qf = q.astype(F32)
            un = u_in[r, vcols]
            s0 = s_in[n, h]
            tb = t_in[n, h]
            beta = beta_c[:, heads + h : heads + h + 1]
            st = start[:, h : h + 1]
            tl = tail[:, h : h + 1]
            carry_scale = start[CH - 1 : CH, h : h + 1]
            ratio = jnp.exp(jnp.minimum(cum[:, h : h + 1] - cum_t[h : h + 1], 0.0)) * keepf
            both = mm_nt(jnp.concatenate([q, k], axis=0), k)
            scores = ratio * both[:CH]
            rs = ratio * strict
            amat = rs * both[CH:]
            qk_state = mm(jnp.concatenate([q, k], axis=0), s0)
            ks = qk_state[CH:]
            ds1 = dstate[h]
            ds1b = ds1.astype(BF16)
            ktail = (kf * tl).astype(BF16)
            dun = mm_tn(scores, dob) + mm(ktail, ds1b)
            dres = mm_tn(tb, dun)
            dresb = dres.astype(BF16)
            dks0 = (-(beta * st) * dres).astype(BF16)
            qst = (qf * st).astype(BF16)
            dstate[h] = carry_scale * ds1 + mm_tn(jnp.concatenate([qst, k], axis=0), jnp.concatenate([dob, dks0], axis=0))
            both_d = mm_nt(jnp.concatenate([dob, dresb], axis=0), un)
            dscore = both_d[:CH]
            da = -both_d[CH:]
            dqk = (dscore * ratio).astype(BF16)
            dkk = (da * beta * rs).astype(BF16)
            dspread = dscore * scores + da * beta * amat
            dbeta = jnp.sum(da * amat, axis=-1, keepdims=True) + jnp.sum(
                dres * (vn[r, vcols] - st * ks), axis=-1, keepdims=True
            )
            dvs[r, vcols] = beta * dres
            by_state = mm_nt(jnp.concatenate([dob, dks0, un], axis=0), jnp.concatenate([s0, ds1b], axis=0))
            dq_state = by_state[:CH, :DK]
            dq = st * dq_state + mm(dqk, k)
            dktail = by_state[2 * CH :, DK:]
            dk = (
                by_state[CH : 2 * CH, :DK]
                + tl * dktail
                + mm_tn(dqk, q)
                + mm(dkk, k)
                + mm_tn(dkk, k)
            )
            dqs[r, qc] = dq
            dks[r, qc] = dk
            dstart_s = st * jnp.sum(qf * dq_state, axis=-1, keepdims=True) + st * (
                -beta * jnp.sum(dres * ks, axis=-1, keepdims=True)
            )
            dtail_s = tl * jnp.sum(kf * dktail, axis=-1, keepdims=True)
            dcarry = carry_scale * jnp.sum(jnp.sum(ds1 * s0.astype(F32), axis=-1, keepdims=True), axis=0, keepdims=True)
            colsum = exact_cols(dspread, ones)
            dcum = jnp.sum(dspread, axis=-1, keepdims=True) - colsum[:, 0:1] + dstart_s - dtail_s
            dlast = jnp.sum(dtail_s, axis=0, keepdims=True) + dcarry
            dcum_all = dcum_all + dcum * here
            dlast_all = dlast_all + dlast * here
            dbeta_all = dbeta_all + dbeta * (lane == heads + h).astype(F32)
        dcum_all = dcum_all + dlast_all * (row == CH - 1).astype(F32)
        gcol[r] = exact_tn(lower, dcum_all) + dbeta_all * beta_c * (1.0 - beta_c)

    slope = -jnp.exp(gate_par[0:1]) * sigmoid(z_all)
    dab[...] = (gcol[...] * jnp.where(lane < heads, slope, 1.0)).astype(BF16)

    def back_tile(h, carry):
        cols = pl.ds(pl.multiple_of(h * DK, DK), DK)
        for save, dsrc, taps, dst, scale in ((cq, dqs, taps_q, dpq, INV_ROOT), (ck, dks, taps_k, dpk, 1.0)):
            c = save[:, cols].astype(F32)
            sg = sigmoid(c)
            u = c * sg
            n = lax.rsqrt(jnp.sum(u * u, axis=-1, keepdims=True) + EPSILON)
            un = u * n
            d = dsrc[:, cols] * scale
            du = n * (d - un * jnp.sum(d * un, axis=-1, keepdims=True))
            dc = du * (sg * (1.0 + c * (1.0 - sg)))
            dst[:, cols] = conv_rows_back(dc, taps[:, cols], masks, length).astype(BF16)
        for half in range(2):
            vcols = pl.ds(pl.multiple_of(h * DVAL + half * DK, DK), DK)
            c = cv[:, vcols].astype(F32)
            sg = sigmoid(c)
            dc = dvs[:, vcols] * (sg * (1.0 + c * (1.0 - sg)))
            dpv[:, vcols] = conv_rows_back(dc, taps_v[:, vcols], masks, length).astype(BF16)
        return carry

    lax.fori_loop(0, heads, back_tile, 0)


def exact_cols(x, ones):
    hi = x.astype(BF16)
    lo = (x - hi.astype(F32)).astype(BF16)
    return mm_tn(hi, ones) + mm_tn(lo, ones)


def mixer_bwd(dmix, preg, ab, masks, segc, segr, taps_q, taps_k, taps_v, gate_par, gain, saved):
    length = dmix.shape[0]
    heads = dmix.shape[1] // DVAL
    vm = pl.BlockSpec(memory_space=pltpu.VMEM)
    out_shape = (
        jax.ShapeDtypeStruct((length, heads * DK), BF16),
        jax.ShapeDtypeStruct((length, heads * DK), BF16),
        jax.ShapeDtypeStruct((length, heads * DVAL), BF16),
        jax.ShapeDtypeStruct((length, heads * DVAL), BF16),
        jax.ShapeDtypeStruct((length, CH), BF16),
    )
    return pl.pallas_call(
        functools.partial(mixer_bwd_kernel, heads),
        out_shape=out_shape,
        in_specs=[vm] * 18,
        out_specs=[vm] * len(out_shape),
        scratch_shapes=[
            pltpu.VMEM((length, heads * DK), BF16),
            pltpu.VMEM((length, heads * DK), BF16),
            pltpu.VMEM((length, heads * DVAL), F32),
            pltpu.VMEM((length, CH), F32),
            pltpu.VMEM((heads, DK, DVAL), F32),
            pltpu.VMEM((length, heads * DK), F32),
            pltpu.VMEM((length, heads * DK), F32),
            pltpu.VMEM((length, heads * DVAL), F32),
            pltpu.VMEM((length, CH), F32),
        ],
        compiler_params=pltpu.CompilerParams(vmem_limit_bytes=60 * 2**20),
        name="mixer_backward",
    )(dmix, preg, ab, masks, segc, segr, taps_q, taps_k, taps_v, gate_par, gain, *saved)
ADAPTER_RANK = 16


def rms_norm(values, gain_vec):
    return values * lax.rsqrt(jnp.mean(values * values, axis=-1, keepdims=True) + EPSILON) * gain_vec


def rms_back(values, gain_vec, grad):
    n = lax.rsqrt(jnp.mean(values * values, axis=-1, keepdims=True) + EPSILON)
    v = values * n
    g = grad * gain_vec
    return n * (g - v * jnp.mean(g * v, axis=-1, keepdims=True))


def dot(a, b):
    return jnp.dot(a, b, preferred_element_type=F32)


def dot_nt(a, b):
    return lax.dot_general(a, b, (((1,), (1,)), ((), ())), preferred_element_type=F32)


def dot_tn(a, b):
    return lax.dot_general(a, b, (((0,), (0,)), ((), ())), preferred_element_type=F32)


def one_hot(flag):
    return flag.astype(BF16)


def per_device(
    tokens,
    cotangent,
    token_grouped_position,
    sequence_lengths,
    adapter_index_per_seq,
    mixer_norm_gain,
    query_key_matrix,
    value_gate_matrix,
    decay_step_matrix,
    query_key_filters,
    value_filters,
    decay_scale_logarithm,
    decay_step_bias,
    head_output_norm_gain,
    output_matrix,
    feedfwd_norm_gain,
    gate_up_matrix,
    down_matrix,
    adapter_mixer_first,
    adapter_query_key_second,
    adapter_value_gate_second,
    adapter_decay_step_second,
    adapter_output_first,
    adapter_output_second,
    adapter_feedfwd_first,
    adapter_gate_up_second,
    adapter_down_first,
    adapter_down_second,
):
    rows = tokens.shape[0]
    width = tokens.shape[1]
    n_dp = lax.axis_size("dp")
    n_mp = lax.axis_size("mp")
    group = rows * n_mp
    share = rows // n_dp
    dp = lax.axis_index("dp")
    mp = lax.axis_index("mp")
    ac = adapter_output_second.shape[0]
    heads = decay_scale_logarithm.shape[0]
    i32 = jnp.int32

    column = lax.dynamic_index_in_dim(
        token_grouped_position.reshape(n_dp, n_mp, rows), mp, axis=1, keepdims=False
    )
    own_dest = lax.dynamic_index_in_dim(column, dp, axis=0, keepdims=False) // group
    slot_r = jnp.arange(rows, dtype=i32)
    before = slot_r[None, :] < slot_r[:, None]
    rank = jnp.sum(((own_dest[:, None] == own_dest[None, :]) & before).astype(i32), axis=1)
    send_pos = own_dest * share + rank
    send_map = one_hot(slot_r[:, None] == send_pos[None, :])
    mask = column // group == dp
    in_rank = dot(mask.astype(BF16), one_hot(slot_r[:, None] < slot_r[None, :])).astype(i32)
    slot_val = column - dp * group - mp * rows
    slots = jnp.sum(
        jnp.where(
            (mask & True)[:, None, :] & (in_rank[:, None, :] == jnp.arange(share, dtype=i32)[None, :, None]),
            slot_val[:, None, :],
            0,
        ),
        axis=2,
    ).reshape(-1)
    place_map = one_hot(slot_r[:, None] == slots[None, :])

    def exchange(x):
        return lax.all_to_all(
            x.reshape(n_dp, share, -1), "dp", split_axis=0, concat_axis=0, tiled=True
        ).reshape(rows, -1)

    arrived = exchange(dot(send_map, tokens).astype(BF16))
    resid = dot(place_map, arrived)
    arrived_cot = exchange(dot(send_map, cotangent).astype(BF16))
    cot = dot(place_map, arrived_cot).astype(BF16)

    position = jnp.arange(group, dtype=i32)
    lens = sequence_lengths[0]
    ends = jnp.stack([jnp.sum(lens[: n + 1]) for n in range(lens.shape[0])])
    segment = jnp.sum((position[:, None] >= ends[None, :]).astype(i32), axis=1)
    which = jnp.sum(
        jnp.where(
            segment[:, None] == jnp.arange(ends.shape[0], dtype=i32)[None, :], adapter_index_per_seq[0][None, :], 0
        ),
        axis=1,
    )
    select = (jnp.arange(ac, dtype=i32)[None, :] // ADAPTER_RANK == which[:, None]).astype(F32)
    select_own = lax.dynamic_slice_in_dim(select, mp * rows, rows, axis=0)
    select6 = jnp.tile(select, (1, 6))
    select2 = jnp.tile(select, (1, 2))
    segf = segment.astype(F32)
    masks = jnp.stack(
        [
            jnp.broadcast_to(
                ((position >= s) & (jnp.roll(segment, s) == segment)).astype(F32)[:, None], (group, CH)
            )
            for s in (1, 2, 3)
        ]
    )
    segc = jnp.broadcast_to(segf[:, None], (group, CH))
    segr = jnp.broadcast_to(segf[None, :], (8, group))
    gate_par = jnp.zeros((8, CH), F32)
    gate_par = gate_par.at[0, :heads].set(decay_scale_logarithm).at[1, :heads].set(decay_step_bias)
    w_ab = jnp.pad(jnp.concatenate([decay_step_matrix[0], decay_step_matrix[1]], axis=1), ((0, 0), (0, CH - 2 * heads)))
    b_a = jnp.pad(adapter_decay_step_second[0], ((0, 0), (0, CH - heads)))
    b_b = jnp.pad(adapter_decay_step_second[1], ((0, 0), (heads, CH - 2 * heads)))

    def gather(x):
        return lax.all_gather(x, "mp", axis=0, tiled=True)

    def scatter(x):
        return lax.psum_scatter(x.astype(BF16), "mp", scatter_dimension=0, tiled=True).astype(F32)

    normed = gather(rms_norm(resid, mixer_norm_gain).astype(BF16))
    low = (dot(normed, adapter_mixer_first) * select6).astype(BF16)
    lows = [low[:, n * ac : (n + 1) * ac] for n in range(6)]
    pre_q = dot(normed, query_key_matrix[0]) + dot(lows[0], adapter_query_key_second[0])
    pre_k = dot(normed, query_key_matrix[1]) + dot(lows[1], adapter_query_key_second[1])
    pre_v = dot(normed, value_gate_matrix[0]) + dot(lows[2], adapter_value_gate_second[0])
    pre_g = dot(normed, value_gate_matrix[1]) + dot(lows[3], adapter_value_gate_second[1])
    pre_ab = dot(normed, w_ab) + dot(lows[4], b_a) + dot(lows[5], b_b)
    shared = (
        masks,
        segc,
        segr,
        query_key_filters[0],
        query_key_filters[1],
        value_filters,
        gate_par,
        head_output_norm_gain[None],
    )
    mixed, *saved = mixer_fwd(pre_q, pre_k, pre_v, pre_g, pre_ab, *shared)
    branch = scatter(dot(mixed, output_matrix))
    rank_out = (scatter(dot(mixed, adapter_output_first)) * select_own).astype(BF16)
    middle = resid + branch + dot(rank_out, adapter_output_second)
    normed2 = gather(rms_norm(middle, feedfwd_norm_gain).astype(BF16))
    rank2 = (dot(normed2, adapter_feedfwd_first) * select2).astype(BF16)
    gate = dot(normed2, gate_up_matrix[0]) + dot(rank2[:, :ac], adapter_gate_up_second[0])
    up = dot(normed2, gate_up_matrix[1]) + dot(rank2[:, ac:], adapter_gate_up_second[1])
    sg = jax.nn.sigmoid(gate)
    hidden = (gate * sg * up).astype(BF16)
    down_sum = scatter(dot(hidden, down_matrix))
    rank_down = (scatter(dot(hidden, adapter_down_first)) * select_own).astype(BF16)
    block_rows = (middle + down_sum + dot(rank_down, adapter_down_second)).astype(BF16)
    out_rows = dot_tn(send_map, exchange(dot_tn(place_map, block_rows).astype(BF16))).astype(BF16)

    cot_all = gather(cot)
    rank_down_all = gather(rank_down)
    rank_out_all = gather(rank_out)
    g_rank_down = (dot_nt(cot_all, adapter_down_second) * select).astype(BF16)
    g_hidden = dot_nt(cot_all, down_matrix) + dot_nt(g_rank_down, adapter_down_first)
    g_gate = (g_hidden * up * (sg * (1.0 + gate * (1.0 - sg)))).astype(BF16)
    g_up = (g_hidden * gate * sg).astype(BF16)
    g_rank2 = (
        jnp.concatenate(
            [dot_nt(g_gate, adapter_gate_up_second[0]), dot_nt(g_up, adapter_gate_up_second[1])], axis=1
        )
        * select2
    ).astype(BF16)
    g_normed2 = scatter(
        dot_nt(g_gate, gate_up_matrix[0]) + dot_nt(g_up, gate_up_matrix[1]) + dot_nt(g_rank2, adapter_feedfwd_first)
    )
    g_middle = cot.astype(F32) + rms_back(middle, feedfwd_norm_gain, g_normed2)
    g_branch = gather(g_middle.astype(BF16))
    g_rank_out = (dot_nt(g_branch, adapter_output_second) * select).astype(BF16)
    g_mixed = dot_nt(g_branch, output_matrix) + dot_nt(g_rank_out, adapter_output_first)

    quarter = ac // share
    lane = jnp.arange(ac, dtype=i32)

    def pick(total, per):
        line = jnp.arange(total, dtype=i32)
        blocks = []
        for b in range(-(-per // share)):
            inner = b * share + lane % share
            want = (lane // share * n_mp + mp) * per + inner
            blocks.append(one_hot((line[:, None] == want[None, :]) & (inner < per)[None, :]))
        return jnp.concatenate(blocks, axis=1)

    per_out = width // (n_dp * n_mp)
    pick_out = pick(width, per_out)
    blocks_out = per_out // share

    def side(grad_rows, ranks):
        chosen = dot(grad_rows, pick_out).astype(BF16)
        return [dot_tn(chosen[:, b * ac : (b + 1) * ac], ranks) for b in range(blocks_out)]

    def reduce_dp(pieces):
        flat = jnp.concatenate([p.astype(BF16) for p in pieces], axis=1)
        got = lax.all_to_all(flat.reshape(n_dp, share, -1), "dp", split_axis=0, concat_axis=0, tiled=True)
        return jnp.sum(got.astype(F32), axis=0)

    early = reduce_dp(
        [
            dot_tn(rank2[:, :ac], g_gate),
            dot_tn(rank2[:, ac:], g_up),
            dot_tn(g_rank_down, hidden),
            dot_tn(g_rank_out, mixed),
        ]
        + side(cot_all, rank_down_all)
        + side(g_branch, rank_out_all)
    )

    dq, dk, dv, dg, dab = mixer_bwd(g_mixed, pre_g, pre_ab, *shared, saved)
    g_rank = (
        jnp.concatenate(
            [
                dot_nt(dq, adapter_query_key_second[0]),
                dot_nt(dk, adapter_query_key_second[1]),
                dot_nt(dv, adapter_value_gate_second[0]),
                dot_nt(dg, adapter_value_gate_second[1]),
                dot_nt(dab, b_a),
                dot_nt(dab, b_b),
            ],
            axis=1,
        )
        * select6
    ).astype(BF16)
    g_normed = scatter(
        dot_nt(dq, query_key_matrix[0])
        + dot_nt(dk, query_key_matrix[1])
        + dot_nt(dv, value_gate_matrix[0])
        + dot_nt(dg, value_gate_matrix[1])
        + dot_nt(dab, w_ab)
        + dot_nt(g_rank, adapter_mixer_first)
    )
    g_tokens = (g_middle + rms_back(resid, mixer_norm_gain, g_normed)).astype(BF16)
    grad_rows = dot_tn(send_map, exchange(dot_tn(place_map, g_tokens).astype(BF16))).astype(BF16)

    per_in = 6 * ac // (n_dp * n_mp)
    per_ffn = 2 * ac // (n_dp * n_mp)

    def by_place(g, per):
        line = jnp.arange(g.shape[1], dtype=i32)
        slot = jnp.arange(n_mp * n_dp * per, dtype=i32)
        place, rest = slot // (n_dp * per), slot % (n_dp * per)
        want = (rest // per * n_mp + place) * per + rest % per
        moved = dot(g, one_hot(line[:, None] == want[None, :])).astype(BF16)
        return lax.psum_scatter(moved, "mp", scatter_dimension=1, tiled=True)

    g_in = by_place(g_rank, per_in)
    g_ffn = by_place(g_rank2, per_ffn)

    def to_rows(per, offset):
        line = jnp.arange(n_dp * per, dtype=i32)
        blocks = []
        for b in range(2):
            inner = b * share + lane % share - offset
            blocks.append(
                one_hot(
                    (line[:, None] == (lane // share * per + inner)[None, :])
                    & (inner >= 0)[None, :]
                    & (inner < per)[None, :]
                )
            )
        return blocks

    in_maps = to_rows(per_in, 0)
    ffn_map = to_rows(per_ffn, per_in)[1]
    late = reduce_dp(
        [
            dot_tn(lows[0], dq),
            dot_tn(lows[1], dk),
            dot_tn(lows[2], dv),
            dot_tn(lows[3], dg),
            dot_tn(dot(g_in, in_maps[0]).astype(BF16), normed),
            dot_tn(dot(g_in, in_maps[1]).astype(BF16), normed)
            + dot_tn(dot(g_ffn, ffn_map).astype(BF16), normed2),
            dot_tn(lows[4], dab),
            dot_tn(lows[5], dab),
        ]
    )

    def cut(x, sizes):
        out, at = [], 0
        for s in sizes:
            out.append(x[:, at : at + s])
            at += s
        return out

    ff = gate.shape[1]
    kw, vw = dq.shape[1], dv.shape[1]
    e = cut(early, [ff, ff, ff, vw] + [ac] * (2 * blocks_out))
    grad_gu = jnp.stack([e[0], e[1]])
    grad_down_in = e[2].T
    grad_out_in = e[3].T

    def side_out(pieces):
        return jnp.concatenate(pieces, axis=0).T

    grad_down = side_out(e[4 : 4 + blocks_out])
    grad_out = side_out(e[4 + blocks_out :])
    f = cut(late, [kw, kw, vw, vw, width, width, CH, CH])
    both = jnp.concatenate([f[4], f[5]], axis=0).T
    return (
        out_rows,
        grad_rows,
        both[:, :per_in],
        jnp.stack([f[0], f[1]]),
        jnp.stack([f[2], f[3]]),
        jnp.stack([f[6][:, :heads], f[7][:, heads : 2 * heads]]),
        grad_out_in,
        grad_out,
        both[:, per_in : per_in + per_ffn],
        grad_gu,
        grad_down_in,
        grad_down,
    )


def solution(mesh):
    return jax.shard_map(
        per_device,
        mesh=mesh,
        in_specs=(
            P(("dp", "mp"), None),
            P(("dp", "mp"), None),
            P(),
            P("dp", None),
            P("dp", None),
            P(),
            P(None, None, "mp"),
            P(None, None, "mp"),
            P(None, None, "mp"),
            P(None, None, "mp"),
            P(None, "mp"),
            P("mp"),
            P("mp"),
            P(),
            P("mp", None),
            P(),
            P(None, None, "mp"),
            P("mp", None),
            P(),
            P(None, None, "mp"),
            P(None, None, "mp"),
            P(None, None, "mp"),
            P("mp", None),
            P(),
            P(),
            P(None, None, "mp"),
            P("mp", None),
            P(),
        ),
        out_specs=(
            P(("dp", "mp"), None),
            P(("dp", "mp"), None),
            P(None, ("dp", "mp")),
            P(None, "dp", "mp"),
            P(None, "dp", "mp"),
            P(None, "dp", "mp"),
            P("mp", "dp"),
            P(None, ("dp", "mp")),
            P(None, ("dp", "mp")),
            P(None, "dp", "mp"),
            P("mp", "dp"),
            P(None, ("dp", "mp")),
        ),
        check_vma=False,
    )
```

```python
import functools
import jax
import jax.numpy as jnp
from jax import lax
from jax.experimental import pallas as pl
from jax.experimental.pallas import tpu as pltpu
from jax.sharding import PartitionSpec as P

EPSILON = 1e-06
F32 = jnp.float32
BF16 = jnp.bfloat16
CH = 128
BASE = 16
DK = 128
DVAL = 256
INV_ROOT = DK ** -0.5


def mm(a, b):
    return jnp.dot(a.astype(BF16), b.astype(BF16), preferred_element_type=F32)


def mm_nt(a, b):
    return lax.dot_general(a.astype(BF16), b.astype(BF16), (((1,), (1,)), ((), ())), preferred_element_type=F32)


def mm_tn(a, b):
    return lax.dot_general(a.astype(BF16), b.astype(BF16), (((0,), (0,)), ((), ())), preferred_element_type=F32)


def exact_tn(a, b):
    b1 = b.astype(BF16)
    r1 = b - b1.astype(F32)
    b2 = r1.astype(BF16)
    b3 = (r1 - b2.astype(F32)).astype(BF16)
    return mm_tn(a, b1) + mm_tn(a, b2) + mm_tn(a, b3)


def iota2(shape, dim):
    return lax.broadcasted_iota(jnp.int32, shape, dim)


def sigmoid(x):
    return 1.0 / (1.0 + jnp.exp(-x))


def conv_rows(x, taps, masks_ref, length):
    total = x * taps[0:1]
    for shift in range(1, 4):
        total = total + pltpu.roll(x, shift, 0) * masks_ref[shift - 1] * taps[shift : shift + 1]
    return total


def conv_rows_back(d, taps, masks_ref, length):
    total = d * taps[0:1]
    for shift in range(1, 4):
        total = total + pltpu.roll(d * masks_ref[shift - 1], length - shift, 0) * taps[shift : shift + 1]
    return total


def gate_columns(ab, dsl, bias):
    z = ab + bias
    soft = jnp.maximum(z, 0.0) + jnp.log1p(jnp.exp(-jnp.abs(z)))
    return -jnp.exp(dsl) * soft, z


def base_inverse(mats):
    nb = CH // BASE
    lane = iota2((1, CH), 1)
    lane_masks = [(lane // BASE == b).astype(F32) for b in range(nb)]
    packed = []
    for a in mats:
        d = a[0:BASE] * lane_masks[0]
        for b in range(1, nb):
            d = d + a[b * BASE : (b + 1) * BASE] * lane_masks[b]
        packed.append(d)
    d = jnp.concatenate(packed, axis=0)
    hi = d.astype(BF16)
    lo = (d - hi.astype(F32)).astype(BF16)
    row = iota2((CH, CH), 0)
    col = iota2((CH, CH), 1)
    same = row // BASE == col // BASE
    spread = jnp.concatenate(
        [(same & (row % BASE == j)).astype(BF16) for j in range(BASE - 1)], axis=1
    )
    wide = mm(hi, spread) + mm(lo, spread)
    sub = iota2((BASE, CH), 0)
    eye = (sub == iota2((BASE, CH), 1) % BASE).astype(F32)
    out = []
    for n in range(len(mats)):
        t = eye
        for j in range(BASE - 1):
            t = t - wide[n * BASE : (n + 1) * BASE, j * CH : (j + 1) * CH] * t[j : j + 1]
        out.append(jnp.concatenate([t * lane_masks[b] for b in range(nb)], axis=0))
    return out


def full_inverse(mats):
    ts = base_inverse(mats)
    row = iota2((CH, CH), 0)
    col = iota2((CH, CH), 1)
    size = BASE
    while size < CH:
        pick = ((row // size) % 2 == 1) & (col // size == row // size - 1)
        steps = [mm(jnp.where(pick, a, 0.0), t) for a, t in zip(mats, ts)]
        ts = [t - mm(t, s) for t, s in zip(ts, steps)]
        size *= 2
    return ts


def mixer_fwd_kernel(
    heads, preq, prek, prev, preg, ab_ref, masks, segc, segr, taps_q, taps_k, taps_v, gate_par, gain,
    mixed, cq, ck, cv, t_out, s_out, u_out, o_out,
    qn, kn, vn, cum_s, state,
):
    length = preq.shape[0]
    count = length // CH

    def key_tile(h, carry):
        cols = pl.ds(pl.multiple_of(h * DK, DK), DK)
        for src, taps, save, dst, scale in ((preq, taps_q, cq, qn, INV_ROOT), (prek, taps_k, ck, kn, 1.0)):
            c = conv_rows(src[:, cols].astype(F32), taps[:, cols], masks, length)
            save[:, cols] = c.astype(BF16)
            u = c * sigmoid(c)
            n = lax.rsqrt(jnp.sum(u * u, axis=-1, keepdims=True) + EPSILON) * scale
            dst[:, cols] = (u * n).astype(BF16)
        for half in range(2):
            vcols = pl.ds(pl.multiple_of(h * DVAL + half * DK, DK), DK)
            c = conv_rows(prev[:, vcols].astype(F32), taps_v[:, vcols], masks, length)
            cv[:, vcols] = c.astype(BF16)
            vn[:, vcols] = c * sigmoid(c)
        return carry

    lax.fori_loop(0, heads, key_tile, 0)
    row = iota2((CH, CH), 0)
    col = iota2((CH, CH), 1)
    upper = (row <= col).astype(BF16)
    log_decay, _ = gate_columns(ab_ref[...], gate_par[0:1], gate_par[1:2])
    beta_all = sigmoid(ab_ref[...])
    for n in range(count):
        cum_s[n * CH : (n + 1) * CH] = exact_tn(upper, log_decay[n * CH : (n + 1) * CH])
    cum_s[length : length + CH] = jnp.zeros((CH, DK), F32)
    for h in range(heads):
        state[h] = jnp.zeros((DK, DVAL), F32)

    for n in range(count):
        r = pl.ds(n * CH, CH)
        seg_col = segc[r]
        seg_row = segr[0:1, n * CH : (n + 1) * CH]
        keep = (seg_col == seg_row) & (row >= col)
        keepf = keep.astype(F32)
        strict = (row > col).astype(F32)
        cum = cum_s[r]
        cum_t = cum.T
        beta_c = beta_all[n * CH : (n + 1) * CH]
        prev_last = segc[n * CH - 1 : n * CH] if n else jnp.full((1, CH), -1.0, F32)
        start = jnp.exp(cum) * (seg_col == prev_last).astype(F32)
        last_seg = segc[(n + 1) * CH - 1 : (n + 1) * CH]
        tail = jnp.exp(cum[CH - 1 : CH] - cum) * (seg_col == last_seg).astype(F32)
        mats, scores = [], []
        for h in range(heads):
            q = qn[r, h * DK : (h + 1) * DK]
            k = kn[r, h * DK : (h + 1) * DK]
            ratio = jnp.exp(jnp.minimum(cum[:, h : h + 1] - cum_t[h : h + 1], 0.0)) * keepf
            beta = beta_c[:, heads + h : heads + h + 1]
            both = mm_nt(jnp.concatenate([q, k], axis=0), k)
            scores.append((ratio * both[:CH]).astype(BF16))
            mats.append(beta * ratio * strict * both[CH:])
        ts = full_inverse(mats)
        for h in range(heads):
            q = qn[r, h * DK : (h + 1) * DK]
            k = kn[r, h * DK : (h + 1) * DK]
            vcols = slice(h * DVAL, (h + 1) * DVAL)
            beta = beta_c[:, heads + h : heads + h + 1]
            st = start[:, h : h + 1]
            tb = ts[h].astype(BF16)
            s0 = state[h]
            s0b = s0.astype(BF16)
            t_out[n, h] = tb
            s_out[n, h] = s0b
            both = mm(jnp.concatenate([q, k], axis=0), s0b)
            res = beta * (vn[r, vcols] - st * both[CH:])
            un = mm(tb, res).astype(BF16)
            u_out[r, vcols] = un
            o = st * both[:CH] + mm(scores[h], un)
            state[h] = start[CH - 1 : CH, h : h + 1] * s0 + mm_tn(k.astype(F32) * tail[:, h : h + 1], un)
            o_out[r, vcols] = o.astype(BF16)
            g = preg[r, vcols].astype(F32)
            rn = lax.rsqrt(jnp.mean(o * o, axis=-1, keepdims=True) + EPSILON)
            mixed[r, vcols] = (o * rn * gain[...] * (g * sigmoid(g))).astype(BF16)


def mixer_fwd(preq, prek, prev, preg, ab, masks, segc, segr, taps_q, taps_k, taps_v, gate_par, gain):
    length = preq.shape[0]
    heads = preq.shape[1] // DK
    count = length // CH
    vm = pl.BlockSpec(memory_space=pltpu.VMEM)
    out_shape = (
        jax.ShapeDtypeStruct((length, heads * DVAL), BF16),
        jax.ShapeDtypeStruct((length, heads * DK), BF16),
        jax.ShapeDtypeStruct((length, heads * DK), BF16),
        jax.ShapeDtypeStruct((length, heads * DVAL), BF16),
        jax.ShapeDtypeStruct((count, heads, CH, CH), BF16),
        jax.ShapeDtypeStruct((count, heads, DK, DVAL), BF16),
        jax.ShapeDtypeStruct((length, heads * DVAL), BF16),
        jax.ShapeDtypeStruct((length, heads * DVAL), BF16),
    )
    return pl.pallas_call(
        functools.partial(mixer_fwd_kernel, heads),
        out_shape=out_shape,
        in_specs=[vm] * 13,
        out_specs=[vm] * len(out_shape),
        scratch_shapes=[
            pltpu.VMEM((length, heads * DK), BF16),
            pltpu.VMEM((length, heads * DK), BF16),
            pltpu.VMEM((length, heads * DVAL), F32),
            pltpu.VMEM((length + CH, CH), F32),
            pltpu.VMEM((heads, DK, DVAL), F32),
        ],
        compiler_params=pltpu.CompilerParams(vmem_limit_bytes=60 * 2**20),
        cost_estimate=pl.CostEstimate(flops=20 * 10**9, bytes_accessed=70 * 2**20, transcendentals=0),
        name="mixer_forward",
    )(preq, prek, prev, preg, ab, masks, segc, segr, taps_q, taps_k, taps_v, gate_par, gain)


def mixer_bwd_kernel(
    heads, dmix, preg, ab_ref, masks, segc, segr, taps_q, taps_k, taps_v, gate_par, gain,
    cq, ck, cv, t_in, s_in, u_in, o_in,
    dpq, dpk, dpv, dpg, dab,
    qn, kn, vn, cum_s, dstate, dqs, dks, dvs, gcol,
):
    length = dmix.shape[0]
    count = length // CH

    def key_tile(h, carry):
        cols = pl.ds(pl.multiple_of(h * DK, DK), DK)
        for save, dst, scale in ((cq, qn, INV_ROOT), (ck, kn, 1.0)):
            c = save[:, cols].astype(F32)
            u = c * sigmoid(c)
            n = lax.rsqrt(jnp.sum(u * u, axis=-1, keepdims=True) + EPSILON) * scale
            dst[:, cols] = (u * n).astype(BF16)
        for half in range(2):
            vcols = pl.ds(pl.multiple_of(h * DVAL + half * DK, DK), DK)
            c = cv[:, vcols].astype(F32)
            vn[:, vcols] = c * sigmoid(c)
        return carry

    lax.fori_loop(0, heads, key_tile, 0)
    row = iota2((CH, CH), 0)
    col = iota2((CH, CH), 1)
    upper = (row <= col).astype(BF16)
    lower = (row >= col).astype(BF16)
    log_decay, z_all = gate_columns(ab_ref[...], gate_par[0:1], gate_par[1:2])
    beta_all = sigmoid(ab_ref[...])
    for n in range(count):
        cum_s[n * CH : (n + 1) * CH] = exact_tn(upper, log_decay[n * CH : (n + 1) * CH])
    for h in range(heads):
        dstate[h] = jnp.zeros((DK, DVAL), F32)
    lane = iota2((1, CH), 1)
    strict = (row > col).astype(F32)
    ones = jnp.ones((CH, CH), BF16)

    for n in range(count - 1, -1, -1):
        r = pl.ds(n * CH, CH)
        seg_col = segc[r]
        seg_row = segr[0:1, n * CH : (n + 1) * CH]
        keepf = ((seg_col == seg_row) & (row >= col)).astype(F32)
        cum = cum_s[r]
        cum_t = cum.T
        beta_c = beta_all[n * CH : (n + 1) * CH]
        prev_last = segc[n * CH - 1 : n * CH] if n else jnp.full((1, CH), -1.0, F32)
        start = jnp.exp(cum) * (seg_col == prev_last).astype(F32)
        last_seg = segc[(n + 1) * CH - 1 : (n + 1) * CH]
        tail = jnp.exp(cum[CH - 1 : CH] - cum) * (seg_col == last_seg).astype(F32)
        dcum_all = jnp.zeros((CH, CH), F32)
        dbeta_all = jnp.zeros((CH, CH), F32)
        dlast_all = jnp.zeros((1, CH), F32)
        for h in range(heads):
            qc = slice(h * DK, (h + 1) * DK)
            vcols = slice(h * DVAL, (h + 1) * DVAL)
            here = (lane == h).astype(F32)
            o = o_in[r, vcols].astype(F32)
            g = preg[r, vcols].astype(F32)
            dm = dmix[r, vcols].astype(F32)
            sg = sigmoid(g)
            rn = lax.rsqrt(jnp.mean(o * o, axis=-1, keepdims=True) + EPSILON)
            on = o * rn
            y = on * gain[...]
            dpg[r, vcols] = (dm * y * (sg * (1.0 + g * (1.0 - sg)))).astype(BF16)
            dy = dm * (g * sg) * gain[...]
            do = rn * (dy - on * jnp.mean(dy * on, axis=-1, keepdims=True))
            dob = do.astype(BF16)
            q = qn[r, qc]
            k = kn[r, qc]
            kf = k.astype(F32)
            qf = q.astype(F32)
            un = u_in[r, vcols]
            s0 = s_in[n, h]
            tb = t_in[n, h]
            beta = beta_c[:, heads + h : heads + h + 1]
            st = start[:, h : h + 1]
            tl = tail[:, h : h + 1]
            carry_scale = start[CH - 1 : CH, h : h + 1]
            ratio = jnp.exp(jnp.minimum(cum[:, h : h + 1] - cum_t[h : h + 1], 0.0)) * keepf
            both = mm_nt(jnp.concatenate([q, k], axis=0), k)
            scores = ratio * both[:CH]
            rs = ratio * strict
            amat = rs * both[CH:]
            qk_state = mm(jnp.concatenate([q, k], axis=0), s0)
            ks = qk_state[CH:]
            ds1 = dstate[h]
            ds1b = ds1.astype(BF16)
            ktail = (kf * tl).astype(BF16)
            dun = mm_tn(scores, dob) + mm(ktail, ds1b)
            dres = mm_tn(tb, dun)
            dresb = dres.astype(BF16)
            dks0 = (-(beta * st) * dres).astype(BF16)
            qst = (qf * st).astype(BF16)
            dstate[h] = carry_scale * ds1 + mm_tn(jnp.concatenate([qst, k], axis=0), jnp.concatenate([dob, dks0], axis=0))
            both_d = mm_nt(jnp.concatenate([dob, dresb], axis=0), un)
            dscore = both_d[:CH]
            da = -both_d[CH:]
            dqk = (dscore * ratio).astype(BF16)
            dkk = (da * beta * rs).astype(BF16)
            dspread = dscore * scores + da * beta * amat
            dbeta = jnp.sum(da * amat, axis=-1, keepdims=True) + jnp.sum(
                dres * (vn[r, vcols] - st * ks), axis=-1, keepdims=True
            )
            dvs[r, vcols] = beta * dres
            by_state = mm_nt(jnp.concatenate([dob, dks0, un], axis=0), jnp.concatenate([s0, ds1b], axis=0))
            dq_state = by_state[:CH, :DK]
            dq = st * dq_state + mm(dqk, k)
            dktail = by_state[2 * CH :, DK:]
            dk = (
                by_state[CH : 2 * CH, :DK]
                + tl * dktail
                + mm_tn(dqk, q)
                + mm(dkk, k)
                + mm_tn(dkk, k)
            )
            dqs[r, qc] = dq
            dks[r, qc] = dk
            dstart_s = st * jnp.sum(qf * dq_state, axis=-1, keepdims=True) + st * (
                -beta * jnp.sum(dres * ks, axis=-1, keepdims=True)
            )
            dtail_s = tl * jnp.sum(kf * dktail, axis=-1, keepdims=True)
            dcarry = carry_scale * jnp.sum(jnp.sum(ds1 * s0.astype(F32), axis=-1, keepdims=True), axis=0, keepdims=True)
            colsum = exact_cols(dspread, ones)
            dcum = jnp.sum(dspread, axis=-1, keepdims=True) - colsum[:, 0:1] + dstart_s - dtail_s
            dlast = jnp.sum(dtail_s, axis=0, keepdims=True) + dcarry
            dcum_all = dcum_all + dcum * here
            dlast_all = dlast_all + dlast * here
            dbeta_all = dbeta_all + dbeta * (lane == heads + h).astype(F32)
        dcum_all = dcum_all + dlast_all * (row == CH - 1).astype(F32)
        gcol[r] = exact_tn(lower, dcum_all) + dbeta_all * beta_c * (1.0 - beta_c)

    slope = -jnp.exp(gate_par[0:1]) * sigmoid(z_all)
    dab[...] = (gcol[...] * jnp.where(lane < heads, slope, 1.0)).astype(BF16)

    def back_tile(h, carry):
        cols = pl.ds(pl.multiple_of(h * DK, DK), DK)
        for save, dsrc, taps, dst, scale in ((cq, dqs, taps_q, dpq, INV_ROOT), (ck, dks, taps_k, dpk, 1.0)):
            c = save[:, cols].astype(F32)
            sg = sigmoid(c)
            u = c * sg
            n = lax.rsqrt(jnp.sum(u * u, axis=-1, keepdims=True) + EPSILON)
            un = u * n
            d = dsrc[:, cols] * scale
            du = n * (d - un * jnp.sum(d * un, axis=-1, keepdims=True))
            dc = du * (sg * (1.0 + c * (1.0 - sg)))
            dst[:, cols] = conv_rows_back(dc, taps[:, cols], masks, length).astype(BF16)
        for half in range(2):
            vcols = pl.ds(pl.multiple_of(h * DVAL + half * DK, DK), DK)
            c = cv[:, vcols].astype(F32)
            sg = sigmoid(c)
            dc = dvs[:, vcols] * (sg * (1.0 + c * (1.0 - sg)))
            dpv[:, vcols] = conv_rows_back(dc, taps_v[:, vcols], masks, length).astype(BF16)
        return carry

    lax.fori_loop(0, heads, back_tile, 0)


def exact_cols(x, ones):
    hi = x.astype(BF16)
    lo = (x - hi.astype(F32)).astype(BF16)
    return mm_tn(hi, ones) + mm_tn(lo, ones)


def mixer_bwd(dmix, preg, ab, masks, segc, segr, taps_q, taps_k, taps_v, gate_par, gain, saved):
    length = dmix.shape[0]
    heads = dmix.shape[1] // DVAL
    vm = pl.BlockSpec(memory_space=pltpu.VMEM)
    out_shape = (
        jax.ShapeDtypeStruct((length, heads * DK), BF16),
        jax.ShapeDtypeStruct((length, heads * DK), BF16),
        jax.ShapeDtypeStruct((length, heads * DVAL), BF16),
        jax.ShapeDtypeStruct((length, heads * DVAL), BF16),
        jax.ShapeDtypeStruct((length, CH), BF16),
    )
    return pl.pallas_call(
        functools.partial(mixer_bwd_kernel, heads),
        out_shape=out_shape,
        in_specs=[vm] * 18,
        out_specs=[vm] * len(out_shape),
        scratch_shapes=[
            pltpu.VMEM((length, heads * DK), BF16),
            pltpu.VMEM((length, heads * DK), BF16),
            pltpu.VMEM((length, heads * DVAL), F32),
            pltpu.VMEM((length, CH), F32),
            pltpu.VMEM((heads, DK, DVAL), F32),
            pltpu.VMEM((length, heads * DK), F32),
            pltpu.VMEM((length, heads * DK), F32),
            pltpu.VMEM((length, heads * DVAL), F32),
            pltpu.VMEM((length, CH), F32),
        ],
        compiler_params=pltpu.CompilerParams(vmem_limit_bytes=60 * 2**20),
        cost_estimate=pl.CostEstimate(flops=30 * 10**9, bytes_accessed=100 * 2**20, transcendentals=0),
        name="mixer_backward",
    )(dmix, preg, ab, masks, segc, segr, taps_q, taps_k, taps_v, gate_par, gain, *saved)


MESH_ID = pl.DeviceIdType.MESH
RING = 4
PIECES = 4
WIDE_VMEM = 60 * 2**20


def ring_places():
    m = lax.axis_index("mp")
    return m, lax.rem(m + 3, RING), lax.rem(m + 1, RING), lax.rem(m + 2, RING)


def ring_barrier(places):
    _, left, right, _ = places
    barrier = pltpu.get_barrier_semaphore()
    for neighbour in (left, right):
        pl.semaphore_signal(barrier, inc=1, device_id={"mp": neighbour}, device_id_type=MESH_ID)
    pl.semaphore_wait(barrier, 2)


class RingGather:
    def __init__(self, buf, send, recv, places):
        self.buf, self.send, self.recv = buf, send, recv
        self.m, self.left, self.right, self.opp = places
        half = buf.shape[1] // 2
        self.top, self.bot = pl.ds(0, half), pl.ds(half, half)

    def begin(self, i, slot, part, to):
        step = part.size // PIECES
        for n in range(PIECES):
            self.copy(i, slot, pl.ds(part.start + n * step, step), to).start()

    def copy(self, i, slot, part, to):
        ref = self.buf.at[slot, part]
        return pltpu.make_async_remote_copy(
            src_ref=ref,
            dst_ref=ref,
            send_sem=self.send.at[i],
            recv_sem=self.recv.at[i],
            device_id={"mp": to},
            device_id_type=MESH_ID,
        )

    def start(self):
        self.begin(0, self.m, self.top, self.right)
        self.begin(1, self.m, self.bot, self.left)
        self.begin(2, self.m, self.bot, self.right)
        self.begin(3, self.m, self.top, self.left)

    def forward(self):
        self.copy(0, self.left, self.top, self.right).wait_recv()
        self.begin(4, self.left, self.top, self.right)
        self.copy(1, self.right, self.bot, self.left).wait_recv()
        self.begin(5, self.right, self.bot, self.left)

    def wait_left(self):
        self.copy(2, self.left, self.bot, self.right).wait_recv()

    def wait_right(self):
        self.copy(3, self.right, self.top, self.left).wait_recv()

    def wait_opp(self):
        self.copy(4, self.opp, self.top, self.right).wait_recv()
        self.copy(5, self.opp, self.bot, self.left).wait_recv()

    def finish(self):
        self.copy(0, self.m, self.top, self.right).wait_send()
        self.copy(1, self.m, self.bot, self.left).wait_send()
        self.copy(2, self.m, self.bot, self.right).wait_send()
        self.copy(3, self.m, self.top, self.left).wait_send()
        self.copy(4, self.left, self.top, self.right).wait_send()
        self.copy(5, self.right, self.bot, self.left).wait_send()


class RingScatter:
    def __init__(self, sbuf, rbuf, acc, send, recv, places):
        self.sbuf, self.rbuf, self.acc, self.send, self.recv = sbuf, rbuf, acc, send, recv
        self.m, self.left, self.right, self.opp = places
        self.half = sbuf.shape[1]

    def begin(self, i):
        step = self.half // PIECES
        for n in range(PIECES):
            self.copy(i, pl.ds(n * step, step)).start()

    def copy(self, i, part=slice(None)):
        to = self.right if i % 2 == 0 else self.left
        return pltpu.make_async_remote_copy(
            src_ref=self.sbuf.at[i, part],
            dst_ref=self.rbuf.at[i, part],
            send_sem=self.send.at[i],
            recv_sem=self.recv.at[i],
            device_id={"mp": to},
            device_id_type=MESH_ID,
        )

    def run(self, part):
        half = self.half
        rows = 2 * half

        def put_far(cols, val):
            self.sbuf[0, :, cols] = val[:half].astype(BF16)
            self.sbuf[1, :, cols] = val[half:rows].astype(BF16)
            self.acc[0, :, cols] = val[rows:]
            self.sbuf[2, :, cols] = val[rows + half :].astype(BF16)

        part((self.opp, self.right), put_far)
        self.begin(0)
        self.begin(1)
        self.begin(2)

        def put_near(cols, val):
            self.acc[1, :, cols] = val[:rows]
            self.sbuf[3, :, cols] = val[:half].astype(BF16)
            self.acc[2, :, cols] = val[rows:]

        part((self.left, self.m), put_near)
        self.begin(3)
        self.copy(0).wait_recv()
        self.sbuf[4] = (self.acc[0, 0:half] + self.rbuf[0].astype(F32)).astype(BF16)
        self.begin(4)
        self.copy(1).wait_recv()
        self.sbuf[5] = (self.acc[1, half:rows] + self.rbuf[1].astype(F32)).astype(BF16)
        self.begin(5)
        for i in range(2, 6):
            self.copy(i).wait_recv()

    def total(self, rows, cols):
        lo, hi = rows
        if hi <= self.half:
            a, b, r = self.rbuf[4, lo:hi, cols], self.rbuf[3, lo:hi, cols], slice(lo, hi)
        else:
            r = slice(lo, hi)
            lo, hi = lo - self.half, hi - self.half
            a, b = self.rbuf[2, lo:hi, cols], self.rbuf[5, lo:hi, cols]
        return self.acc[2, r, cols] + a.astype(F32) + b.astype(F32)

    def finish(self):
        for i in range(6):
            self.copy(i).wait_send()


class Loads:
    def __init__(self, pairs, sems):
        self.copies = [pltpu.make_async_copy(src, dst, sems.at[n]) for n, (src, dst) in enumerate(pairs)]
        self.waited = set()

    def start(self):
        for c in self.copies:
            c.start()

    def wait(self, *which):
        for n in which:
            if n not in self.waited:
                self.copies[n].wait()
                self.waited.add(n)


def tiles(total, step=512):
    return [(at, min(step, total - at)) for at in range(0, total, step)]


def block_rows(place, rows):
    return pl.ds(pl.multiple_of(place * rows, rows), rows)


def both_rows(ref, pair, rows, cols=slice(None)):
    return jnp.concatenate([ref[block_rows(place, rows), cols] for place in pair], axis=0)


def put_rows(ref, pair, rows, cols, val):
    for n, place in enumerate(pair):
        ref[block_rows(place, rows), cols] = val[n * rows : (n + 1) * rows]


def norm_factor(v):
    return lax.rsqrt(jnp.mean(v * v, axis=-1, keepdims=True) + EPSILON)


def project_kernel(
    resid, gain, select, bab, wqk_h, wvg_h, wab_h, ain_h, bqk_h, bvg_h,
    normed_h, low, pq, pk, pv, pg, pab,
    gath, wqk, wvg, wab, ain, bqk, bvg, wsem, osem, send, recv,
):
    rows = resid.shape[0]
    places = ring_places()
    loads = Loads(
        [(ain_h, ain), (wqk_h, wqk), (bqk_h, bqk), (wvg_h, wvg), (bvg_h, bvg), (wab_h, wab)], wsem
    )
    loads.start()
    m = places[0]
    for at in range(0, rows, 32):
        v = resid[at : at + 32]
        gath[m, at : at + 32] = (v * norm_factor(v) * gain[...]).astype(BF16)
    ring_barrier(places)
    ring = RingGather(gath, send, recv, places)
    ring.start()
    ac = select.shape[1]

    def compute(place):
        r = block_rows(place, rows)
        x = gath[place]
        sel = select[r]
        loads.wait(0)
        for n in range(ain.shape[1] // ac):
            low[r, n * ac : (n + 1) * ac] = (mm(x, ain[:, n * ac : (n + 1) * ac]) * sel).astype(BF16)
        loads.wait(1, 2)
        for n, dst in enumerate((pq, pk)):
            lo = low[r, n * ac : (n + 1) * ac]
            dst[r] = (mm(x, wqk[n]) + mm(lo, bqk[n])).astype(BF16)
        loads.wait(3, 4)
        for n, dst in enumerate((pv, pg)):
            lo = low[r, (n + 2) * ac : (n + 3) * ac]
            for at, size in tiles(wvg.shape[2]):
                c = slice(at, at + size)
                dst[r, c] = (mm(x, wvg[n, :, c]) + mm(lo, bvg[n, :, c])).astype(BF16)
        loads.wait(5)
        pab[r] = (
            mm(x, wab[...]) + mm(low[r, 4 * ac : 5 * ac], bab[0]) + mm(low[r, 5 * ac : 6 * ac], bab[1])
        )

    compute(m)
    ring.forward()
    ring.wait_left()
    compute(places[1])
    ring.wait_right()
    compute(places[2])
    ring.wait_opp()
    out = pltpu.make_async_copy(gath, normed_h, osem)
    out.start()
    compute(places[3])
    ring.finish()
    out.wait()


def specs(n_vmem, n_any):
    return [pl.BlockSpec(memory_space=pltpu.VMEM)] * n_vmem + [pl.BlockSpec(memory_space=pl.ANY)] * n_any


def sds(shape, dtype=BF16):
    return jax.ShapeDtypeStruct(shape, dtype)


def ring_params(collective_id):
    return pltpu.CompilerParams(
        collective_id=collective_id, has_side_effects=True, vmem_limit_bytes=WIDE_VMEM
    )


def like(a):
    return pltpu.VMEM(a.shape, a.dtype)


DMA_SEMS = pltpu.SemaphoreType.DMA


def project(resid, gain, select, bab, wqk, wvg, wab, ain, bqk, bvg):
    rows, width = resid.shape
    group = rows * RING
    kw, vw = wqk.shape[2], wvg.shape[2]
    vm, hb = specs(1, 1)
    return pl.pallas_call(
        project_kernel,
        out_shape=(
            sds((RING, rows, width)),
            sds((group, ain.shape[1])),
            sds((group, kw)),
            sds((group, kw)),
            sds((group, vw)),
            sds((group, vw)),
            sds((group, CH), F32),
        ),
        in_specs=[vm] * 4 + [hb] * 6,
        out_specs=[hb] + [vm] * 6,
        scratch_shapes=[
            pltpu.VMEM((RING, rows, width), BF16),
            like(wqk), like(wvg), like(wab), like(ain), like(bqk), like(bvg),
            DMA_SEMS((6,)), DMA_SEMS(()), DMA_SEMS((6,)), DMA_SEMS((6,)),
        ],
        compiler_params=ring_params(1),
        cost_estimate=pl.CostEstimate(flops=8 * 10**9, bytes_accessed=30 * 2**20, transcendentals=0),
        name="gather_project",
    )(resid, gain, select, bab, wqk, wvg, wab, ain, bqk, bvg)


def feed_kernel(
    mixed, resid, gain, select, wout_h, aout_h, bout_h, affn_h, gu_h, bgu_h, down_h, adown_h,
    middle, rank_out, normed_h, rank2, gate, up, hidden, dpart, rpart,
    gath, wout, aout, bout, affn, gu, bgu, down, adown, sbuf, rbuf, acc, wsem, osem, send, recv, send2, recv2,
):
    rows, width = resid.shape
    places = ring_places()
    m = places[0]
    loads = Loads(
        [
            (wout_h, wout), (aout_h, aout), (bout_h, bout), (affn_h, affn),
            (gu_h, gu), (bgu_h, bgu), (down_h, down), (adown_h, adown),
        ],
        wsem,
    )
    loads.start()
    ac = select.shape[1]
    ff = gu.shape[2]
    loads.wait(0, 1)
    ring_barrier(places)
    scatter = RingScatter(sbuf, rbuf, acc, send, recv, places)

    def part(pair, put):
        x = both_rows(mixed, pair, rows)
        for at, size in tiles(width):
            put(slice(at, at + size), mm(x, wout[:, at : at + size]))
        put(slice(width, width + ac), mm(x, aout[...]))

    scatter.run(part)
    loads.wait(2)
    sel_own = select[block_rows(m, rows)]
    half = rows // 2
    for lo in (0, half):
        bounds = (lo, lo + half)
        gath[m, lo : lo + half, width : width + ac] = (
            scatter.total(bounds, slice(width, width + ac)) * sel_own[lo : lo + half]
        ).astype(BF16)
    ro = gath[m, :, width : width + ac]
    for at, size in tiles(width):
        c = slice(at, at + size)
        extra = mm(ro, bout[:, c])
        for lo in (0, half):
            middle[lo : lo + half, c] = (
                resid[lo : lo + half, c] + scatter.total((lo, lo + half), c) + extra[lo : lo + half]
            )
    for at in range(0, rows, 32):
        v = middle[at : at + 32]
        gath[m, at : at + 32, 0:width] = (v * norm_factor(v) * gain[...]).astype(BF16)
    ring = RingGather(gath, send2, recv2, places)
    ring.start()

    def compute(place):
        r = block_rows(place, rows)
        x = gath[place, :, 0:width]
        rank_out[r] = gath[place, :, width : width + ac]
        sel = select[r]
        loads.wait(3)
        for n in range(2):
            rank2[r, n * ac : (n + 1) * ac] = (mm(x, affn[:, n * ac : (n + 1) * ac]) * sel).astype(BF16)
        loads.wait(4, 5)
        r0 = rank2[r, 0:ac]
        r1 = rank2[r, ac : 2 * ac]
        for at, size in tiles(ff):
            c = slice(at, at + size)
            g = mm(x, gu[0, :, c]) + mm(r0, bgu[0, :, c])
            u = mm(x, gu[1, :, c]) + mm(r1, bgu[1, :, c])
            gate[r, c] = g.astype(BF16)
            up[r, c] = u.astype(BF16)
            hidden[r, c] = (g * sigmoid(g) * u).astype(BF16)
        loads.wait(6, 7)
        h = hidden[r]
        for at, size in tiles(width):
            c = slice(at, at + size)
            dpart[r, c] = mm(h, down[:, c]).astype(BF16)
        rpart[r] = mm(h, adown[...]).astype(BF16)

    compute(m)
    ring.forward()
    ring.wait_left()
    compute(places[1])
    ring.wait_right()
    compute(places[2])
    ring.wait_opp()
    out = pltpu.make_async_copy(gath.at[:, :, pl.ds(0, width)], normed_h, osem)
    out.start()
    compute(places[3])
    scatter.finish()
    ring.finish()
    out.wait()


def feed(mixed, resid, gain, select, wout, aout, bout, affn, gu, bgu, down, adown):
    rows, width = resid.shape
    group = rows * RING
    ff = gu.shape[2]
    ac = select.shape[1]
    cols = width + ac
    vm, hb = specs(1, 1)
    return pl.pallas_call(
        feed_kernel,
        out_shape=(
            sds((rows, width), F32),
            sds((group, ac)),
            sds((RING, rows, width)),
            sds((group, 2 * ac)),
            sds((group, ff)),
            sds((group, ff)),
            sds((group, ff)),
            sds((group, width)),
            sds((group, ac)),
        ),
        in_specs=[vm] * 4 + [hb] * 8,
        out_specs=[vm, vm, hb] + [vm] * 6,
        scratch_shapes=[
            pltpu.VMEM((RING, rows, cols), BF16),
            like(wout), like(aout), like(bout), like(affn), like(gu), like(bgu), like(down), like(adown),
            pltpu.VMEM((6, rows // 2, cols), BF16),
            pltpu.VMEM((6, rows // 2, cols), BF16),
            pltpu.VMEM((3, rows, cols), F32),
            DMA_SEMS((8,)), DMA_SEMS(()),
            DMA_SEMS((6,)), DMA_SEMS((6,)), DMA_SEMS((6,)), DMA_SEMS((6,)),
        ],
        compiler_params=ring_params(2),
        cost_estimate=pl.CostEstimate(flops=13 * 10**9, bytes_accessed=40 * 2**20, transcendentals=0),
        name="feed_forward",
    )(mixed, resid, gain, select, wout, aout, bout, affn, gu, bgu, down, adown)


def feed_back_kernel(
    cot, middle, gate, up, rpart, select, gain, bdown_h, down_h, adown_h, gu_h, bgu_h, affn_h, bout_h, wout_h, aout_h,
    g_rank_down, g_gate, g_up, g_rank2, g_middle, g_branch_h, g_rank_out, g_mixed, rank_down,
    gath, bdown, down, adown, gu, bgu, affn, bout, wout, aout,
    sbuf, rbuf, acc, wsem, osem, send, recv, send2, recv2,
):
    rows, width = middle.shape
    places = ring_places()
    m = places[0]
    loads = Loads(
        [
            (bdown_h, bdown), (down_h, down), (adown_h, adown), (gu_h, gu), (bgu_h, bgu),
            (affn_h, affn), (bout_h, bout), (wout_h, wout), (aout_h, aout),
        ],
        wsem,
    )
    loads.start()
    ac = select.shape[1]
    ff = gu.shape[2]
    ring_barrier(places)
    scatter = RingScatter(sbuf, rbuf, acc, send, recv, places)

    def part(pair, put):
        x = both_rows(cot, pair, rows)
        sel = both_rows(select, pair, rows)
        loads.wait(0)
        grd = (mm_nt(x, bdown[...]) * sel).astype(BF16)
        put_rows(g_rank_down, pair, rows, slice(None), grd)
        loads.wait(1, 2)
        for at, size in tiles(ff, 256):
            c = slice(at, at + size)
            gh = mm_nt(x, down[c]) + mm_nt(grd, adown[c])
            g = both_rows(gate, pair, rows, c).astype(F32)
            u = both_rows(up, pair, rows, c).astype(F32)
            sg = sigmoid(g)
            put_rows(g_gate, pair, rows, c, (gh * u * (sg * (1.0 + g * (1.0 - sg)))).astype(BF16))
            put_rows(g_up, pair, rows, c, (gh * g * sg).astype(BF16))
        loads.wait(3, 4, 5)
        gg = both_rows(g_gate, pair, rows)
        gu_ = both_rows(g_up, pair, rows)
        r2a = (mm_nt(gg, bgu[0]) * sel).astype(BF16)
        r2b = (mm_nt(gu_, bgu[1]) * sel).astype(BF16)
        put_rows(g_rank2, pair, rows, slice(0, ac), r2a)
        put_rows(g_rank2, pair, rows, slice(ac, 2 * ac), r2b)
        r2 = jnp.concatenate([r2a, r2b], axis=1)
        for at, size in tiles(width, 256):
            c = slice(at, at + size)
            put(c, mm_nt(gg, gu[0, c]) + mm_nt(gu_, gu[1, c]) + mm_nt(r2, affn[c]))
        put(slice(width, width + ac), both_rows(rpart, pair, rows).astype(F32))

    scatter.run(part)
    sel_own = select[block_rows(m, rows)]
    step = 16
    for at in range(0, rows, step):
        b = (at, at + step)
        g = scatter.total(b, slice(0, width)) * gain[...]
        v = middle[at : at + step]
        n = norm_factor(v)
        v = v * n
        gm = cot[pl.ds(pl.multiple_of(m * rows + at, step), step)].astype(F32) + n * (
            g - v * jnp.mean(g * v, axis=-1, keepdims=True)
        )
        g_middle[at : at + step] = gm
        gath[m, at : at + step, 0:width] = gm.astype(BF16)
        gath[m, at : at + step, width : width + ac] = (
            scatter.total(b, slice(width, width + ac)) * sel_own[at : at + step]
        ).astype(BF16)
    ring = RingGather(gath, send2, recv2, places)
    ring.start()

    def compute(*pair):
        x = jnp.concatenate([gath[place, :, 0:width] for place in pair], axis=0)
        loads.wait(6, 7, 8)
        gro = (mm_nt(x, bout[...]) * both_rows(select, pair, rows)).astype(BF16)
        put_rows(g_rank_out, pair, rows, slice(None), gro)
        for at, size in tiles(wout.shape[0], 256):
            c = slice(at, at + size)
            put_rows(g_mixed, pair, rows, c, (mm_nt(x, wout[c]) + mm_nt(gro, aout[c])).astype(BF16))
        for place in pair:
            rank_down[block_rows(place, rows)] = gath[place, :, width : width + ac]

    compute(m)
    ring.forward()
    ring.wait_left()
    ring.wait_right()
    compute(places[1], places[2])
    ring.wait_opp()
    out = pltpu.make_async_copy(gath.at[:, :, pl.ds(0, width)], g_branch_h, osem)
    out.start()
    compute(places[3])
    scatter.finish()
    ring.finish()
    out.wait()


def feed_back(cot, middle, gate, up, rpart, select, gain, bdown, down, adown, gu, bgu, affn, bout, wout, aout):
    rows, width = middle.shape
    group = rows * RING
    ff = gu.shape[2]
    ac = select.shape[1]
    vm, hb = specs(1, 1)
    return pl.pallas_call(
        feed_back_kernel,
        out_shape=(
            sds((group, ac)),
            sds((group, ff)),
            sds((group, ff)),
            sds((group, 2 * ac)),
            sds((rows, width), F32),
            sds((RING, rows, width)),
            sds((group, ac)),
            sds((group, wout.shape[0])),
            sds((group, ac)),
        ),
        in_specs=[vm] * 7 + [hb] * 9,
        out_specs=[vm] * 5 + [hb] + [vm] * 3,
        scratch_shapes=[
            pltpu.VMEM((RING, rows, width + ac), BF16),
            like(bdown), like(down), like(adown), like(gu), like(bgu), like(affn), like(bout), like(wout), like(aout),
            pltpu.VMEM((6, rows // 2, width + ac), BF16),
            pltpu.VMEM((6, rows // 2, width + ac), BF16),
            pltpu.VMEM((3, rows, width + ac), F32),
            DMA_SEMS((9,)), DMA_SEMS(()),
            DMA_SEMS((6,)), DMA_SEMS((6,)), DMA_SEMS((6,)), DMA_SEMS((6,)),
        ],
        compiler_params=ring_params(3),
        cost_estimate=pl.CostEstimate(flops=13 * 10**9, bytes_accessed=40 * 2**20, transcendentals=0),
        name="feed_backward",
    )(cot, middle, gate, up, rpart, select, gain, bdown, down, adown, gu, bgu, affn, bout, wout, aout)


def project_back_kernel(
    dq, dk, dv, dg, dab, resid, g_middle, select, gain, bab, wqk_h, wvg_h, wab_h, ain_h, bqk_h, bvg_h,
    g_rank, g_tokens,
    wqk, wvg, wab, ain, bqk, bvg, sbuf, rbuf, acc, wsem, send, recv,
):
    rows, width = resid.shape
    places = ring_places()
    m = places[0]
    loads = Loads(
        [(bqk_h, bqk), (bvg_h, bvg), (ain_h, ain), (wqk_h, wqk), (wvg_h, wvg), (wab_h, wab)], wsem
    )
    loads.start()
    ac = select.shape[1]
    ring_barrier(places)
    scatter = RingScatter(sbuf, rbuf, acc, send, recv, places)

    def part(pair, put):
        sel = both_rows(select, pair, rows)
        xs = [both_rows(d, pair, rows) for d in (dq, dk, dv, dg, dab)]
        loads.wait(0, 1)
        seconds = [bqk[0], bqk[1], bvg[0], bvg[1], bab[0], bab[1]]
        for n in range(6):
            c = slice(n * ac, (n + 1) * ac)
            put_rows(g_rank, pair, rows, c, (mm_nt(xs[min(n, 4)], seconds[n]) * sel).astype(BF16))
        gr = both_rows(g_rank, pair, rows)
        loads.wait(2, 3, 4, 5)
        for at, size in tiles(width, 256):
            c = slice(at, at + size)
            put(
                c,
                mm_nt(xs[0], wqk[0, c])
                + mm_nt(xs[1], wqk[1, c])
                + mm_nt(xs[2], wvg[0, c])
                + mm_nt(xs[3], wvg[1, c])
                + mm_nt(xs[4], wab[c])
                + mm_nt(gr, ain[c]),
            )

    scatter.run(part)
    step = 16
    for at in range(0, rows, step):
        g = scatter.total((at, at + step), slice(0, width)) * gain[...]
        v = resid[at : at + step]
        n = norm_factor(v)
        v = v * n
        g_tokens[at : at + step] = (
            g_middle[at : at + step] + n * (g - v * jnp.mean(g * v, axis=-1, keepdims=True))
        ).astype(BF16)
    scatter.finish()


def project_back(dq, dk, dv, dg, dab, resid, g_middle, select, gain, bab, wqk, wvg, wab, ain, bqk, bvg):
    rows, width = resid.shape
    group = rows * RING
    vm, hb = specs(1, 1)
    return pl.pallas_call(
        project_back_kernel,
        out_shape=(sds((group, ain.shape[1])), sds((rows, width))),
        in_specs=[vm] * 10 + [hb] * 6,
        out_specs=[vm, vm],
        scratch_shapes=[
            like(wqk), like(wvg), like(wab), like(ain), like(bqk), like(bvg),
            pltpu.VMEM((6, rows // 2, width), BF16),
            pltpu.VMEM((6, rows // 2, width), BF16),
            pltpu.VMEM((3, rows, width), F32),
            DMA_SEMS((6,)), DMA_SEMS((6,)), DMA_SEMS((6,)),
        ],
        compiler_params=ring_params(4),
        cost_estimate=pl.CostEstimate(flops=9 * 10**9, bytes_accessed=30 * 2**20, transcendentals=0),
        name="project_backward",
    )(dq, dk, dv, dg, dab, resid, g_middle, select, gain, bab, wqk, wvg, wab, ain, bqk, bvg)


def exchange_kernel(share, idx_in, idx_out, xa, xb, oa, ob, stage, land, send, recv):
    n = land.shape[0]
    me = lax.axis_index("dp")
    rows, width = xa.shape
    slots = n * 16
    parts = 16 // share
    pw = width // parts
    barrier = pltpu.get_barrier_semaphore()

    def greet(s, carry):
        pl.semaphore_signal(barrier, inc=1, device_id={"dp": lax.rem(me + s, n)}, device_id_type=MESH_ID)
        return carry

    lax.fori_loop(1, n, greet, 0)
    row = iota2((rows, slots), 0)
    part_of = (iota2((1, slots), 1) // share) % parts
    into = row == idx_in[0:1]
    outof = row == idx_out[0:1]
    into = [(into & (part_of == p)).astype(F32).astype(BF16) for p in range(parts)]
    for x, at in ((xa, 0), (xb, 16)):
        acc = jnp.zeros((slots, pw), F32)
        for p in range(parts):
            acc = acc + mm_tn(into[p], x[:, p * pw : (p + 1) * pw])
        stage[:, at : at + 16, :] = acc.astype(BF16).reshape(n, 16, pw)
    land[me] = stage[me]
    pl.semaphore_wait(barrier, n - 1)

    def copy(to, source):
        return pltpu.make_async_remote_copy(
            src_ref=stage.at[to],
            dst_ref=land.at[source],
            send_sem=send.at[to],
            recv_sem=recv.at[source],
            device_id={"dp": to},
            device_id_type=MESH_ID,
        )

    def go(s, carry):
        copy(lax.rem(me + s, n), me).start()
        return carry

    lax.fori_loop(1, n, go, 0)

    def take(s, carry):
        source = lax.rem(me + n - s, n)
        copy(source, source).wait_recv()
        return carry

    lax.fori_loop(1, n, take, 0)
    outof = [(outof & (part_of == p)).astype(F32).astype(BF16) for p in range(parts)]
    for o, at in ((oa, 0), (ob, 16)):
        got = land[:, at : at + 16, :].reshape(slots, pw)
        for p in range(parts):
            o[:, p * pw : (p + 1) * pw] = mm(outof[p], got).astype(o.dtype)

    def done(s, carry):
        copy(lax.rem(me + s, n), me).wait_send()
        return carry

    lax.fori_loop(1, n, done, 0)


def exchange(collective_id, idx_in, idx_out, xa, xb, types):
    rows, width = xa.shape
    n = lax.axis_size("dp")
    share = rows // n
    parts = 16 // share
    vm, _ = specs(1, 1)
    return pl.pallas_call(
        functools.partial(exchange_kernel, share),
        out_shape=(sds((rows, width), types[0]), sds((rows, width), types[1])),
        in_specs=[vm] * 4,
        out_specs=[vm] * 2,
        scratch_shapes=[
            pltpu.VMEM((n, 32, width // parts), BF16),
            pltpu.VMEM((n, 32, width // parts), BF16),
            DMA_SEMS((n,)),
            DMA_SEMS((n,)),
        ],
        compiler_params=ring_params(collective_id),
        cost_estimate=pl.CostEstimate(flops=10**9, bytes_accessed=20 * 2**20, transcendentals=0),
        name="exchange_rows",
    )(idx_in, idx_out, xa, xb)


ADAPTER_RANK = 16


def dot(a, b):
    return jnp.dot(a, b, preferred_element_type=F32)


def dot_nt(a, b):
    return lax.dot_general(a, b, (((1,), (1,)), ((), ())), preferred_element_type=F32)


def dot_tn(a, b):
    return lax.dot_general(a, b, (((0,), (0,)), ((), ())), preferred_element_type=F32)


def one_hot(flag):
    return flag.astype(BF16)


def per_device(
    tokens,
    cotangent,
    token_grouped_position,
    sequence_lengths,
    adapter_index_per_seq,
    mixer_norm_gain,
    query_key_matrix,
    value_gate_matrix,
    decay_step_matrix,
    query_key_filters,
    value_filters,
    decay_scale_logarithm,
    decay_step_bias,
    head_output_norm_gain,
    output_matrix,
    feedfwd_norm_gain,
    gate_up_matrix,
    down_matrix,
    adapter_mixer_first,
    adapter_query_key_second,
    adapter_value_gate_second,
    adapter_decay_step_second,
    adapter_output_first,
    adapter_output_second,
    adapter_feedfwd_first,
    adapter_gate_up_second,
    adapter_down_first,
    adapter_down_second,
):
    rows = tokens.shape[0]
    width = tokens.shape[1]
    n_dp = lax.axis_size("dp")
    n_mp = lax.axis_size("mp")
    group = rows * n_mp
    share = rows // n_dp
    dp = lax.axis_index("dp")
    mp = lax.axis_index("mp")
    ac = adapter_output_second.shape[0]
    heads = decay_scale_logarithm.shape[0]
    i32 = jnp.int32

    column = lax.dynamic_index_in_dim(
        token_grouped_position.reshape(n_dp, n_mp, rows), mp, axis=1, keepdims=False
    )
    own_dest = lax.dynamic_index_in_dim(column, dp, axis=0, keepdims=False) // group
    slot_r = jnp.arange(rows, dtype=i32)
    before = slot_r[None, :] < slot_r[:, None]
    rank = jnp.sum(((own_dest[:, None] == own_dest[None, :]) & before).astype(i32), axis=1)
    send_pos = own_dest * share + rank
    token_at = jnp.sum(jnp.where(send_pos[None, :] == slot_r[:, None], slot_r[None, :], 0), axis=1)
    mask = column // group == dp
    in_rank = dot(mask.astype(BF16), one_hot(slot_r[:, None] < slot_r[None, :])).astype(i32)
    slot_val = column - dp * group - mp * rows
    slots = jnp.sum(
        jnp.where(
            mask[:, None, :] & (in_rank[:, None, :] == jnp.arange(share, dtype=i32)[None, :, None]),
            slot_val[:, None, :],
            0,
        ),
        axis=2,
    ).reshape(-1)

    def spread(index):
        parts = 16 // share
        wide = jnp.broadcast_to(index.reshape(n_dp, 1, share), (n_dp, parts, share)).reshape(1, -1)
        return jnp.broadcast_to(wide, (8, n_dp * 16))

    index_tokens, index_slots = spread(token_at), spread(slots)
    resid, cot = exchange(5, index_tokens, index_slots, tokens, cotangent, (F32, BF16))

    position = jnp.arange(group, dtype=i32)
    lens = sequence_lengths[0]
    ends = jnp.stack([jnp.sum(lens[: n + 1]) for n in range(lens.shape[0])])
    segment = jnp.sum((position[:, None] >= ends[None, :]).astype(i32), axis=1)
    which = jnp.sum(
        jnp.where(
            segment[:, None] == jnp.arange(ends.shape[0], dtype=i32)[None, :], adapter_index_per_seq[0][None, :], 0
        ),
        axis=1,
    )
    select = (jnp.arange(ac, dtype=i32)[None, :] // ADAPTER_RANK == which[:, None]).astype(F32)
    segf = segment.astype(F32)
    masks = jnp.stack(
        [
            jnp.broadcast_to(
                ((position >= s) & (jnp.roll(segment, s) == segment)).astype(F32)[:, None], (group, CH)
            )
            for s in (1, 2, 3)
        ]
    )
    segc = jnp.broadcast_to(segf[:, None], (group, CH))
    segr = jnp.broadcast_to(segf[None, :], (8, group))
    gate_par = jnp.zeros((8, CH), F32)
    gate_par = gate_par.at[0, :heads].set(decay_scale_logarithm).at[1, :heads].set(decay_step_bias)
    w_ab = jnp.pad(jnp.concatenate([decay_step_matrix[0], decay_step_matrix[1]], axis=1), ((0, 0), (0, CH - 2 * heads)))
    b_a = jnp.pad(adapter_decay_step_second[0], ((0, 0), (0, CH - heads)))
    b_b = jnp.pad(adapter_decay_step_second[1], ((0, 0), (heads, CH - 2 * heads)))

    def gather(x):
        return lax.all_gather(x, "mp", axis=0, tiled=True)

    def scatter(x):
        return lax.psum_scatter(x.astype(BF16), "mp", scatter_dimension=0, tiled=True).astype(F32)

    bab = jnp.stack([b_a, b_b])
    gain_one, gain_two = mixer_norm_gain[None], feedfwd_norm_gain[None]
    normed, low, pre_q, pre_k, pre_v, pre_g, pre_ab = project(
        resid,
        gain_one,
        select,
        bab,
        query_key_matrix,
        value_gate_matrix,
        w_ab,
        adapter_mixer_first,
        adapter_query_key_second,
        adapter_value_gate_second,
    )
    normed = normed.reshape(group, width)
    lows = [low[:, n * ac : (n + 1) * ac] for n in range(6)]
    cot_later, pre_ab = lax.optimization_barrier((cot, pre_ab))
    cot_all = gather(cot_later)
    shared = (
        masks,
        segc,
        segr,
        query_key_filters[0],
        query_key_filters[1],
        value_filters,
        gate_par,
        head_output_norm_gain[None],
    )
    mixed, *saved = mixer_fwd(pre_q, pre_k, pre_v, pre_g, pre_ab, *shared)
    mixed, cot_all = lax.optimization_barrier((mixed, cot_all))
    middle, rank_out, normed2, rank2, gate, up, hidden, down_part, rank_part = feed(
        mixed,
        resid,
        gain_two,
        select,
        output_matrix,
        adapter_output_first,
        adapter_output_second,
        adapter_feedfwd_first,
        gate_up_matrix,
        adapter_gate_up_second,
        down_matrix,
        adapter_down_first,
    )
    normed2 = normed2.reshape(group, width)
    g_rank_down, g_gate, g_up, g_rank2, g_middle, g_branch, g_rank_out, g_mixed, rank_down = feed_back(
        cot_all,
        middle,
        gate,
        up,
        rank_part,
        select,
        gain_two,
        adapter_down_second,
        down_matrix,
        adapter_down_first,
        gate_up_matrix,
        adapter_gate_up_second,
        adapter_feedfwd_first,
        adapter_output_second,
        output_matrix,
        adapter_output_first,
    )
    g_branch = g_branch.reshape(group, width)
    down_later, g_mixed = lax.optimization_barrier((down_part, g_mixed))
    down_sum = scatter(down_later)
    rank_down_own = lax.dynamic_slice_in_dim(rank_down, mp * rows, rows, axis=0)

    quarter = ac // share
    lane = jnp.arange(ac, dtype=i32)

    def pick(total, per):
        line = jnp.arange(total, dtype=i32)
        blocks = []
        for b in range(-(-per // share)):
            inner = b * share + lane % share
            want = (lane // share * n_mp + mp) * per + inner
            blocks.append(one_hot((line[:, None] == want[None, :]) & (inner < per)[None, :]))
        return jnp.concatenate(blocks, axis=1)

    per_out = width // (n_dp * n_mp)
    pick_out = pick(width, per_out)
    blocks_out = per_out // share

    def side(grad_rows, ranks):
        chosen = dot(grad_rows, pick_out).astype(BF16)
        return [dot_tn(chosen[:, b * ac : (b + 1) * ac], ranks) for b in range(blocks_out)]

    def reduce_dp(pieces):
        flat = jnp.concatenate([p.astype(BF16) for p in pieces], axis=1)
        got = lax.all_to_all(flat.reshape(n_dp, share, -1), "dp", split_axis=0, concat_axis=0, tiled=True)
        return jnp.sum(got.astype(F32), axis=0)

    early = reduce_dp(
        [
            dot_tn(rank2[:, :ac], g_gate),
            dot_tn(rank2[:, ac:], g_up),
            dot_tn(g_rank_down, hidden),
            dot_tn(g_rank_out, mixed),
        ]
        + side(cot_all, rank_down)
        + side(g_branch, rank_out)
    )

    dq, dk, dv, dg, dab = mixer_bwd(g_mixed, pre_g, pre_ab, *shared, saved)
    dq, down_sum, early = lax.optimization_barrier((dq, down_sum, early))
    block_rows_out = (middle + down_sum + dot(rank_down_own, adapter_down_second)).astype(BF16)
    g_rank, g_tokens = project_back(
        dq,
        dk,
        dv,
        dg,
        dab,
        resid,
        g_middle,
        select,
        gain_one,
        bab,
        query_key_matrix,
        value_gate_matrix,
        w_ab,
        adapter_mixer_first,
        adapter_query_key_second,
        adapter_value_gate_second,
    )
    out_rows, grad_rows = exchange(6, index_slots, index_tokens, block_rows_out, g_tokens, (BF16, BF16))

    per_in = 6 * ac // (n_dp * n_mp)
    per_ffn = 2 * ac // (n_dp * n_mp)

    def by_place(g, per):
        line = jnp.arange(g.shape[1], dtype=i32)
        slot = jnp.arange(n_mp * n_dp * per, dtype=i32)
        place, rest = slot // (n_dp * per), slot % (n_dp * per)
        want = (rest // per * n_mp + place) * per + rest % per
        moved = dot(g, one_hot(line[:, None] == want[None, :])).astype(BF16)
        return lax.psum_scatter(moved, "mp", scatter_dimension=1, tiled=True)

    g_in = by_place(g_rank, per_in)
    g_ffn = by_place(g_rank2, per_ffn)

    def to_rows(per, offset):
        line = jnp.arange(n_dp * per, dtype=i32)
        blocks = []
        for b in range(2):
            inner = b * share + lane % share - offset
            blocks.append(
                one_hot(
                    (line[:, None] == (lane // share * per + inner)[None, :])
                    & (inner >= 0)[None, :]
                    & (inner < per)[None, :]
                )
            )
        return blocks

    in_maps = to_rows(per_in, 0)
    ffn_map = to_rows(per_ffn, per_in)[1]
    late = reduce_dp(
        [
            dot_tn(lows[0], dq),
            dot_tn(lows[1], dk),
            dot_tn(lows[2], dv),
            dot_tn(lows[3], dg),
            dot_tn(dot(g_in, in_maps[0]).astype(BF16), normed),
            dot_tn(dot(g_in, in_maps[1]).astype(BF16), normed)
            + dot_tn(dot(g_ffn, ffn_map).astype(BF16), normed2),
            dot_tn(lows[4], dab),
            dot_tn(lows[5], dab),
        ]
    )

    def cut(x, sizes):
        out, at = [], 0
        for s in sizes:
            out.append(x[:, at : at + s])
            at += s
        return out

    ff = gate.shape[1]
    kw, vw = dq.shape[1], dv.shape[1]
    e = cut(early, [ff, ff, ff, vw] + [ac] * (2 * blocks_out))
    grad_gu = jnp.stack([e[0], e[1]])
    grad_down_in = e[2].T
    grad_out_in = e[3].T

    def side_out(pieces):
        return jnp.concatenate(pieces, axis=0).T

    grad_down = side_out(e[4 : 4 + blocks_out])
    grad_out = side_out(e[4 + blocks_out :])
    f = cut(late, [kw, kw, vw, vw, width, width, CH, CH])
    both = jnp.concatenate([f[4], f[5]], axis=0).T
    return (
        out_rows,
        grad_rows,
        both[:, :per_in],
        jnp.stack([f[0], f[1]]),
        jnp.stack([f[2], f[3]]),
        jnp.stack([f[6][:, :heads], f[7][:, heads : 2 * heads]]),
        grad_out_in,
        grad_out,
        both[:, per_in : per_in + per_ffn],
        grad_gu,
        grad_down_in,
        grad_down,
    )


def solution(mesh):
    return jax.shard_map(
        per_device,
        mesh=mesh,
        in_specs=(
            P(("dp", "mp"), None),
            P(("dp", "mp"), None),
            P(),
            P("dp", None),
            P("dp", None),
            P(),
            P(None, None, "mp"),
            P(None, None, "mp"),
            P(None, None, "mp"),
            P(None, None, "mp"),
            P(None, "mp"),
            P("mp"),
            P("mp"),
            P(),
            P("mp", None),
            P(),
            P(None, None, "mp"),
            P("mp", None),
            P(),
            P(None, None, "mp"),
            P(None, None, "mp"),
            P(None, None, "mp"),
            P("mp", None),
            P(),
            P(),
            P(None, None, "mp"),
            P("mp", None),
            P(),
        ),
        out_specs=(
            P(("dp", "mp"), None),
            P(("dp", "mp"), None),
            P(None, ("dp", "mp")),
            P(None, "dp", "mp"),
            P(None, "dp", "mp"),
            P(None, "dp", "mp"),
            P("mp", "dp"),
            P(None, ("dp", "mp")),
            P(None, ("dp", "mp")),
            P(None, "dp", "mp"),
            P("mp", "dp"),
            P(None, ("dp", "mp")),
        ),
        check_vma=False,
    )
```

```python
import functools
import jax
import jax.numpy as jnp
from jax import lax
from jax.experimental import pallas as pl
from jax.experimental.pallas import tpu as pltpu
from jax.sharding import PartitionSpec as P

EPSILON = 1e-06
F32 = jnp.float32
BF16 = jnp.bfloat16
CH = 128
BASE = 16
DK = 128
DVAL = 256
INV_ROOT = DK ** -0.5


def mm(a, b):
    return jnp.dot(a.astype(BF16), b.astype(BF16), preferred_element_type=F32)


def mm_nt(a, b):
    return lax.dot_general(a.astype(BF16), b.astype(BF16), (((1,), (1,)), ((), ())), preferred_element_type=F32)


def mm_tn(a, b):
    return lax.dot_general(a.astype(BF16), b.astype(BF16), (((0,), (0,)), ((), ())), preferred_element_type=F32)


def exact_tn(a, b):
    b1 = b.astype(BF16)
    r1 = b - b1.astype(F32)
    b2 = r1.astype(BF16)
    b3 = (r1 - b2.astype(F32)).astype(BF16)
    return mm_tn(a, b1) + mm_tn(a, b2) + mm_tn(a, b3)


def iota2(shape, dim):
    return lax.broadcasted_iota(jnp.int32, shape, dim)


def sigmoid(x):
    return 1.0 / (1.0 + jnp.exp(-x))


def conv_rows(x, taps, masks_ref, length):
    total = x * taps[0:1]
    for shift in range(1, 4):
        total = total + pltpu.roll(x, shift, 0) * masks_ref[shift - 1] * taps[shift : shift + 1]
    return total


def conv_rows_back(d, taps, masks_ref, length):
    total = d * taps[0:1]
    for shift in range(1, 4):
        total = total + pltpu.roll(d * masks_ref[shift - 1], length - shift, 0) * taps[shift : shift + 1]
    return total


def gate_columns(ab, dsl, bias):
    z = ab + bias
    soft = jnp.maximum(z, 0.0) + jnp.log1p(jnp.exp(-jnp.abs(z)))
    return -jnp.exp(dsl) * soft, z


def base_inverse(mats):
    nb = CH // BASE
    lane = iota2((1, CH), 1)
    lane_masks = [(lane // BASE == b).astype(F32) for b in range(nb)]
    packed = []
    for a in mats:
        d = a[0:BASE] * lane_masks[0]
        for b in range(1, nb):
            d = d + a[b * BASE : (b + 1) * BASE] * lane_masks[b]
        packed.append(d)
    d = jnp.concatenate(packed, axis=0)
    hi = d.astype(BF16)
    lo = (d - hi.astype(F32)).astype(BF16)
    row = iota2((CH, CH), 0)
    col = iota2((CH, CH), 1)
    same = row // BASE == col // BASE
    spread = jnp.concatenate(
        [(same & (row % BASE == j)).astype(BF16) for j in range(BASE - 1)], axis=1
    )
    wide = mm(hi, spread) + mm(lo, spread)
    sub = iota2((BASE, CH), 0)
    eye = (sub == iota2((BASE, CH), 1) % BASE).astype(F32)
    out = []
    for n in range(len(mats)):
        t = eye
        for j in range(BASE - 1):
            t = t - wide[n * BASE : (n + 1) * BASE, j * CH : (j + 1) * CH] * t[j : j + 1]
        out.append(jnp.concatenate([t * lane_masks[b] for b in range(nb)], axis=0))
    return out


def full_inverse(mats):
    ts = base_inverse(mats)
    row = iota2((CH, CH), 0)
    col = iota2((CH, CH), 1)
    size = BASE
    while size < CH:
        pick = ((row // size) % 2 == 1) & (col // size == row // size - 1)
        steps = [mm(jnp.where(pick, a, 0.0), t) for a, t in zip(mats, ts)]
        ts = [t - mm(t, s) for t, s in zip(ts, steps)]
        size *= 2
    return ts


def mixer_fwd_kernel(
    heads, preq, prek, prev, preg, ab_ref, masks, segc, segr, taps_q, taps_k, taps_v, gate_par, gain,
    mixed, cq, ck, cv, t_out, s_out, u_out, o_out,
    qn, kn, vn, cum_s, state,
):
    length = preq.shape[0]
    count = length // CH

    def key_tile(h, carry):
        cols = pl.ds(pl.multiple_of(h * DK, DK), DK)
        for src, taps, save, dst, scale in ((preq, taps_q, cq, qn, INV_ROOT), (prek, taps_k, ck, kn, 1.0)):
            c = conv_rows(src[:, cols].astype(F32), taps[:, cols], masks, length)
            save[:, cols] = c.astype(BF16)
            u = c * sigmoid(c)
            n = lax.rsqrt(jnp.sum(u * u, axis=-1, keepdims=True) + EPSILON) * scale
            dst[:, cols] = (u * n).astype(BF16)
        for half in range(2):
            vcols = pl.ds(pl.multiple_of(h * DVAL + half * DK, DK), DK)
            c = conv_rows(prev[:, vcols].astype(F32), taps_v[:, vcols], masks, length)
            cv[:, vcols] = c.astype(BF16)
            vn[:, vcols] = c * sigmoid(c)
        return carry

    lax.fori_loop(0, heads, key_tile, 0)
    row = iota2((CH, CH), 0)
    col = iota2((CH, CH), 1)
    upper = (row <= col).astype(BF16)
    log_decay, _ = gate_columns(ab_ref[...], gate_par[0:1], gate_par[1:2])
    beta_all = sigmoid(ab_ref[...])
    for n in range(count):
        cum_s[n * CH : (n + 1) * CH] = exact_tn(upper, log_decay[n * CH : (n + 1) * CH])
    cum_s[length : length + CH] = jnp.zeros((CH, DK), F32)
    for h in range(heads):
        state[h] = jnp.zeros((DK, DVAL), F32)

    for n in range(count):
        r = pl.ds(n * CH, CH)
        seg_col = segc[r]
        seg_row = segr[0:1, n * CH : (n + 1) * CH]
        keep = (seg_col == seg_row) & (row >= col)
        keepf = keep.astype(F32)
        strict = (row > col).astype(F32)
        cum = cum_s[r]
        cum_t = cum.T
        beta_c = beta_all[n * CH : (n + 1) * CH]
        prev_last = segc[n * CH - 1 : n * CH] if n else jnp.full((1, CH), -1.0, F32)
        start = jnp.exp(cum) * (seg_col == prev_last).astype(F32)
        last_seg = segc[(n + 1) * CH - 1 : (n + 1) * CH]
        tail = jnp.exp(cum[CH - 1 : CH] - cum) * (seg_col == last_seg).astype(F32)
        mats, scores = [], []
        for h in range(heads):
            q = qn[r, h * DK : (h + 1) * DK]
            k = kn[r, h * DK : (h + 1) * DK]
            ratio = jnp.exp(jnp.minimum(cum[:, h : h + 1] - cum_t[h : h + 1], 0.0)) * keepf
            beta = beta_c[:, heads + h : heads + h + 1]
            both = mm_nt(jnp.concatenate([q, k], axis=0), k)
            scores.append((ratio * both[:CH]).astype(BF16))
            mats.append(beta * ratio * strict * both[CH:])
        ts = full_inverse(mats)
        for h in range(heads):
            q = qn[r, h * DK : (h + 1) * DK]
            k = kn[r, h * DK : (h + 1) * DK]
            vcols = slice(h * DVAL, (h + 1) * DVAL)
            beta = beta_c[:, heads + h : heads + h + 1]
            st = start[:, h : h + 1]
            tb = ts[h].astype(BF16)
            s0 = state[h]
            s0b = s0.astype(BF16)
            t_out[n, h] = tb
            s_out[n, h] = s0b
            both = mm(jnp.concatenate([q, k], axis=0), s0b)
            res = beta * (vn[r, vcols] - st * both[CH:])
            un = mm(tb, res).astype(BF16)
            u_out[r, vcols] = un
            o = st * both[:CH] + mm(scores[h], un)
            state[h] = start[CH - 1 : CH, h : h + 1] * s0 + mm_tn(k.astype(F32) * tail[:, h : h + 1], un)
            o_out[r, vcols] = o.astype(BF16)
            g = preg[r, vcols].astype(F32)
            rn = lax.rsqrt(jnp.mean(o * o, axis=-1, keepdims=True) + EPSILON)
            mixed[r, vcols] = (o * rn * gain[...] * (g * sigmoid(g))).astype(BF16)


def mixer_fwd(preq, prek, prev, preg, ab, masks, segc, segr, taps_q, taps_k, taps_v, gate_par, gain):
    length = preq.shape[0]
    heads = preq.shape[1] // DK
    count = length // CH
    vm = pl.BlockSpec(memory_space=pltpu.VMEM)
    out_shape = (
        jax.ShapeDtypeStruct((length, heads * DVAL), BF16),
        jax.ShapeDtypeStruct((length, heads * DK), BF16),
        jax.ShapeDtypeStruct((length, heads * DK), BF16),
        jax.ShapeDtypeStruct((length, heads * DVAL), BF16),
        jax.ShapeDtypeStruct((count, heads, CH, CH), BF16),
        jax.ShapeDtypeStruct((count, heads, DK, DVAL), BF16),
        jax.ShapeDtypeStruct((length, heads * DVAL), BF16),
        jax.ShapeDtypeStruct((length, heads * DVAL), BF16),
    )
    return pl.pallas_call(
        functools.partial(mixer_fwd_kernel, heads),
        out_shape=out_shape,
        in_specs=[vm] * 13,
        out_specs=[vm] * len(out_shape),
        scratch_shapes=[
            pltpu.VMEM((length, heads * DK), BF16),
            pltpu.VMEM((length, heads * DK), BF16),
            pltpu.VMEM((length, heads * DVAL), F32),
            pltpu.VMEM((length + CH, CH), F32),
            pltpu.VMEM((heads, DK, DVAL), F32),
        ],
        compiler_params=pltpu.CompilerParams(vmem_limit_bytes=60 * 2**20),
        cost_estimate=pl.CostEstimate(flops=20 * 10**9, bytes_accessed=70 * 2**20, transcendentals=0),
        name="mixer_forward",
    )(preq, prek, prev, preg, ab, masks, segc, segr, taps_q, taps_k, taps_v, gate_par, gain)


def mixer_bwd_kernel(
    heads, dmix, preg, ab_ref, masks, segc, segr, taps_q, taps_k, taps_v, gate_par, gain,
    cq, ck, cv, t_in, s_in, u_in, o_in,
    dpq, dpk, dpv, dpg, dab,
    qn, kn, vn, cum_s, dstate, dqs, dks, dvs, gcol,
):
    length = dmix.shape[0]
    count = length // CH

    def key_tile(h, carry):
        cols = pl.ds(pl.multiple_of(h * DK, DK), DK)
        for save, dst, scale in ((cq, qn, INV_ROOT), (ck, kn, 1.0)):
            c = save[:, cols].astype(F32)
            u = c * sigmoid(c)
            n = lax.rsqrt(jnp.sum(u * u, axis=-1, keepdims=True) + EPSILON) * scale
            dst[:, cols] = (u * n).astype(BF16)
        for half in range(2):
            vcols = pl.ds(pl.multiple_of(h * DVAL + half * DK, DK), DK)
            c = cv[:, vcols].astype(F32)
            vn[:, vcols] = c * sigmoid(c)
        return carry

    lax.fori_loop(0, heads, key_tile, 0)
    row = iota2((CH, CH), 0)
    col = iota2((CH, CH), 1)
    upper = (row <= col).astype(BF16)
    lower = (row >= col).astype(BF16)
    log_decay, z_all = gate_columns(ab_ref[...], gate_par[0:1], gate_par[1:2])
    beta_all = sigmoid(ab_ref[...])
    for n in range(count):
        cum_s[n * CH : (n + 1) * CH] = exact_tn(upper, log_decay[n * CH : (n + 1) * CH])
    for h in range(heads):
        dstate[h] = jnp.zeros((DK, DVAL), F32)
    lane = iota2((1, CH), 1)
    strict = (row > col).astype(F32)
    ones = jnp.ones((CH, CH), BF16)

    for n in range(count - 1, -1, -1):
        r = pl.ds(n * CH, CH)
        seg_col = segc[r]
        seg_row = segr[0:1, n * CH : (n + 1) * CH]
        keepf = ((seg_col == seg_row) & (row >= col)).astype(F32)
        cum = cum_s[r]
        cum_t = cum.T
        beta_c = beta_all[n * CH : (n + 1) * CH]
        prev_last = segc[n * CH - 1 : n * CH] if n else jnp.full((1, CH), -1.0, F32)
        start = jnp.exp(cum) * (seg_col == prev_last).astype(F32)
        last_seg = segc[(n + 1) * CH - 1 : (n + 1) * CH]
        tail = jnp.exp(cum[CH - 1 : CH] - cum) * (seg_col == last_seg).astype(F32)
        dcum_all = jnp.zeros((CH, CH), F32)
        dbeta_all = jnp.zeros((CH, CH), F32)
        dlast_all = jnp.zeros((1, CH), F32)
        for h in range(heads):
            qc = slice(h * DK, (h + 1) * DK)
            vcols = slice(h * DVAL, (h + 1) * DVAL)
            here = (lane == h).astype(F32)
            o = o_in[r, vcols].astype(F32)
            g = preg[r, vcols].astype(F32)
            dm = dmix[r, vcols].astype(F32)
            sg = sigmoid(g)
            rn = lax.rsqrt(jnp.mean(o * o, axis=-1, keepdims=True) + EPSILON)
            on = o * rn
            y = on * gain[...]
            dpg[r, vcols] = (dm * y * (sg * (1.0 + g * (1.0 - sg)))).astype(BF16)
            dy = dm * (g * sg) * gain[...]
            do = rn * (dy - on * jnp.mean(dy * on, axis=-1, keepdims=True))
            dob = do.astype(BF16)
            q = qn[r, qc]
            k = kn[r, qc]
            kf = k.astype(F32)
            qf = q.astype(F32)
            un = u_in[r, vcols]
            s0 = s_in[n, h]
            tb = t_in[n, h]
            beta = beta_c[:, heads + h : heads + h + 1]
            st = start[:, h : h + 1]
            tl = tail[:, h : h + 1]
            carry_scale = start[CH - 1 : CH, h : h + 1]
            ratio = jnp.exp(jnp.minimum(cum[:, h : h + 1] - cum_t[h : h + 1], 0.0)) * keepf
            both = mm_nt(jnp.concatenate([q, k], axis=0), k)
            scores = ratio * both[:CH]
            rs = ratio * strict
            amat = rs * both[CH:]
            qk_state = mm(jnp.concatenate([q, k], axis=0), s0)
            ks = qk_state[CH:]
            ds1 = dstate[h]
            ds1b = ds1.astype(BF16)
            ktail = (kf * tl).astype(BF16)
            dun = mm_tn(scores, dob) + mm(ktail, ds1b)
            dres = mm_tn(tb, dun)
            dresb = dres.astype(BF16)
            dks0 = (-(beta * st) * dres).astype(BF16)
            qst = (qf * st).astype(BF16)
            dstate[h] = carry_scale * ds1 + mm_tn(jnp.concatenate([qst, k], axis=0), jnp.concatenate([dob, dks0], axis=0))
            both_d = mm_nt(jnp.concatenate([dob, dresb], axis=0), un)
            dscore = both_d[:CH]
            da = -both_d[CH:]
            dqk = (dscore * ratio).astype(BF16)
            dkk = (da * beta * rs).astype(BF16)
            dspread = dscore * scores + da * beta * amat
            dbeta = jnp.sum(da * amat, axis=-1, keepdims=True) + jnp.sum(
                dres * (vn[r, vcols] - st * ks), axis=-1, keepdims=True
            )
            dvs[r, vcols] = beta * dres
            by_state = mm_nt(jnp.concatenate([dob, dks0, un], axis=0), jnp.concatenate([s0, ds1b], axis=0))
            dq_state = by_state[:CH, :DK]
            dq = st * dq_state + mm(dqk, k)
            dktail = by_state[2 * CH :, DK:]
            dk = (
                by_state[CH : 2 * CH, :DK]
                + tl * dktail
                + mm_tn(dqk, q)
                + mm(dkk, k)
                + mm_tn(dkk, k)
            )
            dqs[r, qc] = dq
            dks[r, qc] = dk
            dstart_s = st * jnp.sum(qf * dq_state, axis=-1, keepdims=True) + st * (
                -beta * jnp.sum(dres * ks, axis=-1, keepdims=True)
            )
            dtail_s = tl * jnp.sum(kf * dktail, axis=-1, keepdims=True)
            dcarry = carry_scale * jnp.sum(jnp.sum(ds1 * s0.astype(F32), axis=-1, keepdims=True), axis=0, keepdims=True)
            colsum = exact_cols(dspread, ones)
            dcum = jnp.sum(dspread, axis=-1, keepdims=True) - colsum[:, 0:1] + dstart_s - dtail_s
            dlast = jnp.sum(dtail_s, axis=0, keepdims=True) + dcarry
            dcum_all = dcum_all + dcum * here
            dlast_all = dlast_all + dlast * here
            dbeta_all = dbeta_all + dbeta * (lane == heads + h).astype(F32)
        dcum_all = dcum_all + dlast_all * (row == CH - 1).astype(F32)
        gcol[r] = exact_tn(lower, dcum_all) + dbeta_all * beta_c * (1.0 - beta_c)

    slope = -jnp.exp(gate_par[0:1]) * sigmoid(z_all)
    dab[...] = (gcol[...] * jnp.where(lane < heads, slope, 1.0)).astype(BF16)

    def back_tile(h, carry):
        cols = pl.ds(pl.multiple_of(h * DK, DK), DK)
        for save, dsrc, taps, dst, scale in ((cq, dqs, taps_q, dpq, INV_ROOT), (ck, dks, taps_k, dpk, 1.0)):
            c = save[:, cols].astype(F32)
            sg = sigmoid(c)
            u = c * sg
            n = lax.rsqrt(jnp.sum(u * u, axis=-1, keepdims=True) + EPSILON)
            un = u * n
            d = dsrc[:, cols] * scale
            du = n * (d - un * jnp.sum(d * un, axis=-1, keepdims=True))
            dc = du * (sg * (1.0 + c * (1.0 - sg)))
            dst[:, cols] = conv_rows_back(dc, taps[:, cols], masks, length).astype(BF16)
        for half in range(2):
            vcols = pl.ds(pl.multiple_of(h * DVAL + half * DK, DK), DK)
            c = cv[:, vcols].astype(F32)
            sg = sigmoid(c)
            dc = dvs[:, vcols] * (sg * (1.0 + c * (1.0 - sg)))
            dpv[:, vcols] = conv_rows_back(dc, taps_v[:, vcols], masks, length).astype(BF16)
        return carry

    lax.fori_loop(0, heads, back_tile, 0)


def exact_cols(x, ones):
    hi = x.astype(BF16)
    lo = (x - hi.astype(F32)).astype(BF16)
    return mm_tn(hi, ones) + mm_tn(lo, ones)


def mixer_bwd(dmix, preg, ab, masks, segc, segr, taps_q, taps_k, taps_v, gate_par, gain, saved):
    length = dmix.shape[0]
    heads = dmix.shape[1] // DVAL
    vm = pl.BlockSpec(memory_space=pltpu.VMEM)
    out_shape = (
        jax.ShapeDtypeStruct((length, heads * DK), BF16),
        jax.ShapeDtypeStruct((length, heads * DK), BF16),
        jax.ShapeDtypeStruct((length, heads * DVAL), BF16),
        jax.ShapeDtypeStruct((length, heads * DVAL), BF16),
        jax.ShapeDtypeStruct((length, CH), BF16),
    )
    return pl.pallas_call(
        functools.partial(mixer_bwd_kernel, heads),
        out_shape=out_shape,
        in_specs=[vm] * 18,
        out_specs=[vm] * len(out_shape),
        scratch_shapes=[
            pltpu.VMEM((length, heads * DK), BF16),
            pltpu.VMEM((length, heads * DK), BF16),
            pltpu.VMEM((length, heads * DVAL), F32),
            pltpu.VMEM((length, CH), F32),
            pltpu.VMEM((heads, DK, DVAL), F32),
            pltpu.VMEM((length, heads * DK), F32),
            pltpu.VMEM((length, heads * DK), F32),
            pltpu.VMEM((length, heads * DVAL), F32),
            pltpu.VMEM((length, CH), F32),
        ],
        compiler_params=pltpu.CompilerParams(vmem_limit_bytes=60 * 2**20),
        cost_estimate=pl.CostEstimate(flops=30 * 10**9, bytes_accessed=100 * 2**20, transcendentals=0),
        name="mixer_backward",
    )(dmix, preg, ab, masks, segc, segr, taps_q, taps_k, taps_v, gate_par, gain, *saved)


MESH_ID = pl.DeviceIdType.MESH
RING = 4
PIECES = 4
WIDE_VMEM = 60 * 2**20
SHARE = 4
ADAPTER_RANK = 16


def ring_places():
    m = lax.axis_index("mp")
    return m, lax.rem(m + 3, RING), lax.rem(m + 1, RING), lax.rem(m + 2, RING)


def ring_barrier(places):
    _, left, right, _ = places
    barrier = pltpu.get_barrier_semaphore()
    for neighbour in (left, right):
        pl.semaphore_signal(barrier, inc=1, device_id={"mp": neighbour}, device_id_type=MESH_ID)
    pl.semaphore_wait(barrier, 2)


class RingGather:
    def __init__(self, buf, send, recv, places):
        self.buf, self.send, self.recv = buf, send, recv
        self.m, self.left, self.right, self.opp = places
        half = buf.shape[1] // 2
        self.top, self.bot = pl.ds(0, half), pl.ds(half, half)

    def begin(self, i, slot, part, to):
        step = part.size // PIECES
        for n in range(PIECES):
            self.copy(i, slot, pl.ds(part.start + n * step, step), to).start()

    def copy(self, i, slot, part, to):
        ref = self.buf.at[slot, part]
        return pltpu.make_async_remote_copy(
            src_ref=ref,
            dst_ref=ref,
            send_sem=self.send.at[i],
            recv_sem=self.recv.at[i],
            device_id={"mp": to},
            device_id_type=MESH_ID,
        )

    def start(self):
        self.begin(0, self.m, self.top, self.right)
        self.begin(1, self.m, self.bot, self.left)
        self.begin(2, self.m, self.bot, self.right)
        self.begin(3, self.m, self.top, self.left)

    def forward(self):
        self.copy(0, self.left, self.top, self.right).wait_recv()
        self.begin(4, self.left, self.top, self.right)
        self.copy(1, self.right, self.bot, self.left).wait_recv()
        self.begin(5, self.right, self.bot, self.left)

    def wait_left(self):
        self.copy(2, self.left, self.bot, self.right).wait_recv()

    def wait_right(self):
        self.copy(3, self.right, self.top, self.left).wait_recv()

    def wait_opp(self):
        self.copy(4, self.opp, self.top, self.right).wait_recv()
        self.copy(5, self.opp, self.bot, self.left).wait_recv()

    def finish(self):
        self.copy(0, self.m, self.top, self.right).wait_send()
        self.copy(1, self.m, self.bot, self.left).wait_send()
        self.copy(2, self.m, self.bot, self.right).wait_send()
        self.copy(3, self.m, self.top, self.left).wait_send()
        self.copy(4, self.left, self.top, self.right).wait_send()
        self.copy(5, self.right, self.bot, self.left).wait_send()


class RingScatter:
    def __init__(self, sbuf, rbuf, acc, send, recv, places):
        self.sbuf, self.rbuf, self.acc, self.send, self.recv = sbuf, rbuf, acc, send, recv
        self.m, self.left, self.right, self.opp = places
        self.half = sbuf.shape[1]

    def begin(self, i):
        step = self.half // PIECES
        for n in range(PIECES):
            self.copy(i, pl.ds(n * step, step)).start()

    def copy(self, i, part=slice(None)):
        to = self.right if i % 2 == 0 else self.left
        return pltpu.make_async_remote_copy(
            src_ref=self.sbuf.at[i, part],
            dst_ref=self.rbuf.at[i, part],
            send_sem=self.send.at[i],
            recv_sem=self.recv.at[i],
            device_id={"mp": to},
            device_id_type=MESH_ID,
        )

    def run(self, part, meanwhile=None):
        half = self.half
        rows = 2 * half

        def put_far(cols, val):
            self.sbuf[0, :, cols] = val[:half].astype(BF16)
            self.sbuf[1, :, cols] = val[half:rows].astype(BF16)
            self.acc[0, :, cols] = val[rows:]
            self.sbuf[2, :, cols] = val[rows + half :].astype(BF16)

        part((self.opp, self.right), put_far)
        self.begin(0)
        self.begin(1)
        self.begin(2)

        def put_near(cols, val):
            self.acc[1, :, cols] = val[:rows]
            self.sbuf[3, :, cols] = val[:half].astype(BF16)
            self.acc[2, :, cols] = val[rows:]

        part((self.left, self.m), put_near)
        self.begin(3)
        if meanwhile is not None:
            meanwhile()
        self.copy(0).wait_recv()
        self.sbuf[4] = (self.acc[0, 0:half] + self.rbuf[0].astype(F32)).astype(BF16)
        self.begin(4)
        self.copy(1).wait_recv()
        self.sbuf[5] = (self.acc[1, half:rows] + self.rbuf[1].astype(F32)).astype(BF16)
        self.begin(5)
        for i in range(2, 6):
            self.copy(i).wait_recv()

    def total(self, rows, cols):
        lo, hi = rows
        if hi <= self.half:
            a, b, r = self.rbuf[4, lo:hi, cols], self.rbuf[3, lo:hi, cols], slice(lo, hi)
        else:
            r = slice(lo, hi)
            lo, hi = lo - self.half, hi - self.half
            a, b = self.rbuf[2, lo:hi, cols], self.rbuf[5, lo:hi, cols]
        return self.acc[2, r, cols] + a.astype(F32) + b.astype(F32)

    def finish(self):
        for i in range(6):
            self.copy(i).wait_send()


class Loads:
    def __init__(self, pairs, sems):
        self.copies = [pltpu.make_async_copy(src, dst, sems.at[n]) for n, (src, dst) in enumerate(pairs)]
        self.waited = set()

    def start(self):
        for c in self.copies:
            c.start()

    def wait(self, *which):
        for n in which:
            if n not in self.waited:
                self.copies[n].wait()
                self.waited.add(n)


def tiles(total, step=512):
    return [(at, min(step, total - at)) for at in range(0, total, step)]


def block_rows(place, rows):
    return pl.ds(pl.multiple_of(place * rows, rows), rows)


def both_rows(ref, pair, rows, cols=slice(None)):
    return jnp.concatenate([ref[block_rows(place, rows), cols] for place in pair], axis=0)


def put_rows(ref, pair, rows, cols, val):
    for n, place in enumerate(pair):
        ref[block_rows(place, rows), cols] = val[n * rows : (n + 1) * rows]


def norm_factor(v):
    return lax.rsqrt(jnp.mean(v * v, axis=-1, keepdims=True) + EPSILON)


def project_kernel(
    resid, gain, select, bab, wqk_h, wvg_h, wab_h, ain_h, bqk_h, bvg_h,
    normed_h, low, pq, pk, pv, pg, pab,
    gath, wqk, wvg, wab, ain, bqk, bvg, wsem, osem, send, recv,
):
    rows = resid.shape[0]
    places = ring_places()
    loads = Loads(
        [(ain_h, ain), (wqk_h, wqk), (bqk_h, bqk), (wvg_h, wvg), (bvg_h, bvg), (wab_h, wab)], wsem
    )
    loads.start()
    m = places[0]
    for at in range(0, rows, 32):
        v = resid[at : at + 32]
        gath[m, at : at + 32] = (v * norm_factor(v) * gain[...]).astype(BF16)
    ring_barrier(places)
    ring = RingGather(gath, send, recv, places)
    ring.start()
    ac = select.shape[1]

    def compute(place):
        r = block_rows(place, rows)
        x = gath[place]
        sel = select[r]
        loads.wait(0)
        for n in range(ain.shape[1] // ac):
            low[r, n * ac : (n + 1) * ac] = (mm(x, ain[:, n * ac : (n + 1) * ac]) * sel).astype(BF16)
        loads.wait(1, 2)
        for n, dst in enumerate((pq, pk)):
            lo = low[r, n * ac : (n + 1) * ac]
            dst[r] = (mm(x, wqk[n]) + mm(lo, bqk[n])).astype(BF16)
        loads.wait(3, 4)
        for n, dst in enumerate((pv, pg)):
            lo = low[r, (n + 2) * ac : (n + 3) * ac]
            for at, size in tiles(wvg.shape[2]):
                c = slice(at, at + size)
                dst[r, c] = (mm(x, wvg[n, :, c]) + mm(lo, bvg[n, :, c])).astype(BF16)
        loads.wait(5)
        pab[r] = (
            mm(x, wab[...]) + mm(low[r, 4 * ac : 5 * ac], bab[0]) + mm(low[r, 5 * ac : 6 * ac], bab[1])
        )

    compute(m)
    ring.forward()
    ring.wait_left()
    compute(places[1])
    ring.wait_right()
    compute(places[2])
    ring.wait_opp()
    out = pltpu.make_async_copy(gath, normed_h, osem)
    out.start()
    compute(places[3])
    ring.finish()
    out.wait()


def specs(n_vmem, n_any):
    return [pl.BlockSpec(memory_space=pltpu.VMEM)] * n_vmem + [pl.BlockSpec(memory_space=pl.ANY)] * n_any


def sds(shape, dtype=BF16):
    return jax.ShapeDtypeStruct(shape, dtype)


def ring_params(collective_id):
    return pltpu.CompilerParams(
        collective_id=collective_id, has_side_effects=True, vmem_limit_bytes=WIDE_VMEM
    )


def like(a):
    return pltpu.VMEM(a.shape, a.dtype)


DMA_SEMS = pltpu.SemaphoreType.DMA


def project(resid, gain, select, bab, wqk, wvg, wab, ain, bqk, bvg):
    rows, width = resid.shape
    group = rows * RING
    kw, vw = wqk.shape[2], wvg.shape[2]
    vm, hb = specs(1, 1)
    return pl.pallas_call(
        project_kernel,
        out_shape=(
            sds((RING, rows, width)),
            sds((group, ain.shape[1])),
            sds((group, kw)),
            sds((group, kw)),
            sds((group, vw)),
            sds((group, vw)),
            sds((group, CH), F32),
        ),
        in_specs=[vm] * 4 + [hb] * 6,
        out_specs=[hb] + [vm] * 6,
        scratch_shapes=[
            pltpu.VMEM((RING, rows, width), BF16),
            like(wqk), like(wvg), like(wab), like(ain), like(bqk), like(bvg),
            DMA_SEMS((6,)), DMA_SEMS(()), DMA_SEMS((6,)), DMA_SEMS((6,)),
        ],
        compiler_params=ring_params(1),
        cost_estimate=pl.CostEstimate(flops=8 * 10**9, bytes_accessed=30 * 2**20, transcendentals=0),
        name="gather_project",
    )(resid, gain, select, bab, wqk, wvg, wab, ain, bqk, bvg)


def feed_kernel(
    mixed, resid, gain, select, wout_h, aout_h, bout_h, affn_h, gu_h, bgu_h, down_h, adown_h,
    middle, rank_out, normed_h, rank2, gate, up, hidden, dpart, rpart,
    gath, wout, aout, bout, affn, gu, bgu, down, adown, sbuf, rbuf, acc, wsem, osem, send, recv, send2, recv2,
):
    rows, width = resid.shape
    places = ring_places()
    m = places[0]
    loads = Loads(
        [
            (wout_h, wout), (aout_h, aout), (bout_h, bout), (affn_h, affn),
            (gu_h, gu), (bgu_h, bgu), (down_h, down), (adown_h, adown),
        ],
        wsem,
    )
    loads.start()
    ac = select.shape[1]
    ff = gu.shape[2]
    loads.wait(0, 1)
    ring_barrier(places)
    scatter = RingScatter(sbuf, rbuf, acc, send, recv, places)

    def part(pair, put):
        x = both_rows(mixed, pair, rows)
        for at, size in tiles(width):
            put(slice(at, at + size), mm(x, wout[:, at : at + size]))
        put(slice(width, width + ac), mm(x, aout[...]))

    scatter.run(part)
    loads.wait(2)
    sel_own = select[block_rows(m, rows)]
    half = rows // 2
    for lo in (0, half):
        bounds = (lo, lo + half)
        gath[m, lo : lo + half, width : width + ac] = (
            scatter.total(bounds, slice(width, width + ac)) * sel_own[lo : lo + half]
        ).astype(BF16)
    ro = gath[m, :, width : width + ac]
    for at, size in tiles(width):
        c = slice(at, at + size)
        extra = mm(ro, bout[:, c])
        for lo in (0, half):
            middle[lo : lo + half, c] = (
                resid[lo : lo + half, c] + scatter.total((lo, lo + half), c) + extra[lo : lo + half]
            )
    for at in range(0, rows, 32):
        v = middle[at : at + 32]
        gath[m, at : at + 32, 0:width] = (v * norm_factor(v) * gain[...]).astype(BF16)
    ring = RingGather(gath, send2, recv2, places)
    ring.start()

    def compute(place):
        r = block_rows(place, rows)
        x = gath[place, :, 0:width]
        rank_out[r] = gath[place, :, width : width + ac]
        sel = select[r]
        loads.wait(3)
        for n in range(2):
            rank2[r, n * ac : (n + 1) * ac] = (mm(x, affn[:, n * ac : (n + 1) * ac]) * sel).astype(BF16)
        loads.wait(4, 5)
        r0 = rank2[r, 0:ac]
        r1 = rank2[r, ac : 2 * ac]
        for at, size in tiles(ff):
            c = slice(at, at + size)
            g = mm(x, gu[0, :, c]) + mm(r0, bgu[0, :, c])
            u = mm(x, gu[1, :, c]) + mm(r1, bgu[1, :, c])
            gate[r, c] = g.astype(BF16)
            up[r, c] = u.astype(BF16)
            hidden[r, c] = (g * sigmoid(g) * u).astype(BF16)
        loads.wait(6, 7)
        h = hidden[r]
        for at, size in tiles(width):
            c = slice(at, at + size)
            dpart[r, c] = mm(h, down[:, c]).astype(BF16)
        rpart[r] = mm(h, adown[...]).astype(BF16)

    compute(m)
    ring.forward()
    ring.wait_left()
    compute(places[1])
    ring.wait_right()
    compute(places[2])
    ring.wait_opp()
    out = pltpu.make_async_copy(gath.at[:, :, pl.ds(0, width)], normed_h, osem)
    out.start()
    compute(places[3])
    scatter.finish()
    ring.finish()
    out.wait()


def feed(mixed, resid, gain, select, wout, aout, bout, affn, gu, bgu, down, adown):
    rows, width = resid.shape
    group = rows * RING
    ff = gu.shape[2]
    ac = select.shape[1]
    cols = width + ac
    vm, hb = specs(1, 1)
    return pl.pallas_call(
        feed_kernel,
        out_shape=(
            sds((rows, width), F32),
            sds((group, ac)),
            sds((RING, rows, width)),
            sds((group, 2 * ac)),
            sds((group, ff)),
            sds((group, ff)),
            sds((group, ff)),
            sds((group, width)),
            sds((group, ac)),
        ),
        in_specs=[vm] * 4 + [hb] * 8,
        out_specs=[vm, vm, hb] + [vm] * 6,
        scratch_shapes=[
            pltpu.VMEM((RING, rows, cols), BF16),
            like(wout), like(aout), like(bout), like(affn), like(gu), like(bgu), like(down), like(adown),
            pltpu.VMEM((6, rows // 2, cols), BF16),
            pltpu.VMEM((6, rows // 2, cols), BF16),
            pltpu.VMEM((3, rows, cols), F32),
            DMA_SEMS((8,)), DMA_SEMS(()),
            DMA_SEMS((6,)), DMA_SEMS((6,)), DMA_SEMS((6,)), DMA_SEMS((6,)),
        ],
        compiler_params=ring_params(2),
        cost_estimate=pl.CostEstimate(flops=13 * 10**9, bytes_accessed=40 * 2**20, transcendentals=0),
        name="feed_forward",
    )(mixed, resid, gain, select, wout, aout, bout, affn, gu, bgu, down, adown)


def feed_back_kernel(
    cot, middle, gate, up, rpart, select, gain, bdown_h, down_h, adown_h, gu_h, bgu_h, affn_h, bout_h, wout_h, aout_h,
    g_rank_down, g_gate, g_up, g_rank2, g_middle, g_branch_h, g_rank_out, g_mixed, rank_down,
    gath, bdown, down, adown, gu, bgu, affn, bout, wout, aout,
    sbuf, rbuf, acc, wsem, osem, send, recv, send2, recv2,
):
    rows, width = middle.shape
    places = ring_places()
    m = places[0]
    loads = Loads(
        [
            (bdown_h, bdown), (down_h, down), (adown_h, adown), (gu_h, gu), (bgu_h, bgu),
            (affn_h, affn), (bout_h, bout), (wout_h, wout), (aout_h, aout),
        ],
        wsem,
    )
    loads.start()
    ac = select.shape[1]
    ff = gu.shape[2]
    ring_barrier(places)
    scatter = RingScatter(sbuf, rbuf, acc, send, recv, places)

    def part(pair, put):
        x = both_rows(cot, pair, rows)
        sel = both_rows(select, pair, rows)
        loads.wait(0)
        grd = (mm_nt(x, bdown[...]) * sel).astype(BF16)
        put_rows(g_rank_down, pair, rows, slice(None), grd)
        loads.wait(1, 2)
        for at, size in tiles(ff, 256):
            c = slice(at, at + size)
            gh = mm_nt(x, down[c]) + mm_nt(grd, adown[c])
            g = both_rows(gate, pair, rows, c).astype(F32)
            u = both_rows(up, pair, rows, c).astype(F32)
            sg = sigmoid(g)
            put_rows(g_gate, pair, rows, c, (gh * u * (sg * (1.0 + g * (1.0 - sg)))).astype(BF16))
            put_rows(g_up, pair, rows, c, (gh * g * sg).astype(BF16))
        loads.wait(3, 4, 5)
        gg = both_rows(g_gate, pair, rows)
        gu_ = both_rows(g_up, pair, rows)
        r2a = (mm_nt(gg, bgu[0]) * sel).astype(BF16)
        r2b = (mm_nt(gu_, bgu[1]) * sel).astype(BF16)
        put_rows(g_rank2, pair, rows, slice(0, ac), r2a)
        put_rows(g_rank2, pair, rows, slice(ac, 2 * ac), r2b)
        r2 = jnp.concatenate([r2a, r2b], axis=1)
        for at, size in tiles(width, 256):
            c = slice(at, at + size)
            put(c, mm_nt(gg, gu[0, c]) + mm_nt(gu_, gu[1, c]) + mm_nt(r2, affn[c]))
        put(slice(width, width + ac), both_rows(rpart, pair, rows).astype(F32))

    scatter.run(part)
    sel_own = select[block_rows(m, rows)]
    step = 16
    for at in range(0, rows, step):
        b = (at, at + step)
        g = scatter.total(b, slice(0, width)) * gain[...]
        v = middle[at : at + step]
        n = norm_factor(v)
        v = v * n
        gm = cot[pl.ds(pl.multiple_of(m * rows + at, step), step)].astype(F32) + n * (
            g - v * jnp.mean(g * v, axis=-1, keepdims=True)
        )
        g_middle[at : at + step] = gm
        gath[m, at : at + step, 0:width] = gm.astype(BF16)
        gath[m, at : at + step, width : width + ac] = (
            scatter.total(b, slice(width, width + ac)) * sel_own[at : at + step]
        ).astype(BF16)
    ring = RingGather(gath, send2, recv2, places)
    ring.start()

    def compute(*pair):
        x = jnp.concatenate([gath[place, :, 0:width] for place in pair], axis=0)
        loads.wait(6, 7, 8)
        gro = (mm_nt(x, bout[...]) * both_rows(select, pair, rows)).astype(BF16)
        put_rows(g_rank_out, pair, rows, slice(None), gro)
        for at, size in tiles(wout.shape[0], 256):
            c = slice(at, at + size)
            put_rows(g_mixed, pair, rows, c, (mm_nt(x, wout[c]) + mm_nt(gro, aout[c])).astype(BF16))
        for place in pair:
            rank_down[block_rows(place, rows)] = gath[place, :, width : width + ac]

    compute(m)
    ring.forward()
    ring.wait_left()
    ring.wait_right()
    compute(places[1], places[2])
    ring.wait_opp()
    out = pltpu.make_async_copy(gath.at[:, :, pl.ds(0, width)], g_branch_h, osem)
    out.start()
    compute(places[3])
    scatter.finish()
    ring.finish()
    out.wait()


def feed_back(cot, middle, gate, up, rpart, select, gain, bdown, down, adown, gu, bgu, affn, bout, wout, aout):
    rows, width = middle.shape
    group = rows * RING
    ff = gu.shape[2]
    ac = select.shape[1]
    vm, hb = specs(1, 1)
    return pl.pallas_call(
        feed_back_kernel,
        out_shape=(
            sds((group, ac)),
            sds((group, ff)),
            sds((group, ff)),
            sds((group, 2 * ac)),
            sds((rows, width), F32),
            sds((RING, rows, width)),
            sds((group, ac)),
            sds((group, wout.shape[0])),
            sds((group, ac)),
        ),
        in_specs=[vm] * 7 + [hb] * 9,
        out_specs=[vm] * 5 + [hb] + [vm] * 3,
        scratch_shapes=[
            pltpu.VMEM((RING, rows, width + ac), BF16),
            like(bdown), like(down), like(adown), like(gu), like(bgu), like(affn), like(bout), like(wout), like(aout),
            pltpu.VMEM((6, rows // 2, width + ac), BF16),
            pltpu.VMEM((6, rows // 2, width + ac), BF16),
            pltpu.VMEM((3, rows, width + ac), F32),
            DMA_SEMS((9,)), DMA_SEMS(()),
            DMA_SEMS((6,)), DMA_SEMS((6,)), DMA_SEMS((6,)), DMA_SEMS((6,)),
        ],
        compiler_params=ring_params(3),
        cost_estimate=pl.CostEstimate(flops=13 * 10**9, bytes_accessed=40 * 2**20, transcendentals=0),
        name="feed_backward",
    )(cot, middle, gate, up, rpart, select, gain, bdown, down, adown, gu, bgu, affn, bout, wout, aout)


def unfold(n, per):
    row = iota2((n, n), 0)
    col = iota2((n, n), 1)
    part = per // SHARE
    wide = n // part
    hit = (row // per == (col % wide) // SHARE) & (row % SHARE == col % SHARE) & ((row // SHARE) % part == col // wide)
    return hit.astype(F32).astype(BF16)


def fold_maps(count, base, ac):
    line = iota2((count, ac), 0)
    col = iota2((count, ac), 1)
    hit = (line // ac) * ADAPTER_RANK + line % ADAPTER_RANK + base == col
    return hit.astype(F32).astype(BF16)


def project_back_kernel(
    dq, dk, dv, dg, dab, resid, g_middle, select, gain, bab, low, g_rank2, normed, normed2,
    wqk_h, wvg_h, wab_h, ain_h, bqk_h, bvg_h,
    g_tokens, stage,
    wqk, wvg, wab, ain, bqk, bvg, g_rank, sbuf, rbuf, acc, small, wsem, send, recv, send2, recv2,
):
    rows, width = resid.shape
    places = ring_places()
    m = places[0]
    loads = Loads(
        [(bqk_h, bqk), (bvg_h, bvg), (ain_h, ain), (wqk_h, wqk), (wvg_h, wvg), (wab_h, wab)], wsem
    )
    loads.start()
    ac = select.shape[1]
    n_dp = stage.shape[0]
    heads = dq.shape[1] // DK
    ring_barrier(places)
    scatter = RingScatter(sbuf, rbuf, acc, send, recv, places)
    six = ain.shape[1] // ac
    fold_in = fold_maps(six * ac, 0, ac)
    fold_two = fold_maps(2 * ac, six * ADAPTER_RANK, ac)

    def part(pair, put):
        sel = both_rows(select, pair, rows)
        xs = [both_rows(d, pair, rows) for d in (dq, dk, dv, dg, dab)]
        loads.wait(0, 1)
        seconds = [bqk[0], bqk[1], bvg[0], bvg[1], bab[0], bab[1]]
        for n in range(six):
            g_rank[:, n * ac : (n + 1) * ac] = (mm_nt(xs[min(n, 4)], seconds[n]) * sel).astype(BF16)
        gr = g_rank[...]
        put(slice(width, width + ac), mm(gr, fold_in) + mm(both_rows(g_rank2, pair, rows), fold_two))
        loads.wait(2, 3, 4, 5)
        for at, size in tiles(width, 256):
            c = slice(at, at + size)
            put(
                c,
                mm_nt(xs[0], wqk[0, c])
                + mm_nt(xs[1], wqk[1, c])
                + mm_nt(xs[2], wvg[0, c])
                + mm_nt(xs[3], wvg[1, c])
                + mm_nt(xs[4], wab[c])
                + mm_nt(gr, ain[c]),
            )

    deal = unfold(n_dp * 16, 16)
    parts = 16 // SHARE

    def keep(pieces, at):
        w = pieces[0].shape[1]
        rest = deal if len(pieces) == parts else deal[:, 0 : len(pieces) * n_dp * SHARE]
        got = mm(rest, jnp.concatenate([p.astype(BF16) for p in pieces], axis=0))
        stage[:, :, at : at + w] = got.astype(BF16).reshape(n_dp, 16, w)
        return at + w

    def late():
        at = 0
        for n, d in enumerate((dq, dk, dv, dg)):
            w = d.shape[1] // parts
            lo = low[:, n * ac : (n + 1) * ac]
            at = keep([mm_tn(lo, d[:, p * w : (p + 1) * w]) for p in range(parts)], at)
        lane = iota2((1, CH), 1)
        ga = mm_tn(low[:, 4 * ac : 5 * ac], dab[...])
        gb = mm_tn(low[:, 5 * ac : 6 * ac], dab[...])
        keep([jnp.where(lane < heads, ga, gb)], at)

    scatter.run(part, late)
    half = rows // 2
    for lo in (0, half):
        small[m, lo : lo + half] = scatter.total((lo, lo + half), slice(width, width + ac)).astype(BF16)
    ring = RingGather(small, send2, recv2, places)
    ring.start()
    step = 16

    def back(at):
        g = scatter.total((at, at + step), slice(0, width)) * gain[...]
        v = resid[at : at + step]
        n = norm_factor(v)
        v = v * n
        g_tokens[at : at + step] = (
            g_middle[at : at + step] + n * (g - v * jnp.mean(g * v, axis=-1, keepdims=True))
        ).astype(BF16)

    for at in range(0, half, step):
        back(at)
    ring.forward()
    for at in range(half, rows, step):
        back(at)
    line = iota2((ac, 2 * ac), 0)
    slot = iota2((ac, 2 * ac), 1)
    inner = (slot // ac) * SHARE + slot % SHARE
    owner = ((slot % ac) // SHARE) * RING + m
    first = inner < six
    column = jnp.where(first, owner * six + inner, owner * 2 + inner - six)
    place_of = (column // ac) * ADAPTER_RANK + column % ADAPTER_RANK + jnp.where(first, 0, six * ADAPTER_RANK)
    adapter_of = (column % ac) // ADAPTER_RANK
    chosen = (line == place_of).astype(F32).astype(BF16)
    same = (line == adapter_of * ADAPTER_RANK).astype(F32).astype(BF16)
    ring.wait_left()
    ring.wait_right()
    ring.wait_opp()
    sums = jnp.concatenate([small[n] for n in range(RING)], axis=0)
    picked = (mm(sums, chosen) * mm(select[...], same)).astype(BF16)
    w = width // parts
    at = stage.shape[2] - 2 * w
    lane = iota2((1, ac), 1)
    upper = picked[:, 0:ac]
    lower = picked[:, ac : 2 * ac].astype(F32)
    lower_in = jnp.where(lane % SHARE < six - SHARE, lower, 0.0).astype(BF16)
    lower_two = jnp.where(lane % SHARE < six - SHARE, 0.0, lower).astype(BF16)
    at = keep([mm_tn(upper, normed[:, p * w : (p + 1) * w]) for p in range(parts)], at)
    keep(
        [
            mm_tn(lower_in, normed[:, p * w : (p + 1) * w]) + mm_tn(lower_two, normed2[:, p * w : (p + 1) * w])
            for p in range(parts)
        ],
        at,
    )
    scatter.finish()
    ring.finish()


def late_widths(kw, vw, width):
    parts = 16 // SHARE
    return [kw // parts, kw // parts, vw // parts, vw // parts, CH, width // parts, width // parts]


def project_back(
    dq, dk, dv, dg, dab, resid, g_middle, select, gain, bab, low, g_rank2, normed, normed2, wqk, wvg, wab, ain, bqk, bvg
):
    rows, width = resid.shape
    ac = select.shape[1]
    n_dp = lax.axis_size("dp")
    vm, hb = specs(1, 1)
    cols = width + ac
    return pl.pallas_call(
        project_back_kernel,
        out_shape=(sds((rows, width)), sds((n_dp, 16, sum(late_widths(dq.shape[1], dv.shape[1], width))))),
        in_specs=[vm] * 14 + [hb] * 6,
        out_specs=[vm, vm],
        scratch_shapes=[
            like(wqk), like(wvg), like(wab), like(ain), like(bqk), like(bvg),
            pltpu.VMEM((2 * rows, ain.shape[1]), BF16),
            pltpu.VMEM((6, rows // 2, cols), BF16),
            pltpu.VMEM((6, rows // 2, cols), BF16),
            pltpu.VMEM((3, rows, cols), F32),
            pltpu.VMEM((RING, rows, ac), BF16),
            DMA_SEMS((6,)), DMA_SEMS((6,)), DMA_SEMS((6,)), DMA_SEMS((6,)), DMA_SEMS((6,)),
        ],
        compiler_params=ring_params(4),
        cost_estimate=pl.CostEstimate(flops=9 * 10**9, bytes_accessed=30 * 2**20, transcendentals=0),
        name="project_backward",
    )(dq, dk, dv, dg, dab, resid, g_middle, select, gain, bab, low, g_rank2, normed, normed2, wqk, wvg, wab, ain, bqk, bvg)


def exchange_kernel(share, idx_in, idx_out, xa, xb, oa, ob, stage, land, send, recv):
    n = land.shape[0]
    me = lax.axis_index("dp")
    rows, width = xa.shape
    slots = n * 16
    parts = 16 // share
    pw = width // parts
    barrier = pltpu.get_barrier_semaphore()

    def greet(s, carry):
        pl.semaphore_signal(barrier, inc=1, device_id={"dp": lax.rem(me + s, n)}, device_id_type=MESH_ID)
        return carry

    lax.fori_loop(1, n, greet, 0)
    row = iota2((rows, slots), 0)
    part_of = (iota2((1, slots), 1) // share) % parts
    into = row == idx_in[0:1]
    outof = row == idx_out[0:1]
    into = [(into & (part_of == p)).astype(F32).astype(BF16) for p in range(parts)]
    for x, at in ((xa, 0), (xb, 16)):
        acc = jnp.zeros((slots, pw), F32)
        for p in range(parts):
            acc = acc + mm_tn(into[p], x[:, p * pw : (p + 1) * pw])
        stage[:, at : at + 16, :] = acc.astype(BF16).reshape(n, 16, pw)
    land[me] = stage[me]
    pl.semaphore_wait(barrier, n - 1)

    def copy(to, source):
        return pltpu.make_async_remote_copy(
            src_ref=stage.at[to],
            dst_ref=land.at[source],
            send_sem=send.at[to],
            recv_sem=recv.at[source],
            device_id={"dp": to},
            device_id_type=MESH_ID,
        )

    def go(s, carry):
        copy(lax.rem(me + s, n), me).start()
        return carry

    lax.fori_loop(1, n, go, 0)

    def take(s, carry):
        source = lax.rem(me + n - s, n)
        copy(source, source).wait_recv()
        return carry

    lax.fori_loop(1, n, take, 0)
    outof = [(outof & (part_of == p)).astype(F32).astype(BF16) for p in range(parts)]
    for o, at in ((oa, 0), (ob, 16)):
        got = land[:, at : at + 16, :].reshape(slots, pw)
        for p in range(parts):
            o[:, p * pw : (p + 1) * pw] = mm(outof[p], got).astype(o.dtype)

    def done(s, carry):
        copy(lax.rem(me + s, n), me).wait_send()
        return carry

    lax.fori_loop(1, n, done, 0)


def exchange(collective_id, idx_in, idx_out, xa, xb, types):
    rows, width = xa.shape
    n = lax.axis_size("dp")
    share = rows // n
    parts = 16 // share
    vm, _ = specs(1, 1)
    return pl.pallas_call(
        functools.partial(exchange_kernel, share),
        out_shape=(sds((rows, width), types[0]), sds((rows, width), types[1])),
        in_specs=[vm] * 4,
        out_specs=[vm] * 2,
        scratch_shapes=[
            pltpu.VMEM((n, 32, width // parts), BF16),
            pltpu.VMEM((n, 32, width // parts), BF16),
            DMA_SEMS((n,)),
            DMA_SEMS((n,)),
        ],
        compiler_params=ring_params(collective_id),
        cost_estimate=pl.CostEstimate(flops=10**9, bytes_accessed=20 * 2**20, transcendentals=0),
        name="exchange_rows",
    )(idx_in, idx_out, xa, xb)


def finish_kernel(
    widths, idx_in, idx_out, xa, xb, grads,
    oa, ob, sums,
    stage, land, pair_land, mine, sum_land, send, recv, send2, recv2, send3, recv3,
):
    n = land.shape[0]
    me = lax.axis_index("dp")
    core = lax.rem(me, 2)
    other = me + 1 - 2 * core
    rows, width = xa.shape
    slots = n * 16
    parts = 16 // SHARE
    pw = width // parts
    pairs = n // 2
    here = me // 2
    barrier = pltpu.get_barrier_semaphore()

    def greet(s, carry):
        pl.semaphore_signal(barrier, inc=1, device_id={"dp": lax.rem(me + s, n)}, device_id_type=MESH_ID)
        return carry

    lax.fori_loop(1, n, greet, 0)
    row = iota2((rows, slots), 0)
    part_of = (iota2((1, slots), 1) // SHARE) % parts
    into = row == idx_in[0:1]
    outof = row == idx_out[0:1]
    into = [(into & (part_of == p)).astype(F32).astype(BF16) for p in range(parts)]
    outof = [(outof & (part_of == p)).astype(F32).astype(BF16) for p in range(parts)]
    for x, at in ((xa, 0), (xb, 16)):
        acc = jnp.zeros((slots, pw), F32)
        for p in range(parts):
            acc = acc + mm_tn(into[p], x[:, p * pw : (p + 1) * pw])
        stage[:, at : at + 16, :] = acc.astype(BF16).reshape(n, 16, pw)
    land[me] = stage[me]
    pl.semaphore_wait(barrier, n - 1)

    def pair_copy(i):
        return pltpu.make_async_remote_copy(
            src_ref=grads.at[2 * i + 1 - core],
            dst_ref=pair_land.at[i],
            send_sem=send2.at[i],
            recv_sem=recv2.at[i],
            device_id={"dp": other},
            device_id_type=MESH_ID,
        )

    def sum_copy(to, source):
        return pltpu.make_async_remote_copy(
            src_ref=mine.at[to],
            dst_ref=sum_land.at[source],
            send_sem=send3.at[to],
            recv_sem=recv3.at[source],
            device_id={"dp": 2 * to + core},
            device_id_type=MESH_ID,
        )

    def row_copy(to, source):
        return pltpu.make_async_remote_copy(
            src_ref=stage.at[to],
            dst_ref=land.at[source],
            send_sem=send.at[to],
            recv_sem=recv.at[source],
            device_id={"dp": to},
            device_id_type=MESH_ID,
        )

    def loop(lo, hi, body):
        def step(s, carry):
            body(s)
            return carry

        lax.fori_loop(lo, hi, step, 0)

    def ahead(s):
        return lax.rem(here + s, pairs)

    loop(1, pairs + 1, lambda s: pair_copy(ahead(s)).start())
    loop(1, n, lambda s: row_copy(lax.rem(me + s, n), me).start())

    def add(i):
        pair_copy(i).wait_recv()
        mine[i] = (grads[2 * i + core].astype(F32) + pair_land[i].astype(F32)).astype(BF16)

    def add_send(s):
        i = ahead(s)
        add(i)
        sum_copy(i, here).start()

    loop(1, pairs, add_send)
    add(here)
    sum_land[here] = mine[here]
    loop(1, n, lambda s: row_copy(lax.rem(me + n - s, n), lax.rem(me + n - s, n)).wait_recv())
    for o, at in ((oa, 0), (ob, 16)):
        got = land[:, at : at + 16, :].reshape(slots, pw)
        for p in range(parts):
            o[:, p * pw : (p + 1) * pw] = mm(outof[p], got).astype(o.dtype)

    def wait_sum(s):
        source = lax.rem(here + pairs - s, pairs)
        sum_copy(source, source).wait_recv()

    loop(1, pairs, wait_sum)
    at = 0
    for w in widths:
        total = sum_land[0, :, at : at + w].astype(F32)
        for i in range(1, pairs):
            total = total + sum_land[i, :, at : at + w].astype(F32)
        for p in range(parts):
            c = parts * at + p * w
            sums[:, c : c + w] = total[p * SHARE : (p + 1) * SHARE]
        at += w
    loop(1, pairs + 1, lambda s: pair_copy(ahead(s)).wait_send())
    loop(1, pairs, lambda s: sum_copy(ahead(s), here).wait_send())
    loop(1, n, lambda s: row_copy(lax.rem(me + s, n), me).wait_send())


def finish(collective_id, widths, idx_in, idx_out, xa, xb, grads):
    rows, width = xa.shape
    n = lax.axis_size("dp")
    parts = 16 // SHARE
    total = grads.shape[2]
    vm, _ = specs(1, 1)
    return pl.pallas_call(
        functools.partial(finish_kernel, widths),
        out_shape=(sds((rows, width)), sds((rows, width)), sds((SHARE, parts * total), F32)),
        in_specs=[vm] * 5,
        out_specs=[vm] * 3,
        scratch_shapes=[
            pltpu.VMEM((n, 32, width // parts), BF16),
            pltpu.VMEM((n, 32, width // parts), BF16),
            pltpu.VMEM((n // 2, 16, total), BF16),
            pltpu.VMEM((n // 2, 16, total), BF16),
            pltpu.VMEM((n // 2, 16, total), BF16),
            DMA_SEMS((n,)), DMA_SEMS((n,)),
            DMA_SEMS((n // 2,)), DMA_SEMS((n // 2,)),
            DMA_SEMS((n // 2,)), DMA_SEMS((n // 2,)),
        ],
        compiler_params=ring_params(collective_id),
        cost_estimate=pl.CostEstimate(flops=10**9, bytes_accessed=20 * 2**20, transcendentals=0),
        name="finish_rows",
    )(idx_in, idx_out, xa, xb, grads)


def dot(a, b):
    return jnp.dot(a, b, preferred_element_type=F32)


def dot_nt(a, b):
    return lax.dot_general(a, b, (((1,), (1,)), ((), ())), preferred_element_type=F32)


def dot_tn(a, b):
    return lax.dot_general(a, b, (((0,), (0,)), ((), ())), preferred_element_type=F32)


def one_hot(flag):
    return flag.astype(BF16)


def per_device(
    tokens,
    cotangent,
    token_grouped_position,
    sequence_lengths,
    adapter_index_per_seq,
    mixer_norm_gain,
    query_key_matrix,
    value_gate_matrix,
    decay_step_matrix,
    query_key_filters,
    value_filters,
    decay_scale_logarithm,
    decay_step_bias,
    head_output_norm_gain,
    output_matrix,
    feedfwd_norm_gain,
    gate_up_matrix,
    down_matrix,
    adapter_mixer_first,
    adapter_query_key_second,
    adapter_value_gate_second,
    adapter_decay_step_second,
    adapter_output_first,
    adapter_output_second,
    adapter_feedfwd_first,
    adapter_gate_up_second,
    adapter_down_first,
    adapter_down_second,
):
    rows = tokens.shape[0]
    width = tokens.shape[1]
    n_dp = lax.axis_size("dp")
    n_mp = lax.axis_size("mp")
    group = rows * n_mp
    share = rows // n_dp
    dp = lax.axis_index("dp")
    mp = lax.axis_index("mp")
    ac = adapter_output_second.shape[0]
    heads = decay_scale_logarithm.shape[0]
    i32 = jnp.int32

    column = lax.dynamic_index_in_dim(
        token_grouped_position.reshape(n_dp, n_mp, rows), mp, axis=1, keepdims=False
    )
    own_dest = lax.dynamic_index_in_dim(column, dp, axis=0, keepdims=False) // group
    slot_r = jnp.arange(rows, dtype=i32)
    before = slot_r[None, :] < slot_r[:, None]
    rank = jnp.sum(((own_dest[:, None] == own_dest[None, :]) & before).astype(i32), axis=1)
    send_pos = own_dest * share + rank
    token_at = jnp.sum(jnp.where(send_pos[None, :] == slot_r[:, None], slot_r[None, :], 0), axis=1)
    mask = column // group == dp
    in_rank = dot(mask.astype(BF16), one_hot(slot_r[:, None] < slot_r[None, :])).astype(i32)
    slot_val = column - dp * group - mp * rows
    slots = jnp.sum(
        jnp.where(
            mask[:, None, :] & (in_rank[:, None, :] == jnp.arange(share, dtype=i32)[None, :, None]),
            slot_val[:, None, :],
            0,
        ),
        axis=2,
    ).reshape(-1)

    def spread(index):
        parts = 16 // share
        wide = jnp.broadcast_to(index.reshape(n_dp, 1, share), (n_dp, parts, share)).reshape(1, -1)
        return jnp.broadcast_to(wide, (8, n_dp * 16))

    index_tokens, index_slots = spread(token_at), spread(slots)
    resid, cot = exchange(5, index_tokens, index_slots, tokens, cotangent, (F32, BF16))

    position = jnp.arange(group, dtype=i32)
    lens = sequence_lengths[0]
    ends = jnp.stack([jnp.sum(lens[: n + 1]) for n in range(lens.shape[0])])
    segment = jnp.sum((position[:, None] >= ends[None, :]).astype(i32), axis=1)
    which = jnp.sum(
        jnp.where(
            segment[:, None] == jnp.arange(ends.shape[0], dtype=i32)[None, :], adapter_index_per_seq[0][None, :], 0
        ),
        axis=1,
    )
    select = (jnp.arange(ac, dtype=i32)[None, :] // ADAPTER_RANK == which[:, None]).astype(F32)
    segf = segment.astype(F32)
    masks = jnp.stack(
        [
            jnp.broadcast_to(
                ((position >= s) & (jnp.roll(segment, s) == segment)).astype(F32)[:, None], (group, CH)
            )
            for s in (1, 2, 3)
        ]
    )
    segc = jnp.broadcast_to(segf[:, None], (group, CH))
    segr = jnp.broadcast_to(segf[None, :], (8, group))
    gate_par = jnp.zeros((8, CH), F32)
    gate_par = gate_par.at[0, :heads].set(decay_scale_logarithm).at[1, :heads].set(decay_step_bias)
    w_ab = jnp.pad(jnp.concatenate([decay_step_matrix[0], decay_step_matrix[1]], axis=1), ((0, 0), (0, CH - 2 * heads)))
    b_a = jnp.pad(adapter_decay_step_second[0], ((0, 0), (0, CH - heads)))
    b_b = jnp.pad(adapter_decay_step_second[1], ((0, 0), (heads, CH - 2 * heads)))

    def gather(x):
        return lax.all_gather(x, "mp", axis=0, tiled=True)

    def scatter(x):
        return lax.psum_scatter(x.astype(BF16), "mp", scatter_dimension=0, tiled=True).astype(F32)

    bab = jnp.stack([b_a, b_b])
    gain_one, gain_two = mixer_norm_gain[None], feedfwd_norm_gain[None]
    normed, low, pre_q, pre_k, pre_v, pre_g, pre_ab = project(
        resid,
        gain_one,
        select,
        bab,
        query_key_matrix,
        value_gate_matrix,
        w_ab,
        adapter_mixer_first,
        adapter_query_key_second,
        adapter_value_gate_second,
    )
    normed = normed.reshape(group, width)
    cot_later, pre_ab = lax.optimization_barrier((cot, pre_ab))
    cot_all = gather(cot_later)
    shared = (
        masks,
        segc,
        segr,
        query_key_filters[0],
        query_key_filters[1],
        value_filters,
        gate_par,
        head_output_norm_gain[None],
    )
    mixed, *saved = mixer_fwd(pre_q, pre_k, pre_v, pre_g, pre_ab, *shared)
    mixed, cot_all = lax.optimization_barrier((mixed, cot_all))
    middle, rank_out, normed2, rank2, gate, up, hidden, down_part, rank_part = feed(
        mixed,
        resid,
        gain_two,
        select,
        output_matrix,
        adapter_output_first,
        adapter_output_second,
        adapter_feedfwd_first,
        gate_up_matrix,
        adapter_gate_up_second,
        down_matrix,
        adapter_down_first,
    )
    normed2 = normed2.reshape(group, width)
    g_rank_down, g_gate, g_up, g_rank2, g_middle, g_branch, g_rank_out, g_mixed, rank_down = feed_back(
        cot_all,
        middle,
        gate,
        up,
        rank_part,
        select,
        gain_two,
        adapter_down_second,
        down_matrix,
        adapter_down_first,
        gate_up_matrix,
        adapter_gate_up_second,
        adapter_feedfwd_first,
        adapter_output_second,
        output_matrix,
        adapter_output_first,
    )
    g_branch = g_branch.reshape(group, width)
    down_later, g_mixed = lax.optimization_barrier((down_part, g_mixed))
    down_sum = scatter(down_later)
    rank_down_own = lax.dynamic_slice_in_dim(rank_down, mp * rows, rows, axis=0)

    lane = jnp.arange(ac, dtype=i32)

    def pick(total, per):
        line = jnp.arange(total, dtype=i32)
        blocks = []
        for b in range(-(-per // share)):
            inner = b * share + lane % share
            want = (lane // share * n_mp + mp) * per + inner
            blocks.append(one_hot((line[:, None] == want[None, :]) & (inner < per)[None, :]))
        return jnp.concatenate(blocks, axis=1)

    per_out = width // (n_dp * n_mp)
    pick_out = pick(width, per_out)
    blocks_out = per_out // share

    def side(grad_rows, ranks):
        chosen = dot(grad_rows, pick_out).astype(BF16)
        return [dot_tn(chosen[:, b * ac : (b + 1) * ac], ranks) for b in range(blocks_out)]

    def reduce_dp(pieces):
        flat = jnp.concatenate([p.astype(BF16) for p in pieces], axis=1)
        got = lax.all_to_all(flat.reshape(n_dp, share, -1), "dp", split_axis=0, concat_axis=0, tiled=True)
        return jnp.sum(got.astype(F32), axis=0)

    early = reduce_dp(
        [
            dot_tn(rank2[:, :ac], g_gate),
            dot_tn(rank2[:, ac:], g_up),
            dot_tn(g_rank_down, hidden),
            dot_tn(g_rank_out, mixed),
        ]
        + side(cot_all, rank_down)
        + side(g_branch, rank_out)
    )

    dq, dk, dv, dg, dab = mixer_bwd(g_mixed, pre_g, pre_ab, *shared, saved)
    dq, down_sum, early = lax.optimization_barrier((dq, down_sum, early))
    block_rows_out = (middle + down_sum + dot(rank_down_own, adapter_down_second)).astype(BF16)
    g_tokens, late_parts = project_back(
        dq,
        dk,
        dv,
        dg,
        dab,
        resid,
        g_middle,
        select,
        gain_one,
        bab,
        low,
        g_rank2,
        normed,
        normed2,
        query_key_matrix,
        value_gate_matrix,
        w_ab,
        adapter_mixer_first,
        adapter_query_key_second,
        adapter_value_gate_second,
    )
    widths = late_widths(dq.shape[1], dv.shape[1], width)
    out_rows, grad_rows, late = finish(6, widths, index_slots, index_tokens, block_rows_out, g_tokens, late_parts)
    per_in = 6 * ac // (n_dp * n_mp)
    per_ffn = 2 * ac // (n_dp * n_mp)

    def cut(x, sizes):
        out, at = [], 0
        for s in sizes:
            out.append(x[:, at : at + s])
            at += s
        return out

    ff = gate.shape[1]
    kw, vw = dq.shape[1], dv.shape[1]
    e = cut(early, [ff, ff, ff, vw] + [ac] * (2 * blocks_out))
    grad_gu = jnp.stack([e[0], e[1]])
    grad_down_in = e[2].T
    grad_out_in = e[3].T

    def side_out(pieces):
        return jnp.concatenate(pieces, axis=0).T

    grad_down = side_out(e[4 : 4 + blocks_out])
    grad_out = side_out(e[4 + blocks_out :])
    f = cut(late, [kw, kw, vw, vw, share * CH, width, width])
    both = jnp.concatenate([f[5], f[6]], axis=0).T
    return (
        out_rows,
        grad_rows,
        both[:, :per_in],
        jnp.stack([f[0], f[1]]),
        jnp.stack([f[2], f[3]]),
        jnp.stack([f[4][:, :heads], f[4][:, heads : 2 * heads]]),
        grad_out_in,
        grad_out,
        both[:, per_in : per_in + per_ffn],
        grad_gu,
        grad_down_in,
        grad_down,
    )


def solution(mesh):
    return jax.shard_map(
        per_device,
        mesh=mesh,
        in_specs=(
            P(("dp", "mp"), None),
            P(("dp", "mp"), None),
            P(),
            P("dp", None),
            P("dp", None),
            P(),
            P(None, None, "mp"),
            P(None, None, "mp"),
            P(None, None, "mp"),
            P(None, None, "mp"),
            P(None, "mp"),
            P("mp"),
            P("mp"),
            P(),
            P("mp", None),
            P(),
            P(None, None, "mp"),
            P("mp", None),
            P(),
            P(None, None, "mp"),
            P(None, None, "mp"),
            P(None, None, "mp"),
            P("mp", None),
            P(),
            P(),
            P(None, None, "mp"),
            P("mp", None),
            P(),
        ),
        out_specs=(
            P(("dp", "mp"), None),
            P(("dp", "mp"), None),
            P(None, ("dp", "mp")),
            P(None, "dp", "mp"),
            P(None, "dp", "mp"),
            P(None, "dp", "mp"),
            P("mp", "dp"),
            P(None, ("dp", "mp")),
            P(None, ("dp", "mp")),
            P(None, "dp", "mp"),
            P("mp", "dp"),
            P(None, ("dp", "mp")),
        ),
        check_vma=False,
    )
```

```python
import functools
import jax
import jax.numpy as jnp
from jax import lax
from jax.experimental import pallas as pl
from jax.experimental.pallas import tpu as pltpu
from jax.sharding import PartitionSpec as P

EPSILON = 1e-06
F32 = jnp.float32
BF16 = jnp.bfloat16
CH = 128
BASE = 16
DK = 128
DVAL = 256
INV_ROOT = DK ** -0.5


def mm(a, b):
    return jnp.dot(a.astype(BF16), b.astype(BF16), preferred_element_type=F32)


def mm_nt(a, b):
    return lax.dot_general(a.astype(BF16), b.astype(BF16), (((1,), (1,)), ((), ())), preferred_element_type=F32)


def mm_tn(a, b):
    return lax.dot_general(a.astype(BF16), b.astype(BF16), (((0,), (0,)), ((), ())), preferred_element_type=F32)


def exact_tn(a, b):
    b1 = b.astype(BF16)
    r1 = b - b1.astype(F32)
    b2 = r1.astype(BF16)
    b3 = (r1 - b2.astype(F32)).astype(BF16)
    return mm_tn(a, b1) + mm_tn(a, b2) + mm_tn(a, b3)


def iota2(shape, dim):
    return lax.broadcasted_iota(jnp.int32, shape, dim)


def sigmoid(x):
    return 1.0 / (1.0 + jnp.exp(-x))


def conv_rows(x, taps, masks_ref, length):
    total = x * taps[0:1]
    for shift in range(1, 4):
        total = total + pltpu.roll(x, shift, 0) * masks_ref[shift - 1] * taps[shift : shift + 1]
    return total


def conv_rows_back(d, taps, masks_ref, length):
    total = d * taps[0:1]
    for shift in range(1, 4):
        total = total + pltpu.roll(d * masks_ref[shift - 1], length - shift, 0) * taps[shift : shift + 1]
    return total


def gate_columns(ab, dsl, bias):
    z = ab + bias
    soft = jnp.maximum(z, 0.0) + jnp.log1p(jnp.exp(-jnp.abs(z)))
    return -jnp.exp(dsl) * soft, z


def segment_at(position, lens):
    end = lens[0, 0]
    count = as_int(position >= end)
    for n in range(1, lens.shape[1] - 1):
        end = end + lens[0, n]
        count = count + as_int(position >= end)
    return count


def as_int(flag):
    return jnp.where(flag, 1, 0)


def fill_masks(masks, lens):
    shape = masks.shape[1:]
    position = iota2(shape, 0)
    seg = segment_at(position, lens)
    for shift in range(1, 4):
        same = (position >= shift) & (segment_at(position - shift, lens) == seg)
        masks[shift - 1] = same.astype(F32)


def gate_rows(dsl, bias):
    lane = iota2((1, CH), 1)
    rows = []
    for source in (dsl, bias):
        out = jnp.zeros((1, CH), F32)
        for h in range(source.shape[0]):
            out = jnp.where(lane == h, source[h], out)
        rows.append(out)
    return rows


def base_inverse(mats):
    nb = CH // BASE
    lane = iota2((1, CH), 1)
    lane_masks = [(lane // BASE == b).astype(F32) for b in range(nb)]
    packed = []
    for a in mats:
        d = a[0:BASE] * lane_masks[0]
        for b in range(1, nb):
            d = d + a[b * BASE : (b + 1) * BASE] * lane_masks[b]
        packed.append(d)
    d = jnp.concatenate(packed, axis=0)
    hi = d.astype(BF16)
    lo = (d - hi.astype(F32)).astype(BF16)
    row = iota2((CH, CH), 0)
    col = iota2((CH, CH), 1)
    same = row // BASE == col // BASE
    spread = jnp.concatenate(
        [(same & (row % BASE == j)).astype(BF16) for j in range(BASE - 1)], axis=1
    )
    wide = mm(hi, spread) + mm(lo, spread)
    sub = iota2((BASE, CH), 0)
    eye = (sub == iota2((BASE, CH), 1) % BASE).astype(F32)
    out = []
    for n in range(len(mats)):
        t = eye
        for j in range(BASE - 1):
            t = t - wide[n * BASE : (n + 1) * BASE, j * CH : (j + 1) * CH] * t[j : j + 1]
        out.append(jnp.concatenate([t * lane_masks[b] for b in range(nb)], axis=0))
    return out


def full_inverse(mats):
    ts = base_inverse(mats)
    row = iota2((CH, CH), 0)
    col = iota2((CH, CH), 1)
    size = BASE
    while size < CH:
        pick = ((row // size) % 2 == 1) & (col // size == row // size - 1)
        steps = [mm(jnp.where(pick, a, 0.0), t) for a, t in zip(mats, ts)]
        ts = [t - mm(t, s) for t, s in zip(ts, steps)]
        size *= 2
    return ts


def mixer_fwd_kernel(
    heads, lens, dsl, bias, preq, prek, prev, preg, ab_ref, taps_qk, taps_v, gain,
    mixed, cq, ck, cv, t_out, s_out, u_out, o_out,
    masks, qn, kn, vn, cum_s, state,
):
    length = preq.shape[0]
    count = length // CH
    taps_q, taps_k = taps_qk.at[0], taps_qk.at[1]
    fill_masks(masks, lens)
    gate_par = gate_rows(dsl, bias)

    def key_tile(h, carry):
        cols = pl.ds(pl.multiple_of(h * DK, DK), DK)
        for src, taps, save, dst, scale in ((preq, taps_q, cq, qn, INV_ROOT), (prek, taps_k, ck, kn, 1.0)):
            c = conv_rows(src[:, cols].astype(F32), taps[:, cols], masks, length)
            save[:, cols] = c.astype(BF16)
            u = c * sigmoid(c)
            n = lax.rsqrt(jnp.sum(u * u, axis=-1, keepdims=True) + EPSILON) * scale
            dst[:, cols] = (u * n).astype(BF16)
        for half in range(2):
            vcols = pl.ds(pl.multiple_of(h * DVAL + half * DK, DK), DK)
            c = conv_rows(prev[:, vcols].astype(F32), taps_v[:, vcols], masks, length)
            cv[:, vcols] = c.astype(BF16)
            vn[:, vcols] = c * sigmoid(c)
        return carry

    lax.fori_loop(0, heads, key_tile, 0)
    row = iota2((CH, CH), 0)
    col = iota2((CH, CH), 1)
    upper = (row <= col).astype(BF16)
    log_decay, _ = gate_columns(ab_ref[...], gate_par[0], gate_par[1])
    beta_all = sigmoid(ab_ref[...])
    for n in range(count):
        cum_s[n * CH : (n + 1) * CH] = exact_tn(upper, log_decay[n * CH : (n + 1) * CH])
    cum_s[length : length + CH] = jnp.zeros((CH, DK), F32)
    for h in range(heads):
        state[h] = jnp.zeros((DK, DVAL), F32)

    for n in range(count):
        r = pl.ds(n * CH, CH)
        seg_col = segment_at(row + n * CH, lens)
        seg_row = segment_at(col + n * CH, lens)
        keep = (seg_col == seg_row) & (row >= col)
        keepf = keep.astype(F32)
        strict = (row > col).astype(F32)
        cum = cum_s[r]
        cum_t = cum.T
        beta_c = beta_all[n * CH : (n + 1) * CH]
        prev_last = segment_at(n * CH - 1, lens) if n else -1
        start = jnp.exp(cum) * (seg_col == prev_last).astype(F32)
        last_seg = segment_at((n + 1) * CH - 1, lens)
        tail = jnp.exp(cum[CH - 1 : CH] - cum) * (seg_col == last_seg).astype(F32)
        mats, scores = [], []
        for h in range(heads):
            q = qn[r, h * DK : (h + 1) * DK]
            k = kn[r, h * DK : (h + 1) * DK]
            ratio = jnp.exp(jnp.minimum(cum[:, h : h + 1] - cum_t[h : h + 1], 0.0)) * keepf
            beta = beta_c[:, heads + h : heads + h + 1]
            both = mm_nt(jnp.concatenate([q, k], axis=0), k)
            scores.append((ratio * both[:CH]).astype(BF16))
            mats.append(beta * ratio * strict * both[CH:])
        ts = full_inverse(mats)
        for h in range(heads):
            q = qn[r, h * DK : (h + 1) * DK]
            k = kn[r, h * DK : (h + 1) * DK]
            vcols = slice(h * DVAL, (h + 1) * DVAL)
            beta = beta_c[:, heads + h : heads + h + 1]
            st = start[:, h : h + 1]
            tb = ts[h].astype(BF16)
            s0 = state[h]
            s0b = s0.astype(BF16)
            t_out[n, h] = tb
            s_out[n, h] = s0b
            both = mm(jnp.concatenate([q, k], axis=0), s0b)
            res = beta * (vn[r, vcols] - st * both[CH:])
            un = mm(tb, res).astype(BF16)
            u_out[r, vcols] = un
            o = st * both[:CH] + mm(scores[h], un)
            state[h] = start[CH - 1 : CH, h : h + 1] * s0 + mm_tn(k.astype(F32) * tail[:, h : h + 1], un)
            o_out[r, vcols] = o.astype(BF16)
            g = preg[r, vcols].astype(F32)
            rn = lax.rsqrt(jnp.mean(o * o, axis=-1, keepdims=True) + EPSILON)
            mixed[r, vcols] = (o * rn * gain[...] * (g * sigmoid(g))).astype(BF16)


def mixer_fwd(lens, dsl, bias, preq, prek, prev, preg, ab, taps_qk, taps_v, gain):
    length = preq.shape[0]
    heads = preq.shape[1] // DK
    count = length // CH
    vm = pl.BlockSpec(memory_space=pltpu.VMEM)
    sm = pl.BlockSpec(memory_space=pltpu.SMEM)
    out_shape = (
        jax.ShapeDtypeStruct((length, heads * DVAL), BF16),
        jax.ShapeDtypeStruct((length, heads * DK), BF16),
        jax.ShapeDtypeStruct((length, heads * DK), BF16),
        jax.ShapeDtypeStruct((length, heads * DVAL), BF16),
        jax.ShapeDtypeStruct((count, heads, CH, CH), BF16),
        jax.ShapeDtypeStruct((count, heads, DK, DVAL), BF16),
        jax.ShapeDtypeStruct((length, heads * DVAL), BF16),
        jax.ShapeDtypeStruct((length, heads * DVAL), BF16),
    )
    return pl.pallas_call(
        functools.partial(mixer_fwd_kernel, heads),
        out_shape=out_shape,
        in_specs=[sm] * 3 + [vm] * 8,
        out_specs=[vm] * len(out_shape),
        scratch_shapes=[
            pltpu.VMEM((3, length, CH), F32),
            pltpu.VMEM((length, heads * DK), BF16),
            pltpu.VMEM((length, heads * DK), BF16),
            pltpu.VMEM((length, heads * DVAL), F32),
            pltpu.VMEM((length + CH, CH), F32),
            pltpu.VMEM((heads, DK, DVAL), F32),
        ],
        compiler_params=pltpu.CompilerParams(vmem_limit_bytes=60 * 2**20),
        cost_estimate=pl.CostEstimate(flops=20 * 10**9, bytes_accessed=70 * 2**20, transcendentals=0),
        name="mixer_forward",
    )(lens, dsl, bias, preq, prek, prev, preg, ab, taps_qk, taps_v, gain)


def mixer_bwd_kernel(
    heads, lens, dsl, bias, dmix, preg, ab_ref, taps_qk, taps_v, gain,
    cq, ck, cv, t_in, s_in, u_in, o_in,
    dpq, dpk, dpv, dpg, dab,
    masks, qn, kn, vn, cum_s, dstate, dqs, dks, dvs, gcol,
):
    length = dmix.shape[0]
    count = length // CH
    taps_q, taps_k = taps_qk.at[0], taps_qk.at[1]
    fill_masks(masks, lens)
    gate_par = gate_rows(dsl, bias)

    def key_tile(h, carry):
        cols = pl.ds(pl.multiple_of(h * DK, DK), DK)
        for save, dst, scale in ((cq, qn, INV_ROOT), (ck, kn, 1.0)):
            c = save[:, cols].astype(F32)
            u = c * sigmoid(c)
            n = lax.rsqrt(jnp.sum(u * u, axis=-1, keepdims=True) + EPSILON) * scale
            dst[:, cols] = (u * n).astype(BF16)
        for half in range(2):
            vcols = pl.ds(pl.multiple_of(h * DVAL + half * DK, DK), DK)
            c = cv[:, vcols].astype(F32)
            vn[:, vcols] = c * sigmoid(c)
        return carry

    lax.fori_loop(0, heads, key_tile, 0)
    row = iota2((CH, CH), 0)
    col = iota2((CH, CH), 1)
    upper = (row <= col).astype(BF16)
    lower = (row >= col).astype(BF16)
    log_decay, z_all = gate_columns(ab_ref[...], gate_par[0], gate_par[1])
    beta_all = sigmoid(ab_ref[...])
    for n in range(count):
        cum_s[n * CH : (n + 1) * CH] = exact_tn(upper, log_decay[n * CH : (n + 1) * CH])
    for h in range(heads):
        dstate[h] = jnp.zeros((DK, DVAL), F32)
    lane = iota2((1, CH), 1)
    strict = (row > col).astype(F32)
    ones = jnp.ones((CH, CH), BF16)

    for n in range(count - 1, -1, -1):
        r = pl.ds(n * CH, CH)
        seg_col = segment_at(row + n * CH, lens)
        seg_row = segment_at(col + n * CH, lens)
        keepf = ((seg_col == seg_row) & (row >= col)).astype(F32)
        cum = cum_s[r]
        cum_t = cum.T
        beta_c = beta_all[n * CH : (n + 1) * CH]
        prev_last = segment_at(n * CH - 1, lens) if n else -1
        start = jnp.exp(cum) * (seg_col == prev_last).astype(F32)
        last_seg = segment_at((n + 1) * CH - 1, lens)
        tail = jnp.exp(cum[CH - 1 : CH] - cum) * (seg_col == last_seg).astype(F32)
        dcum_all = jnp.zeros((CH, CH), F32)
        dbeta_all = jnp.zeros((CH, CH), F32)
        dlast_all = jnp.zeros((1, CH), F32)
        for h in range(heads):
            qc = slice(h * DK, (h + 1) * DK)
            vcols = slice(h * DVAL, (h + 1) * DVAL)
            here = (lane == h).astype(F32)
            o = o_in[r, vcols].astype(F32)
            g = preg[r, vcols].astype(F32)
            dm = dmix[r, vcols].astype(F32)
            sg = sigmoid(g)
            rn = lax.rsqrt(jnp.mean(o * o, axis=-1, keepdims=True) + EPSILON)
            on = o * rn
            y = on * gain[...]
            dpg[r, vcols] = (dm * y * (sg * (1.0 + g * (1.0 - sg)))).astype(BF16)
            dy = dm * (g * sg) * gain[...]
            do = rn * (dy - on * jnp.mean(dy * on, axis=-1, keepdims=True))
            dob = do.astype(BF16)
            q = qn[r, qc]
            k = kn[r, qc]
            kf = k.astype(F32)
            qf = q.astype(F32)
            un = u_in[r, vcols]
            s0 = s_in[n, h]
            tb = t_in[n, h]
            beta = beta_c[:, heads + h : heads + h + 1]
            st = start[:, h : h + 1]
            tl = tail[:, h : h + 1]
            carry_scale = start[CH - 1 : CH, h : h + 1]
            ratio = jnp.exp(jnp.minimum(cum[:, h : h + 1] - cum_t[h : h + 1], 0.0)) * keepf
            both = mm_nt(jnp.concatenate([q, k], axis=0), k)
            scores = ratio * both[:CH]
            rs = ratio * strict
            amat = rs * both[CH:]
            qk_state = mm(jnp.concatenate([q, k], axis=0), s0)
            ks = qk_state[CH:]
            ds1 = dstate[h]
            ds1b = ds1.astype(BF16)
            ktail = (kf * tl).astype(BF16)
            dun = mm_tn(scores, dob) + mm(ktail, ds1b)
            dres = mm_tn(tb, dun)
            dresb = dres.astype(BF16)
            dks0 = (-(beta * st) * dres).astype(BF16)
            qst = (qf * st).astype(BF16)
            dstate[h] = carry_scale * ds1 + mm_tn(jnp.concatenate([qst, k], axis=0), jnp.concatenate([dob, dks0], axis=0))
            both_d = mm_nt(jnp.concatenate([dob, dresb], axis=0), un)
            dscore = both_d[:CH]
            da = -both_d[CH:]
            dqk = (dscore * ratio).astype(BF16)
            dkk = (da * beta * rs).astype(BF16)
            dspread = dscore * scores + da * beta * amat
            dbeta = jnp.sum(da * amat, axis=-1, keepdims=True) + jnp.sum(
                dres * (vn[r, vcols] - st * ks), axis=-1, keepdims=True
            )
            dvs[r, vcols] = beta * dres
            by_state = mm_nt(jnp.concatenate([dob, dks0, un], axis=0), jnp.concatenate([s0, ds1b], axis=0))
            dq_state = by_state[:CH, :DK]
            dq = st * dq_state + mm(dqk, k)
            dktail = by_state[2 * CH :, DK:]
            dk = (
                by_state[CH : 2 * CH, :DK]
                + tl * dktail
                + mm_tn(dqk, q)
                + mm(dkk, k)
                + mm_tn(dkk, k)
            )
            dqs[r, qc] = dq
            dks[r, qc] = dk
            dstart_s = st * jnp.sum(qf * dq_state, axis=-1, keepdims=True) + st * (
                -beta * jnp.sum(dres * ks, axis=-1, keepdims=True)
            )
            dtail_s = tl * jnp.sum(kf * dktail, axis=-1, keepdims=True)
            dcarry = carry_scale * jnp.sum(jnp.sum(ds1 * s0.astype(F32), axis=-1, keepdims=True), axis=0, keepdims=True)
            colsum = exact_cols(dspread, ones)
            dcum = jnp.sum(dspread, axis=-1, keepdims=True) - colsum[:, 0:1] + dstart_s - dtail_s
            dlast = jnp.sum(dtail_s, axis=0, keepdims=True) + dcarry
            dcum_all = dcum_all + dcum * here
            dlast_all = dlast_all + dlast * here
            dbeta_all = dbeta_all + dbeta * (lane == heads + h).astype(F32)
        dcum_all = dcum_all + dlast_all * (row == CH - 1).astype(F32)
        gcol[r] = exact_tn(lower, dcum_all) + dbeta_all * beta_c * (1.0 - beta_c)

    slope = -jnp.exp(gate_par[0]) * sigmoid(z_all)
    dab[...] = (gcol[...] * jnp.where(lane < heads, slope, 1.0)).astype(BF16)

    def back_tile(h, carry):
        cols = pl.ds(pl.multiple_of(h * DK, DK), DK)
        for save, dsrc, taps, dst, scale in ((cq, dqs, taps_q, dpq, INV_ROOT), (ck, dks, taps_k, dpk, 1.0)):
            c = save[:, cols].astype(F32)
            sg = sigmoid(c)
            u = c * sg
            n = lax.rsqrt(jnp.sum(u * u, axis=-1, keepdims=True) + EPSILON)
            un = u * n
            d = dsrc[:, cols] * scale
            du = n * (d - un * jnp.sum(d * un, axis=-1, keepdims=True))
            dc = du * (sg * (1.0 + c * (1.0 - sg)))
            dst[:, cols] = conv_rows_back(dc, taps[:, cols], masks, length).astype(BF16)
        for half in range(2):
            vcols = pl.ds(pl.multiple_of(h * DVAL + half * DK, DK), DK)
            c = cv[:, vcols].astype(F32)
            sg = sigmoid(c)
            dc = dvs[:, vcols] * (sg * (1.0 + c * (1.0 - sg)))
            dpv[:, vcols] = conv_rows_back(dc, taps_v[:, vcols], masks, length).astype(BF16)
        return carry

    lax.fori_loop(0, heads, back_tile, 0)


def exact_cols(x, ones):
    hi = x.astype(BF16)
    lo = (x - hi.astype(F32)).astype(BF16)
    return mm_tn(hi, ones) + mm_tn(lo, ones)


def mixer_bwd(lens, dsl, bias, dmix, preg, ab, taps_qk, taps_v, gain, saved):
    length = dmix.shape[0]
    heads = dmix.shape[1] // DVAL
    vm = pl.BlockSpec(memory_space=pltpu.VMEM)
    sm = pl.BlockSpec(memory_space=pltpu.SMEM)
    out_shape = (
        jax.ShapeDtypeStruct((length, heads * DK), BF16),
        jax.ShapeDtypeStruct((length, heads * DK), BF16),
        jax.ShapeDtypeStruct((length, heads * DVAL), BF16),
        jax.ShapeDtypeStruct((length, heads * DVAL), BF16),
        jax.ShapeDtypeStruct((length, CH), BF16),
    )
    return pl.pallas_call(
        functools.partial(mixer_bwd_kernel, heads),
        out_shape=out_shape,
        in_specs=[sm] * 3 + [vm] * 13,
        out_specs=[vm] * len(out_shape),
        scratch_shapes=[
            pltpu.VMEM((3, length, CH), F32),
            pltpu.VMEM((length, heads * DK), BF16),
            pltpu.VMEM((length, heads * DK), BF16),
            pltpu.VMEM((length, heads * DVAL), F32),
            pltpu.VMEM((length, CH), F32),
            pltpu.VMEM((heads, DK, DVAL), F32),
            pltpu.VMEM((length, heads * DK), F32),
            pltpu.VMEM((length, heads * DK), F32),
            pltpu.VMEM((length, heads * DVAL), F32),
            pltpu.VMEM((length, CH), F32),
        ],
        compiler_params=pltpu.CompilerParams(vmem_limit_bytes=60 * 2**20),
        cost_estimate=pl.CostEstimate(flops=30 * 10**9, bytes_accessed=100 * 2**20, transcendentals=0),
        name="mixer_backward",
    )(lens, dsl, bias, dmix, preg, ab, taps_qk, taps_v, gain, *saved)


MESH_ID = pl.DeviceIdType.MESH
RING = 4
DMA_SEMS = pltpu.SemaphoreType.DMA
PIECES = 4
WIDE_VMEM = 60 * 2**20
SHARE = 4
ADAPTER_RANK = 16


def ring_places():
    m = lax.axis_index("mp")
    return m, lax.rem(m + 3, RING), lax.rem(m + 1, RING), lax.rem(m + 2, RING)


def ring_barrier(places):
    _, left, right, _ = places
    barrier = pltpu.get_barrier_semaphore()
    for neighbour in (left, right):
        pl.semaphore_signal(barrier, inc=1, device_id={"mp": neighbour}, device_id_type=MESH_ID)
    pl.semaphore_wait(barrier, 2)


class RingGather:
    def __init__(self, buf, send, recv, places):
        self.buf, self.send, self.recv = buf, send, recv
        self.m, self.left, self.right, self.opp = places
        half = buf.shape[1] // 2
        self.top, self.bot = pl.ds(0, half), pl.ds(half, half)

    def begin(self, i, slot, part, to):
        step = part.size // PIECES
        for n in range(PIECES):
            self.copy(i, slot, pl.ds(part.start + n * step, step), to).start()

    def copy(self, i, slot, part, to):
        ref = self.buf.at[slot, part]
        return pltpu.make_async_remote_copy(
            src_ref=ref,
            dst_ref=ref,
            send_sem=self.send.at[i],
            recv_sem=self.recv.at[i],
            device_id={"mp": to},
            device_id_type=MESH_ID,
        )

    def start(self):
        self.begin(0, self.m, self.top, self.right)
        self.begin(1, self.m, self.bot, self.left)
        self.begin(2, self.m, self.bot, self.right)
        self.begin(3, self.m, self.top, self.left)

    def forward(self):
        self.copy(0, self.left, self.top, self.right).wait_recv()
        self.begin(4, self.left, self.top, self.right)
        self.copy(1, self.right, self.bot, self.left).wait_recv()
        self.begin(5, self.right, self.bot, self.left)

    def wait_left(self):
        self.copy(2, self.left, self.bot, self.right).wait_recv()

    def wait_right(self):
        self.copy(3, self.right, self.top, self.left).wait_recv()

    def wait_opp(self):
        self.copy(4, self.opp, self.top, self.right).wait_recv()
        self.copy(5, self.opp, self.bot, self.left).wait_recv()

    def finish(self):
        self.copy(0, self.m, self.top, self.right).wait_send()
        self.copy(1, self.m, self.bot, self.left).wait_send()
        self.copy(2, self.m, self.bot, self.right).wait_send()
        self.copy(3, self.m, self.top, self.left).wait_send()
        self.copy(4, self.left, self.top, self.right).wait_send()
        self.copy(5, self.right, self.bot, self.left).wait_send()


class RingScatter:
    def __init__(self, sbuf, rbuf, acc, send, recv, places):
        self.sbuf, self.rbuf, self.acc, self.send, self.recv = sbuf, rbuf, acc, send, recv
        self.m, self.left, self.right, self.opp = places
        self.half = sbuf.shape[1]

    def begin(self, i):
        step = self.half // PIECES
        for n in range(PIECES):
            self.copy(i, pl.ds(n * step, step)).start()

    def copy(self, i, part=slice(None)):
        to = self.right if i % 2 == 0 else self.left
        return pltpu.make_async_remote_copy(
            src_ref=self.sbuf.at[i, part],
            dst_ref=self.rbuf.at[i, part],
            send_sem=self.send.at[i],
            recv_sem=self.recv.at[i],
            device_id={"mp": to},
            device_id_type=MESH_ID,
        )

    def run(self, part, meanwhile=None, ready=None):
        half = self.half
        rows = 2 * half

        def put_far(cols, val):
            self.sbuf[0, :, cols] = val[:half].astype(BF16)
            self.sbuf[1, :, cols] = val[half:rows].astype(BF16)
            self.acc[0, :, cols] = val[rows:]
            self.sbuf[2, :, cols] = val[rows + half :].astype(BF16)

        part((self.opp, self.right), put_far)
        if ready is not None:
            ready()
        self.begin(0)
        self.begin(1)
        self.begin(2)

        def put_near(cols, val):
            self.acc[1, :, cols] = val[:rows]
            self.sbuf[3, :, cols] = val[:half].astype(BF16)
            self.acc[2, :, cols] = val[rows:]

        part((self.left, self.m), put_near)
        self.begin(3)
        if meanwhile is not None:
            meanwhile()
        self.copy(0).wait_recv()
        self.sbuf[4] = (self.acc[0, 0:half] + self.rbuf[0].astype(F32)).astype(BF16)
        self.begin(4)
        self.copy(1).wait_recv()
        self.sbuf[5] = (self.acc[1, half:rows] + self.rbuf[1].astype(F32)).astype(BF16)
        self.begin(5)
        for i in range(2, 6):
            self.copy(i).wait_recv()

    def total(self, rows, cols):
        lo, hi = rows
        if hi <= self.half:
            a, b, r = self.rbuf[4, lo:hi, cols], self.rbuf[3, lo:hi, cols], slice(lo, hi)
        else:
            r = slice(lo, hi)
            lo, hi = lo - self.half, hi - self.half
            a, b = self.rbuf[2, lo:hi, cols], self.rbuf[5, lo:hi, cols]
        return self.acc[2, r, cols] + a.astype(F32) + b.astype(F32)

    def finish(self):
        for i in range(6):
            self.copy(i).wait_send()


class Loads:
    def __init__(self, pairs, sems):
        self.copies = [pltpu.make_async_copy(src, dst, sems.at[n]) for n, (src, dst) in enumerate(pairs)]
        self.waited = set()

    def start(self, *which):
        for n in which or range(len(self.copies)):
            self.copies[n].start()

    def wait(self, *which):
        for n in which:
            if n not in self.waited:
                self.copies[n].wait()
                self.waited.add(n)


def loop(lo, hi, body):
    def step(s, carry):
        body(s)
        return carry

    lax.fori_loop(lo, hi, step, 0)


def greet_dp(n, me):
    barrier = pltpu.get_barrier_semaphore()
    loop(
        1,
        n,
        lambda s: pl.semaphore_signal(barrier, inc=1, device_id={"dp": lax.rem(me + s, n)}, device_id_type=MESH_ID),
    )


def greet_ring(places):
    barrier = pltpu.get_barrier_semaphore()
    for neighbour in (places[1], places[2]):
        pl.semaphore_signal(barrier, inc=1, device_id={"mp": neighbour}, device_id_type=MESH_ID)


def wait_greetings(count):
    pl.semaphore_wait(pltpu.get_barrier_semaphore(), count)


class DpRows:
    def __init__(self, stage, land, send, recv):
        self.stage, self.land, self.send, self.recv = stage, land, send, recv
        self.n, _, self.pw = stage.shape
        self.parts = 16 // SHARE
        self.me = lax.axis_index("dp")

    def maps(self, index, rows):
        slots = self.n * 16
        hit = iota2((rows, slots), 0).astype(F32) == index[0:1]
        part_of = (iota2((1, slots), 1) // SHARE) % self.parts
        return [(hit & (part_of == p)).astype(F32).astype(BF16) for p in range(self.parts)]

    def fill(self, index, rows, value):
        acc = jnp.zeros((self.n * 16, self.pw), F32)
        for p, hit in enumerate(self.maps(index, rows)):
            acc = acc + mm_tn(hit, value(slice(p * self.pw, (p + 1) * self.pw)))
        self.stage[...] = acc.astype(BF16).reshape(self.n, 16, self.pw)
        self.land[self.me] = self.stage[self.me]

    def copy(self, to, source):
        return pltpu.make_async_remote_copy(
            src_ref=self.stage.at[to],
            dst_ref=self.land.at[source],
            send_sem=self.send.at[to],
            recv_sem=self.recv.at[source],
            device_id={"dp": to},
            device_id_type=MESH_ID,
        )

    def ahead(self, s):
        return lax.rem(self.me + s, self.n)

    def behind(self, s):
        return lax.rem(self.me + self.n - s, self.n)

    def start(self):
        loop(1, self.n, lambda s: self.copy(self.ahead(s), self.me).start())

    def take(self, index, rows, put):
        loop(1, self.n, lambda s: self.copy(self.behind(s), self.behind(s)).wait_recv())
        got = self.land[...].reshape(self.n * 16, self.pw)
        for p, hit in enumerate(self.maps(index, rows)):
            put(slice(p * self.pw, (p + 1) * self.pw), mm(hit, got))

    def finish(self):
        loop(1, self.n, lambda s: self.copy(self.ahead(s), self.me).wait_send())


class DpSums:
    def __init__(self, grads, pair_land, mine, sum_land, send, recv, send2, recv2):
        self.grads, self.pair_land, self.mine, self.sum_land = grads, pair_land, mine, sum_land
        self.send, self.recv, self.send2, self.recv2 = send, recv, send2, recv2
        self.me = lax.axis_index("dp")
        self.core = lax.rem(self.me, 2)
        self.here = self.me // 2
        self.pairs = pair_land.shape[0]

    def pair_copy(self, i):
        return pltpu.make_async_remote_copy(
            src_ref=self.grads.at[2 * i + 1 - self.core],
            dst_ref=self.pair_land.at[i],
            send_sem=self.send.at[i],
            recv_sem=self.recv.at[i],
            device_id={"dp": self.me + 1 - 2 * self.core},
            device_id_type=MESH_ID,
        )

    def sum_copy(self, to, source):
        return pltpu.make_async_remote_copy(
            src_ref=self.mine.at[to],
            dst_ref=self.sum_land.at[source],
            send_sem=self.send2.at[to],
            recv_sem=self.recv2.at[source],
            device_id={"dp": 2 * to + self.core},
            device_id_type=MESH_ID,
        )

    def ahead(self, s):
        return lax.rem(self.here + s, self.pairs)

    def behind(self, s):
        return lax.rem(self.here + self.pairs - s, self.pairs)

    def start(self):
        loop(1, self.pairs + 1, lambda s: self.pair_copy(self.ahead(s)).start())

    def add(self, i):
        self.pair_copy(i).wait_recv()
        self.mine[i] = (self.grads[2 * i + self.core].astype(F32) + self.pair_land[i].astype(F32)).astype(BF16)

    def forward(self):
        def one(s):
            i = self.ahead(s)
            self.add(i)
            self.sum_copy(i, self.here).start()

        loop(1, self.pairs, one)
        self.add(self.here)
        self.sum_land[self.here] = self.mine[self.here]

    def take(self, widths, sink):
        parts = 16 // SHARE
        loop(1, self.pairs, lambda s: self.sum_copy(self.behind(s), self.behind(s)).wait_recv())
        at = 0
        for k, w in enumerate(widths):
            total = self.sum_land[0, :, at : at + w].astype(F32)
            for i in range(1, self.pairs):
                total = total + self.sum_land[i, :, at : at + w].astype(F32)
            for p in range(parts):
                sink(k, (p * w, (p + 1) * w), total[p * SHARE : (p + 1) * SHARE])
            at += w

    def finish(self):
        loop(1, self.pairs + 1, lambda s: self.pair_copy(self.ahead(s)).wait_send())
        loop(1, self.pairs, lambda s: self.sum_copy(self.ahead(s), self.here).wait_send())


def rows_scratch(n, pw):
    return [pltpu.VMEM((n, 16, pw), BF16), pltpu.VMEM((n, 16, pw), BF16), DMA_SEMS((n,)), DMA_SEMS((n,))]


def sums_scratch(n, w):
    half = n // 2
    return [pltpu.VMEM((half, 16, w), BF16)] * 3 + [DMA_SEMS((half,))] * 4


def unfold(n, per):
    row = iota2((n, n), 0)
    col = iota2((n, n), 1)
    part = per // SHARE
    wide = n // part
    hit = (row // per == (col % wide) // SHARE) & (row % SHARE == col % SHARE) & ((row // SHARE) % part == col // wide)
    return hit.astype(F32).astype(BF16)


def keep_chunks(stage, deal, pieces, at):
    n = stage.shape[0]
    w = pieces[0].shape[1]
    used = deal[:, 0 : len(pieces) * n * SHARE]
    got = mm(used, jnp.concatenate([p.astype(BF16) for p in pieces], axis=0))
    stage[:, :, at : at + w] = got.astype(BF16).reshape(n, 16, w)
    return at + w


def fill_select(select, lens, adapters):
    seg = segment_at(iota2(select.shape, 0), lens)
    which = jnp.full(select.shape, adapters[0, 0], jnp.int32)
    for n in range(1, lens.shape[1]):
        which = jnp.where(seg == n, adapters[0, n], which)
    select[...] = (iota2(select.shape, 1) // ADAPTER_RANK == which).astype(F32)


def fill_gates(wdec, bdec, wab, bab):
    heads = wdec.shape[2]
    for n in range(2):
        at = (iota2((heads, CH), 1) == iota2((heads, CH), 0) + n * heads).astype(F32).astype(BF16)
        bab[n] = mm(bdec[n], at).astype(BF16)
        part = mm(wdec[n], at)
        if n == 0:
            wab[...] = part.astype(BF16)
        else:
            wab[...] = (wab[...].astype(F32) + part).astype(BF16)


def route_indices(routes, rows):
    me, mp = lax.axis_index("dp"), lax.axis_index("mp")
    n = routes.shape[0]
    slots = n * 16
    column = routes[:, 0, :]
    for k in range(1, routes.shape[1]):
        column = jnp.where(mp == k, routes[:, k, :], column)
    group = rows * RING
    dest = (column // group).astype(F32)
    mine = iota2((n, rows), 0) == me
    own = jnp.sum(jnp.where(mine, dest, 0.0), axis=0, keepdims=True)
    across = jnp.broadcast_to(own, (rows, rows))
    down = across.T
    line = iota2((rows, rows), 0)
    lane = iota2((rows, rows), 1)
    rank = jnp.sum(((across == down) & (lane < line)).astype(F32), axis=1, keepdims=True)
    place = down[:, 0:1] * SHARE + rank
    slot = iota2((1, slots), 1)
    slot_row = ((slot // 16) * SHARE + slot % SHARE).astype(F32)
    leaves = jnp.sum(
        jnp.where(place == slot_row, iota2((rows, slots), 0).astype(F32), 0.0), axis=0, keepdims=True
    )
    here = dest == me.astype(F32)
    order = mm(here.astype(F32), (line < lane).astype(F32))
    value = (column - me * group - mp * rows).astype(F32)
    owner = iota2((n, slots), 0) == slot // 16
    lands = jnp.zeros((1, slots), F32)
    for j in range(SHARE):
        found = jnp.sum(jnp.where(here & (order == float(j)), value, 0.0), axis=1, keepdims=True)
        lands = lands + jnp.sum(jnp.where(owner & (slot % SHARE == j), found, 0.0), axis=0, keepdims=True)
    return leaves, lands


def tiles(total, step=512):
    return [(at, min(step, total - at)) for at in range(0, total, step)]


def block_rows(place, rows):
    return pl.ds(pl.multiple_of(place * rows, rows), rows)


def both_rows(ref, pair, rows, cols=slice(None)):
    return jnp.concatenate([ref[block_rows(place, rows), cols] for place in pair], axis=0)


def put_rows(ref, pair, rows, cols, val):
    for n, place in enumerate(pair):
        ref[block_rows(place, rows), cols] = val[n * rows : (n + 1) * rows]


def norm_factor(v):
    return lax.rsqrt(jnp.mean(v * v, axis=-1, keepdims=True) + EPSILON)


def project_kernel(
    lens, adapters, routes, tokens, cot_in, gain, wdec, bdec, wqk_h, wvg_h, ain_h, bqk_h, bvg_h,
    index_in, index_out, select, resid, cot, normed_h, low, pq, pk, pv, pg, pab,
    gath, wqk, wvg, ain, bqk, bvg, wab, bab, wsem, osem, send, recv,
    st1, ld1, se1, re1, st2, ld2, se2, re2,
):
    rows = tokens.shape[0]
    places = ring_places()
    m = places[0]
    first = DpRows(st1, ld1, se1, re1)
    second = DpRows(st2, ld2, se2, re2)
    greet_dp(first.n, first.me)
    greet_ring(places)
    loads = Loads([(ain_h, ain), (wqk_h, wqk), (bqk_h, bqk), (wvg_h, wvg), (bvg_h, bvg)], wsem)
    loads.start()
    leaves, lands = route_indices(routes, rows)
    index_in[...] = jnp.broadcast_to(leaves, index_in.shape)
    index_out[...] = jnp.broadcast_to(lands, index_out.shape)
    first.fill(index_in, rows, lambda c: tokens[:, c])
    wait_greetings(first.n + 1)
    first.start()
    second.fill(index_in, rows, lambda c: cot_in[:, c])
    fill_select(select, lens, adapters)
    fill_gates(wdec, bdec, wab, bab)

    def put_tokens(c, val):
        resid[:, c] = val.astype(BF16)

    first.take(index_out, rows, put_tokens)
    second.start()
    for at in range(0, rows, 32):
        v = resid[at : at + 32].astype(F32)
        gath[m, at : at + 32] = (v * norm_factor(v) * gain[...]).astype(BF16)
    ring = RingGather(gath, send, recv, places)
    ring.start()
    ac = select.shape[1]

    def compute(place):
        r = block_rows(place, rows)
        x = gath[place]
        sel = select[r]
        loads.wait(0)
        for n in range(ain.shape[1] // ac):
            low[r, n * ac : (n + 1) * ac] = (mm(x, ain[:, n * ac : (n + 1) * ac]) * sel).astype(BF16)
        loads.wait(1, 2)
        for n, dst in enumerate((pq, pk)):
            lo = low[r, n * ac : (n + 1) * ac]
            dst[r] = (mm(x, wqk[n]) + mm(lo, bqk[n])).astype(BF16)
        loads.wait(3, 4)
        for n, dst in enumerate((pv, pg)):
            lo = low[r, (n + 2) * ac : (n + 3) * ac]
            for at, size in tiles(wvg.shape[2]):
                c = slice(at, at + size)
                dst[r, c] = (mm(x, wvg[n, :, c]) + mm(lo, bvg[n, :, c])).astype(BF16)
        pab[r] = (
            mm(x, wab[...]) + mm(low[r, 4 * ac : 5 * ac], bab[0]) + mm(low[r, 5 * ac : 6 * ac], bab[1])
        )

    compute(m)
    ring.forward()
    ring.wait_left()
    compute(places[1])
    ring.wait_right()
    compute(places[2])

    def put_cot(c, val):
        cot[:, c] = val.astype(BF16)

    second.take(index_out, rows, put_cot)
    ring.wait_opp()
    out = pltpu.make_async_copy(gath, normed_h, osem)
    out.start()
    compute(places[3])
    ring.finish()
    first.finish()
    second.finish()
    out.wait()


def specs(n_vmem, n_any):
    return [pl.BlockSpec(memory_space=pltpu.VMEM)] * n_vmem + [pl.BlockSpec(memory_space=pl.ANY)] * n_any


def sds(shape, dtype=BF16):
    return jax.ShapeDtypeStruct(shape, dtype)


def ring_params(collective_id):
    return pltpu.CompilerParams(
        collective_id=collective_id, has_side_effects=True, vmem_limit_bytes=WIDE_VMEM
    )


def like(a):
    return pltpu.VMEM(a.shape, a.dtype)


def project(lens, adapters, routes, tokens, cot, gain, wdec, bdec, wqk, wvg, ain, bqk, bvg):
    rows, width = tokens.shape
    n_dp = lax.axis_size("dp")
    group = rows * RING
    kw, vw = wqk.shape[2], wvg.shape[2]
    ac = bqk.shape[1]
    vm, hb = specs(1, 1)
    sm = pl.BlockSpec(memory_space=pltpu.SMEM)
    pw = width * SHARE // 16
    return pl.pallas_call(
        project_kernel,
        out_shape=(
            sds((8, n_dp * 16), F32),
            sds((8, n_dp * 16), F32),
            sds((group, ac), F32),
            sds((rows, width)),
            sds((rows, width)),
            sds((RING, rows, width)),
            sds((group, ain.shape[1])),
            sds((group, kw)),
            sds((group, kw)),
            sds((group, vw)),
            sds((group, vw)),
            sds((group, CH), F32),
        ),
        in_specs=[sm] * 2 + [vm] * 6 + [hb] * 5,
        out_specs=[vm] * 5 + [hb] + [vm] * 6,
        scratch_shapes=[
            pltpu.VMEM((RING, rows, width), BF16),
            like(wqk), like(wvg), like(ain), like(bqk), like(bvg),
            pltpu.VMEM((width, CH), BF16), pltpu.VMEM((2, ac, CH), BF16),
            DMA_SEMS((5,)), DMA_SEMS(()), DMA_SEMS((6,)), DMA_SEMS((6,)),
            *rows_scratch(n_dp, pw), *rows_scratch(n_dp, pw),
        ],
        compiler_params=ring_params(1),
        cost_estimate=pl.CostEstimate(flops=8 * 10**9, bytes_accessed=30 * 2**20, transcendentals=0),
        name="gather_project",
    )(lens, adapters, routes, tokens, cot, gain, wdec, bdec, wqk, wvg, ain, bqk, bvg)


def feed_kernel(
    mixed, resid, gain, select, wout_h, aout_h, bout_h, affn_h, gu_h, bgu_h, down_h, adown_h,
    middle, rank_out, normed_h, rank2, gate, up, hidden, dpart, rpart,
    gath, wout, aout, bout, affn, gu, bgu, down, adown, sbuf, rbuf, acc, wsem, osem, send, recv, send2, recv2,
):
    rows, width = resid.shape
    places = ring_places()
    m = places[0]
    loads = Loads(
        [
            (wout_h, wout), (aout_h, aout), (bout_h, bout), (affn_h, affn),
            (gu_h, gu), (bgu_h, bgu), (down_h, down), (adown_h, adown),
        ],
        wsem,
    )
    loads.start(0, 1)
    ac = select.shape[1]
    ff = gu.shape[2]
    greet_ring(places)
    loads.wait(0, 1)
    scatter = RingScatter(sbuf, rbuf, acc, send, recv, places)

    def part(pair, put):
        x = both_rows(mixed, pair, rows)
        for at, size in tiles(width):
            put(slice(at, at + size), mm(x, wout[:, at : at + size]))
        put(slice(width, width + ac), mm(x, aout[...]))

    def ready():
        loads.start(2, 3, 4, 5, 6, 7)
        wait_greetings(2)

    scatter.run(part, None, ready)
    loads.wait(2)
    sel_own = select[block_rows(m, rows)]
    half = rows // 2
    for lo in (0, half):
        bounds = (lo, lo + half)
        gath[m, lo : lo + half, width : width + ac] = (
            scatter.total(bounds, slice(width, width + ac)) * sel_own[lo : lo + half]
        ).astype(BF16)
    ro = gath[m, :, width : width + ac]
    for at, size in tiles(width):
        c = slice(at, at + size)
        extra = mm(ro, bout[:, c])
        for lo in (0, half):
            middle[lo : lo + half, c] = (
                resid[lo : lo + half, c].astype(F32) + scatter.total((lo, lo + half), c) + extra[lo : lo + half]
            )
    for at in range(0, rows, 32):
        v = middle[at : at + 32]
        gath[m, at : at + 32, 0:width] = (v * norm_factor(v) * gain[...]).astype(BF16)
    ring = RingGather(gath, send2, recv2, places)
    ring.start()

    def compute(place):
        r = block_rows(place, rows)
        x = gath[place, :, 0:width]
        rank_out[r] = gath[place, :, width : width + ac]
        sel = select[r]
        loads.wait(3)
        for n in range(2):
            rank2[r, n * ac : (n + 1) * ac] = (mm(x, affn[:, n * ac : (n + 1) * ac]) * sel).astype(BF16)
        loads.wait(4, 5)
        r0 = rank2[r, 0:ac]
        r1 = rank2[r, ac : 2 * ac]
        for at, size in tiles(ff):
            c = slice(at, at + size)
            g = mm(x, gu[0, :, c]) + mm(r0, bgu[0, :, c])
            u = mm(x, gu[1, :, c]) + mm(r1, bgu[1, :, c])
            gate[r, c] = g.astype(BF16)
            up[r, c] = u.astype(BF16)
            hidden[r, c] = (g * sigmoid(g) * u).astype(BF16)
        loads.wait(6, 7)
        h = hidden[r]
        for at, size in tiles(width):
            c = slice(at, at + size)
            dpart[r, c] = mm(h, down[:, c]).astype(BF16)
        rpart[r] = mm(h, adown[...]).astype(BF16)

    compute(m)
    ring.forward()
    ring.wait_left()
    compute(places[1])
    ring.wait_right()
    compute(places[2])
    ring.wait_opp()
    out = pltpu.make_async_copy(gath.at[:, :, pl.ds(0, width)], normed_h, osem)
    out.start()
    compute(places[3])
    scatter.finish()
    ring.finish()
    out.wait()


def feed(mixed, resid, gain, select, wout, aout, bout, affn, gu, bgu, down, adown):
    rows, width = resid.shape
    group = rows * RING
    ff = gu.shape[2]
    ac = select.shape[1]
    cols = width + ac
    vm, hb = specs(1, 1)
    return pl.pallas_call(
        feed_kernel,
        out_shape=(
            sds((rows, width), F32),
            sds((group, ac)),
            sds((RING, rows, width)),
            sds((group, 2 * ac)),
            sds((group, ff)),
            sds((group, ff)),
            sds((group, ff)),
            sds((group, width)),
            sds((group, ac)),
        ),
        in_specs=[vm] * 4 + [hb] * 8,
        out_specs=[vm, vm, hb] + [vm] * 6,
        scratch_shapes=[
            pltpu.VMEM((RING, rows, cols), BF16),
            like(wout), like(aout), like(bout), like(affn), like(gu), like(bgu), like(down), like(adown),
            pltpu.VMEM((6, rows // 2, cols), BF16),
            pltpu.VMEM((6, rows // 2, cols), BF16),
            pltpu.VMEM((3, rows, cols), F32),
            DMA_SEMS((8,)), DMA_SEMS(()),
            DMA_SEMS((6,)), DMA_SEMS((6,)), DMA_SEMS((6,)), DMA_SEMS((6,)),
        ],
        compiler_params=ring_params(2),
        cost_estimate=pl.CostEstimate(flops=13 * 10**9, bytes_accessed=40 * 2**20, transcendentals=0),
        name="feed_forward",
    )(mixed, resid, gain, select, wout, aout, bout, affn, gu, bgu, down, adown)


def feed_back_kernel(
    cot, middle, gate, up, rpart, select, gain,
    bdown_h, down_h, adown_h, gu_h, bgu_h, affn_h, bout_h, wout_h, aout_h, rank2_h, hidden_h, mixed_h, rank_out_h,
    g_rank2, g_middle, g_mixed, rank_down, stage,
    gath, bdown, down, adown, gu, bgu, affn, bout, wout, aout, rank2, hidden, mixed, rank_out,
    g_rank_down, g_gate, g_up, g_rank_out, flat, pick, chosen,
    sbuf, rbuf, acc, wsem, send, recv, send2, recv2,
):
    rows, width = middle.shape
    places = ring_places()
    m = places[0]
    loads = Loads(
        [
            (bdown_h, bdown), (down_h, down), (adown_h, adown), (gu_h, gu), (bgu_h, bgu),
            (affn_h, affn), (bout_h, bout), (wout_h, wout), (aout_h, aout),
            (rank2_h, rank2), (hidden_h, hidden), (mixed_h, mixed), (rank_out_h, rank_out),
        ],
        wsem,
    )
    loads.start(0, 1, 2)
    loads.start(3, 4, 5)
    ac = select.shape[1]
    ff = gu.shape[2]
    greet_ring(places)
    scatter = RingScatter(sbuf, rbuf, acc, send, recv, places)

    def part(pair, put):
        x = both_rows(cot, pair, rows)
        sel = both_rows(select, pair, rows)
        loads.wait(0)
        grd = (mm_nt(x, bdown[...]) * sel).astype(BF16)
        put_rows(g_rank_down, pair, rows, slice(None), grd)
        loads.wait(1, 2)
        for at, size in tiles(ff, 256):
            c = slice(at, at + size)
            gh = mm_nt(x, down[c]) + mm_nt(grd, adown[c])
            g = both_rows(gate, pair, rows, c).astype(F32)
            u = both_rows(up, pair, rows, c).astype(F32)
            sg = sigmoid(g)
            put_rows(g_gate, pair, rows, c, (gh * u * (sg * (1.0 + g * (1.0 - sg)))).astype(BF16))
            put_rows(g_up, pair, rows, c, (gh * g * sg).astype(BF16))
        loads.wait(3, 4, 5)
        gg = both_rows(g_gate, pair, rows)
        gu_ = both_rows(g_up, pair, rows)
        r2a = (mm_nt(gg, bgu[0]) * sel).astype(BF16)
        r2b = (mm_nt(gu_, bgu[1]) * sel).astype(BF16)
        put_rows(g_rank2, pair, rows, slice(0, ac), r2a)
        put_rows(g_rank2, pair, rows, slice(ac, 2 * ac), r2b)
        r2 = jnp.concatenate([r2a, r2b], axis=1)
        for at, size in tiles(width, 256):
            c = slice(at, at + size)
            put(c, mm_nt(gg, gu[0, c]) + mm_nt(gu_, gu[1, c]) + mm_nt(r2, affn[c]))
        put(slice(width, width + ac), both_rows(rpart, pair, rows).astype(F32))

    n_dp = stage.shape[0]
    parts = 16 // SHARE
    deal = unfold(n_dp * 16, 16)

    def grads():
        loads.wait(9, 10)
        for at, size in tiles(ff):
            c = slice(at, at + size)
            flat[:, at : at + size] = mm_tn(rank2[:, 0:ac], g_gate[:, c]).astype(BF16)
            flat[:, ff + at : ff + at + size] = mm_tn(rank2[:, ac : 2 * ac], g_up[:, c]).astype(BF16)
            flat[:, 2 * ff + at : 2 * ff + at + size] = mm_tn(g_rank_down[...], hidden[:, c]).astype(BF16)
        flat[:, 3 * ff :] = jnp.zeros((ac, flat.shape[1] - 3 * ff), BF16)
        w = flat.shape[1] // parts
        keep_chunks(stage, deal, [flat[:, p * w : (p + 1) * w] for p in range(parts)], 0)

    def ready():
        loads.start(*range(6, 13))
        wait_greetings(2)

    scatter.run(part, grads, ready)
    sel_own = select[block_rows(m, rows)]
    step = 16
    for at in range(0, rows, step):
        b = (at, at + step)
        g = scatter.total(b, slice(0, width)) * gain[...]
        v = middle[at : at + step]
        n = norm_factor(v)
        v = v * n
        gm = cot[pl.ds(pl.multiple_of(m * rows + at, step), step)].astype(F32) + n * (
            g - v * jnp.mean(g * v, axis=-1, keepdims=True)
        )
        g_middle[at : at + step] = gm
        gath[m, at : at + step, 0:width] = gm.astype(BF16)
        gath[m, at : at + step, width : width + ac] = (
            scatter.total(b, slice(width, width + ac)) * sel_own[at : at + step]
        ).astype(BF16)
    ring = RingGather(gath, send2, recv2, places)
    ring.start()
    per = width // (n_dp * RING)
    for at in range(0, width, 256):
        line = iota2((256, pick.shape[1]), 0) + at
        slot = iota2((256, pick.shape[1]), 1)
        want = (((slot % ac) // SHARE) * RING + m) * per + (slot // ac) * SHARE + slot % SHARE
        pick[at : at + 256] = (line == want).astype(F32).astype(BF16)
    cot_chosen = mm(cot[...], pick[...]).astype(BF16)

    def compute(*pair):
        x = jnp.concatenate([gath[place, :, 0:width] for place in pair], axis=0)
        loads.wait(6, 7, 8)
        gro = (mm_nt(x, bout[...]) * both_rows(select, pair, rows)).astype(BF16)
        put_rows(g_rank_out, pair, rows, slice(None), gro)
        for at, size in tiles(wout.shape[0], 256):
            c = slice(at, at + size)
            put_rows(g_mixed, pair, rows, c, (mm_nt(x, wout[c]) + mm_nt(gro, aout[c])).astype(BF16))
        put_rows(chosen, pair, rows, slice(None), mm(x, pick[...]).astype(BF16))
        for place in pair:
            rank_down[block_rows(place, rows)] = gath[place, :, width : width + ac]

    compute(m)
    ring.forward()
    ring.wait_left()
    ring.wait_right()
    compute(places[1], places[2])
    ring.wait_opp()
    compute(places[3])
    loads.wait(11, 12)
    at = flat.shape[1] // parts
    w = mixed.shape[1] // parts
    gro = g_rank_out[...]
    at = keep_chunks(stage, deal, [mm_tn(gro, mixed[:, p * w : (p + 1) * w]) for p in range(parts)], at)
    for rows_of, ranks in ((cot_chosen, rank_down), (chosen[...], rank_out)):
        at = keep_chunks(
            stage, deal, [mm_tn(rows_of[:, b * ac : (b + 1) * ac], ranks[...]) for b in range(rows_of.shape[1] // ac)], at
        )
    scatter.finish()
    ring.finish()


def early_widths(ff, vw, ac):
    parts = 16 // SHARE
    return [-(-3 * ff // (parts * CH)) * CH, vw // parts, ac, ac]


def feed_back(
    cot, middle, gate, up, rpart, select, gain,
    bdown, down, adown, gu, bgu, affn, bout, wout, aout, rank2, hidden, mixed, rank_out,
):
    rows, width = middle.shape
    group = rows * RING
    ff = gu.shape[2]
    ac = select.shape[1]
    n_dp = lax.axis_size("dp")
    parts = 16 // SHARE
    vw = wout.shape[0]
    widths = early_widths(ff, vw, ac)
    vm, hb = specs(1, 1)
    loaded = (bdown, down, adown, gu, bgu, affn, bout, wout, aout, rank2, hidden, mixed, rank_out)
    return pl.pallas_call(
        feed_back_kernel,
        out_shape=(
            sds((group, 2 * ac)),
            sds((rows, width), F32),
            sds((group, vw)),
            sds((group, ac)),
            sds((n_dp, 16, sum(widths))),
        ),
        in_specs=[vm] * 7 + [hb] * len(loaded),
        out_specs=[vm] * 5,
        scratch_shapes=[
            pltpu.VMEM((RING, rows, width + ac), BF16),
            *[like(a) for a in loaded],
            pltpu.VMEM((group, ac), BF16),
            pltpu.VMEM((group, ff), BF16),
            pltpu.VMEM((group, ff), BF16),
            pltpu.VMEM((group, ac), BF16),
            pltpu.VMEM((ac, parts * widths[0]), BF16),
            pltpu.VMEM((width, width // RING), BF16),
            pltpu.VMEM((group, width // RING), BF16),
            pltpu.VMEM((6, rows // 2, width + ac), BF16),
            pltpu.VMEM((6, rows // 2, width + ac), BF16),
            pltpu.VMEM((3, rows, width + ac), F32),
            DMA_SEMS((len(loaded),)),
            DMA_SEMS((6,)), DMA_SEMS((6,)), DMA_SEMS((6,)), DMA_SEMS((6,)),
        ],
        compiler_params=ring_params(3),
        cost_estimate=pl.CostEstimate(flops=13 * 10**9, bytes_accessed=40 * 2**20, transcendentals=0),
        name="feed_backward",
    )(cot, middle, gate, up, rpart, select, gain, *loaded)


def fold_maps(count, base, ac):
    line = iota2((count, ac), 0)
    col = iota2((count, ac), 1)
    hit = (line // ac) * ADAPTER_RANK + line % ADAPTER_RANK + base == col
    return hit.astype(F32).astype(BF16)


def project_back_kernel(
    widths, index_in, index_out, dq, dk, dv, dg, dab, resid, g_middle, select, gain, wdec, bdec, g_rank2, early, middle, down_sum, rank_down,
    wqk_h, wvg_h, ain_h, bqk_h, bvg_h, bdown_h, low_h, normed_h, normed2_h,
    g_tokens, stage, out_rows, o_gu, o_down_in, o_out_in, o_down, o_out, o_qk, o_vg, o_ab,
    wqk, wvg, ain, bqk, bvg, bdown, low, normed, normed2,
    wab, bab, stage_a, g_rank, sbuf, rbuf, acc, small, wsem, send, recv, send2, recv2, *more
):
    rows, width = resid.shape
    places = ring_places()
    m = places[0]
    loads = Loads(
        [
            (bdown_h, bdown), (bqk_h, bqk), (bvg_h, bvg), (ain_h, ain), (wqk_h, wqk), (wvg_h, wvg),
            (low_h, low), (normed_h, normed), (normed2_h, normed2),
        ],
        wsem,
    )
    loads.start(1, 2)
    loads.start(3, 4, 5, 0)
    block = DpRows(*more[:4])
    reduce = DpSums(early, *more[4:11])
    reduce_a = DpSums(stage_a, *more[11:])
    greet_dp(block.n, block.me)
    greet_ring(places)
    ac = select.shape[1]
    n_dp = stage.shape[0]
    heads = dq.shape[1] // DK
    fill_gates(wdec, bdec, wab, bab)
    scatter = RingScatter(sbuf, rbuf, acc, send, recv, places)
    six = ain.shape[1] // ac
    fold_in = fold_maps(six * ac, 0, ac)
    fold_two = fold_maps(2 * ac, six * ADAPTER_RANK, ac)

    def part(pair, put):
        sel = both_rows(select, pair, rows)
        xs = [both_rows(d, pair, rows) for d in (dq, dk, dv, dg, dab)]
        loads.wait(1, 2)
        seconds = [bqk[0], bqk[1], bvg[0], bvg[1], bab[0], bab[1]]
        for n in range(six):
            g_rank[:, n * ac : (n + 1) * ac] = (mm_nt(xs[min(n, 4)], seconds[n]) * sel).astype(BF16)
        gr = g_rank[...]
        put(slice(width, width + ac), mm(gr, fold_in) + mm(both_rows(g_rank2, pair, rows), fold_two))
        loads.wait(3, 4, 5)
        for at, size in tiles(width, 256):
            c = slice(at, at + size)
            put(
                c,
                mm_nt(xs[0], wqk[0, c])
                + mm_nt(xs[1], wqk[1, c])
                + mm_nt(xs[2], wvg[0, c])
                + mm_nt(xs[3], wvg[1, c])
                + mm_nt(xs[4], wab[c])
                + mm_nt(gr, ain[c]),
            )

    deal = unfold(n_dp * 16, 16)
    parts = 16 // SHARE

    def keep(pieces, at):
        return keep_chunks(stage_a, deal, pieces, at)

    def ready():
        loads.wait(0)
        own = rank_down[block_rows(m, rows)]

        def value(c):
            return (middle[:, c] + down_sum[:, c].astype(F32) + mm(own, bdown[:, c])).astype(BF16)

        block.fill(index_in, rows, value)
        loads.start(6, 7, 8)
        wait_greetings(block.n + 1)
        reduce.start()

    def late():
        block.start()
        reduce.forward()
        loads.wait(6)
        at = 0
        for n, d in enumerate((dq, dk, dv, dg)):
            w = d.shape[1] // parts
            lo = low[:, n * ac : (n + 1) * ac]
            at = keep([mm_tn(lo, d[:, p * w : (p + 1) * w]) for p in range(parts)], at)
        lane = iota2((1, CH), 1)
        ga = mm_tn(low[:, 4 * ac : 5 * ac], dab[...])
        gb = mm_tn(low[:, 5 * ac : 6 * ac], dab[...])
        keep([jnp.where(lane < heads, ga, gb)], at)
        reduce_a.start()

    scatter.run(part, late, ready)
    half = rows // 2
    for lo in (0, half):
        small[m, lo : lo + half] = scatter.total((lo, lo + half), slice(width, width + ac)).astype(BF16)
    ring = RingGather(small, send2, recv2, places)
    ring.start()
    reduce_a.forward()
    step = 16

    def back(at):
        g = scatter.total((at, at + step), slice(0, width)) * gain[...]
        v = resid[at : at + step].astype(F32)
        n = norm_factor(v)
        v = v * n
        g_tokens[at : at + step] = (
            g_middle[at : at + step] + n * (g - v * jnp.mean(g * v, axis=-1, keepdims=True))
        ).astype(BF16)

    for at in range(0, half, step):
        back(at)
    ring.forward()
    for at in range(half, rows, step):
        back(at)
    line = iota2((ac, 2 * ac), 0)
    slot = iota2((ac, 2 * ac), 1)
    inner = (slot // ac) * SHARE + slot % SHARE
    owner = ((slot % ac) // SHARE) * RING + m
    first = inner < six
    column = jnp.where(first, owner * six + inner, owner * 2 + inner - six)
    place_of = (column // ac) * ADAPTER_RANK + column % ADAPTER_RANK + jnp.where(first, 0, six * ADAPTER_RANK)
    adapter_of = (column % ac) // ADAPTER_RANK
    chosen = (line == place_of).astype(F32).astype(BF16)
    same = (line == adapter_of * ADAPTER_RANK).astype(F32).astype(BF16)

    def put_rows_out(c, val):
        out_rows[:, c] = val.astype(BF16)

    block.take(index_out, rows, put_rows_out)
    ff = o_gu.shape[2]

    def sink_early(k, cols, val):
        lo, hi = cols
        if k:
            (o_out_in, o_down, o_out)[k - 1][:, lo:hi] = val
            return
        for n in range(3):
            a, b = max(lo, n * ff), min(hi, (n + 1) * ff)
            if a < b:
                piece = val[:, a - lo : b - lo]
                if n < 2:
                    o_gu[n, :, a - n * ff : b - n * ff] = piece
                else:
                    o_down_in[:, a - n * ff : b - n * ff] = piece

    reduce.take(widths, sink_early)
    loads.wait(7, 8)
    ring.wait_left()
    ring.wait_right()
    ring.wait_opp()
    rank_sums = jnp.concatenate([small[n] for n in range(RING)], axis=0)
    picked = (mm(rank_sums, chosen) * mm(select[...], same)).astype(BF16)
    w = width // parts
    at = 0
    lane = iota2((1, ac), 1)
    upper = picked[:, 0:ac]
    lower = picked[:, ac : 2 * ac].astype(F32)
    lower_in = jnp.where(lane % SHARE < six - SHARE, lower, 0.0).astype(BF16)
    lower_two = jnp.where(lane % SHARE < six - SHARE, 0.0, lower).astype(BF16)
    at = keep_chunks(stage, deal, [mm_tn(upper, normed[:, p * w : (p + 1) * w]) for p in range(parts)], at)
    keep_chunks(
        stage,
        deal,
        [
            mm_tn(lower_in, normed[:, p * w : (p + 1) * w]) + mm_tn(lower_two, normed2[:, p * w : (p + 1) * w])
            for p in range(parts)
        ],
        at,
    )

    def sink_late(k, cols, val):
        lo, hi = cols
        if k < 2:
            o_qk[k, :, lo:hi] = val
        elif k < 4:
            o_vg[k - 2, :, lo:hi] = val
        elif lo == 0:
            o_ab[...] = val

    reduce_a.take(late_widths(dq.shape[1], dv.shape[1]), sink_late)
    scatter.finish()
    ring.finish()
    block.finish()
    reduce.finish()
    reduce_a.finish()


def late_widths(kw, vw):
    parts = 16 // SHARE
    return [kw // parts, kw // parts, vw // parts, vw // parts, CH]


def project_back(
    widths, index_in, index_out, dq, dk, dv, dg, dab, resid, g_middle, select, gain, wdec, bdec, g_rank2, early, middle, down_sum, rank_down,
    wqk, wvg, ain, bqk, bvg, bdown, low, normed, normed2, ff,
):
    rows, width = resid.shape
    ac = select.shape[1]
    n_dp = lax.axis_size("dp")
    parts = 16 // SHARE
    vm, hb = specs(1, 1)
    cols = width + ac
    kw, vw = dq.shape[1], dv.shape[1]
    late = late_widths(kw, vw)
    loaded = (wqk, wvg, ain, bqk, bvg, bdown, low, normed, normed2)
    return pl.pallas_call(
        functools.partial(project_back_kernel, widths),
        out_shape=(
            sds((rows, width)),
            sds((n_dp, 16, 2 * width // parts)),
            sds((rows, width)),
            sds((2, SHARE, ff), F32),
            sds((SHARE, ff), F32),
            sds((SHARE, vw), F32),
            sds((SHARE, parts * ac), F32),
            sds((SHARE, parts * ac), F32),
            sds((2, SHARE, kw), F32),
            sds((2, SHARE, vw), F32),
            sds((SHARE, CH), F32),
        ),
        in_specs=[vm] * 18 + [hb] * len(loaded),
        out_specs=[vm] * 11,
        scratch_shapes=[
            *[like(a) for a in loaded],
            pltpu.VMEM((width, CH), BF16),
            pltpu.VMEM((2, ac, CH), BF16),
            pltpu.VMEM((n_dp, 16, sum(late)), BF16),
            pltpu.VMEM((2 * rows, ain.shape[1]), BF16),
            pltpu.VMEM((6, rows // 2, cols), BF16),
            pltpu.VMEM((6, rows // 2, cols), BF16),
            pltpu.VMEM((3, rows, cols), F32),
            pltpu.VMEM((RING, rows, ac), BF16),
            DMA_SEMS((len(loaded),)), DMA_SEMS((6,)), DMA_SEMS((6,)), DMA_SEMS((6,)), DMA_SEMS((6,)),
            *rows_scratch(n_dp, width // parts), *sums_scratch(n_dp, sum(widths)), *sums_scratch(n_dp, sum(late)),
        ],
        compiler_params=ring_params(4),
        cost_estimate=pl.CostEstimate(flops=9 * 10**9, bytes_accessed=30 * 2**20, transcendentals=0),
        name="project_backward",
    )(
        index_in, index_out, dq, dk, dv, dg, dab, resid, g_middle, select, gain, wdec, bdec, g_rank2, early, middle, down_sum, rank_down,
        *loaded,
    )


def finish_kernel(widths, index_in, index_out, g_tokens, grads, rows_out, sums, *scratch):
    rows, width = g_tokens.shape
    back = DpRows(*scratch[:4])
    reduce = DpSums(grads, *scratch[4:])
    greet_dp(back.n, back.me)
    back.fill(index_in, rows, lambda c: g_tokens[:, c])
    wait_greetings(back.n - 1)
    reduce.start()
    back.start()
    reduce.forward()

    def put(c, val):
        rows_out[:, c] = val.astype(BF16)

    back.take(index_out, rows, put)

    def sink(k, cols, val):
        c = k * width + cols[0]
        sums[:, c : c + cols[1] - cols[0]] = val

    reduce.take(widths, sink)
    back.finish()
    reduce.finish()


def finish(collective_id, widths, index_in, index_out, g_tokens, grads):
    rows, width = g_tokens.shape
    n = lax.axis_size("dp")
    parts = 16 // SHARE
    total = grads.shape[2]
    vm, _ = specs(1, 1)
    return pl.pallas_call(
        functools.partial(finish_kernel, widths),
        out_shape=(sds((rows, width)), sds((SHARE, parts * total), F32)),
        in_specs=[vm] * 4,
        out_specs=[vm] * 2,
        scratch_shapes=[*rows_scratch(n, width // parts), *sums_scratch(n, total)],
        compiler_params=ring_params(collective_id),
        cost_estimate=pl.CostEstimate(flops=10**9, bytes_accessed=20 * 2**20, transcendentals=0),
        name="finish_rows",
    )(index_in, index_out, g_tokens, grads)


def per_device(
    tokens,
    cotangent,
    token_grouped_position,
    sequence_lengths,
    adapter_index_per_seq,
    mixer_norm_gain,
    query_key_matrix,
    value_gate_matrix,
    decay_step_matrix,
    query_key_filters,
    value_filters,
    decay_scale_logarithm,
    decay_step_bias,
    head_output_norm_gain,
    output_matrix,
    feedfwd_norm_gain,
    gate_up_matrix,
    down_matrix,
    adapter_mixer_first,
    adapter_query_key_second,
    adapter_value_gate_second,
    adapter_decay_step_second,
    adapter_output_first,
    adapter_output_second,
    adapter_feedfwd_first,
    adapter_gate_up_second,
    adapter_down_first,
    adapter_down_second,
):
    rows = tokens.shape[0]
    width = tokens.shape[1]
    n_dp = lax.axis_size("dp")
    n_mp = lax.axis_size("mp")
    group = rows * n_mp
    share = rows // n_dp
    ac = adapter_output_second.shape[0]
    heads = decay_scale_logarithm.shape[0]

    routes = token_grouped_position.reshape(n_dp, n_mp, rows)
    def gather(x):
        return lax.all_gather(x, "mp", axis=0, tiled=True)

    def scatter(x):
        return lax.psum_scatter(x, "mp", scatter_dimension=0, tiled=True)

    gain_one, gain_two = mixer_norm_gain[None], feedfwd_norm_gain[None]
    index_tokens, index_slots, select, resid, cot, normed, low, pre_q, pre_k, pre_v, pre_g, pre_ab = project(
        sequence_lengths,
        adapter_index_per_seq,
        routes,
        tokens,
        cotangent,
        gain_one,
        decay_step_matrix,
        adapter_decay_step_second,
        query_key_matrix,
        value_gate_matrix,
        adapter_mixer_first,
        adapter_query_key_second,
        adapter_value_gate_second,
    )
    normed = normed.reshape(group, width)
    cot_later, pre_ab = lax.optimization_barrier((cot, pre_ab))
    cot_all = gather(cot_later)
    gates = (sequence_lengths, decay_scale_logarithm, decay_step_bias)
    shared = (query_key_filters, value_filters, head_output_norm_gain[None])
    mixed, *saved = mixer_fwd(*gates, pre_q, pre_k, pre_v, pre_g, pre_ab, *shared)
    middle, rank_out, normed2, rank2, gate, up, hidden, down_part, rank_part = feed(
        mixed,
        resid,
        gain_two,
        select,
        output_matrix,
        adapter_output_first,
        adapter_output_second,
        adapter_feedfwd_first,
        gate_up_matrix,
        adapter_gate_up_second,
        down_matrix,
        adapter_down_first,
    )
    normed2 = normed2.reshape(group, width)
    g_rank2, g_middle, g_mixed, rank_down, early_parts = feed_back(
        cot_all,
        middle,
        gate,
        up,
        rank_part,
        select,
        gain_two,
        adapter_down_second,
        down_matrix,
        adapter_down_first,
        gate_up_matrix,
        adapter_gate_up_second,
        adapter_feedfwd_first,
        adapter_output_second,
        output_matrix,
        adapter_output_first,
        rank2,
        hidden,
        mixed,
        rank_out,
    )
    down_later, g_mixed = lax.optimization_barrier((down_part, g_mixed))
    down_sum = scatter(down_later)
    dq, dk, dv, dg, dab = mixer_bwd(*gates, g_mixed, pre_g, pre_ab, *shared, saved)
    dq, down_sum = lax.optimization_barrier((dq, down_sum))
    widths = early_widths(gate.shape[1], dv.shape[1], ac)
    g_tokens, late_parts, out_rows, grad_gu, down_in, out_in, side_down, side_branch, grad_qk, grad_vg, gates_ab = project_back(
        widths,
        index_slots,
        index_tokens,
        dq,
        dk,
        dv,
        dg,
        dab,
        resid,
        g_middle,
        select,
        gain_one,
        decay_step_matrix,
        adapter_decay_step_second,
        g_rank2,
        early_parts,
        middle,
        down_sum,
        rank_down,
        query_key_matrix,
        value_gate_matrix,
        adapter_mixer_first,
        adapter_query_key_second,
        adapter_value_gate_second,
        adapter_down_second,
        low,
        normed,
        normed2,
        gate.shape[1],
    )
    parts = 16 // share
    grad_rows, late = finish(6, [width // parts] * 2, index_slots, index_tokens, g_tokens, late_parts)
    per_in = 6 * ac // (n_dp * n_mp)
    per_ffn = 2 * ac // (n_dp * n_mp)
    both = jnp.concatenate([late[:, :width], late[:, width:]], axis=0).T

    def side_out(x):
        return jnp.swapaxes(x.reshape(share, -1, ac), 0, 1).reshape(-1, ac).T

    return (
        out_rows,
        grad_rows,
        both[:, :per_in],
        grad_qk,
        grad_vg,
        jnp.stack([gates_ab[:, :heads], gates_ab[:, heads : 2 * heads]]),
        out_in.T,
        side_out(side_branch),
        both[:, per_in : per_in + per_ffn],
        grad_gu,
        down_in.T,
        side_out(side_down),
    )


def solution(mesh):
    return jax.shard_map(
        per_device,
        mesh=mesh,
        in_specs=(
            P(("dp", "mp"), None),
            P(("dp", "mp"), None),
            P(),
            P("dp", None),
            P("dp", None),
            P(),
            P(None, None, "mp"),
            P(None, None, "mp"),
            P(None, None, "mp"),
            P(None, None, "mp"),
            P(None, "mp"),
            P("mp"),
            P("mp"),
            P(),
            P("mp", None),
            P(),
            P(None, None, "mp"),
            P("mp", None),
            P(),
            P(None, None, "mp"),
            P(None, None, "mp"),
            P(None, None, "mp"),
            P("mp", None),
            P(),
            P(),
            P(None, None, "mp"),
            P("mp", None),
            P(),
        ),
        out_specs=(
            P(("dp", "mp"), None),
            P(("dp", "mp"), None),
            P(None, ("dp", "mp")),
            P(None, "dp", "mp"),
            P(None, "dp", "mp"),
            P(None, "dp", "mp"),
            P("mp", "dp"),
            P(None, ("dp", "mp")),
            P(None, ("dp", "mp")),
            P(None, "dp", "mp"),
            P("mp", "dp"),
            P(None, ("dp", "mp")),
        ),
        check_vma=False,
    )
```

```python
import functools
import jax
import jax.numpy as jnp
from jax import lax
from jax.experimental import pallas as pl
from jax.experimental.pallas import tpu as pltpu
from jax.sharding import PartitionSpec as P

EPSILON = 1e-06
F32 = jnp.float32
BF16 = jnp.bfloat16
CH = 128
BASE = 16
DK = 128
DVAL = 256
INV_ROOT = DK ** -0.5


def mm(a, b):
    return jnp.dot(a.astype(BF16), b.astype(BF16), preferred_element_type=F32)


def mm_nt(a, b):
    return lax.dot_general(a.astype(BF16), b.astype(BF16), (((1,), (1,)), ((), ())), preferred_element_type=F32)


def mm_tn(a, b):
    return lax.dot_general(a.astype(BF16), b.astype(BF16), (((0,), (0,)), ((), ())), preferred_element_type=F32)


def exact_tn(a, b):
    b1 = b.astype(BF16)
    r1 = b - b1.astype(F32)
    b2 = r1.astype(BF16)
    b3 = (r1 - b2.astype(F32)).astype(BF16)
    return mm_tn(a, b1) + mm_tn(a, b2) + mm_tn(a, b3)


def iota2(shape, dim):
    return lax.broadcasted_iota(jnp.int32, shape, dim)


def sigmoid(x):
    return 1.0 / (1.0 + jnp.exp(-x))


def conv_rows(x, taps, masks_ref, length):
    total = x * taps[0:1]
    for shift in range(1, 4):
        total = total + pltpu.roll(x, shift, 0) * masks_ref[shift - 1] * taps[shift : shift + 1]
    return total


def conv_rows_back(d, taps, masks_ref, length):
    total = d * taps[0:1]
    for shift in range(1, 4):
        total = total + pltpu.roll(d * masks_ref[shift - 1], length - shift, 0) * taps[shift : shift + 1]
    return total


class Saves:
    def __init__(self, sems):
        self.sems, self.live = sems, []

    def start(self, src, dst):
        copy = pltpu.make_async_copy(src, dst, self.sems.at[len(self.live)])
        copy.start()
        self.live.append(copy)

    def finish(self):
        for copy in self.live:
            copy.wait()


def start_loads(pairs, sems):
    copies = [pltpu.make_async_copy(src, dst, sems.at[n]) for n, (src, dst) in enumerate(pairs)]
    for copy in copies:
        copy.start()
    return copies


def gate_columns(ab, dsl, bias):
    z = ab + bias
    soft = jnp.maximum(z, 0.0) + jnp.log1p(jnp.exp(-jnp.abs(z)))
    return -jnp.exp(dsl) * soft, z


def segment_at(position, lens):
    end = lens[0, 0]
    count = as_int(position >= end)
    for n in range(1, lens.shape[1] - 1):
        end = end + lens[0, n]
        count = count + as_int(position >= end)
    return count


def as_int(flag):
    return jnp.where(flag, 1, 0)


def fill_masks(masks, lens):
    shape = masks.shape[1:]
    position = iota2(shape, 0)
    seg = segment_at(position, lens)
    for shift in range(1, 4):
        same = (position >= shift) & (segment_at(position - shift, lens) == seg)
        masks[shift - 1] = same.astype(F32)


def gate_rows(dsl, bias):
    lane = iota2((1, CH), 1)
    rows = []
    for source in (dsl, bias):
        out = jnp.zeros((1, CH), F32)
        for h in range(source.shape[0]):
            out = jnp.where(lane == h, source[h], out)
        rows.append(out)
    return rows


def base_inverse(mats):
    nb = CH // BASE
    lane = iota2((1, CH), 1)
    lane_masks = [(lane // BASE == b).astype(F32) for b in range(nb)]
    packed = []
    for a in mats:
        d = a[0:BASE] * lane_masks[0]
        for b in range(1, nb):
            d = d + a[b * BASE : (b + 1) * BASE] * lane_masks[b]
        packed.append(d)
    d = jnp.concatenate(packed, axis=0)
    hi = d.astype(BF16)
    lo = (d - hi.astype(F32)).astype(BF16)
    row = iota2((CH, CH), 0)
    col = iota2((CH, CH), 1)
    same = row // BASE == col // BASE
    spread = jnp.concatenate(
        [(same & (row % BASE == j)).astype(BF16) for j in range(BASE - 1)], axis=1
    )
    wide = mm(hi, spread) + mm(lo, spread)
    sub = iota2((BASE, CH), 0)
    eye = (sub == iota2((BASE, CH), 1) % BASE).astype(F32)
    out = []
    for n in range(len(mats)):
        t = eye
        for j in range(BASE - 1):
            t = t - wide[n * BASE : (n + 1) * BASE, j * CH : (j + 1) * CH] * t[j : j + 1]
        out.append(jnp.concatenate([t * lane_masks[b] for b in range(nb)], axis=0))
    return out


def full_inverse(mats):
    ts = base_inverse(mats)
    row = iota2((CH, CH), 0)
    col = iota2((CH, CH), 1)
    size = BASE
    while size < CH:
        pick = ((row // size) % 2 == 1) & (col // size == row // size - 1)
        steps = [mm(jnp.where(pick, a, 0.0), t) for a, t in zip(mats, ts)]
        ts = [t - mm(t, s) for t, s in zip(ts, steps)]
        size *= 2
    return ts


def mixer_fwd_kernel(
    heads, lens, dsl, bias, preq, prek, prev, ab_ref, taps_qk, taps_v, gain, preg_h,
    mixed_h, cq_h, ck_h, cv_h, t_h, s_h, u_h, o_h,
    preg, mixed, cq, ck, cv, t_out, s_out, u_out, o_out, lsem, ssem, masks, qn, kn, vn, cum_s, state,
):
    length = preq.shape[0]
    count = length // CH
    gate_load = start_loads([(preg_h, preg)], lsem)
    saves = Saves(ssem)
    taps_q, taps_k = taps_qk.at[0], taps_qk.at[1]
    fill_masks(masks, lens)
    gate_par = gate_rows(dsl, bias)

    def key_tile(h, carry):
        cols = pl.ds(pl.multiple_of(h * DK, DK), DK)
        for src, taps, save, dst, scale in ((preq, taps_q, cq, qn, INV_ROOT), (prek, taps_k, ck, kn, 1.0)):
            c = conv_rows(src[:, cols].astype(F32), taps[:, cols], masks, length)
            save[:, cols] = c.astype(BF16)
            u = c * sigmoid(c)
            n = lax.rsqrt(jnp.sum(u * u, axis=-1, keepdims=True) + EPSILON) * scale
            dst[:, cols] = (u * n).astype(BF16)
        for half in range(2):
            vcols = pl.ds(pl.multiple_of(h * DVAL + half * DK, DK), DK)
            c = conv_rows(prev[:, vcols].astype(F32), taps_v[:, vcols], masks, length)
            cv[:, vcols] = c.astype(BF16)
            vn[:, vcols] = c * sigmoid(c)
        return carry

    lax.fori_loop(0, heads, key_tile, 0)
    for src, dst in ((cq, cq_h), (ck, ck_h), (cv, cv_h)):
        saves.start(src, dst)
    gate_load[0].wait()
    row = iota2((CH, CH), 0)
    col = iota2((CH, CH), 1)
    upper = (row <= col).astype(BF16)
    log_decay, _ = gate_columns(ab_ref[...], gate_par[0], gate_par[1])
    beta_all = sigmoid(ab_ref[...])
    for n in range(count):
        cum_s[n * CH : (n + 1) * CH] = exact_tn(upper, log_decay[n * CH : (n + 1) * CH])
    cum_s[length : length + CH] = jnp.zeros((CH, DK), F32)
    for h in range(heads):
        state[h] = jnp.zeros((DK, DVAL), F32)

    for n in range(count):
        r = pl.ds(n * CH, CH)
        seg_col = segment_at(row + n * CH, lens)
        seg_row = segment_at(col + n * CH, lens)
        keep = (seg_col == seg_row) & (row >= col)
        keepf = keep.astype(F32)
        strict = (row > col).astype(F32)
        cum = cum_s[r]
        cum_t = cum.T
        beta_c = beta_all[n * CH : (n + 1) * CH]
        prev_last = segment_at(n * CH - 1, lens) if n else -1
        start = jnp.exp(cum) * (seg_col == prev_last).astype(F32)
        last_seg = segment_at((n + 1) * CH - 1, lens)
        tail = jnp.exp(cum[CH - 1 : CH] - cum) * (seg_col == last_seg).astype(F32)
        mats, scores = [], []
        for h in range(heads):
            q = qn[r, h * DK : (h + 1) * DK]
            k = kn[r, h * DK : (h + 1) * DK]
            ratio = jnp.exp(jnp.minimum(cum[:, h : h + 1] - cum_t[h : h + 1], 0.0)) * keepf
            beta = beta_c[:, heads + h : heads + h + 1]
            both = mm_nt(jnp.concatenate([q, k], axis=0), k)
            scores.append((ratio * both[:CH]).astype(BF16))
            mats.append(beta * ratio * strict * both[CH:])
        ts = full_inverse(mats)
        for h in range(heads):
            q = qn[r, h * DK : (h + 1) * DK]
            k = kn[r, h * DK : (h + 1) * DK]
            vcols = slice(h * DVAL, (h + 1) * DVAL)
            beta = beta_c[:, heads + h : heads + h + 1]
            st = start[:, h : h + 1]
            tb = ts[h].astype(BF16)
            s0 = state[h]
            s0b = s0.astype(BF16)
            t_out[n, h] = tb
            s_out[n, h] = s0b
            both = mm(jnp.concatenate([q, k], axis=0), s0b)
            res = beta * (vn[r, vcols] - st * both[CH:])
            un = mm(tb, res).astype(BF16)
            u_out[r, vcols] = un
            o = st * both[:CH] + mm(scores[h], un)
            state[h] = start[CH - 1 : CH, h : h + 1] * s0 + mm_tn(k.astype(F32) * tail[:, h : h + 1], un)
            o_out[r, vcols] = o.astype(BF16)
            g = preg[r, vcols].astype(F32)
            rn = lax.rsqrt(jnp.mean(o * o, axis=-1, keepdims=True) + EPSILON)
            mixed[r, vcols] = (o * rn * gain[...] * (g * sigmoid(g))).astype(BF16)
        saves.start(t_out.at[n], t_h.at[n])
        saves.start(s_out.at[n], s_h.at[n])
        for src, dst in ((u_out, u_h), (o_out, o_h), (mixed, mixed_h)):
            saves.start(src.at[r], dst.at[r])
    saves.finish()


def mixer_fwd(lens, dsl, bias, preq, prek, prev, preg, ab, taps_qk, taps_v, gain):
    length = preq.shape[0]
    heads = preq.shape[1] // DK
    count = length // CH
    vm = pl.BlockSpec(memory_space=pltpu.VMEM)
    sm = pl.BlockSpec(memory_space=pltpu.SMEM)
    hb = pl.BlockSpec(memory_space=pl.ANY)
    out_shape = (
        jax.ShapeDtypeStruct((length, heads * DVAL), BF16),
        jax.ShapeDtypeStruct((length, heads * DK), BF16),
        jax.ShapeDtypeStruct((length, heads * DK), BF16),
        jax.ShapeDtypeStruct((length, heads * DVAL), BF16),
        jax.ShapeDtypeStruct((count, heads, CH, CH), BF16),
        jax.ShapeDtypeStruct((count, heads, DK, DVAL), BF16),
        jax.ShapeDtypeStruct((length, heads * DVAL), BF16),
        jax.ShapeDtypeStruct((length, heads * DVAL), BF16),
    )
    return pl.pallas_call(
        functools.partial(mixer_fwd_kernel, heads),
        out_shape=out_shape,
        in_specs=[sm] * 3 + [vm] * 7 + [hb],
        out_specs=[hb] * len(out_shape),
        scratch_shapes=[
            pltpu.VMEM(preg.shape, BF16),
            *[pltpu.VMEM(o.shape, o.dtype) for o in out_shape],
            pltpu.SemaphoreType.DMA((1,)),
            pltpu.SemaphoreType.DMA((3 + 5 * count,)),
            pltpu.VMEM((3, length, CH), F32),
            pltpu.VMEM((length, heads * DK), BF16),
            pltpu.VMEM((length, heads * DK), BF16),
            pltpu.VMEM((length, heads * DVAL), F32),
            pltpu.VMEM((length + CH, CH), F32),
            pltpu.VMEM((heads, DK, DVAL), F32),
        ],
        compiler_params=pltpu.CompilerParams(vmem_limit_bytes=60 * 2**20),
        cost_estimate=pl.CostEstimate(flops=20 * 10**9, bytes_accessed=70 * 2**20, transcendentals=0),
        name="mixer_forward",
    )(lens, dsl, bias, preq, prek, prev, ab, taps_qk, taps_v, gain, preg)


def mixer_bwd_kernel(
    heads, lens, dsl, bias, ab_ref, taps_qk, taps_v, gain,
    cq, ck, cv, dmix_h, preg_h, t_h, s_h, u_h, o_h,
    dpq, dpk, dpv, dpg_h, dab,
    dpg, dmix, preg, t_in, s_in, u_in, o_in, lsem, ssem, masks, qn, kn, vn, cum_s, dstate, dqs, dks, dvs, gcol,
):
    length = dmix.shape[0]
    count = length // CH
    arriving = start_loads(
        [(o_h, o_in), (preg_h, preg), (dmix_h, dmix), (u_h, u_in), (s_h, s_in), (t_h, t_in)], lsem
    )
    saves = Saves(ssem)
    taps_q, taps_k = taps_qk.at[0], taps_qk.at[1]
    fill_masks(masks, lens)
    gate_par = gate_rows(dsl, bias)

    def key_tile(h, carry):
        cols = pl.ds(pl.multiple_of(h * DK, DK), DK)
        for save, dst, scale in ((cq, qn, INV_ROOT), (ck, kn, 1.0)):
            c = save[:, cols].astype(F32)
            u = c * sigmoid(c)
            n = lax.rsqrt(jnp.sum(u * u, axis=-1, keepdims=True) + EPSILON) * scale
            dst[:, cols] = (u * n).astype(BF16)
        for half in range(2):
            vcols = pl.ds(pl.multiple_of(h * DVAL + half * DK, DK), DK)
            c = cv[:, vcols].astype(F32)
            vn[:, vcols] = c * sigmoid(c)
        return carry

    lax.fori_loop(0, heads, key_tile, 0)
    for copy in arriving:
        copy.wait()
    row = iota2((CH, CH), 0)
    col = iota2((CH, CH), 1)
    upper = (row <= col).astype(BF16)
    lower = (row >= col).astype(BF16)
    log_decay, z_all = gate_columns(ab_ref[...], gate_par[0], gate_par[1])
    beta_all = sigmoid(ab_ref[...])
    for n in range(count):
        cum_s[n * CH : (n + 1) * CH] = exact_tn(upper, log_decay[n * CH : (n + 1) * CH])
    for h in range(heads):
        dstate[h] = jnp.zeros((DK, DVAL), F32)
    lane = iota2((1, CH), 1)
    strict = (row > col).astype(F32)
    ones = jnp.ones((CH, CH), BF16)

    for n in range(count - 1, -1, -1):
        r = pl.ds(n * CH, CH)
        seg_col = segment_at(row + n * CH, lens)
        seg_row = segment_at(col + n * CH, lens)
        keepf = ((seg_col == seg_row) & (row >= col)).astype(F32)
        cum = cum_s[r]
        cum_t = cum.T
        beta_c = beta_all[n * CH : (n + 1) * CH]
        prev_last = segment_at(n * CH - 1, lens) if n else -1
        start = jnp.exp(cum) * (seg_col == prev_last).astype(F32)
        last_seg = segment_at((n + 1) * CH - 1, lens)
        tail = jnp.exp(cum[CH - 1 : CH] - cum) * (seg_col == last_seg).astype(F32)
        dcum_all = jnp.zeros((CH, CH), F32)
        dbeta_all = jnp.zeros((CH, CH), F32)
        dlast_all = jnp.zeros((1, CH), F32)
        for h in range(heads):
            qc = slice(h * DK, (h + 1) * DK)
            vcols = slice(h * DVAL, (h + 1) * DVAL)
            here = (lane == h).astype(F32)
            o = o_in[r, vcols].astype(F32)
            g = preg[r, vcols].astype(F32)
            dm = dmix[r, vcols].astype(F32)
            sg = sigmoid(g)
            rn = lax.rsqrt(jnp.mean(o * o, axis=-1, keepdims=True) + EPSILON)
            on = o * rn
            y = on * gain[...]
            dpg[r, vcols] = (dm * y * (sg * (1.0 + g * (1.0 - sg)))).astype(BF16)
            dy = dm * (g * sg) * gain[...]
            do = rn * (dy - on * jnp.mean(dy * on, axis=-1, keepdims=True))
            dob = do.astype(BF16)
            q = qn[r, qc]
            k = kn[r, qc]
            kf = k.astype(F32)
            qf = q.astype(F32)
            un = u_in[r, vcols]
            s0 = s_in[n, h]
            tb = t_in[n, h]
            beta = beta_c[:, heads + h : heads + h + 1]
            st = start[:, h : h + 1]
            tl = tail[:, h : h + 1]
            carry_scale = start[CH - 1 : CH, h : h + 1]
            ratio = jnp.exp(jnp.minimum(cum[:, h : h + 1] - cum_t[h : h + 1], 0.0)) * keepf
            both = mm_nt(jnp.concatenate([q, k], axis=0), k)
            scores = ratio * both[:CH]
            rs = ratio * strict
            amat = rs * both[CH:]
            qk_state = mm(jnp.concatenate([q, k], axis=0), s0)
            ks = qk_state[CH:]
            ds1 = dstate[h]
            ds1b = ds1.astype(BF16)
            ktail = (kf * tl).astype(BF16)
            dun = mm_tn(scores, dob) + mm(ktail, ds1b)
            dres = mm_tn(tb, dun)
            dresb = dres.astype(BF16)
            dks0 = (-(beta * st) * dres).astype(BF16)
            qst = (qf * st).astype(BF16)
            dstate[h] = carry_scale * ds1 + mm_tn(jnp.concatenate([qst, k], axis=0), jnp.concatenate([dob, dks0], axis=0))
            both_d = mm_nt(jnp.concatenate([dob, dresb], axis=0), un)
            dscore = both_d[:CH]
            da = -both_d[CH:]
            dqk = (dscore * ratio).astype(BF16)
            dkk = (da * beta * rs).astype(BF16)
            dspread = dscore * scores + da * beta * amat
            dbeta = jnp.sum(da * amat, axis=-1, keepdims=True) + jnp.sum(
                dres * (vn[r, vcols] - st * ks), axis=-1, keepdims=True
            )
            dvs[r, vcols] = beta * dres
            by_state = mm_nt(jnp.concatenate([dob, dks0, un], axis=0), jnp.concatenate([s0, ds1b], axis=0))
            dq_state = by_state[:CH, :DK]
            dq = st * dq_state + mm(dqk, k)
            dktail = by_state[2 * CH :, DK:]
            dk = (
                by_state[CH : 2 * CH, :DK]
                + tl * dktail
                + mm_tn(dqk, q)
                + mm(dkk, k)
                + mm_tn(dkk, k)
            )
            dqs[r, qc] = dq
            dks[r, qc] = dk
            dstart_s = st * jnp.sum(qf * dq_state, axis=-1, keepdims=True) + st * (
                -beta * jnp.sum(dres * ks, axis=-1, keepdims=True)
            )
            dtail_s = tl * jnp.sum(kf * dktail, axis=-1, keepdims=True)
            dcarry = carry_scale * jnp.sum(jnp.sum(ds1 * s0.astype(F32), axis=-1, keepdims=True), axis=0, keepdims=True)
            colsum = exact_cols(dspread, ones)
            dcum = jnp.sum(dspread, axis=-1, keepdims=True) - colsum[:, 0:1] + dstart_s - dtail_s
            dlast = jnp.sum(dtail_s, axis=0, keepdims=True) + dcarry
            dcum_all = dcum_all + dcum * here
            dlast_all = dlast_all + dlast * here
            dbeta_all = dbeta_all + dbeta * (lane == heads + h).astype(F32)
        saves.start(dpg.at[r], dpg_h.at[r])
        dcum_all = dcum_all + dlast_all * (row == CH - 1).astype(F32)
        gcol[r] = exact_tn(lower, dcum_all) + dbeta_all * beta_c * (1.0 - beta_c)

    slope = -jnp.exp(gate_par[0]) * sigmoid(z_all)
    dab[...] = (gcol[...] * jnp.where(lane < heads, slope, 1.0)).astype(BF16)

    def back_tile(h, carry):
        cols = pl.ds(pl.multiple_of(h * DK, DK), DK)
        for save, dsrc, taps, dst, scale in ((cq, dqs, taps_q, dpq, INV_ROOT), (ck, dks, taps_k, dpk, 1.0)):
            c = save[:, cols].astype(F32)
            sg = sigmoid(c)
            u = c * sg
            n = lax.rsqrt(jnp.sum(u * u, axis=-1, keepdims=True) + EPSILON)
            un = u * n
            d = dsrc[:, cols] * scale
            du = n * (d - un * jnp.sum(d * un, axis=-1, keepdims=True))
            dc = du * (sg * (1.0 + c * (1.0 - sg)))
            dst[:, cols] = conv_rows_back(dc, taps[:, cols], masks, length).astype(BF16)
        for half in range(2):
            vcols = pl.ds(pl.multiple_of(h * DVAL + half * DK, DK), DK)
            c = cv[:, vcols].astype(F32)
            sg = sigmoid(c)
            dc = dvs[:, vcols] * (sg * (1.0 + c * (1.0 - sg)))
            dpv[:, vcols] = conv_rows_back(dc, taps_v[:, vcols], masks, length).astype(BF16)
        return carry

    lax.fori_loop(0, heads, back_tile, 0)
    saves.finish()


def exact_cols(x, ones):
    hi = x.astype(BF16)
    lo = (x - hi.astype(F32)).astype(BF16)
    return mm_tn(hi, ones) + mm_tn(lo, ones)


def mixer_bwd(lens, dsl, bias, dmix, preg, ab, taps_qk, taps_v, gain, saved):
    length = dmix.shape[0]
    heads = dmix.shape[1] // DVAL
    vm = pl.BlockSpec(memory_space=pltpu.VMEM)
    sm = pl.BlockSpec(memory_space=pltpu.SMEM)
    hb = pl.BlockSpec(memory_space=pl.ANY)
    out_shape = (
        jax.ShapeDtypeStruct((length, heads * DK), BF16),
        jax.ShapeDtypeStruct((length, heads * DK), BF16),
        jax.ShapeDtypeStruct((length, heads * DVAL), BF16),
        jax.ShapeDtypeStruct((length, heads * DVAL), BF16),
        jax.ShapeDtypeStruct((length, CH), BF16),
    )
    return pl.pallas_call(
        functools.partial(mixer_bwd_kernel, heads),
        out_shape=out_shape,
        in_specs=[sm] * 3 + [vm] * 7 + [hb] * 6,
        out_specs=[vm, vm, vm, hb, vm],
        scratch_shapes=[
            pltpu.VMEM(dmix.shape, BF16),
            *[pltpu.VMEM(a.shape, a.dtype) for a in (dmix, preg, *saved[3:])],
            pltpu.SemaphoreType.DMA((6,)),
            pltpu.SemaphoreType.DMA((length // CH,)),
            pltpu.VMEM((3, length, CH), F32),
            pltpu.VMEM((length, heads * DK), BF16),
            pltpu.VMEM((length, heads * DK), BF16),
            pltpu.VMEM((length, heads * DVAL), F32),
            pltpu.VMEM((length, CH), F32),
            pltpu.VMEM((heads, DK, DVAL), F32),
            pltpu.VMEM((length, heads * DK), F32),
            pltpu.VMEM((length, heads * DK), F32),
            pltpu.VMEM((length, heads * DVAL), F32),
            pltpu.VMEM((length, CH), F32),
        ],
        compiler_params=pltpu.CompilerParams(vmem_limit_bytes=60 * 2**20),
        cost_estimate=pl.CostEstimate(flops=30 * 10**9, bytes_accessed=100 * 2**20, transcendentals=0),
        name="mixer_backward",
    )(lens, dsl, bias, ab, taps_qk, taps_v, gain, *saved[:3], dmix, preg, *saved[3:])


MESH_ID = pl.DeviceIdType.MESH
RING = 4
DMA_SEMS = pltpu.SemaphoreType.DMA
PIECES = 4
WIDE_VMEM = 60 * 2**20
SHARE = 4
ADAPTER_RANK = 16


def ring_places():
    m = lax.axis_index("mp")
    return m, lax.rem(m + 3, RING), lax.rem(m + 1, RING), lax.rem(m + 2, RING)


def ring_barrier(places):
    _, left, right, _ = places
    barrier = pltpu.get_barrier_semaphore()
    for neighbour in (left, right):
        pl.semaphore_signal(barrier, inc=1, device_id={"mp": neighbour}, device_id_type=MESH_ID)
    pl.semaphore_wait(barrier, 2)


class RingGather:
    def __init__(self, buf, send, recv, places):
        self.buf, self.send, self.recv = buf, send, recv
        self.m, self.left, self.right, self.opp = places
        half = buf.shape[1] // 2
        self.top, self.bot = pl.ds(0, half), pl.ds(half, half)

    def begin(self, i, slot, part, to):
        step = part.size // PIECES
        for n in range(PIECES):
            self.copy(i, slot, pl.ds(part.start + n * step, step), to).start()

    def copy(self, i, slot, part, to):
        ref = self.buf.at[slot, part]
        return pltpu.make_async_remote_copy(
            src_ref=ref,
            dst_ref=ref,
            send_sem=self.send.at[i],
            recv_sem=self.recv.at[i],
            device_id={"mp": to},
            device_id_type=MESH_ID,
        )

    def start(self):
        self.begin(0, self.m, self.top, self.right)
        self.begin(1, self.m, self.bot, self.left)
        self.begin(2, self.m, self.bot, self.right)
        self.begin(3, self.m, self.top, self.left)

    def forward(self):
        self.copy(0, self.left, self.top, self.right).wait_recv()
        self.begin(4, self.left, self.top, self.right)
        self.copy(1, self.right, self.bot, self.left).wait_recv()
        self.begin(5, self.right, self.bot, self.left)

    def wait_left(self):
        self.copy(2, self.left, self.bot, self.right).wait_recv()

    def wait_right(self):
        self.copy(3, self.right, self.top, self.left).wait_recv()

    def wait_opp(self):
        self.copy(4, self.opp, self.top, self.right).wait_recv()
        self.copy(5, self.opp, self.bot, self.left).wait_recv()

    def finish(self):
        self.copy(0, self.m, self.top, self.right).wait_send()
        self.copy(1, self.m, self.bot, self.left).wait_send()
        self.copy(2, self.m, self.bot, self.right).wait_send()
        self.copy(3, self.m, self.top, self.left).wait_send()
        self.copy(4, self.left, self.top, self.right).wait_send()
        self.copy(5, self.right, self.bot, self.left).wait_send()


class RingScatter:
    def __init__(self, sbuf, rbuf, acc, send, recv, places):
        self.sbuf, self.rbuf, self.acc, self.send, self.recv = sbuf, rbuf, acc, send, recv
        self.m, self.left, self.right, self.opp = places
        self.half = sbuf.shape[1]

    def begin(self, i):
        step = self.half // PIECES
        for n in range(PIECES):
            self.copy(i, pl.ds(n * step, step)).start()

    def copy(self, i, part=slice(None)):
        to = self.right if i % 2 == 0 else self.left
        return pltpu.make_async_remote_copy(
            src_ref=self.sbuf.at[i, part],
            dst_ref=self.rbuf.at[i, part],
            send_sem=self.send.at[i],
            recv_sem=self.recv.at[i],
            device_id={"mp": to},
            device_id_type=MESH_ID,
        )

    def run(self, part, meanwhile=None, ready=None):
        half = self.half
        rows = 2 * half

        def put_far(cols, val):
            self.sbuf[0, :, cols] = val[:half].astype(BF16)
            self.sbuf[1, :, cols] = val[half:rows].astype(BF16)
            self.acc[0, :, cols] = val[rows:]
            self.sbuf[2, :, cols] = val[rows + half :].astype(BF16)

        part((self.opp, self.right), put_far)
        if ready is not None:
            ready()
        self.begin(0)
        self.begin(1)
        self.begin(2)

        def put_near(cols, val):
            self.acc[1, :, cols] = val[:rows]
            self.sbuf[3, :, cols] = val[:half].astype(BF16)
            self.acc[2, :, cols] = val[rows:]

        part((self.left, self.m), put_near)
        self.begin(3)
        if meanwhile is not None:
            meanwhile()
        self.copy(0).wait_recv()
        self.sbuf[4] = (self.acc[0, 0:half] + self.rbuf[0].astype(F32)).astype(BF16)
        self.begin(4)
        self.copy(1).wait_recv()
        self.sbuf[5] = (self.acc[1, half:rows] + self.rbuf[1].astype(F32)).astype(BF16)
        self.begin(5)
        for i in range(2, 6):
            self.copy(i).wait_recv()

    def total(self, rows, cols):
        lo, hi = rows
        if hi <= self.half:
            a, b, r = self.rbuf[4, lo:hi, cols], self.rbuf[3, lo:hi, cols], slice(lo, hi)
        else:
            r = slice(lo, hi)
            lo, hi = lo - self.half, hi - self.half
            a, b = self.rbuf[2, lo:hi, cols], self.rbuf[5, lo:hi, cols]
        return self.acc[2, r, cols] + a.astype(F32) + b.astype(F32)

    def finish(self):
        for i in range(6):
            self.copy(i).wait_send()


class Loads:
    def __init__(self, pairs, sems):
        self.copies = [pltpu.make_async_copy(src, dst, sems.at[n]) for n, (src, dst) in enumerate(pairs)]
        self.waited = set()

    def start(self, *which):
        for n in which or range(len(self.copies)):
            self.copies[n].start()

    def wait(self, *which):
        for n in which:
            if n not in self.waited:
                self.copies[n].wait()
                self.waited.add(n)


def loop(lo, hi, body):
    def step(s, carry):
        body(s)
        return carry

    lax.fori_loop(lo, hi, step, 0)


def greet_dp(n, me):
    barrier = pltpu.get_barrier_semaphore()
    loop(
        1,
        n,
        lambda s: pl.semaphore_signal(barrier, inc=1, device_id={"dp": lax.rem(me + s, n)}, device_id_type=MESH_ID),
    )


def greet_ring(places):
    barrier = pltpu.get_barrier_semaphore()
    for neighbour in (places[1], places[2]):
        pl.semaphore_signal(barrier, inc=1, device_id={"mp": neighbour}, device_id_type=MESH_ID)


def wait_greetings(count):
    pl.semaphore_wait(pltpu.get_barrier_semaphore(), count)


class DpRows:
    def __init__(self, stage, land, send, recv):
        self.stage, self.land, self.send, self.recv = stage, land, send, recv
        self.n, _, self.pw = stage.shape
        self.parts = 16 // SHARE
        self.me = lax.axis_index("dp")

    def maps(self, index, rows):
        slots = self.n * 16
        hit = iota2((rows, slots), 0).astype(F32) == index[0:1]
        part_of = (iota2((1, slots), 1) // SHARE) % self.parts
        return [(hit & (part_of == p)).astype(F32).astype(BF16) for p in range(self.parts)]

    def fill(self, index, rows, value):
        acc = jnp.zeros((self.n * 16, self.pw), F32)
        for p, hit in enumerate(self.maps(index, rows)):
            acc = acc + mm_tn(hit, value(slice(p * self.pw, (p + 1) * self.pw)))
        self.stage[...] = acc.astype(BF16).reshape(self.n, 16, self.pw)
        self.land[self.me] = self.stage[self.me]

    def copy(self, to, source):
        return pltpu.make_async_remote_copy(
            src_ref=self.stage.at[to],
            dst_ref=self.land.at[source],
            send_sem=self.send.at[to],
            recv_sem=self.recv.at[source],
            device_id={"dp": to},
            device_id_type=MESH_ID,
        )

    def ahead(self, s):
        return lax.rem(self.me + s, self.n)

    def behind(self, s):
        return lax.rem(self.me + self.n - s, self.n)

    def start(self):
        loop(1, self.n, lambda s: self.copy(self.ahead(s), self.me).start())

    def take(self, index, rows, put):
        loop(1, self.n, lambda s: self.copy(self.behind(s), self.behind(s)).wait_recv())
        got = self.land[...].reshape(self.n * 16, self.pw)
        for p, hit in enumerate(self.maps(index, rows)):
            put(slice(p * self.pw, (p + 1) * self.pw), mm(hit, got))

    def finish(self):
        loop(1, self.n, lambda s: self.copy(self.ahead(s), self.me).wait_send())


class DpSums:
    def __init__(self, grads, pair_land, mine, sum_land, send, recv, send2, recv2):
        self.grads, self.pair_land, self.mine, self.sum_land = grads, pair_land, mine, sum_land
        self.send, self.recv, self.send2, self.recv2 = send, recv, send2, recv2
        self.me = lax.axis_index("dp")
        self.core = lax.rem(self.me, 2)
        self.here = self.me // 2
        self.pairs = pair_land.shape[0]

    def pair_copy(self, i):
        return pltpu.make_async_remote_copy(
            src_ref=self.grads.at[2 * i + 1 - self.core],
            dst_ref=self.pair_land.at[i],
            send_sem=self.send.at[i],
            recv_sem=self.recv.at[i],
            device_id={"dp": self.me + 1 - 2 * self.core},
            device_id_type=MESH_ID,
        )

    def sum_copy(self, to, source):
        return pltpu.make_async_remote_copy(
            src_ref=self.mine.at[to],
            dst_ref=self.sum_land.at[source],
            send_sem=self.send2.at[to],
            recv_sem=self.recv2.at[source],
            device_id={"dp": 2 * to + self.core},
            device_id_type=MESH_ID,
        )

    def ahead(self, s):
        return lax.rem(self.here + s, self.pairs)

    def behind(self, s):
        return lax.rem(self.here + self.pairs - s, self.pairs)

    def start(self):
        loop(1, self.pairs + 1, lambda s: self.pair_copy(self.ahead(s)).start())

    def add(self, i):
        self.pair_copy(i).wait_recv()
        self.mine[i] = (self.grads[2 * i + self.core].astype(F32) + self.pair_land[i].astype(F32)).astype(BF16)

    def forward(self):
        def one(s):
            i = self.ahead(s)
            self.add(i)
            self.sum_copy(i, self.here).start()

        loop(1, self.pairs, one)
        self.add(self.here)
        self.sum_land[self.here] = self.mine[self.here]

    def take(self, widths, sink):
        parts = 16 // SHARE
        loop(1, self.pairs, lambda s: self.sum_copy(self.behind(s), self.behind(s)).wait_recv())
        at = 0
        for k, w in enumerate(widths):
            total = self.sum_land[0, :, at : at + w].astype(F32)
            for i in range(1, self.pairs):
                total = total + self.sum_land[i, :, at : at + w].astype(F32)
            for p in range(parts):
                sink(k, (p * w, (p + 1) * w), total[p * SHARE : (p + 1) * SHARE])
            at += w

    def finish(self):
        loop(1, self.pairs + 1, lambda s: self.pair_copy(self.ahead(s)).wait_send())
        loop(1, self.pairs, lambda s: self.sum_copy(self.ahead(s), self.here).wait_send())


def rows_scratch(n, pw):
    return [pltpu.VMEM((n, 16, pw), BF16), pltpu.VMEM((n, 16, pw), BF16), DMA_SEMS((n,)), DMA_SEMS((n,))]


def sums_scratch(n, w):
    half = n // 2
    return [pltpu.VMEM((half, 16, w), BF16)] * 3 + [DMA_SEMS((half,))] * 4


def unfold(n, per):
    row = iota2((n, n), 0)
    col = iota2((n, n), 1)
    part = per // SHARE
    wide = n // part
    hit = (row // per == (col % wide) // SHARE) & (row % SHARE == col % SHARE) & ((row // SHARE) % part == col // wide)
    return hit.astype(F32).astype(BF16)


def keep_chunks(stage, deal, pieces, at):
    n = stage.shape[0]
    w = pieces[0].shape[1]
    used = deal[:, 0 : len(pieces) * n * SHARE]
    got = mm(used, jnp.concatenate([p.astype(BF16) for p in pieces], axis=0))
    stage[:, :, at : at + w] = got.astype(BF16).reshape(n, 16, w)
    return at + w


def fill_select(select, lens, adapters):
    seg = segment_at(iota2(select.shape, 0), lens)
    which = jnp.full(select.shape, adapters[0, 0], jnp.int32)
    for n in range(1, lens.shape[1]):
        which = jnp.where(seg == n, adapters[0, n], which)
    select[...] = (iota2(select.shape, 1) // ADAPTER_RANK == which).astype(F32)


def fill_gates(heads, wdec, bdec, wab, bab):
    depth = wdec.shape[1]
    total = jnp.zeros(wab.shape, F32)
    for n in range(2):
        line, k = iota2((CH, depth), 0), iota2((CH, depth), 1)
        at = ((line == k + n * heads) & (k < heads)).astype(F32).astype(BF16)
        total = total + mm(at, wdec[n])
        bab[n] = mm_nt(bdec[n].astype(F32).T, at).astype(BF16)
    wab[...] = total.astype(BF16)


def route_indices(routes, rows):
    me, mp = lax.axis_index("dp"), lax.axis_index("mp")
    n = routes.shape[0]
    slots = n * 16
    column = routes[:, 0, :]
    for k in range(1, routes.shape[1]):
        column = jnp.where(mp == k, routes[:, k, :], column)
    group = rows * RING
    dest = (column // group).astype(F32)
    mine = iota2((n, rows), 0) == me
    own = jnp.sum(jnp.where(mine, dest, 0.0), axis=0, keepdims=True)
    across = jnp.broadcast_to(own, (rows, rows))
    down = across.T
    line = iota2((rows, rows), 0)
    lane = iota2((rows, rows), 1)
    rank = jnp.sum(((across == down) & (lane < line)).astype(F32), axis=1, keepdims=True)
    place = down[:, 0:1] * SHARE + rank
    slot = iota2((1, slots), 1)
    slot_row = ((slot // 16) * SHARE + slot % SHARE).astype(F32)
    leaves = jnp.sum(
        jnp.where(place == slot_row, iota2((rows, slots), 0).astype(F32), 0.0), axis=0, keepdims=True
    )
    here = dest == me.astype(F32)
    order = mm(here.astype(F32), (line < lane).astype(F32))
    value = (column - me * group - mp * rows).astype(F32)
    owner = iota2((n, slots), 0) == slot // 16
    lands = jnp.zeros((1, slots), F32)
    for j in range(SHARE):
        found = jnp.sum(jnp.where(here & (order == float(j)), value, 0.0), axis=1, keepdims=True)
        lands = lands + jnp.sum(jnp.where(owner & (slot % SHARE == j), found, 0.0), axis=0, keepdims=True)
    return leaves, lands


def tiles(total, step=512):
    return [(at, min(step, total - at)) for at in range(0, total, step)]


def block_rows(place, rows):
    return pl.ds(pl.multiple_of(place * rows, rows), rows)


def both_rows(ref, pair, rows, cols=slice(None)):
    return jnp.concatenate([ref[block_rows(place, rows), cols] for place in pair], axis=0)


def put_rows(ref, pair, rows, cols, val):
    for n, place in enumerate(pair):
        ref[block_rows(place, rows), cols] = val[n * rows : (n + 1) * rows]


def norm_factor(v):
    return lax.rsqrt(jnp.mean(v * v, axis=-1, keepdims=True) + EPSILON)


def project_kernel(
    lens, adapters, routes, tokens, cot_in, gain, wdec, bdec, wqk_h, wvg_h, ain_h, bqk_h, bvg_h,
    index_in, index_out, select, resid, cot, normed_h, low, pq, pk, pv, pg, pab,
    gath, wqk, wvg, ain, bqk, bvg, wab, bab, wsem, osem, send, recv,
    st1, ld1, se1, re1, st2, ld2, se2, re2,
):
    rows = tokens.shape[0]
    places = ring_places()
    m = places[0]
    first = DpRows(st1, ld1, se1, re1)
    second = DpRows(st2, ld2, se2, re2)
    greet_dp(first.n, first.me)
    greet_ring(places)
    loads = Loads([(ain_h, ain), (wqk_h, wqk), (bqk_h, bqk), (wvg_h, wvg), (bvg_h, bvg)], wsem)
    loads.start()
    leaves, lands = route_indices(routes, rows)
    index_in[...] = jnp.broadcast_to(leaves, index_in.shape)
    index_out[...] = jnp.broadcast_to(lands, index_out.shape)
    first.fill(index_in, rows, lambda c: tokens[:, c])
    wait_greetings(first.n + 1)
    first.start()
    second.fill(index_in, rows, lambda c: cot_in[:, c])
    fill_select(select, lens, adapters)
    fill_gates(wqk.shape[2] // DK, wdec, bdec, wab, bab)

    def put_tokens(c, val):
        resid[:, c] = val.astype(BF16)

    first.take(index_out, rows, put_tokens)
    second.start()
    for at in range(0, rows, 32):
        v = resid[at : at + 32].astype(F32)
        gath[m, at : at + 32] = (v * norm_factor(v) * gain[...]).astype(BF16)
    ring = RingGather(gath, send, recv, places)
    ring.start()
    ac = select.shape[1]

    def compute(place):
        r = block_rows(place, rows)
        x = gath[place]
        sel = select[r]
        loads.wait(0)
        for n in range(ain.shape[1] // ac):
            low[r, n * ac : (n + 1) * ac] = (mm(x, ain[:, n * ac : (n + 1) * ac]) * sel).astype(BF16)
        loads.wait(1, 2)
        for n, dst in enumerate((pq, pk)):
            lo = low[r, n * ac : (n + 1) * ac]
            dst[r] = (mm(x, wqk[n]) + mm(lo, bqk[n])).astype(BF16)
        loads.wait(3, 4)
        for n, dst in enumerate((pv, pg)):
            lo = low[r, (n + 2) * ac : (n + 3) * ac]
            for at, size in tiles(wvg.shape[2]):
                c = slice(at, at + size)
                dst[r, c] = (mm(x, wvg[n, :, c]) + mm(lo, bvg[n, :, c])).astype(BF16)
        pab[r] = (
            mm_nt(x, wab[...]) + mm(low[r, 4 * ac : 5 * ac], bab[0]) + mm(low[r, 5 * ac : 6 * ac], bab[1])
        )

    compute(m)
    ring.forward()
    ring.wait_left()
    compute(places[1])
    ring.wait_right()
    compute(places[2])

    def put_cot(c, val):
        cot[:, c] = val.astype(BF16)

    second.take(index_out, rows, put_cot)
    ring.wait_opp()
    out = pltpu.make_async_copy(gath, normed_h, osem)
    out.start()
    compute(places[3])
    ring.finish()
    first.finish()
    second.finish()
    out.wait()


def specs(n_vmem, n_any):
    return [pl.BlockSpec(memory_space=pltpu.VMEM)] * n_vmem + [pl.BlockSpec(memory_space=pl.ANY)] * n_any


def sds(shape, dtype=BF16):
    return jax.ShapeDtypeStruct(shape, dtype)


def ring_params(collective_id):
    return pltpu.CompilerParams(
        collective_id=collective_id, has_side_effects=True, vmem_limit_bytes=WIDE_VMEM
    )


def like(a):
    return pltpu.VMEM(a.shape, a.dtype)


def project(lens, adapters, routes, tokens, cot, gain, wdec, bdec, wqk, wvg, ain, bqk, bvg):
    rows, width = tokens.shape
    n_dp = lax.axis_size("dp")
    group = rows * RING
    kw, vw = wqk.shape[2], wvg.shape[2]
    ac = bqk.shape[1]
    vm, hb = specs(1, 1)
    sm = pl.BlockSpec(memory_space=pltpu.SMEM)
    pw = width * SHARE // 16
    return pl.pallas_call(
        project_kernel,
        out_shape=(
            sds((8, n_dp * 16), F32),
            sds((8, n_dp * 16), F32),
            sds((group, ac), F32),
            sds((rows, width)),
            sds((rows, width)),
            sds((RING, rows, width)),
            sds((group, ain.shape[1])),
            sds((group, kw)),
            sds((group, kw)),
            sds((group, vw)),
            sds((group, vw)),
            sds((group, CH), F32),
        ),
        in_specs=[sm] * 2 + [vm] * 6 + [hb] * 5,
        out_specs=[vm] * 5 + [hb] + [vm] * 6,
        scratch_shapes=[
            pltpu.VMEM((RING, rows, width), BF16),
            like(wqk), like(wvg), like(ain), like(bqk), like(bvg),
            pltpu.VMEM((CH, width), BF16), pltpu.VMEM((2, ac, CH), BF16),
            DMA_SEMS((5,)), DMA_SEMS(()), DMA_SEMS((6,)), DMA_SEMS((6,)),
            *rows_scratch(n_dp, pw), *rows_scratch(n_dp, pw),
        ],
        compiler_params=ring_params(1),
        cost_estimate=pl.CostEstimate(flops=8 * 10**9, bytes_accessed=30 * 2**20, transcendentals=0),
        name="gather_project",
    )(lens, adapters, routes, tokens, cot, gain, wdec, bdec, wqk, wvg, ain, bqk, bvg)


def feed_kernel(
    mixed, resid, gain, select, wout_h, aout_h, bout_h, affn_h, gu_h, bgu_h, down_h, adown_h,
    middle, rank_out, normed_h, rank2, gate, up, hidden, dpart, rpart,
    gath, wout, aout, bout, affn, gu, bgu, down, adown, sbuf, rbuf, acc, wsem, osem, send, recv, send2, recv2,
):
    rows, width = resid.shape
    places = ring_places()
    m = places[0]
    loads = Loads(
        [
            (wout_h, wout), (aout_h, aout), (bout_h, bout), (affn_h, affn),
            (gu_h, gu), (bgu_h, bgu), (down_h, down), (adown_h, adown),
        ],
        wsem,
    )
    loads.start(0, 1)
    ac = select.shape[1]
    ff = gu.shape[2]
    greet_ring(places)
    loads.wait(0, 1)
    scatter = RingScatter(sbuf, rbuf, acc, send, recv, places)

    def part(pair, put):
        x = both_rows(mixed, pair, rows)
        for at, size in tiles(width):
            put(slice(at, at + size), mm(x, wout[:, at : at + size]))
        put(slice(width, width + ac), mm(x, aout[...]))

    def ready():
        loads.start(2, 3, 4, 5, 6, 7)
        wait_greetings(2)

    scatter.run(part, None, ready)
    loads.wait(2)
    sel_own = select[block_rows(m, rows)]
    half = rows // 2
    for lo in (0, half):
        bounds = (lo, lo + half)
        gath[m, lo : lo + half, width : width + ac] = (
            scatter.total(bounds, slice(width, width + ac)) * sel_own[lo : lo + half]
        ).astype(BF16)
    ro = gath[m, :, width : width + ac]
    for at, size in tiles(width):
        c = slice(at, at + size)
        extra = mm(ro, bout[:, c])
        for lo in (0, half):
            middle[lo : lo + half, c] = (
                resid[lo : lo + half, c].astype(F32) + scatter.total((lo, lo + half), c) + extra[lo : lo + half]
            )
    for at in range(0, rows, 32):
        v = middle[at : at + 32]
        gath[m, at : at + 32, 0:width] = (v * norm_factor(v) * gain[...]).astype(BF16)
    ring = RingGather(gath, send2, recv2, places)
    ring.start()

    def compute(place):
        r = block_rows(place, rows)
        x = gath[place, :, 0:width]
        rank_out[r] = gath[place, :, width : width + ac]
        sel = select[r]
        loads.wait(3)
        for n in range(2):
            rank2[r, n * ac : (n + 1) * ac] = (mm(x, affn[:, n * ac : (n + 1) * ac]) * sel).astype(BF16)
        loads.wait(4, 5)
        r0 = rank2[r, 0:ac]
        r1 = rank2[r, ac : 2 * ac]
        for at, size in tiles(ff):
            c = slice(at, at + size)
            g = mm(x, gu[0, :, c]) + mm(r0, bgu[0, :, c])
            u = mm(x, gu[1, :, c]) + mm(r1, bgu[1, :, c])
            gate[r, c] = g.astype(BF16)
            up[r, c] = u.astype(BF16)
            hidden[r, c] = (g * sigmoid(g) * u).astype(BF16)
        loads.wait(6, 7)
        h = hidden[r]
        for at, size in tiles(width):
            c = slice(at, at + size)
            dpart[r, c] = mm(h, down[:, c]).astype(BF16)
        rpart[r] = mm(h, adown[...]).astype(BF16)

    compute(m)
    ring.forward()
    ring.wait_left()
    compute(places[1])
    ring.wait_right()
    compute(places[2])
    ring.wait_opp()
    out = pltpu.make_async_copy(gath.at[:, :, pl.ds(0, width)], normed_h, osem)
    out.start()
    compute(places[3])
    scatter.finish()
    ring.finish()
    out.wait()


def feed(mixed, resid, gain, select, wout, aout, bout, affn, gu, bgu, down, adown):
    rows, width = resid.shape
    group = rows * RING
    ff = gu.shape[2]
    ac = select.shape[1]
    cols = width + ac
    vm, hb = specs(1, 1)
    return pl.pallas_call(
        feed_kernel,
        out_shape=(
            sds((rows, width), F32),
            sds((group, ac)),
            sds((RING, rows, width)),
            sds((group, 2 * ac)),
            sds((group, ff)),
            sds((group, ff)),
            sds((group, ff)),
            sds((group, width)),
            sds((group, ac)),
        ),
        in_specs=[vm] * 4 + [hb] * 8,
        out_specs=[vm, vm, hb] + [vm] * 6,
        scratch_shapes=[
            pltpu.VMEM((RING, rows, cols), BF16),
            like(wout), like(aout), like(bout), like(affn), like(gu), like(bgu), like(down), like(adown),
            pltpu.VMEM((6, rows // 2, cols), BF16),
            pltpu.VMEM((6, rows // 2, cols), BF16),
            pltpu.VMEM((3, rows, cols), F32),
            DMA_SEMS((8,)), DMA_SEMS(()),
            DMA_SEMS((6,)), DMA_SEMS((6,)), DMA_SEMS((6,)), DMA_SEMS((6,)),
        ],
        compiler_params=ring_params(2),
        cost_estimate=pl.CostEstimate(flops=13 * 10**9, bytes_accessed=40 * 2**20, transcendentals=0),
        name="feed_forward",
    )(mixed, resid, gain, select, wout, aout, bout, affn, gu, bgu, down, adown)


def feed_back_kernel(
    cot, rpart, select, gain,
    bdown_h, down_h, adown_h, gu_h, bgu_h, affn_h, bout_h, wout_h, aout_h, rank2_h, hidden_h, mixed_h, rank_out_h,
    gate_h, up_h, middle_h,
    g_rank2, g_middle_h, g_mixed, rank_down, stage,
    g_middle, ssem, gath, bdown, down, adown, gu, bgu, affn, bout, wout, aout, rank2, hidden, mixed, rank_out, gate, up, middle,
    g_rank_down, g_gate, g_up, g_rank_out, flat, pick, chosen,
    sbuf, rbuf, acc, wsem, send, recv, send2, recv2,
):
    rows, width = middle.shape
    saves = Saves(ssem)
    places = ring_places()
    m = places[0]
    loads = Loads(
        [
            (bdown_h, bdown), (down_h, down), (adown_h, adown), (gu_h, gu), (bgu_h, bgu),
            (affn_h, affn), (bout_h, bout), (wout_h, wout), (aout_h, aout),
            (rank2_h, rank2), (hidden_h, hidden), (mixed_h, mixed), (rank_out_h, rank_out),
            (gate_h, gate), (up_h, up), (middle_h, middle),
        ],
        wsem,
    )
    loads.start(0, 1, 2, 13, 14, 3, 4, 5, 15)
    ac = select.shape[1]
    ff = gu.shape[2]
    greet_ring(places)
    scatter = RingScatter(sbuf, rbuf, acc, send, recv, places)

    def part(pair, put):
        x = both_rows(cot, pair, rows)
        sel = both_rows(select, pair, rows)
        loads.wait(0)
        grd = (mm_nt(x, bdown[...]) * sel).astype(BF16)
        put_rows(g_rank_down, pair, rows, slice(None), grd)
        loads.wait(1, 2, 13, 14)
        for at, size in tiles(ff, 256):
            c = slice(at, at + size)
            gh = mm_nt(x, down[c]) + mm_nt(grd, adown[c])
            g = both_rows(gate, pair, rows, c).astype(F32)
            u = both_rows(up, pair, rows, c).astype(F32)
            sg = sigmoid(g)
            put_rows(g_gate, pair, rows, c, (gh * u * (sg * (1.0 + g * (1.0 - sg)))).astype(BF16))
            put_rows(g_up, pair, rows, c, (gh * g * sg).astype(BF16))
        loads.wait(3, 4, 5)
        gg = both_rows(g_gate, pair, rows)
        gu_ = both_rows(g_up, pair, rows)
        r2a = (mm_nt(gg, bgu[0]) * sel).astype(BF16)
        r2b = (mm_nt(gu_, bgu[1]) * sel).astype(BF16)
        put_rows(g_rank2, pair, rows, slice(0, ac), r2a)
        put_rows(g_rank2, pair, rows, slice(ac, 2 * ac), r2b)
        r2 = jnp.concatenate([r2a, r2b], axis=1)
        for at, size in tiles(width, 256):
            c = slice(at, at + size)
            put(c, mm_nt(gg, gu[0, c]) + mm_nt(gu_, gu[1, c]) + mm_nt(r2, affn[c]))
        put(slice(width, width + ac), both_rows(rpart, pair, rows).astype(F32))

    n_dp = stage.shape[0]
    parts = 16 // SHARE
    deal = unfold(n_dp * 16, 16)

    def grads():
        loads.wait(9, 10)
        for at, size in tiles(ff):
            c = slice(at, at + size)
            flat[:, at : at + size] = mm_tn(rank2[:, 0:ac], g_gate[:, c]).astype(BF16)
            flat[:, ff + at : ff + at + size] = mm_tn(rank2[:, ac : 2 * ac], g_up[:, c]).astype(BF16)
            flat[:, 2 * ff + at : 2 * ff + at + size] = mm_tn(g_rank_down[...], hidden[:, c]).astype(BF16)
        flat[:, 3 * ff :] = jnp.zeros((ac, flat.shape[1] - 3 * ff), BF16)
        w = flat.shape[1] // parts
        keep_chunks(stage, deal, [flat[:, p * w : (p + 1) * w] for p in range(parts)], 0)

    def ready():
        loads.start(*range(6, 13))
        wait_greetings(2)

    scatter.run(part, grads, ready)
    sel_own = select[block_rows(m, rows)]
    loads.wait(15)
    step = 16
    for at in range(0, rows, step):
        b = (at, at + step)
        g = scatter.total(b, slice(0, width)) * gain[...]
        v = middle[at : at + step]
        n = norm_factor(v)
        v = v * n
        gm = cot[pl.ds(pl.multiple_of(m * rows + at, step), step)].astype(F32) + n * (
            g - v * jnp.mean(g * v, axis=-1, keepdims=True)
        )
        g_middle[at : at + step] = gm
        gath[m, at : at + step, 0:width] = gm.astype(BF16)
        gath[m, at : at + step, width : width + ac] = (
            scatter.total(b, slice(width, width + ac)) * sel_own[at : at + step]
        ).astype(BF16)
    ring = RingGather(gath, send2, recv2, places)
    ring.start()
    saves.start(g_middle, g_middle_h)
    per = width // (n_dp * RING)
    for at in range(0, width, 256):
        line = iota2((256, pick.shape[1]), 0) + at
        slot = iota2((256, pick.shape[1]), 1)
        want = (((slot % ac) // SHARE) * RING + m) * per + (slot // ac) * SHARE + slot % SHARE
        pick[at : at + 256] = (line == want).astype(F32).astype(BF16)
    cot_chosen = mm(cot[...], pick[...]).astype(BF16)

    def compute(*pair):
        x = jnp.concatenate([gath[place, :, 0:width] for place in pair], axis=0)
        loads.wait(6, 7, 8)
        gro = (mm_nt(x, bout[...]) * both_rows(select, pair, rows)).astype(BF16)
        put_rows(g_rank_out, pair, rows, slice(None), gro)
        for at, size in tiles(wout.shape[0], 256):
            c = slice(at, at + size)
            put_rows(g_mixed, pair, rows, c, (mm_nt(x, wout[c]) + mm_nt(gro, aout[c])).astype(BF16))
        put_rows(chosen, pair, rows, slice(None), mm(x, pick[...]).astype(BF16))
        for place in pair:
            rank_down[block_rows(place, rows)] = gath[place, :, width : width + ac]

    compute(m)
    ring.forward()
    ring.wait_left()
    ring.wait_right()
    compute(places[1], places[2])
    ring.wait_opp()
    compute(places[3])
    loads.wait(11, 12)
    at = flat.shape[1] // parts
    w = mixed.shape[1] // parts
    gro = g_rank_out[...]
    at = keep_chunks(stage, deal, [mm_tn(gro, mixed[:, p * w : (p + 1) * w]) for p in range(parts)], at)
    for rows_of, ranks in ((cot_chosen, rank_down), (chosen[...], rank_out)):
        at = keep_chunks(
            stage, deal, [mm_tn(rows_of[:, b * ac : (b + 1) * ac], ranks[...]) for b in range(rows_of.shape[1] // ac)], at
        )
    scatter.finish()
    ring.finish()
    saves.finish()


def early_widths(ff, vw, ac):
    parts = 16 // SHARE
    return [-(-3 * ff // (parts * CH)) * CH, vw // parts, ac, ac]


def feed_back(
    cot, rpart, select, gain,
    bdown, down, adown, gu, bgu, affn, bout, wout, aout, rank2, hidden, mixed, rank_out, gate, up, middle,
):
    rows, width = middle.shape
    group = rows * RING
    ff = gu.shape[2]
    ac = select.shape[1]
    n_dp = lax.axis_size("dp")
    parts = 16 // SHARE
    vw = wout.shape[0]
    widths = early_widths(ff, vw, ac)
    vm, hb = specs(1, 1)
    loaded = (bdown, down, adown, gu, bgu, affn, bout, wout, aout, rank2, hidden, mixed, rank_out, gate, up, middle)
    return pl.pallas_call(
        feed_back_kernel,
        out_shape=(
            sds((group, 2 * ac)),
            sds((rows, width), F32),
            sds((group, vw)),
            sds((group, ac)),
            sds((n_dp, 16, sum(widths))),
        ),
        in_specs=[vm] * 4 + [hb] * len(loaded),
        out_specs=[vm, hb, vm, vm, vm],
        scratch_shapes=[
            pltpu.VMEM((rows, width), F32),
            DMA_SEMS((1,)),
            pltpu.VMEM((RING, rows, width + ac), BF16),
            *[like(a) for a in loaded],
            pltpu.VMEM((group, ac), BF16),
            pltpu.VMEM((group, ff), BF16),
            pltpu.VMEM((group, ff), BF16),
            pltpu.VMEM((group, ac), BF16),
            pltpu.VMEM((ac, parts * widths[0]), BF16),
            pltpu.VMEM((width, width // RING), BF16),
            pltpu.VMEM((group, width // RING), BF16),
            pltpu.VMEM((6, rows // 2, width + ac), BF16),
            pltpu.VMEM((6, rows // 2, width + ac), BF16),
            pltpu.VMEM((3, rows, width + ac), F32),
            DMA_SEMS((len(loaded),)),
            DMA_SEMS((6,)), DMA_SEMS((6,)), DMA_SEMS((6,)), DMA_SEMS((6,)),
        ],
        compiler_params=ring_params(3),
        cost_estimate=pl.CostEstimate(flops=13 * 10**9, bytes_accessed=40 * 2**20, transcendentals=0),
        name="feed_backward",
    )(cot, rpart, select, gain, *loaded)


def fold_maps(count, base, ac):
    line = iota2((count, ac), 0)
    col = iota2((count, ac), 1)
    hit = (line // ac) * ADAPTER_RANK + line % ADAPTER_RANK + base == col
    return hit.astype(F32).astype(BF16)


def project_back_kernel(
    widths, index_in, index_out, dq, dk, dv, dg, dab, select, gain, wdec, bdec, g_rank2, rank_down,
    wqk_h, wvg_h, ain_h, bqk_h, bvg_h, bdown_h, low_h, normed_h, normed2_h,
    resid_h, g_middle_h, early_h, middle_h, down_sum_h,
    g_tokens, stage, out_rows, o_gu, o_down_in, o_out_in, o_down, o_out, o_qk, o_vg, o_ab,
    wqk, wvg, ain, bqk, bvg, bdown, low, normed, normed2, resid, g_middle, early, middle, down_sum,
    wab, bab, stage_a, g_rank, sbuf, rbuf, acc, small, wsem, send, recv, send2, recv2, *more
):
    rows, width = resid.shape
    places = ring_places()
    m = places[0]
    loads = Loads(
        [
            (bdown_h, bdown), (bqk_h, bqk), (bvg_h, bvg), (ain_h, ain), (wqk_h, wqk), (wvg_h, wvg),
            (low_h, low), (normed_h, normed), (normed2_h, normed2),
            (resid_h, resid), (g_middle_h, g_middle), (early_h, early), (middle_h, middle), (down_sum_h, down_sum),
        ],
        wsem,
    )
    loads.start(1, 2)
    loads.start(3, 4, 5, 0, 12, 13, 11)
    block = DpRows(*more[:4])
    reduce = DpSums(early, *more[4:11])
    reduce_a = DpSums(stage_a, *more[11:])
    greet_dp(block.n, block.me)
    greet_ring(places)
    ac = select.shape[1]
    n_dp = stage.shape[0]
    heads = dq.shape[1] // DK
    fill_gates(heads, wdec, bdec, wab, bab)
    scatter = RingScatter(sbuf, rbuf, acc, send, recv, places)
    six = ain.shape[1] // ac
    fold_in = fold_maps(six * ac, 0, ac)
    fold_two = fold_maps(2 * ac, six * ADAPTER_RANK, ac)

    def part(pair, put):
        sel = both_rows(select, pair, rows)
        xs = [both_rows(d, pair, rows) for d in (dq, dk, dv, dg, dab)]
        loads.wait(1, 2)
        seconds = [bqk[0], bqk[1], bvg[0], bvg[1], bab[0], bab[1]]
        for n in range(six):
            g_rank[:, n * ac : (n + 1) * ac] = (mm_nt(xs[min(n, 4)], seconds[n]) * sel).astype(BF16)
        gr = g_rank[...]
        put(slice(width, width + ac), mm(gr, fold_in) + mm(both_rows(g_rank2, pair, rows), fold_two))
        loads.wait(3, 4, 5)
        for at, size in tiles(width, 256):
            c = slice(at, at + size)
            put(
                c,
                mm_nt(xs[0], wqk[0, c])
                + mm_nt(xs[1], wqk[1, c])
                + mm_nt(xs[2], wvg[0, c])
                + mm_nt(xs[3], wvg[1, c])
                + mm(xs[4], wab[:, c])
                + mm_nt(gr, ain[c]),
            )

    deal = unfold(n_dp * 16, 16)
    parts = 16 // SHARE

    def keep(pieces, at):
        return keep_chunks(stage_a, deal, pieces, at)

    def ready():
        loads.wait(0, 12, 13)
        own = rank_down[block_rows(m, rows)]

        def value(c):
            return (middle[:, c] + down_sum[:, c].astype(F32) + mm(own, bdown[:, c])).astype(BF16)

        block.fill(index_in, rows, value)
        loads.start(6, 9, 10, 7, 8)
        wait_greetings(block.n + 1)
        loads.wait(11)
        reduce.start()

    def late():
        block.start()
        reduce.forward()
        loads.wait(6)
        at = 0
        for n, d in enumerate((dq, dk, dv, dg)):
            w = d.shape[1] // parts
            lo = low[:, n * ac : (n + 1) * ac]
            at = keep([mm_tn(lo, d[:, p * w : (p + 1) * w]) for p in range(parts)], at)
        lane = iota2((1, CH), 1)
        ga = mm_tn(low[:, 4 * ac : 5 * ac], dab[...])
        gb = mm_tn(low[:, 5 * ac : 6 * ac], dab[...])
        keep([jnp.where(lane < heads, ga, gb)], at)
        reduce_a.start()

    scatter.run(part, late, ready)
    loads.wait(9, 10)
    half = rows // 2
    for lo in (0, half):
        small[m, lo : lo + half] = scatter.total((lo, lo + half), slice(width, width + ac)).astype(BF16)
    ring = RingGather(small, send2, recv2, places)
    ring.start()
    reduce_a.forward()
    step = 16

    def back(at):
        g = scatter.total((at, at + step), slice(0, width)) * gain[...]
        v = resid[at : at + step].astype(F32)
        n = norm_factor(v)
        v = v * n
        g_tokens[at : at + step] = (
            g_middle[at : at + step] + n * (g - v * jnp.mean(g * v, axis=-1, keepdims=True))
        ).astype(BF16)

    for at in range(0, half, step):
        back(at)
    ring.forward()
    for at in range(half, rows, step):
        back(at)
    line = iota2((ac, 2 * ac), 0)
    slot = iota2((ac, 2 * ac), 1)
    inner = (slot // ac) * SHARE + slot % SHARE
    owner = ((slot % ac) // SHARE) * RING + m
    first = inner < six
    column = jnp.where(first, owner * six + inner, owner * 2 + inner - six)
    place_of = (column // ac) * ADAPTER_RANK + column % ADAPTER_RANK + jnp.where(first, 0, six * ADAPTER_RANK)
    adapter_of = (column % ac) // ADAPTER_RANK
    chosen = (line == place_of).astype(F32).astype(BF16)
    same = (line == adapter_of * ADAPTER_RANK).astype(F32).astype(BF16)

    def put_rows_out(c, val):
        out_rows[:, c] = val.astype(BF16)

    block.take(index_out, rows, put_rows_out)
    ff = o_gu.shape[2]

    def sink_early(k, cols, val):
        lo, hi = cols
        if k:
            (o_out_in, o_down, o_out)[k - 1][:, lo:hi] = val
            return
        for n in range(3):
            a, b = max(lo, n * ff), min(hi, (n + 1) * ff)
            if a < b:
                piece = val[:, a - lo : b - lo]
                if n < 2:
                    o_gu[n, :, a - n * ff : b - n * ff] = piece
                else:
                    o_down_in[:, a - n * ff : b - n * ff] = piece

    reduce.take(widths, sink_early)
    loads.wait(7, 8)
    ring.wait_left()
    ring.wait_right()
    ring.wait_opp()
    rank_sums = jnp.concatenate([small[n] for n in range(RING)], axis=0)
    picked = (mm(rank_sums, chosen) * mm(select[...], same)).astype(BF16)
    w = width // parts
    at = 0
    lane = iota2((1, ac), 1)
    upper = picked[:, 0:ac]
    lower = picked[:, ac : 2 * ac].astype(F32)
    lower_in = jnp.where(lane % SHARE < six - SHARE, lower, 0.0).astype(BF16)
    lower_two = jnp.where(lane % SHARE < six - SHARE, 0.0, lower).astype(BF16)
    at = keep_chunks(stage, deal, [mm_tn(upper, normed[:, p * w : (p + 1) * w]) for p in range(parts)], at)
    keep_chunks(
        stage,
        deal,
        [
            mm_tn(lower_in, normed[:, p * w : (p + 1) * w]) + mm_tn(lower_two, normed2[:, p * w : (p + 1) * w])
            for p in range(parts)
        ],
        at,
    )

    def sink_late(k, cols, val):
        lo, hi = cols
        if k < 2:
            o_qk[k, :, lo:hi] = val
        elif k < 4:
            o_vg[k - 2, :, lo:hi] = val
        elif lo == 0:
            o_ab[...] = val

    reduce_a.take(late_widths(dq.shape[1], dv.shape[1]), sink_late)
    scatter.finish()
    ring.finish()
    block.finish()
    reduce.finish()
    reduce_a.finish()


def late_widths(kw, vw):
    parts = 16 // SHARE
    return [kw // parts, kw // parts, vw // parts, vw // parts, CH]


def project_back(
    widths, index_in, index_out, dq, dk, dv, dg, dab, select, gain, wdec, bdec, g_rank2, rank_down,
    wqk, wvg, ain, bqk, bvg, bdown, low, normed, normed2, resid, g_middle, early, middle, down_sum, ff,
):
    rows, width = resid.shape
    ac = select.shape[1]
    n_dp = lax.axis_size("dp")
    parts = 16 // SHARE
    vm, hb = specs(1, 1)
    cols = width + ac
    kw, vw = dq.shape[1], dv.shape[1]
    late = late_widths(kw, vw)
    loaded = (wqk, wvg, ain, bqk, bvg, bdown, low, normed, normed2, resid, g_middle, early, middle, down_sum)
    return pl.pallas_call(
        functools.partial(project_back_kernel, widths),
        out_shape=(
            sds((rows, width)),
            sds((n_dp, 16, 2 * width // parts)),
            sds((rows, width)),
            sds((2, SHARE, ff), F32),
            sds((SHARE, ff), F32),
            sds((SHARE, vw), F32),
            sds((SHARE, parts * ac), F32),
            sds((SHARE, parts * ac), F32),
            sds((2, SHARE, kw), F32),
            sds((2, SHARE, vw), F32),
            sds((SHARE, CH), F32),
        ),
        in_specs=[vm] * 13 + [hb] * len(loaded),
        out_specs=[vm] * 11,
        scratch_shapes=[
            *[like(a) for a in loaded],
            pltpu.VMEM((CH, width), BF16),
            pltpu.VMEM((2, ac, CH), BF16),
            pltpu.VMEM((n_dp, 16, sum(late)), BF16),
            pltpu.VMEM((2 * rows, ain.shape[1]), BF16),
            pltpu.VMEM((6, rows // 2, cols), BF16),
            pltpu.VMEM((6, rows // 2, cols), BF16),
            pltpu.VMEM((3, rows, cols), F32),
            pltpu.VMEM((RING, rows, ac), BF16),
            DMA_SEMS((len(loaded),)), DMA_SEMS((6,)), DMA_SEMS((6,)), DMA_SEMS((6,)), DMA_SEMS((6,)),
            *rows_scratch(n_dp, width // parts), *sums_scratch(n_dp, sum(widths)), *sums_scratch(n_dp, sum(late)),
        ],
        compiler_params=ring_params(4),
        cost_estimate=pl.CostEstimate(flops=9 * 10**9, bytes_accessed=30 * 2**20, transcendentals=0),
        name="project_backward",
    )(
        index_in, index_out, dq, dk, dv, dg, dab, select, gain, wdec, bdec, g_rank2, rank_down,
        *loaded,
    )


def finish_kernel(widths, index_in, index_out, g_tokens, grads_h, rows_out, sums, grads, lsem, *scratch):
    arriving = pltpu.make_async_copy(grads_h, grads, lsem)
    arriving.start()
    rows, width = g_tokens.shape
    back = DpRows(*scratch[:4])
    reduce = DpSums(grads, *scratch[4:])
    greet_dp(back.n, back.me)
    back.fill(index_in, rows, lambda c: g_tokens[:, c])
    wait_greetings(back.n - 1)
    arriving.wait()
    reduce.start()
    back.start()
    reduce.forward()

    def put(c, val):
        rows_out[:, c] = val.astype(BF16)

    back.take(index_out, rows, put)

    def sink(k, cols, val):
        c = k * width + cols[0]
        sums[:, c : c + cols[1] - cols[0]] = val

    reduce.take(widths, sink)
    back.finish()
    reduce.finish()


def finish(collective_id, widths, index_in, index_out, g_tokens, grads):
    rows, width = g_tokens.shape
    n = lax.axis_size("dp")
    parts = 16 // SHARE
    total = grads.shape[2]
    vm, hb = specs(1, 1)
    return pl.pallas_call(
        functools.partial(finish_kernel, widths),
        out_shape=(sds((rows, width)), sds((SHARE, parts * total), F32)),
        in_specs=[vm] * 3 + [hb],
        out_specs=[vm] * 2,
        scratch_shapes=[like(grads), DMA_SEMS(()), *rows_scratch(n, width // parts), *sums_scratch(n, total)],
        compiler_params=ring_params(collective_id),
        cost_estimate=pl.CostEstimate(flops=10**9, bytes_accessed=20 * 2**20, transcendentals=0),
        name="finish_rows",
    )(index_in, index_out, g_tokens, grads)


def per_device(
    tokens,
    cotangent,
    token_grouped_position,
    sequence_lengths,
    adapter_index_per_seq,
    mixer_norm_gain,
    query_key_matrix,
    value_gate_matrix,
    decay_step_matrix,
    query_key_filters,
    value_filters,
    decay_scale_logarithm,
    decay_step_bias,
    head_output_norm_gain,
    output_matrix,
    feedfwd_norm_gain,
    gate_up_matrix,
    down_matrix,
    adapter_mixer_first,
    adapter_query_key_second,
    adapter_value_gate_second,
    adapter_decay_step_second,
    adapter_output_first,
    adapter_output_second,
    adapter_feedfwd_first,
    adapter_gate_up_second,
    adapter_down_first,
    adapter_down_second,
):
    rows = tokens.shape[0]
    width = tokens.shape[1]
    n_dp = lax.axis_size("dp")
    n_mp = lax.axis_size("mp")
    group = rows * n_mp
    share = rows // n_dp
    ac = adapter_output_second.shape[0]
    heads = decay_scale_logarithm.shape[0]

    routes = token_grouped_position.reshape(n_dp, n_mp, rows)
    def gather(x):
        return lax.all_gather(x, "mp", axis=0, tiled=True)

    def scatter(x):
        return lax.psum_scatter(x, "mp", scatter_dimension=0, tiled=True)

    fill = ((0, 0), (0, 16 - heads), (0, 0))
    w_dec = jnp.pad(jnp.swapaxes(decay_step_matrix, 1, 2), fill)
    b_dec = jnp.pad(jnp.swapaxes(adapter_decay_step_second, 1, 2), fill)
    gain_one, gain_two = mixer_norm_gain[None], feedfwd_norm_gain[None]
    index_tokens, index_slots, select, resid, cot, normed, low, pre_q, pre_k, pre_v, pre_g, pre_ab = project(
        sequence_lengths,
        adapter_index_per_seq,
        routes,
        tokens,
        cotangent,
        gain_one,
        w_dec,
        b_dec,
        query_key_matrix,
        value_gate_matrix,
        adapter_mixer_first,
        adapter_query_key_second,
        adapter_value_gate_second,
    )
    normed = normed.reshape(group, width)
    cot_later, pre_ab = lax.optimization_barrier((cot, pre_ab))
    cot_all = gather(cot_later)
    gates = (sequence_lengths, decay_scale_logarithm, decay_step_bias)
    shared = (query_key_filters, value_filters, head_output_norm_gain[None])
    mixed, *saved = mixer_fwd(*gates, pre_q, pre_k, pre_v, pre_g, pre_ab, *shared)
    middle, rank_out, normed2, rank2, gate, up, hidden, down_part, rank_part = feed(
        mixed,
        resid,
        gain_two,
        select,
        output_matrix,
        adapter_output_first,
        adapter_output_second,
        adapter_feedfwd_first,
        gate_up_matrix,
        adapter_gate_up_second,
        down_matrix,
        adapter_down_first,
    )
    normed2 = normed2.reshape(group, width)
    g_rank2, g_middle, g_mixed, rank_down, early_parts = feed_back(
        cot_all,
        rank_part,
        select,
        gain_two,
        adapter_down_second,
        down_matrix,
        adapter_down_first,
        gate_up_matrix,
        adapter_gate_up_second,
        adapter_feedfwd_first,
        adapter_output_second,
        output_matrix,
        adapter_output_first,
        rank2,
        hidden,
        mixed,
        rank_out,
        gate,
        up,
        middle,
    )
    down_later, g_mixed = lax.optimization_barrier((down_part, g_mixed))
    down_sum = scatter(down_later)
    dq, dk, dv, dg, dab = mixer_bwd(*gates, g_mixed, pre_g, pre_ab, *shared, saved)
    dq, down_sum = lax.optimization_barrier((dq, down_sum))
    widths = early_widths(gate.shape[1], dv.shape[1], ac)
    g_tokens, late_parts, out_rows, grad_gu, down_in, out_in, side_down, side_branch, grad_qk, grad_vg, gates_ab = project_back(
        widths,
        index_slots,
        index_tokens,
        dq,
        dk,
        dv,
        dg,
        dab,
        select,
        gain_one,
        w_dec,
        b_dec,
        g_rank2,
        rank_down,
        query_key_matrix,
        value_gate_matrix,
        adapter_mixer_first,
        adapter_query_key_second,
        adapter_value_gate_second,
        adapter_down_second,
        low,
        normed,
        normed2,
        resid,
        g_middle,
        early_parts,
        middle,
        down_sum,
        gate.shape[1],
    )
    parts = 16 // share
    grad_rows, late = finish(6, [width // parts] * 2, index_slots, index_tokens, g_tokens, late_parts)
    per_in = 6 * ac // (n_dp * n_mp)
    per_ffn = 2 * ac // (n_dp * n_mp)
    both = jnp.concatenate([late[:, :width], late[:, width:]], axis=0).T

    def side_out(x):
        return jnp.swapaxes(x.reshape(share, -1, ac), 0, 1).reshape(-1, ac).T

    return (
        out_rows,
        grad_rows,
        both[:, :per_in],
        grad_qk,
        grad_vg,
        jnp.stack([gates_ab[:, :heads], gates_ab[:, heads : 2 * heads]]),
        out_in.T,
        side_out(side_branch),
        both[:, per_in : per_in + per_ffn],
        grad_gu,
        down_in.T,
        side_out(side_down),
    )


def solution(mesh):
    return jax.shard_map(
        per_device,
        mesh=mesh,
        in_specs=(
            P(("dp", "mp"), None),
            P(("dp", "mp"), None),
            P(),
            P("dp", None),
            P("dp", None),
            P(),
            P(None, None, "mp"),
            P(None, None, "mp"),
            P(None, None, "mp"),
            P(None, None, "mp"),
            P(None, "mp"),
            P("mp"),
            P("mp"),
            P(),
            P("mp", None),
            P(),
            P(None, None, "mp"),
            P("mp", None),
            P(),
            P(None, None, "mp"),
            P(None, None, "mp"),
            P(None, None, "mp"),
            P("mp", None),
            P(),
            P(),
            P(None, None, "mp"),
            P("mp", None),
            P(),
        ),
        out_specs=(
            P(("dp", "mp"), None),
            P(("dp", "mp"), None),
            P(None, ("dp", "mp")),
            P(None, "dp", "mp"),
            P(None, "dp", "mp"),
            P(None, "dp", "mp"),
            P("mp", "dp"),
            P(None, ("dp", "mp")),
            P(None, ("dp", "mp")),
            P(None, "dp", "mp"),
            P("mp", "dp"),
            P(None, ("dp", "mp")),
        ),
        check_vma=False,
    )
```

```python
import functools
import jax
import jax.numpy as jnp
from jax import lax
from jax.experimental import pallas as pl
from jax.experimental.pallas import tpu as pltpu
from jax.sharding import PartitionSpec as P

EPSILON = 1e-06
F32 = jnp.float32
BF16 = jnp.bfloat16
CH = 128
BASE = 16
DK = 128
DVAL = 256
INV_ROOT = DK ** -0.5


def mm(a, b):
    return jnp.dot(a.astype(BF16), b.astype(BF16), preferred_element_type=F32)


def mm_nt(a, b):
    return lax.dot_general(a.astype(BF16), b.astype(BF16), (((1,), (1,)), ((), ())), preferred_element_type=F32)


def mm_tn(a, b):
    return lax.dot_general(a.astype(BF16), b.astype(BF16), (((0,), (0,)), ((), ())), preferred_element_type=F32)


def exact_tn(a, b):
    b1 = b.astype(BF16)
    r1 = b - b1.astype(F32)
    b2 = r1.astype(BF16)
    b3 = (r1 - b2.astype(F32)).astype(BF16)
    return mm_tn(a, b1) + mm_tn(a, b2) + mm_tn(a, b3)


def iota2(shape, dim):
    return lax.broadcasted_iota(jnp.int32, shape, dim)


def sigmoid(x):
    return 1.0 / (1.0 + jnp.exp(-x))


def conv_rows(x, taps, masks_ref, length):
    total = x * taps[0:1]
    for shift in range(1, 4):
        total = total + pltpu.roll(x, shift, 0) * masks_ref[shift - 1] * taps[shift : shift + 1]
    return total


def conv_rows_back(d, taps, masks_ref, length):
    total = d * taps[0:1]
    for shift in range(1, 4):
        total = total + pltpu.roll(d * masks_ref[shift - 1], length - shift, 0) * taps[shift : shift + 1]
    return total


class Saves:
    def __init__(self, sems):
        self.sems, self.live = sems, []

    def start(self, src, dst):
        copy = pltpu.make_async_copy(src, dst, self.sems.at[len(self.live)])
        copy.start()
        self.live.append(copy)

    def finish(self):
        for copy in self.live:
            copy.wait()


def start_loads(pairs, sems):
    copies = [pltpu.make_async_copy(src, dst, sems.at[n]) for n, (src, dst) in enumerate(pairs)]
    for copy in copies:
        copy.start()
    return copies


def gate_columns(ab, dsl, bias):
    z = ab + bias
    soft = jnp.maximum(z, 0.0) + jnp.log1p(jnp.exp(-jnp.abs(z)))
    return -jnp.exp(dsl) * soft, z


def segment_at(position, lens):
    end = lens[0, 0]
    count = as_int(position >= end)
    for n in range(1, lens.shape[1] - 1):
        end = end + lens[0, n]
        count = count + as_int(position >= end)
    return count


def as_int(flag):
    return jnp.where(flag, 1, 0)


def fill_masks(masks, lens):
    shape = masks.shape[1:]
    position = iota2(shape, 0)
    seg = segment_at(position, lens)
    for shift in range(1, 4):
        same = (position >= shift) & (segment_at(position - shift, lens) == seg)
        masks[shift - 1] = same.astype(F32)


def gate_rows(dsl, bias):
    lane = iota2((1, CH), 1)
    rows = []
    for source in (dsl, bias):
        out = jnp.zeros((1, CH), F32)
        for h in range(source.shape[0]):
            out = jnp.where(lane == h, source[h], out)
        rows.append(out)
    return rows


def base_inverse(mats):
    nb = CH // BASE
    lane = iota2((1, CH), 1)
    lane_masks = [(lane // BASE == b).astype(F32) for b in range(nb)]
    packed = []
    for a in mats:
        d = a[0:BASE] * lane_masks[0]
        for b in range(1, nb):
            d = d + a[b * BASE : (b + 1) * BASE] * lane_masks[b]
        packed.append(d)
    d = jnp.concatenate(packed, axis=0)
    hi = d.astype(BF16)
    lo = (d - hi.astype(F32)).astype(BF16)
    row = iota2((CH, CH), 0)
    col = iota2((CH, CH), 1)
    same = row // BASE == col // BASE
    spread = jnp.concatenate(
        [(same & (row % BASE == j)).astype(BF16) for j in range(BASE - 1)], axis=1
    )
    wide = mm(hi, spread) + mm(lo, spread)
    sub = iota2((BASE, CH), 0)
    eye = (sub == iota2((BASE, CH), 1) % BASE).astype(F32)
    out = []
    for n in range(len(mats)):
        t = eye
        for j in range(BASE - 1):
            t = t - wide[n * BASE : (n + 1) * BASE, j * CH : (j + 1) * CH] * t[j : j + 1]
        out.append(jnp.concatenate([t * lane_masks[b] for b in range(nb)], axis=0))
    return out


def full_inverse(mats):
    ts = base_inverse(mats)
    row = iota2((CH, CH), 0)
    col = iota2((CH, CH), 1)
    size = BASE
    while size < CH:
        pick = ((row // size) % 2 == 1) & (col // size == row // size - 1)
        steps = [mm(jnp.where(pick, a, 0.0), t) for a, t in zip(mats, ts)]
        ts = [t - mm(t, s) for t, s in zip(ts, steps)]
        size *= 2
    return ts


def side_by_side(one, count):
    live = [one(n) for n in range(count)]
    while live:
        live = [g for g in live if next(g, "end") != "end"]


def mixer_fwd_kernel(
    heads, lens, dsl, bias, preq, prek, prev, ab_ref, taps_qk, taps_v, gain, preg_h,
    mixed_h, cq_h, ck_h, cv_h, t_h, s_h, u_h, o_h,
    preg, mixed, cq, ck, cv, t_out, s_out, u_out, o_out, lsem, ssem, masks, qn, kn, vn, cum_s, state,
):
    length = preq.shape[0]
    count = length // CH
    gate_load = start_loads([(preg_h, preg)], lsem)
    saves = Saves(ssem)
    taps_q, taps_k = taps_qk.at[0], taps_qk.at[1]
    fill_masks(masks, lens)
    gate_par = gate_rows(dsl, bias)

    def key_tile(h, carry):
        cols = pl.ds(pl.multiple_of(h * DK, DK), DK)
        for src, taps, save, dst, scale in ((preq, taps_q, cq, qn, INV_ROOT), (prek, taps_k, ck, kn, 1.0)):
            c = conv_rows(src[:, cols].astype(F32), taps[:, cols], masks, length)
            save[:, cols] = c.astype(BF16)
            u = c * sigmoid(c)
            n = lax.rsqrt(jnp.sum(u * u, axis=-1, keepdims=True) + EPSILON) * scale
            dst[:, cols] = (u * n).astype(BF16)
        for half in range(2):
            vcols = pl.ds(pl.multiple_of(h * DVAL + half * DK, DK), DK)
            c = conv_rows(prev[:, vcols].astype(F32), taps_v[:, vcols], masks, length)
            cv[:, vcols] = c.astype(BF16)
            vn[:, vcols] = c * sigmoid(c)
        return carry

    lax.fori_loop(0, heads, key_tile, 0)
    for src, dst in ((cq, cq_h), (ck, ck_h), (cv, cv_h)):
        saves.start(src, dst)
    gate_load[0].wait()
    row = iota2((CH, CH), 0)
    col = iota2((CH, CH), 1)
    upper = (row <= col).astype(BF16)
    log_decay, _ = gate_columns(ab_ref[...], gate_par[0], gate_par[1])
    beta_all = sigmoid(ab_ref[...])
    for n in range(count):
        cum_s[n * CH : (n + 1) * CH] = exact_tn(upper, log_decay[n * CH : (n + 1) * CH])
    cum_s[length : length + CH] = jnp.zeros((CH, DK), F32)
    for h in range(heads):
        state[h] = jnp.zeros((DK, DVAL), F32)

    for n in range(count):
        r = pl.ds(n * CH, CH)
        seg_col = segment_at(row + n * CH, lens)
        seg_row = segment_at(col + n * CH, lens)
        keep = (seg_col == seg_row) & (row >= col)
        keepf = keep.astype(F32)
        strict = (row > col).astype(F32)
        cum = cum_s[r]
        cum_t = cum.T
        beta_c = beta_all[n * CH : (n + 1) * CH]
        prev_last = segment_at(n * CH - 1, lens) if n else -1
        start = jnp.exp(cum) * (seg_col == prev_last).astype(F32)
        last_seg = segment_at((n + 1) * CH - 1, lens)
        tail = jnp.exp(cum[CH - 1 : CH] - cum) * (seg_col == last_seg).astype(F32)
        mats, scores = [], []
        for h in range(heads):
            q = qn[r, h * DK : (h + 1) * DK]
            k = kn[r, h * DK : (h + 1) * DK]
            ratio = jnp.exp(jnp.minimum(cum[:, h : h + 1] - cum_t[h : h + 1], 0.0)) * keepf
            beta = beta_c[:, heads + h : heads + h + 1]
            both = mm_nt(jnp.concatenate([q, k], axis=0), k)
            scores.append((ratio * both[:CH]).astype(BF16))
            mats.append(beta * ratio * strict * both[CH:])
        ts = full_inverse(mats)
        def one_head(h):
            q = qn[r, h * DK : (h + 1) * DK]
            k = kn[r, h * DK : (h + 1) * DK]
            vcols = slice(h * DVAL, (h + 1) * DVAL)
            beta = beta_c[:, heads + h : heads + h + 1]
            st = start[:, h : h + 1]
            tb = ts[h].astype(BF16)
            s0 = state[h]
            s0b = s0.astype(BF16)
            t_out[n, h] = tb
            s_out[n, h] = s0b
            yield
            both = mm(jnp.concatenate([q, k], axis=0), s0b)
            res = beta * (vn[r, vcols] - st * both[CH:])
            yield
            un = mm(tb, res).astype(BF16)
            u_out[r, vcols] = un
            yield
            o = st * both[:CH] + mm(scores[h], un)
            state[h] = start[CH - 1 : CH, h : h + 1] * s0 + mm_tn(k.astype(F32) * tail[:, h : h + 1], un)
            yield
            o_out[r, vcols] = o.astype(BF16)
            g = preg[r, vcols].astype(F32)
            rn = lax.rsqrt(jnp.mean(o * o, axis=-1, keepdims=True) + EPSILON)
            mixed[r, vcols] = (o * rn * gain[...] * (g * sigmoid(g))).astype(BF16)

        side_by_side(one_head, heads)
        saves.start(t_out.at[n], t_h.at[n])
        saves.start(s_out.at[n], s_h.at[n])
        for src, dst in ((u_out, u_h), (o_out, o_h), (mixed, mixed_h)):
            saves.start(src.at[r], dst.at[r])
    saves.finish()


def mixer_fwd(lens, dsl, bias, preq, prek, prev, preg, ab, taps_qk, taps_v, gain):
    length = preq.shape[0]
    heads = preq.shape[1] // DK
    count = length // CH
    vm = pl.BlockSpec(memory_space=pltpu.VMEM)
    sm = pl.BlockSpec(memory_space=pltpu.SMEM)
    hb = pl.BlockSpec(memory_space=pl.ANY)
    out_shape = (
        jax.ShapeDtypeStruct((length, heads * DVAL), BF16),
        jax.ShapeDtypeStruct((length, heads * DK), BF16),
        jax.ShapeDtypeStruct((length, heads * DK), BF16),
        jax.ShapeDtypeStruct((length, heads * DVAL), BF16),
        jax.ShapeDtypeStruct((count, heads, CH, CH), BF16),
        jax.ShapeDtypeStruct((count, heads, DK, DVAL), BF16),
        jax.ShapeDtypeStruct((length, heads * DVAL), BF16),
        jax.ShapeDtypeStruct((length, heads * DVAL), BF16),
    )
    return pl.pallas_call(
        functools.partial(mixer_fwd_kernel, heads),
        out_shape=out_shape,
        in_specs=[sm] * 3 + [vm] * 7 + [hb],
        out_specs=[hb] * len(out_shape),
        scratch_shapes=[
            pltpu.VMEM(preg.shape, BF16),
            *[pltpu.VMEM(o.shape, o.dtype) for o in out_shape],
            pltpu.SemaphoreType.DMA((1,)),
            pltpu.SemaphoreType.DMA((3 + 5 * count,)),
            pltpu.VMEM((3, length, CH), F32),
            pltpu.VMEM((length, heads * DK), BF16),
            pltpu.VMEM((length, heads * DK), BF16),
            pltpu.VMEM((length, heads * DVAL), F32),
            pltpu.VMEM((length + CH, CH), F32),
            pltpu.VMEM((heads, DK, DVAL), F32),
        ],
        compiler_params=pltpu.CompilerParams(vmem_limit_bytes=60 * 2**20),
        cost_estimate=pl.CostEstimate(flops=20 * 10**9, bytes_accessed=70 * 2**20, transcendentals=0),
        name="mixer_forward",
    )(lens, dsl, bias, preq, prek, prev, ab, taps_qk, taps_v, gain, preg)


def mixer_bwd_kernel(
    heads, lens, dsl, bias, ab_ref, taps_qk, taps_v, gain,
    cq, ck, cv, dmix_h, preg_h, t_h, s_h, u_h, o_h,
    dpq, dpk, dpv, dpg_h, dab,
    dpg, dmix, preg, t_in, s_in, u_in, o_in, lsem, ssem, masks, qn, kn, vn, cum_s, dstate, dqs, dks, dvs, gcol,
):
    length = dmix.shape[0]
    count = length // CH
    arriving = start_loads(
        [(o_h, o_in), (preg_h, preg), (dmix_h, dmix), (u_h, u_in), (s_h, s_in), (t_h, t_in)], lsem
    )
    saves = Saves(ssem)
    taps_q, taps_k = taps_qk.at[0], taps_qk.at[1]
    fill_masks(masks, lens)
    gate_par = gate_rows(dsl, bias)

    def key_tile(h, carry):
        cols = pl.ds(pl.multiple_of(h * DK, DK), DK)
        for save, dst, scale in ((cq, qn, INV_ROOT), (ck, kn, 1.0)):
            c = save[:, cols].astype(F32)
            u = c * sigmoid(c)
            n = lax.rsqrt(jnp.sum(u * u, axis=-1, keepdims=True) + EPSILON) * scale
            dst[:, cols] = (u * n).astype(BF16)
        for half in range(2):
            vcols = pl.ds(pl.multiple_of(h * DVAL + half * DK, DK), DK)
            c = cv[:, vcols].astype(F32)
            vn[:, vcols] = c * sigmoid(c)
        return carry

    lax.fori_loop(0, heads, key_tile, 0)
    for copy in arriving:
        copy.wait()
    row = iota2((CH, CH), 0)
    col = iota2((CH, CH), 1)
    upper = (row <= col).astype(BF16)
    lower = (row >= col).astype(BF16)
    log_decay, z_all = gate_columns(ab_ref[...], gate_par[0], gate_par[1])
    beta_all = sigmoid(ab_ref[...])
    for n in range(count):
        cum_s[n * CH : (n + 1) * CH] = exact_tn(upper, log_decay[n * CH : (n + 1) * CH])
    for h in range(heads):
        dstate[h] = jnp.zeros((DK, DVAL), F32)
    lane = iota2((1, CH), 1)
    strict = (row > col).astype(F32)
    ones = jnp.ones((CH, CH), BF16)

    for n in range(count - 1, -1, -1):
        r = pl.ds(n * CH, CH)
        seg_col = segment_at(row + n * CH, lens)
        seg_row = segment_at(col + n * CH, lens)
        keepf = ((seg_col == seg_row) & (row >= col)).astype(F32)
        cum = cum_s[r]
        cum_t = cum.T
        beta_c = beta_all[n * CH : (n + 1) * CH]
        prev_last = segment_at(n * CH - 1, lens) if n else -1
        start = jnp.exp(cum) * (seg_col == prev_last).astype(F32)
        last_seg = segment_at((n + 1) * CH - 1, lens)
        tail = jnp.exp(cum[CH - 1 : CH] - cum) * (seg_col == last_seg).astype(F32)
        dcum_all = jnp.zeros((CH, CH), F32)
        dbeta_all = jnp.zeros((CH, CH), F32)
        dlast_all = jnp.zeros((1, CH), F32)
        sums = [dcum_all, dlast_all, dbeta_all]

        def one_head(h):
            qc = slice(h * DK, (h + 1) * DK)
            vcols = slice(h * DVAL, (h + 1) * DVAL)
            here = (lane == h).astype(F32)
            o = o_in[r, vcols].astype(F32)
            g = preg[r, vcols].astype(F32)
            dm = dmix[r, vcols].astype(F32)
            sg = sigmoid(g)
            rn = lax.rsqrt(jnp.mean(o * o, axis=-1, keepdims=True) + EPSILON)
            on = o * rn
            y = on * gain[...]
            dpg[r, vcols] = (dm * y * (sg * (1.0 + g * (1.0 - sg)))).astype(BF16)
            dy = dm * (g * sg) * gain[...]
            do = rn * (dy - on * jnp.mean(dy * on, axis=-1, keepdims=True))
            dob = do.astype(BF16)
            q = qn[r, qc]
            k = kn[r, qc]
            kf = k.astype(F32)
            qf = q.astype(F32)
            un = u_in[r, vcols]
            s0 = s_in[n, h]
            tb = t_in[n, h]
            beta = beta_c[:, heads + h : heads + h + 1]
            st = start[:, h : h + 1]
            tl = tail[:, h : h + 1]
            carry_scale = start[CH - 1 : CH, h : h + 1]
            ratio = jnp.exp(jnp.minimum(cum[:, h : h + 1] - cum_t[h : h + 1], 0.0)) * keepf
            both = mm_nt(jnp.concatenate([q, k], axis=0), k)
            scores = ratio * both[:CH]
            rs = ratio * strict
            amat = rs * both[CH:]
            yield
            qk_state = mm(jnp.concatenate([q, k], axis=0), s0)
            ks = qk_state[CH:]
            ds1 = dstate[h]
            ds1b = ds1.astype(BF16)
            ktail = (kf * tl).astype(BF16)
            yield
            dun = mm_tn(scores, dob) + mm(ktail, ds1b)
            yield
            dres = mm_tn(tb, dun)
            dresb = dres.astype(BF16)
            yield
            dks0 = (-(beta * st) * dres).astype(BF16)
            qst = (qf * st).astype(BF16)
            dstate[h] = carry_scale * ds1 + mm_tn(jnp.concatenate([qst, k], axis=0), jnp.concatenate([dob, dks0], axis=0))
            yield
            both_d = mm_nt(jnp.concatenate([dob, dresb], axis=0), un)
            dscore = both_d[:CH]
            da = -both_d[CH:]
            yield
            dqk = (dscore * ratio).astype(BF16)
            dkk = (da * beta * rs).astype(BF16)
            dspread = dscore * scores + da * beta * amat
            dbeta = jnp.sum(da * amat, axis=-1, keepdims=True) + jnp.sum(
                dres * (vn[r, vcols] - st * ks), axis=-1, keepdims=True
            )
            dvs[r, vcols] = beta * dres
            yield
            by_state = mm_nt(jnp.concatenate([dob, dks0, un], axis=0), jnp.concatenate([s0, ds1b], axis=0))
            dq_state = by_state[:CH, :DK]
            yield
            dq = st * dq_state + mm(dqk, k)
            dktail = by_state[2 * CH :, DK:]
            dk = (
                by_state[CH : 2 * CH, :DK]
                + tl * dktail
                + mm_tn(dqk, q)
                + mm(dkk, k)
                + mm_tn(dkk, k)
            )
            yield
            dqs[r, qc] = dq
            dks[r, qc] = dk
            dstart_s = st * jnp.sum(qf * dq_state, axis=-1, keepdims=True) + st * (
                -beta * jnp.sum(dres * ks, axis=-1, keepdims=True)
            )
            dtail_s = tl * jnp.sum(kf * dktail, axis=-1, keepdims=True)
            dcarry = carry_scale * jnp.sum(jnp.sum(ds1 * s0.astype(F32), axis=-1, keepdims=True), axis=0, keepdims=True)
            yield
            colsum = exact_cols(dspread, ones)
            dcum = jnp.sum(dspread, axis=-1, keepdims=True) - colsum[:, 0:1] + dstart_s - dtail_s
            dlast = jnp.sum(dtail_s, axis=0, keepdims=True) + dcarry
            sums[0] = sums[0] + dcum * here
            sums[1] = sums[1] + dlast * here
            sums[2] = sums[2] + dbeta * (lane == heads + h).astype(F32)

        side_by_side(one_head, heads)
        dcum_all, dlast_all, dbeta_all = sums
        saves.start(dpg.at[r], dpg_h.at[r])
        dcum_all = dcum_all + dlast_all * (row == CH - 1).astype(F32)
        gcol[r] = exact_tn(lower, dcum_all) + dbeta_all * beta_c * (1.0 - beta_c)

    slope = -jnp.exp(gate_par[0]) * sigmoid(z_all)
    dab[...] = (gcol[...] * jnp.where(lane < heads, slope, 1.0)).astype(BF16)

    def back_tile(h, carry):
        cols = pl.ds(pl.multiple_of(h * DK, DK), DK)
        for save, dsrc, taps, dst, scale in ((cq, dqs, taps_q, dpq, INV_ROOT), (ck, dks, taps_k, dpk, 1.0)):
            c = save[:, cols].astype(F32)
            sg = sigmoid(c)
            u = c * sg
            n = lax.rsqrt(jnp.sum(u * u, axis=-1, keepdims=True) + EPSILON)
            un = u * n
            d = dsrc[:, cols] * scale
            du = n * (d - un * jnp.sum(d * un, axis=-1, keepdims=True))
            dc = du * (sg * (1.0 + c * (1.0 - sg)))
            dst[:, cols] = conv_rows_back(dc, taps[:, cols], masks, length).astype(BF16)
        for half in range(2):
            vcols = pl.ds(pl.multiple_of(h * DVAL + half * DK, DK), DK)
            c = cv[:, vcols].astype(F32)
            sg = sigmoid(c)
            dc = dvs[:, vcols] * (sg * (1.0 + c * (1.0 - sg)))
            dpv[:, vcols] = conv_rows_back(dc, taps_v[:, vcols], masks, length).astype(BF16)
        return carry

    lax.fori_loop(0, heads, back_tile, 0)
    saves.finish()


def exact_cols(x, ones):
    hi = x.astype(BF16)
    lo = (x - hi.astype(F32)).astype(BF16)
    return mm_tn(hi, ones) + mm_tn(lo, ones)


def mixer_bwd(lens, dsl, bias, dmix, preg, ab, taps_qk, taps_v, gain, saved):
    length = dmix.shape[0]
    heads = dmix.shape[1] // DVAL
    vm = pl.BlockSpec(memory_space=pltpu.VMEM)
    sm = pl.BlockSpec(memory_space=pltpu.SMEM)
    hb = pl.BlockSpec(memory_space=pl.ANY)
    out_shape = (
        jax.ShapeDtypeStruct((length, heads * DK), BF16),
        jax.ShapeDtypeStruct((length, heads * DK), BF16),
        jax.ShapeDtypeStruct((length, heads * DVAL), BF16),
        jax.ShapeDtypeStruct((length, heads * DVAL), BF16),
        jax.ShapeDtypeStruct((length, CH), BF16),
    )
    return pl.pallas_call(
        functools.partial(mixer_bwd_kernel, heads),
        out_shape=out_shape,
        in_specs=[sm] * 3 + [vm] * 7 + [hb] * 6,
        out_specs=[vm, vm, vm, hb, vm],
        scratch_shapes=[
            pltpu.VMEM(dmix.shape, BF16),
            *[pltpu.VMEM(a.shape, a.dtype) for a in (dmix, preg, *saved[3:])],
            pltpu.SemaphoreType.DMA((6,)),
            pltpu.SemaphoreType.DMA((length // CH,)),
            pltpu.VMEM((3, length, CH), F32),
            pltpu.VMEM((length, heads * DK), BF16),
            pltpu.VMEM((length, heads * DK), BF16),
            pltpu.VMEM((length, heads * DVAL), F32),
            pltpu.VMEM((length, CH), F32),
            pltpu.VMEM((heads, DK, DVAL), F32),
            pltpu.VMEM((length, heads * DK), F32),
            pltpu.VMEM((length, heads * DK), F32),
            pltpu.VMEM((length, heads * DVAL), F32),
            pltpu.VMEM((length, CH), F32),
        ],
        compiler_params=pltpu.CompilerParams(vmem_limit_bytes=60 * 2**20),
        cost_estimate=pl.CostEstimate(flops=30 * 10**9, bytes_accessed=100 * 2**20, transcendentals=0),
        name="mixer_backward",
    )(lens, dsl, bias, ab, taps_qk, taps_v, gain, *saved[:3], dmix, preg, *saved[3:])


MESH_ID = pl.DeviceIdType.MESH
RING = 4
DMA_SEMS = pltpu.SemaphoreType.DMA
PIECES = 4
WIDE_VMEM = 60 * 2**20
SHARE = 4
ADAPTER_RANK = 16


def ring_places():
    m = lax.axis_index("mp")
    return m, lax.rem(m + 3, RING), lax.rem(m + 1, RING), lax.rem(m + 2, RING)


def ring_barrier(places):
    _, left, right, _ = places
    barrier = pltpu.get_barrier_semaphore()
    for neighbour in (left, right):
        pl.semaphore_signal(barrier, inc=1, device_id={"mp": neighbour}, device_id_type=MESH_ID)
    pl.semaphore_wait(barrier, 2)


class RingGather:
    def __init__(self, buf, send, recv, places):
        self.buf, self.send, self.recv = buf, send, recv
        self.m, self.left, self.right, self.opp = places
        half = buf.shape[1] // 2
        self.top, self.bot = pl.ds(0, half), pl.ds(half, half)

    def begin(self, i, slot, part, to):
        step = part.size // PIECES
        for n in range(PIECES):
            self.copy(i, slot, pl.ds(part.start + n * step, step), to).start()

    def copy(self, i, slot, part, to):
        ref = self.buf.at[slot, part]
        return pltpu.make_async_remote_copy(
            src_ref=ref,
            dst_ref=ref,
            send_sem=self.send.at[i],
            recv_sem=self.recv.at[i],
            device_id={"mp": to},
            device_id_type=MESH_ID,
        )

    def start(self):
        self.begin(0, self.m, self.top, self.right)
        self.begin(1, self.m, self.bot, self.left)
        self.begin(2, self.m, self.bot, self.right)
        self.begin(3, self.m, self.top, self.left)

    def forward(self):
        self.copy(0, self.left, self.top, self.right).wait_recv()
        self.begin(4, self.left, self.top, self.right)
        self.copy(1, self.right, self.bot, self.left).wait_recv()
        self.begin(5, self.right, self.bot, self.left)

    def wait_left(self):
        self.copy(2, self.left, self.bot, self.right).wait_recv()

    def wait_right(self):
        self.copy(3, self.right, self.top, self.left).wait_recv()

    def wait_opp(self):
        self.copy(4, self.opp, self.top, self.right).wait_recv()
        self.copy(5, self.opp, self.bot, self.left).wait_recv()

    def finish(self):
        self.copy(0, self.m, self.top, self.right).wait_send()
        self.copy(1, self.m, self.bot, self.left).wait_send()
        self.copy(2, self.m, self.bot, self.right).wait_send()
        self.copy(3, self.m, self.top, self.left).wait_send()
        self.copy(4, self.left, self.top, self.right).wait_send()
        self.copy(5, self.right, self.bot, self.left).wait_send()


class RingScatter:
    def __init__(self, sbuf, rbuf, acc, send, recv, places):
        self.sbuf, self.rbuf, self.acc, self.send, self.recv = sbuf, rbuf, acc, send, recv
        self.m, self.left, self.right, self.opp = places
        self.half = sbuf.shape[1]

    def begin(self, i):
        step = self.half // PIECES
        for n in range(PIECES):
            self.copy(i, pl.ds(n * step, step)).start()

    def copy(self, i, part=slice(None)):
        to = self.right if i % 2 == 0 else self.left
        return pltpu.make_async_remote_copy(
            src_ref=self.sbuf.at[i, part],
            dst_ref=self.rbuf.at[i, part],
            send_sem=self.send.at[i],
            recv_sem=self.recv.at[i],
            device_id={"mp": to},
            device_id_type=MESH_ID,
        )

    def run(self, part, meanwhile=None, ready=None):
        half = self.half
        rows = 2 * half

        def put_far(cols, val):
            self.sbuf[0, :, cols] = val[:half].astype(BF16)
            self.sbuf[1, :, cols] = val[half:rows].astype(BF16)
            self.acc[0, :, cols] = val[rows:]
            self.sbuf[2, :, cols] = val[rows + half :].astype(BF16)

        part((self.opp, self.right), put_far)
        if ready is not None:
            ready()
        self.begin(0)
        self.begin(1)
        self.begin(2)

        def put_near(cols, val):
            self.acc[1, :, cols] = val[:rows]
            self.sbuf[3, :, cols] = val[:half].astype(BF16)
            self.acc[2, :, cols] = val[rows:]

        part((self.left, self.m), put_near)
        self.begin(3)
        if meanwhile is not None:
            meanwhile()
        self.copy(0).wait_recv()
        self.sbuf[4] = (self.acc[0, 0:half] + self.rbuf[0].astype(F32)).astype(BF16)
        self.begin(4)
        self.copy(1).wait_recv()
        self.sbuf[5] = (self.acc[1, half:rows] + self.rbuf[1].astype(F32)).astype(BF16)
        self.begin(5)
        for i in range(2, 6):
            self.copy(i).wait_recv()

    def total(self, rows, cols):
        lo, hi = rows
        if hi <= self.half:
            a, b, r = self.rbuf[4, lo:hi, cols], self.rbuf[3, lo:hi, cols], slice(lo, hi)
        else:
            r = slice(lo, hi)
            lo, hi = lo - self.half, hi - self.half
            a, b = self.rbuf[2, lo:hi, cols], self.rbuf[5, lo:hi, cols]
        return self.acc[2, r, cols] + a.astype(F32) + b.astype(F32)

    def finish(self):
        for i in range(6):
            self.copy(i).wait_send()


class Loads:
    def __init__(self, pairs, sems):
        self.copies = [pltpu.make_async_copy(src, dst, sems.at[n]) for n, (src, dst) in enumerate(pairs)]
        self.waited = set()

    def start(self, *which):
        for n in which or range(len(self.copies)):
            self.copies[n].start()

    def wait(self, *which):
        for n in which:
            if n not in self.waited:
                self.copies[n].wait()
                self.waited.add(n)


def loop(lo, hi, body):
    def step(s, carry):
        body(s)
        return carry

    lax.fori_loop(lo, hi, step, 0)


def greet_dp(n, me):
    barrier = pltpu.get_barrier_semaphore()
    loop(
        1,
        n,
        lambda s: pl.semaphore_signal(barrier, inc=1, device_id={"dp": lax.rem(me + s, n)}, device_id_type=MESH_ID),
    )


def greet_ring(places):
    barrier = pltpu.get_barrier_semaphore()
    for neighbour in (places[1], places[2]):
        pl.semaphore_signal(barrier, inc=1, device_id={"mp": neighbour}, device_id_type=MESH_ID)


def wait_greetings(count):
    pl.semaphore_wait(pltpu.get_barrier_semaphore(), count)


class DpRows:
    def __init__(self, stage, land, send, recv):
        self.stage, self.land, self.send, self.recv = stage, land, send, recv
        self.n, _, self.pw = stage.shape
        self.parts = 16 // SHARE
        self.me = lax.axis_index("dp")

    def maps(self, index, rows):
        slots = self.n * 16
        hit = iota2((rows, slots), 0).astype(F32) == index[0:1]
        part_of = (iota2((1, slots), 1) // SHARE) % self.parts
        return [(hit & (part_of == p)).astype(F32).astype(BF16) for p in range(self.parts)]

    def fill(self, index, rows, value):
        acc = jnp.zeros((self.n * 16, self.pw), F32)
        for p, hit in enumerate(self.maps(index, rows)):
            acc = acc + mm_tn(hit, value(slice(p * self.pw, (p + 1) * self.pw)))
        self.stage[...] = acc.astype(BF16).reshape(self.n, 16, self.pw)
        self.land[self.me] = self.stage[self.me]

    def copy(self, to, source):
        return pltpu.make_async_remote_copy(
            src_ref=self.stage.at[to],
            dst_ref=self.land.at[source],
            send_sem=self.send.at[to],
            recv_sem=self.recv.at[source],
            device_id={"dp": to},
            device_id_type=MESH_ID,
        )

    def ahead(self, s):
        return lax.rem(self.me + s, self.n)

    def behind(self, s):
        return lax.rem(self.me + self.n - s, self.n)

    def start(self):
        loop(1, self.n, lambda s: self.copy(self.ahead(s), self.me).start())

    def take(self, index, rows, put):
        loop(1, self.n, lambda s: self.copy(self.behind(s), self.behind(s)).wait_recv())
        got = self.land[...].reshape(self.n * 16, self.pw)
        for p, hit in enumerate(self.maps(index, rows)):
            put(slice(p * self.pw, (p + 1) * self.pw), mm(hit, got))

    def finish(self):
        loop(1, self.n, lambda s: self.copy(self.ahead(s), self.me).wait_send())


class DpSums:
    def __init__(self, grads, pair_land, mine, sum_land, send, recv, send2, recv2):
        self.grads, self.pair_land, self.mine, self.sum_land = grads, pair_land, mine, sum_land
        self.send, self.recv, self.send2, self.recv2 = send, recv, send2, recv2
        self.me = lax.axis_index("dp")
        self.core = lax.rem(self.me, 2)
        self.here = self.me // 2
        self.pairs = pair_land.shape[0]

    def pair_copy(self, i):
        return pltpu.make_async_remote_copy(
            src_ref=self.grads.at[2 * i + 1 - self.core],
            dst_ref=self.pair_land.at[i],
            send_sem=self.send.at[i],
            recv_sem=self.recv.at[i],
            device_id={"dp": self.me + 1 - 2 * self.core},
            device_id_type=MESH_ID,
        )

    def sum_copy(self, to, source):
        return pltpu.make_async_remote_copy(
            src_ref=self.mine.at[to],
            dst_ref=self.sum_land.at[source],
            send_sem=self.send2.at[to],
            recv_sem=self.recv2.at[source],
            device_id={"dp": 2 * to + self.core},
            device_id_type=MESH_ID,
        )

    def ahead(self, s):
        return lax.rem(self.here + s, self.pairs)

    def behind(self, s):
        return lax.rem(self.here + self.pairs - s, self.pairs)

    def start(self):
        loop(1, self.pairs + 1, lambda s: self.pair_copy(self.ahead(s)).start())

    def add(self, i):
        self.pair_copy(i).wait_recv()
        self.mine[i] = (self.grads[2 * i + self.core].astype(F32) + self.pair_land[i].astype(F32)).astype(BF16)

    def forward(self):
        def one(s):
            i = self.ahead(s)
            self.add(i)
            self.sum_copy(i, self.here).start()

        loop(1, self.pairs, one)
        self.add(self.here)
        self.sum_land[self.here] = self.mine[self.here]

    def take(self, widths, sink):
        parts = 16 // SHARE
        loop(1, self.pairs, lambda s: self.sum_copy(self.behind(s), self.behind(s)).wait_recv())
        at = 0
        for k, w in enumerate(widths):
            total = self.sum_land[0, :, at : at + w].astype(F32)
            for i in range(1, self.pairs):
                total = total + self.sum_land[i, :, at : at + w].astype(F32)
            for p in range(parts):
                sink(k, (p * w, (p + 1) * w), total[p * SHARE : (p + 1) * SHARE])
            at += w

    def finish(self):
        loop(1, self.pairs + 1, lambda s: self.pair_copy(self.ahead(s)).wait_send())
        loop(1, self.pairs, lambda s: self.sum_copy(self.ahead(s), self.here).wait_send())


def rows_scratch(n, pw):
    return [pltpu.VMEM((n, 16, pw), BF16), pltpu.VMEM((n, 16, pw), BF16), DMA_SEMS((n,)), DMA_SEMS((n,))]


def sums_scratch(n, w):
    half = n // 2
    return [pltpu.VMEM((half, 16, w), BF16)] * 3 + [DMA_SEMS((half,))] * 4


def unfold(n, per):
    row = iota2((n, n), 0)
    col = iota2((n, n), 1)
    part = per // SHARE
    wide = n // part
    hit = (row // per == (col % wide) // SHARE) & (row % SHARE == col % SHARE) & ((row // SHARE) % part == col // wide)
    return hit.astype(F32).astype(BF16)


def keep_chunks(stage, deal, pieces, at):
    n = stage.shape[0]
    w = pieces[0].shape[1]
    used = deal[:, 0 : len(pieces) * n * SHARE]
    got = mm(used, jnp.concatenate([p.astype(BF16) for p in pieces], axis=0))
    stage[:, :, at : at + w] = got.astype(BF16).reshape(n, 16, w)
    return at + w


def fill_select(select, lens, adapters):
    seg = segment_at(iota2(select.shape, 0), lens)
    which = jnp.full(select.shape, adapters[0, 0], jnp.int32)
    for n in range(1, lens.shape[1]):
        which = jnp.where(seg == n, adapters[0, n], which)
    select[...] = (iota2(select.shape, 1) // ADAPTER_RANK == which).astype(F32)


def fill_gates(heads, wdec, bdec, wab, bab):
    depth = wdec.shape[1]
    total = jnp.zeros(wab.shape, F32)
    for n in range(2):
        line, k = iota2((CH, depth), 0), iota2((CH, depth), 1)
        at = ((line == k + n * heads) & (k < heads)).astype(F32).astype(BF16)
        total = total + mm(at, wdec[n])
        bab[n] = mm_nt(bdec[n].astype(F32).T, at).astype(BF16)
    wab[...] = total.astype(BF16)


def route_indices(routes, rows):
    me, mp = lax.axis_index("dp"), lax.axis_index("mp")
    n = routes.shape[0]
    slots = n * 16
    column = routes[:, 0, :]
    for k in range(1, routes.shape[1]):
        column = jnp.where(mp == k, routes[:, k, :], column)
    group = rows * RING
    dest = (column // group).astype(F32)
    mine = iota2((n, rows), 0) == me
    own = jnp.sum(jnp.where(mine, dest, 0.0), axis=0, keepdims=True)
    across = jnp.broadcast_to(own, (rows, rows))
    down = across.T
    line = iota2((rows, rows), 0)
    lane = iota2((rows, rows), 1)
    rank = jnp.sum(((across == down) & (lane < line)).astype(F32), axis=1, keepdims=True)
    place = down[:, 0:1] * SHARE + rank
    slot = iota2((1, slots), 1)
    slot_row = ((slot // 16) * SHARE + slot % SHARE).astype(F32)
    leaves = jnp.sum(
        jnp.where(place == slot_row, iota2((rows, slots), 0).astype(F32), 0.0), axis=0, keepdims=True
    )
    here = dest == me.astype(F32)
    order = mm(here.astype(F32), (line < lane).astype(F32))
    value = (column - me * group - mp * rows).astype(F32)
    owner = iota2((n, slots), 0) == slot // 16
    lands = jnp.zeros((1, slots), F32)
    for j in range(SHARE):
        found = jnp.sum(jnp.where(here & (order == float(j)), value, 0.0), axis=1, keepdims=True)
        lands = lands + jnp.sum(jnp.where(owner & (slot % SHARE == j), found, 0.0), axis=0, keepdims=True)
    return leaves, lands


def tiles(total, step=512):
    return [(at, min(step, total - at)) for at in range(0, total, step)]


def block_rows(place, rows):
    return pl.ds(pl.multiple_of(place * rows, rows), rows)


def both_rows(ref, pair, rows, cols=slice(None)):
    return jnp.concatenate([ref[block_rows(place, rows), cols] for place in pair], axis=0)


def put_rows(ref, pair, rows, cols, val):
    for n, place in enumerate(pair):
        ref[block_rows(place, rows), cols] = val[n * rows : (n + 1) * rows]


def norm_factor(v):
    return lax.rsqrt(jnp.mean(v * v, axis=-1, keepdims=True) + EPSILON)


def project_kernel(
    lens, adapters, routes, tokens, cot_in, gain, wdec, bdec, wqk_h, wvg_h, ain_h, bqk_h, bvg_h,
    index_in, index_out, select, resid, cot, normed_h, low, pq, pk, pv, pg, pab,
    gath, wqk, wvg, ain, bqk, bvg, wab, bab, wsem, osem, send, recv,
    st1, ld1, se1, re1, st2, ld2, se2, re2,
):
    rows = tokens.shape[0]
    places = ring_places()
    m = places[0]
    first = DpRows(st1, ld1, se1, re1)
    second = DpRows(st2, ld2, se2, re2)
    greet_dp(first.n, first.me)
    greet_ring(places)
    loads = Loads([(ain_h, ain), (wqk_h, wqk), (bqk_h, bqk), (wvg_h, wvg), (bvg_h, bvg)], wsem)
    loads.start()
    leaves, lands = route_indices(routes, rows)
    index_in[...] = jnp.broadcast_to(leaves, index_in.shape)
    index_out[...] = jnp.broadcast_to(lands, index_out.shape)
    first.fill(index_in, rows, lambda c: tokens[:, c])
    wait_greetings(first.n + 1)
    first.start()
    second.fill(index_in, rows, lambda c: cot_in[:, c])
    fill_select(select, lens, adapters)
    fill_gates(wqk.shape[2] // DK, wdec, bdec, wab, bab)

    def put_tokens(c, val):
        resid[:, c] = val.astype(BF16)

    first.take(index_out, rows, put_tokens)
    second.start()
    for at in range(0, rows, 32):
        v = resid[at : at + 32].astype(F32)
        gath[m, at : at + 32] = (v * norm_factor(v) * gain[...]).astype(BF16)
    ring = RingGather(gath, send, recv, places)
    ring.start()
    ac = select.shape[1]

    def compute(place):
        r = block_rows(place, rows)
        x = gath[place]
        sel = select[r]
        loads.wait(0)
        for n in range(ain.shape[1] // ac):
            low[r, n * ac : (n + 1) * ac] = (mm(x, ain[:, n * ac : (n + 1) * ac]) * sel).astype(BF16)
        loads.wait(1, 2)
        for n, dst in enumerate((pq, pk)):
            lo = low[r, n * ac : (n + 1) * ac]
            dst[r] = (mm(x, wqk[n]) + mm(lo, bqk[n])).astype(BF16)
        loads.wait(3, 4)
        for n, dst in enumerate((pv, pg)):
            lo = low[r, (n + 2) * ac : (n + 3) * ac]
            for at, size in tiles(wvg.shape[2]):
                c = slice(at, at + size)
                dst[r, c] = (mm(x, wvg[n, :, c]) + mm(lo, bvg[n, :, c])).astype(BF16)
        pab[r] = (
            mm_nt(x, wab[...]) + mm(low[r, 4 * ac : 5 * ac], bab[0]) + mm(low[r, 5 * ac : 6 * ac], bab[1])
        )

    compute(m)
    ring.forward()
    ring.wait_left()
    compute(places[1])
    ring.wait_right()
    compute(places[2])

    def put_cot(c, val):
        cot[:, c] = val.astype(BF16)

    second.take(index_out, rows, put_cot)
    ring.wait_opp()
    out = pltpu.make_async_copy(gath, normed_h, osem)
    out.start()
    compute(places[3])
    ring.finish()
    first.finish()
    second.finish()
    out.wait()


def specs(n_vmem, n_any):
    return [pl.BlockSpec(memory_space=pltpu.VMEM)] * n_vmem + [pl.BlockSpec(memory_space=pl.ANY)] * n_any


def sds(shape, dtype=BF16):
    return jax.ShapeDtypeStruct(shape, dtype)


def ring_params(collective_id):
    return pltpu.CompilerParams(
        collective_id=collective_id, has_side_effects=True, vmem_limit_bytes=WIDE_VMEM
    )


def like(a):
    return pltpu.VMEM(a.shape, a.dtype)


def project(lens, adapters, routes, tokens, cot, gain, wdec, bdec, wqk, wvg, ain, bqk, bvg):
    rows, width = tokens.shape
    n_dp = lax.axis_size("dp")
    group = rows * RING
    kw, vw = wqk.shape[2], wvg.shape[2]
    ac = bqk.shape[1]
    vm, hb = specs(1, 1)
    sm = pl.BlockSpec(memory_space=pltpu.SMEM)
    pw = width * SHARE // 16
    return pl.pallas_call(
        project_kernel,
        out_shape=(
            sds((8, n_dp * 16), F32),
            sds((8, n_dp * 16), F32),
            sds((group, ac), F32),
            sds((rows, width)),
            sds((rows, width)),
            sds((RING, rows, width)),
            sds((group, ain.shape[1])),
            sds((group, kw)),
            sds((group, kw)),
            sds((group, vw)),
            sds((group, vw)),
            sds((group, CH), F32),
        ),
        in_specs=[sm] * 2 + [vm] * 6 + [hb] * 5,
        out_specs=[vm] * 5 + [hb] + [vm] * 6,
        scratch_shapes=[
            pltpu.VMEM((RING, rows, width), BF16),
            like(wqk), like(wvg), like(ain), like(bqk), like(bvg),
            pltpu.VMEM((CH, width), BF16), pltpu.VMEM((2, ac, CH), BF16),
            DMA_SEMS((5,)), DMA_SEMS(()), DMA_SEMS((6,)), DMA_SEMS((6,)),
            *rows_scratch(n_dp, pw), *rows_scratch(n_dp, pw),
        ],
        compiler_params=ring_params(1),
        cost_estimate=pl.CostEstimate(flops=8 * 10**9, bytes_accessed=30 * 2**20, transcendentals=0),
        name="gather_project",
    )(lens, adapters, routes, tokens, cot, gain, wdec, bdec, wqk, wvg, ain, bqk, bvg)


def feed_kernel(
    mixed, resid, gain, select, wout_h, aout_h, bout_h, affn_h, gu_h, bgu_h, down_h, adown_h,
    middle, rank_out, normed_h, rank2, gate, up, hidden, dpart, rpart,
    gath, wout, aout, bout, affn, gu, bgu, down, adown, sbuf, rbuf, acc, wsem, osem, send, recv, send2, recv2,
):
    rows, width = resid.shape
    places = ring_places()
    m = places[0]
    loads = Loads(
        [
            (wout_h, wout), (aout_h, aout), (bout_h, bout), (affn_h, affn),
            (gu_h, gu), (bgu_h, bgu), (down_h, down), (adown_h, adown),
        ],
        wsem,
    )
    loads.start(0, 1)
    ac = select.shape[1]
    ff = gu.shape[2]
    greet_ring(places)
    loads.wait(0, 1)
    scatter = RingScatter(sbuf, rbuf, acc, send, recv, places)

    def part(pair, put):
        x = both_rows(mixed, pair, rows)
        for at, size in tiles(width):
            put(slice(at, at + size), mm(x, wout[:, at : at + size]))
        put(slice(width, width + ac), mm(x, aout[...]))

    def ready():
        loads.start(2, 3, 4, 5, 6, 7)
        wait_greetings(2)

    scatter.run(part, None, ready)
    loads.wait(2)
    sel_own = select[block_rows(m, rows)]
    half = rows // 2
    for lo in (0, half):
        bounds = (lo, lo + half)
        gath[m, lo : lo + half, width : width + ac] = (
            scatter.total(bounds, slice(width, width + ac)) * sel_own[lo : lo + half]
        ).astype(BF16)
    ro = gath[m, :, width : width + ac]
    for at, size in tiles(width):
        c = slice(at, at + size)
        extra = mm(ro, bout[:, c])
        for lo in (0, half):
            middle[lo : lo + half, c] = (
                resid[lo : lo + half, c].astype(F32) + scatter.total((lo, lo + half), c) + extra[lo : lo + half]
            )
    for at in range(0, rows, 32):
        v = middle[at : at + 32]
        gath[m, at : at + 32, 0:width] = (v * norm_factor(v) * gain[...]).astype(BF16)
    ring = RingGather(gath, send2, recv2, places)
    ring.start()

    def compute(place):
        r = block_rows(place, rows)
        x = gath[place, :, 0:width]
        rank_out[r] = gath[place, :, width : width + ac]
        sel = select[r]
        loads.wait(3)
        for n in range(2):
            rank2[r, n * ac : (n + 1) * ac] = (mm(x, affn[:, n * ac : (n + 1) * ac]) * sel).astype(BF16)
        loads.wait(4, 5)
        r0 = rank2[r, 0:ac]
        r1 = rank2[r, ac : 2 * ac]
        for at, size in tiles(ff):
            c = slice(at, at + size)
            g = mm(x, gu[0, :, c]) + mm(r0, bgu[0, :, c])
            u = mm(x, gu[1, :, c]) + mm(r1, bgu[1, :, c])
            gate[r, c] = g.astype(BF16)
            up[r, c] = u.astype(BF16)
            hidden[r, c] = (g * sigmoid(g) * u).astype(BF16)
        loads.wait(6, 7)
        h = hidden[r]
        for at, size in tiles(width):
            c = slice(at, at + size)
            dpart[r, c] = mm(h, down[:, c]).astype(BF16)
        rpart[r] = mm(h, adown[...]).astype(BF16)

    compute(m)
    ring.forward()
    ring.wait_left()
    compute(places[1])
    ring.wait_right()
    compute(places[2])
    ring.wait_opp()
    out = pltpu.make_async_copy(gath.at[:, :, pl.ds(0, width)], normed_h, osem)
    out.start()
    compute(places[3])
    scatter.finish()
    ring.finish()
    out.wait()


def feed(mixed, resid, gain, select, wout, aout, bout, affn, gu, bgu, down, adown):
    rows, width = resid.shape
    group = rows * RING
    ff = gu.shape[2]
    ac = select.shape[1]
    cols = width + ac
    vm, hb = specs(1, 1)
    return pl.pallas_call(
        feed_kernel,
        out_shape=(
            sds((rows, width), F32),
            sds((group, ac)),
            sds((RING, rows, width)),
            sds((group, 2 * ac)),
            sds((group, ff)),
            sds((group, ff)),
            sds((group, ff)),
            sds((group, width)),
            sds((group, ac)),
        ),
        in_specs=[vm] * 4 + [hb] * 8,
        out_specs=[vm, vm, hb] + [vm] * 6,
        scratch_shapes=[
            pltpu.VMEM((RING, rows, cols), BF16),
            like(wout), like(aout), like(bout), like(affn), like(gu), like(bgu), like(down), like(adown),
            pltpu.VMEM((6, rows // 2, cols), BF16),
            pltpu.VMEM((6, rows // 2, cols), BF16),
            pltpu.VMEM((3, rows, cols), F32),
            DMA_SEMS((8,)), DMA_SEMS(()),
            DMA_SEMS((6,)), DMA_SEMS((6,)), DMA_SEMS((6,)), DMA_SEMS((6,)),
        ],
        compiler_params=ring_params(2),
        cost_estimate=pl.CostEstimate(flops=13 * 10**9, bytes_accessed=40 * 2**20, transcendentals=0),
        name="feed_forward",
    )(mixed, resid, gain, select, wout, aout, bout, affn, gu, bgu, down, adown)


def feed_back_kernel(
    cot, rpart, select, gain,
    bdown_h, down_h, adown_h, gu_h, bgu_h, affn_h, bout_h, wout_h, aout_h, rank2_h, hidden_h, mixed_h, rank_out_h,
    gate_h, up_h, middle_h,
    g_rank2, g_middle_h, g_mixed, rank_down, stage,
    g_middle, ssem, gath, bdown, down, adown, gu, bgu, affn, bout, wout, aout, rank2, hidden, mixed, rank_out, gate, up, middle,
    g_rank_down, g_gate, g_up, g_rank_out, flat, pick, chosen,
    sbuf, rbuf, acc, wsem, send, recv, send2, recv2,
):
    rows, width = middle.shape
    saves = Saves(ssem)
    places = ring_places()
    m = places[0]
    loads = Loads(
        [
            (bdown_h, bdown), (down_h, down), (adown_h, adown), (gu_h, gu), (bgu_h, bgu),
            (affn_h, affn), (bout_h, bout), (wout_h, wout), (aout_h, aout),
            (rank2_h, rank2), (hidden_h, hidden), (mixed_h, mixed), (rank_out_h, rank_out),
            (gate_h, gate), (up_h, up), (middle_h, middle),
        ],
        wsem,
    )
    loads.start(0, 1, 2, 13, 14, 3, 4, 5, 15)
    ac = select.shape[1]
    ff = gu.shape[2]
    greet_ring(places)
    scatter = RingScatter(sbuf, rbuf, acc, send, recv, places)

    def part(pair, put):
        x = both_rows(cot, pair, rows)
        sel = both_rows(select, pair, rows)
        loads.wait(0)
        grd = (mm_nt(x, bdown[...]) * sel).astype(BF16)
        put_rows(g_rank_down, pair, rows, slice(None), grd)
        loads.wait(1, 2, 13, 14)
        for at, size in tiles(ff, 256):
            c = slice(at, at + size)
            gh = mm_nt(x, down[c]) + mm_nt(grd, adown[c])
            g = both_rows(gate, pair, rows, c).astype(F32)
            u = both_rows(up, pair, rows, c).astype(F32)
            sg = sigmoid(g)
            put_rows(g_gate, pair, rows, c, (gh * u * (sg * (1.0 + g * (1.0 - sg)))).astype(BF16))
            put_rows(g_up, pair, rows, c, (gh * g * sg).astype(BF16))
        loads.wait(3, 4, 5)
        gg = both_rows(g_gate, pair, rows)
        gu_ = both_rows(g_up, pair, rows)
        r2a = (mm_nt(gg, bgu[0]) * sel).astype(BF16)
        r2b = (mm_nt(gu_, bgu[1]) * sel).astype(BF16)
        put_rows(g_rank2, pair, rows, slice(0, ac), r2a)
        put_rows(g_rank2, pair, rows, slice(ac, 2 * ac), r2b)
        r2 = jnp.concatenate([r2a, r2b], axis=1)
        for at, size in tiles(width, 256):
            c = slice(at, at + size)
            put(c, mm_nt(gg, gu[0, c]) + mm_nt(gu_, gu[1, c]) + mm_nt(r2, affn[c]))
        put(slice(width, width + ac), both_rows(rpart, pair, rows).astype(F32))

    n_dp = stage.shape[0]
    parts = 16 // SHARE
    deal = unfold(n_dp * 16, 16)

    def grads():
        loads.wait(9, 10)
        for at, size in tiles(ff):
            c = slice(at, at + size)
            flat[:, at : at + size] = mm_tn(rank2[:, 0:ac], g_gate[:, c]).astype(BF16)
            flat[:, ff + at : ff + at + size] = mm_tn(rank2[:, ac : 2 * ac], g_up[:, c]).astype(BF16)
            flat[:, 2 * ff + at : 2 * ff + at + size] = mm_tn(g_rank_down[...], hidden[:, c]).astype(BF16)
        flat[:, 3 * ff :] = jnp.zeros((ac, flat.shape[1] - 3 * ff), BF16)
        w = flat.shape[1] // parts
        keep_chunks(stage, deal, [flat[:, p * w : (p + 1) * w] for p in range(parts)], 0)

    def ready():
        loads.start(*range(6, 13))
        wait_greetings(2)

    scatter.run(part, grads, ready)
    sel_own = select[block_rows(m, rows)]
    loads.wait(15)
    step = 16
    for at in range(0, rows, step):
        b = (at, at + step)
        g = scatter.total(b, slice(0, width)) * gain[...]
        v = middle[at : at + step]
        n = norm_factor(v)
        v = v * n
        gm = cot[pl.ds(pl.multiple_of(m * rows + at, step), step)].astype(F32) + n * (
            g - v * jnp.mean(g * v, axis=-1, keepdims=True)
        )
        g_middle[at : at + step] = gm
        gath[m, at : at + step, 0:width] = gm.astype(BF16)
        gath[m, at : at + step, width : width + ac] = (
            scatter.total(b, slice(width, width + ac)) * sel_own[at : at + step]
        ).astype(BF16)
    ring = RingGather(gath, send2, recv2, places)
    ring.start()
    saves.start(g_middle, g_middle_h)
    per = width // (n_dp * RING)
    for at in range(0, width, 256):
        line = iota2((256, pick.shape[1]), 0) + at
        slot = iota2((256, pick.shape[1]), 1)
        want = (((slot % ac) // SHARE) * RING + m) * per + (slot // ac) * SHARE + slot % SHARE
        pick[at : at + 256] = (line == want).astype(F32).astype(BF16)
    cot_chosen = mm(cot[...], pick[...]).astype(BF16)

    def compute(*pair):
        x = jnp.concatenate([gath[place, :, 0:width] for place in pair], axis=0)
        loads.wait(6, 7, 8)
        gro = (mm_nt(x, bout[...]) * both_rows(select, pair, rows)).astype(BF16)
        put_rows(g_rank_out, pair, rows, slice(None), gro)
        for at, size in tiles(wout.shape[0], 256):
            c = slice(at, at + size)
            put_rows(g_mixed, pair, rows, c, (mm_nt(x, wout[c]) + mm_nt(gro, aout[c])).astype(BF16))
        put_rows(chosen, pair, rows, slice(None), mm(x, pick[...]).astype(BF16))
        for place in pair:
            rank_down[block_rows(place, rows)] = gath[place, :, width : width + ac]

    compute(m)
    ring.forward()
    ring.wait_left()
    ring.wait_right()
    compute(places[1], places[2])
    ring.wait_opp()
    compute(places[3])
    loads.wait(11, 12)
    at = flat.shape[1] // parts
    w = mixed.shape[1] // parts
    gro = g_rank_out[...]
    at = keep_chunks(stage, deal, [mm_tn(gro, mixed[:, p * w : (p + 1) * w]) for p in range(parts)], at)
    for rows_of, ranks in ((cot_chosen, rank_down), (chosen[...], rank_out)):
        at = keep_chunks(
            stage, deal, [mm_tn(rows_of[:, b * ac : (b + 1) * ac], ranks[...]) for b in range(rows_of.shape[1] // ac)], at
        )
    scatter.finish()
    ring.finish()
    saves.finish()


def early_widths(ff, vw, ac):
    parts = 16 // SHARE
    return [-(-3 * ff // (parts * CH)) * CH, vw // parts, ac, ac]


def feed_back(
    cot, rpart, select, gain,
    bdown, down, adown, gu, bgu, affn, bout, wout, aout, rank2, hidden, mixed, rank_out, gate, up, middle,
):
    rows, width = middle.shape
    group = rows * RING
    ff = gu.shape[2]
    ac = select.shape[1]
    n_dp = lax.axis_size("dp")
    parts = 16 // SHARE
    vw = wout.shape[0]
    widths = early_widths(ff, vw, ac)
    vm, hb = specs(1, 1)
    loaded = (bdown, down, adown, gu, bgu, affn, bout, wout, aout, rank2, hidden, mixed, rank_out, gate, up, middle)
    return pl.pallas_call(
        feed_back_kernel,
        out_shape=(
            sds((group, 2 * ac)),
            sds((rows, width), F32),
            sds((group, vw)),
            sds((group, ac)),
            sds((n_dp, 16, sum(widths))),
        ),
        in_specs=[vm] * 4 + [hb] * len(loaded),
        out_specs=[vm, hb, vm, vm, vm],
        scratch_shapes=[
            pltpu.VMEM((rows, width), F32),
            DMA_SEMS((1,)),
            pltpu.VMEM((RING, rows, width + ac), BF16),
            *[like(a) for a in loaded],
            pltpu.VMEM((group, ac), BF16),
            pltpu.VMEM((group, ff), BF16),
            pltpu.VMEM((group, ff), BF16),
            pltpu.VMEM((group, ac), BF16),
            pltpu.VMEM((ac, parts * widths[0]), BF16),
            pltpu.VMEM((width, width // RING), BF16),
            pltpu.VMEM((group, width // RING), BF16),
            pltpu.VMEM((6, rows // 2, width + ac), BF16),
            pltpu.VMEM((6, rows // 2, width + ac), BF16),
            pltpu.VMEM((3, rows, width + ac), F32),
            DMA_SEMS((len(loaded),)),
            DMA_SEMS((6,)), DMA_SEMS((6,)), DMA_SEMS((6,)), DMA_SEMS((6,)),
        ],
        compiler_params=ring_params(3),
        cost_estimate=pl.CostEstimate(flops=13 * 10**9, bytes_accessed=40 * 2**20, transcendentals=0),
        name="feed_backward",
    )(cot, rpart, select, gain, *loaded)


def fold_maps(count, base, ac):
    line = iota2((count, ac), 0)
    col = iota2((count, ac), 1)
    hit = (line // ac) * ADAPTER_RANK + line % ADAPTER_RANK + base == col
    return hit.astype(F32).astype(BF16)


def project_back_kernel(
    widths, index_in, index_out, dq, dk, dv, dg, dab, select, gain, wdec, bdec, g_rank2, rank_down,
    wqk_h, wvg_h, ain_h, bqk_h, bvg_h, bdown_h, low_h, normed_h, normed2_h,
    resid_h, g_middle_h, early_h, middle_h, down_sum_h,
    g_tokens, stage, out_rows, o_gu, o_down_in, o_out_in, o_down, o_out, o_qk, o_vg, o_ab,
    wqk, wvg, ain, bqk, bvg, bdown, low, normed, normed2, resid, g_middle, early, middle, down_sum,
    wab, bab, stage_a, g_rank, sbuf, rbuf, acc, small, wsem, send, recv, send2, recv2, *more
):
    rows, width = resid.shape
    places = ring_places()
    m = places[0]
    loads = Loads(
        [
            (bdown_h, bdown), (bqk_h, bqk), (bvg_h, bvg), (ain_h, ain), (wqk_h, wqk), (wvg_h, wvg),
            (low_h, low), (normed_h, normed), (normed2_h, normed2),
            (resid_h, resid), (g_middle_h, g_middle), (early_h, early), (middle_h, middle), (down_sum_h, down_sum),
        ],
        wsem,
    )
    loads.start(1, 2)
    loads.start(3, 4, 5, 0, 12, 13, 11)
    block = DpRows(*more[:4])
    reduce = DpSums(early, *more[4:11])
    reduce_a = DpSums(stage_a, *more[11:])
    greet_dp(block.n, block.me)
    greet_ring(places)
    ac = select.shape[1]
    n_dp = stage.shape[0]
    heads = dq.shape[1] // DK
    fill_gates(heads, wdec, bdec, wab, bab)
    scatter = RingScatter(sbuf, rbuf, acc, send, recv, places)
    six = ain.shape[1] // ac
    fold_in = fold_maps(six * ac, 0, ac)
    fold_two = fold_maps(2 * ac, six * ADAPTER_RANK, ac)

    def part(pair, put):
        sel = both_rows(select, pair, rows)
        xs = [both_rows(d, pair, rows) for d in (dq, dk, dv, dg, dab)]
        loads.wait(1, 2)
        seconds = [bqk[0], bqk[1], bvg[0], bvg[1], bab[0], bab[1]]
        for n in range(six):
            g_rank[:, n * ac : (n + 1) * ac] = (mm_nt(xs[min(n, 4)], seconds[n]) * sel).astype(BF16)
        gr = g_rank[...]
        put(slice(width, width + ac), mm(gr, fold_in) + mm(both_rows(g_rank2, pair, rows), fold_two))
        loads.wait(3, 4, 5)
        for at, size in tiles(width, 256):
            c = slice(at, at + size)
            put(
                c,
                mm_nt(xs[0], wqk[0, c])
                + mm_nt(xs[1], wqk[1, c])
                + mm_nt(xs[2], wvg[0, c])
                + mm_nt(xs[3], wvg[1, c])
                + mm(xs[4], wab[:, c])
                + mm_nt(gr, ain[c]),
            )

    deal = unfold(n_dp * 16, 16)
    parts = 16 // SHARE

    def keep(pieces, at):
        return keep_chunks(stage_a, deal, pieces, at)

    def ready():
        loads.wait(0, 12, 13)
        own = rank_down[block_rows(m, rows)]

        def value(c):
            return (middle[:, c] + down_sum[:, c].astype(F32) + mm(own, bdown[:, c])).astype(BF16)

        block.fill(index_in, rows, value)
        loads.start(6, 9, 10, 7, 8)
        wait_greetings(block.n + 1)
        loads.wait(11)
        reduce.start()

    def late():
        block.start()
        reduce.forward()
        loads.wait(6)
        at = 0
        for n, d in enumerate((dq, dk, dv, dg)):
            w = d.shape[1] // parts
            lo = low[:, n * ac : (n + 1) * ac]
            at = keep([mm_tn(lo, d[:, p * w : (p + 1) * w]) for p in range(parts)], at)
        lane = iota2((1, CH), 1)
        ga = mm_tn(low[:, 4 * ac : 5 * ac], dab[...])
        gb = mm_tn(low[:, 5 * ac : 6 * ac], dab[...])
        keep([jnp.where(lane < heads, ga, gb)], at)
        reduce_a.start()

    scatter.run(part, late, ready)
    loads.wait(9, 10)
    half = rows // 2
    for lo in (0, half):
        small[m, lo : lo + half] = scatter.total((lo, lo + half), slice(width, width + ac)).astype(BF16)
    ring = RingGather(small, send2, recv2, places)
    ring.start()
    reduce_a.forward()
    step = 16

    def back(at):
        g = scatter.total((at, at + step), slice(0, width)) * gain[...]
        v = resid[at : at + step].astype(F32)
        n = norm_factor(v)
        v = v * n
        g_tokens[at : at + step] = (
            g_middle[at : at + step] + n * (g - v * jnp.mean(g * v, axis=-1, keepdims=True))
        ).astype(BF16)

    for at in range(0, half, step):
        back(at)
    ring.forward()
    for at in range(half, rows, step):
        back(at)
    line = iota2((ac, 2 * ac), 0)
    slot = iota2((ac, 2 * ac), 1)
    inner = (slot // ac) * SHARE + slot % SHARE
    owner = ((slot % ac) // SHARE) * RING + m
    first = inner < six
    column = jnp.where(first, owner * six + inner, owner * 2 + inner - six)
    place_of = (column // ac) * ADAPTER_RANK + column % ADAPTER_RANK + jnp.where(first, 0, six * ADAPTER_RANK)
    adapter_of = (column % ac) // ADAPTER_RANK
    chosen = (line == place_of).astype(F32).astype(BF16)
    same = (line == adapter_of * ADAPTER_RANK).astype(F32).astype(BF16)

    def put_rows_out(c, val):
        out_rows[:, c] = val.astype(BF16)

    block.take(index_out, rows, put_rows_out)
    ff = o_gu.shape[2]

    def sink_early(k, cols, val):
        lo, hi = cols
        if k:
            (o_out_in, o_down, o_out)[k - 1][:, lo:hi] = val
            return
        for n in range(3):
            a, b = max(lo, n * ff), min(hi, (n + 1) * ff)
            if a < b:
                piece = val[:, a - lo : b - lo]
                if n < 2:
                    o_gu[n, :, a - n * ff : b - n * ff] = piece
                else:
                    o_down_in[:, a - n * ff : b - n * ff] = piece

    reduce.take(widths, sink_early)
    loads.wait(7, 8)
    ring.wait_left()
    ring.wait_right()
    ring.wait_opp()
    rank_sums = jnp.concatenate([small[n] for n in range(RING)], axis=0)
    picked = (mm(rank_sums, chosen) * mm(select[...], same)).astype(BF16)
    w = width // parts
    at = 0
    lane = iota2((1, ac), 1)
    upper = picked[:, 0:ac]
    lower = picked[:, ac : 2 * ac].astype(F32)
    lower_in = jnp.where(lane % SHARE < six - SHARE, lower, 0.0).astype(BF16)
    lower_two = jnp.where(lane % SHARE < six - SHARE, 0.0, lower).astype(BF16)
    at = keep_chunks(stage, deal, [mm_tn(upper, normed[:, p * w : (p + 1) * w]) for p in range(parts)], at)
    keep_chunks(
        stage,
        deal,
        [
            mm_tn(lower_in, normed[:, p * w : (p + 1) * w]) + mm_tn(lower_two, normed2[:, p * w : (p + 1) * w])
            for p in range(parts)
        ],
        at,
    )

    def sink_late(k, cols, val):
        lo, hi = cols
        if k < 2:
            o_qk[k, :, lo:hi] = val
        elif k < 4:
            o_vg[k - 2, :, lo:hi] = val
        elif lo == 0:
            o_ab[...] = val

    reduce_a.take(late_widths(dq.shape[1], dv.shape[1]), sink_late)
    scatter.finish()
    ring.finish()
    block.finish()
    reduce.finish()
    reduce_a.finish()


def late_widths(kw, vw):
    parts = 16 // SHARE
    return [kw // parts, kw // parts, vw // parts, vw // parts, CH]


def project_back(
    widths, index_in, index_out, dq, dk, dv, dg, dab, select, gain, wdec, bdec, g_rank2, rank_down,
    wqk, wvg, ain, bqk, bvg, bdown, low, normed, normed2, resid, g_middle, early, middle, down_sum, ff,
):
    rows, width = resid.shape
    ac = select.shape[1]
    n_dp = lax.axis_size("dp")
    parts = 16 // SHARE
    vm, hb = specs(1, 1)
    cols = width + ac
    kw, vw = dq.shape[1], dv.shape[1]
    late = late_widths(kw, vw)
    loaded = (wqk, wvg, ain, bqk, bvg, bdown, low, normed, normed2, resid, g_middle, early, middle, down_sum)
    return pl.pallas_call(
        functools.partial(project_back_kernel, widths),
        out_shape=(
            sds((rows, width)),
            sds((n_dp, 16, 2 * width // parts)),
            sds((rows, width)),
            sds((2, SHARE, ff), F32),
            sds((SHARE, ff), F32),
            sds((SHARE, vw), F32),
            sds((SHARE, parts * ac), F32),
            sds((SHARE, parts * ac), F32),
            sds((2, SHARE, kw), F32),
            sds((2, SHARE, vw), F32),
            sds((SHARE, CH), F32),
        ),
        in_specs=[vm] * 13 + [hb] * len(loaded),
        out_specs=[vm] * 11,
        scratch_shapes=[
            *[like(a) for a in loaded],
            pltpu.VMEM((CH, width), BF16),
            pltpu.VMEM((2, ac, CH), BF16),
            pltpu.VMEM((n_dp, 16, sum(late)), BF16),
            pltpu.VMEM((2 * rows, ain.shape[1]), BF16),
            pltpu.VMEM((6, rows // 2, cols), BF16),
            pltpu.VMEM((6, rows // 2, cols), BF16),
            pltpu.VMEM((3, rows, cols), F32),
            pltpu.VMEM((RING, rows, ac), BF16),
            DMA_SEMS((len(loaded),)), DMA_SEMS((6,)), DMA_SEMS((6,)), DMA_SEMS((6,)), DMA_SEMS((6,)),
            *rows_scratch(n_dp, width // parts), *sums_scratch(n_dp, sum(widths)), *sums_scratch(n_dp, sum(late)),
        ],
        compiler_params=ring_params(4),
        cost_estimate=pl.CostEstimate(flops=9 * 10**9, bytes_accessed=30 * 2**20, transcendentals=0),
        name="project_backward",
    )(
        index_in, index_out, dq, dk, dv, dg, dab, select, gain, wdec, bdec, g_rank2, rank_down,
        *loaded,
    )


def finish_kernel(widths, index_in, index_out, g_tokens, grads_h, rows_out, sums, grads, lsem, *scratch):
    arriving = pltpu.make_async_copy(grads_h, grads, lsem)
    arriving.start()
    rows, width = g_tokens.shape
    back = DpRows(*scratch[:4])
    reduce = DpSums(grads, *scratch[4:])
    greet_dp(back.n, back.me)
    back.fill(index_in, rows, lambda c: g_tokens[:, c])
    wait_greetings(back.n - 1)
    arriving.wait()
    reduce.start()
    back.start()
    reduce.forward()

    def put(c, val):
        rows_out[:, c] = val.astype(BF16)

    back.take(index_out, rows, put)

    def sink(k, cols, val):
        c = k * width + cols[0]
        sums[:, c : c + cols[1] - cols[0]] = val

    reduce.take(widths, sink)
    back.finish()
    reduce.finish()


def finish(collective_id, widths, index_in, index_out, g_tokens, grads):
    rows, width = g_tokens.shape
    n = lax.axis_size("dp")
    parts = 16 // SHARE
    total = grads.shape[2]
    vm, hb = specs(1, 1)
    return pl.pallas_call(
        functools.partial(finish_kernel, widths),
        out_shape=(sds((rows, width)), sds((SHARE, parts * total), F32)),
        in_specs=[vm] * 3 + [hb],
        out_specs=[vm] * 2,
        scratch_shapes=[like(grads), DMA_SEMS(()), *rows_scratch(n, width // parts), *sums_scratch(n, total)],
        compiler_params=ring_params(collective_id),
        cost_estimate=pl.CostEstimate(flops=10**9, bytes_accessed=20 * 2**20, transcendentals=0),
        name="finish_rows",
    )(index_in, index_out, g_tokens, grads)


def per_device(
    tokens,
    cotangent,
    token_grouped_position,
    sequence_lengths,
    adapter_index_per_seq,
    mixer_norm_gain,
    query_key_matrix,
    value_gate_matrix,
    decay_step_matrix,
    query_key_filters,
    value_filters,
    decay_scale_logarithm,
    decay_step_bias,
    head_output_norm_gain,
    output_matrix,
    feedfwd_norm_gain,
    gate_up_matrix,
    down_matrix,
    adapter_mixer_first,
    adapter_query_key_second,
    adapter_value_gate_second,
    adapter_decay_step_second,
    adapter_output_first,
    adapter_output_second,
    adapter_feedfwd_first,
    adapter_gate_up_second,
    adapter_down_first,
    adapter_down_second,
):
    rows = tokens.shape[0]
    width = tokens.shape[1]
    n_dp = lax.axis_size("dp")
    n_mp = lax.axis_size("mp")
    group = rows * n_mp
    share = rows // n_dp
    ac = adapter_output_second.shape[0]
    heads = decay_scale_logarithm.shape[0]

    routes = token_grouped_position.reshape(n_dp, n_mp, rows)
    def gather(x):
        return lax.all_gather(x, "mp", axis=0, tiled=True)

    def scatter(x):
        return lax.psum_scatter(x, "mp", scatter_dimension=0, tiled=True)

    fill = ((0, 0), (0, 16 - heads), (0, 0))
    w_dec = jnp.pad(jnp.swapaxes(decay_step_matrix, 1, 2), fill)
    b_dec = jnp.pad(jnp.swapaxes(adapter_decay_step_second, 1, 2), fill)
    gain_one, gain_two = mixer_norm_gain[None], feedfwd_norm_gain[None]
    index_tokens, index_slots, select, resid, cot, normed, low, pre_q, pre_k, pre_v, pre_g, pre_ab = project(
        sequence_lengths,
        adapter_index_per_seq,
        routes,
        tokens,
        cotangent,
        gain_one,
        w_dec,
        b_dec,
        query_key_matrix,
        value_gate_matrix,
        adapter_mixer_first,
        adapter_query_key_second,
        adapter_value_gate_second,
    )
    normed = normed.reshape(group, width)
    cot_later, pre_ab = lax.optimization_barrier((cot, pre_ab))
    cot_all = gather(cot_later)
    gates = (sequence_lengths, decay_scale_logarithm, decay_step_bias)
    shared = (query_key_filters, value_filters, head_output_norm_gain[None])
    mixed, *saved = mixer_fwd(*gates, pre_q, pre_k, pre_v, pre_g, pre_ab, *shared)
    middle, rank_out, normed2, rank2, gate, up, hidden, down_part, rank_part = feed(
        mixed,
        resid,
        gain_two,
        select,
        output_matrix,
        adapter_output_first,
        adapter_output_second,
        adapter_feedfwd_first,
        gate_up_matrix,
        adapter_gate_up_second,
        down_matrix,
        adapter_down_first,
    )
    normed2 = normed2.reshape(group, width)
    g_rank2, g_middle, g_mixed, rank_down, early_parts = feed_back(
        cot_all,
        rank_part,
        select,
        gain_two,
        adapter_down_second,
        down_matrix,
        adapter_down_first,
        gate_up_matrix,
        adapter_gate_up_second,
        adapter_feedfwd_first,
        adapter_output_second,
        output_matrix,
        adapter_output_first,
        rank2,
        hidden,
        mixed,
        rank_out,
        gate,
        up,
        middle,
    )
    down_later, g_mixed = lax.optimization_barrier((down_part, g_mixed))
    down_sum = scatter(down_later)
    dq, dk, dv, dg, dab = mixer_bwd(*gates, g_mixed, pre_g, pre_ab, *shared, saved)
    dq, down_sum = lax.optimization_barrier((dq, down_sum))
    widths = early_widths(gate.shape[1], dv.shape[1], ac)
    g_tokens, late_parts, out_rows, grad_gu, down_in, out_in, side_down, side_branch, grad_qk, grad_vg, gates_ab = project_back(
        widths,
        index_slots,
        index_tokens,
        dq,
        dk,
        dv,
        dg,
        dab,
        select,
        gain_one,
        w_dec,
        b_dec,
        g_rank2,
        rank_down,
        query_key_matrix,
        value_gate_matrix,
        adapter_mixer_first,
        adapter_query_key_second,
        adapter_value_gate_second,
        adapter_down_second,
        low,
        normed,
        normed2,
        resid,
        g_middle,
        early_parts,
        middle,
        down_sum,
        gate.shape[1],
    )
    parts = 16 // share
    grad_rows, late = finish(6, [width // parts] * 2, index_slots, index_tokens, g_tokens, late_parts)
    per_in = 6 * ac // (n_dp * n_mp)
    per_ffn = 2 * ac // (n_dp * n_mp)
    both = jnp.concatenate([late[:, :width], late[:, width:]], axis=0).T

    def side_out(x):
        return jnp.swapaxes(x.reshape(share, -1, ac), 0, 1).reshape(-1, ac).T

    return (
        out_rows,
        grad_rows,
        both[:, :per_in],
        grad_qk,
        grad_vg,
        jnp.stack([gates_ab[:, :heads], gates_ab[:, heads : 2 * heads]]),
        out_in.T,
        side_out(side_branch),
        both[:, per_in : per_in + per_ffn],
        grad_gu,
        down_in.T,
        side_out(side_down),
    )


def solution(mesh):
    return jax.shard_map(
        per_device,
        mesh=mesh,
        in_specs=(
            P(("dp", "mp"), None),
            P(("dp", "mp"), None),
            P(),
            P("dp", None),
            P("dp", None),
            P(),
            P(None, None, "mp"),
            P(None, None, "mp"),
            P(None, None, "mp"),
            P(None, None, "mp"),
            P(None, "mp"),
            P("mp"),
            P("mp"),
            P(),
            P("mp", None),
            P(),
            P(None, None, "mp"),
            P("mp", None),
            P(),
            P(None, None, "mp"),
            P(None, None, "mp"),
            P(None, None, "mp"),
            P("mp", None),
            P(),
            P(),
            P(None, None, "mp"),
            P("mp", None),
            P(),
        ),
        out_specs=(
            P(("dp", "mp"), None),
            P(("dp", "mp"), None),
            P(None, ("dp", "mp")),
            P(None, "dp", "mp"),
            P(None, "dp", "mp"),
            P(None, "dp", "mp"),
            P("mp", "dp"),
            P(None, ("dp", "mp")),
            P(None, ("dp", "mp")),
            P(None, "dp", "mp"),
            P("mp", "dp"),
            P(None, ("dp", "mp")),
        ),
        check_vma=False,
    )
```
